32 devices in a mesh: groups: 2 (over x), expert: 16 (over z, y, core).
Axes of the slice: x: 2, y: 2, z: 4, core: 2. Of those that a mesh axis runs over, the one named last changes fastest.
Arguments:
- resid: bfloat16 [4096, 4096], P(('groups', 'expert')), parts along dimension 0, may hold values from -6 to 6
- queries: bfloat16 [4096, 4096], P(('groups', 'expert')), parts along dimension 0, may hold values from -8 to 8
- keys: bfloat16 [4096, 256], P(('groups', 'expert')), parts along dimension 0, may hold values from -6 to 6
- values: bfloat16 [4096, 256], P(('groups', 'expert')), parts along dimension 0, may hold values from -6 to 6
- doc_ids: int32 [4096], P(('groups', 'expert')), parts along dimension 0, may hold values from 0 to 3, never falling along the last dimension, each value on 1 to 1280 neighbouring positions
- norm_gain: float32 [4096], replicated, may hold values from 0.1 to 1.9
- routes: int32 [4096, 4], P(('groups', 'expert')), parts along dimension 0, may hold values from 0 to 127, as said below
- route_weights: float32 [4096, 4], P(('groups', 'expert')), parts along dimension 0, may hold values from 0.2 to 1
- w_gate: bfloat16 [16, 4096, 384], P('expert'), may hold values from -0.09375 to 0.09375
- w_up: bfloat16 [16, 4096, 384], P('expert'), may hold values from -0.09375 to 0.09375
- w_down: bfloat16 [16, 384, 4096], P('expert'), may hold values from -0.15625 to 0.15625
Outputs:
- layer_out: bfloat16 [4096, 4096], P(('groups', 'expert')), parts along dimension 0
The draws below stay inside these ranges and needn't reach their ends.
There are 2 independent parts, one for each index of `groups`. The reference program is written for one: setup_inputs(seed, part) draws one part's arguments, and reference() takes and returns one part's arrays. A program takes and returns all parts, laid end to end along the dimension named above; an argument that names none is the same for every part. Nothing has to cross between parts.
Inputs may be any that keep to these rules, and one draw needn't show every extreme that they name: Each token names 4 different experts; in the tokens of one device no expert is named by more than 6 routes, and in every draw some expert below 4 is named by exactly 6 routes in the tokens of every device. `doc_ids`: document ids never fall along the sequence; no document is longer than 1280 tokens.
All inputs are finite; a program needn't handle non-finite values.
Results may differ from the reference program's by a relative error of at most 0.0045.
Values may be sent and summed in bfloat16 or wider, within the bound.
No kernel may reach another device: no remote copies, remote signals or barrier semaphores. Data moves between devices by JAX's collectives and lax.ppermute only.
A program may use at most 128 MiB of HBM per device.

```python
import math
import jax
import jax.numpy as jnp
import numpy as np
from jax import lax

D = 4096
HEAD_SIZE = 128
FF = 1536
EXPERTS = 128
QUERY_HEADS = 32
KEY_VALUE_HEADS = 2
TOP = 4
SHARDS = 4
DOCS = 4
TOK_DEV = 128
SEQUENCE_TOKENS = 2048
EXP_HELD = 4
HFF = 384
CAP = 6
DOC_MOST = 1280
N_EXPERT = 16


def draw_keys(key, part):
    key = jax.random.fold_in(key, 21)
    sampled_values = jnp.clip(jax.random.normal(key, (SEQUENCE_TOKENS, KEY_VALUE_HEADS * HEAD_SIZE), jnp.float32), -6.0, 6.0)
    return sampled_values.astype(jnp.bfloat16)


def draw_queries(key, part):
    key = jax.random.fold_in(key, 22)
    sampled_values = jnp.clip(jax.random.normal(key, (SEQUENCE_TOKENS, QUERY_HEADS * HEAD_SIZE), jnp.float32), -6.0, 6.0)
    return sampled_values.astype(jnp.bfloat16)


def draw_routes(key, part):
    key = jax.random.fold_in(key, 33)
    block_count_total = SEQUENCE_TOKENS // TOK_DEV
    base_load = TOK_DEV * TOP // EXPERTS
    hot_expert = jax.random.randint(jax.random.fold_in(key, 1), (), 0, EXP_HELD)

    def one_block(block_key):
        first_key, second_key, third_key = jax.random.split(block_key, 3)
        order = jax.random.permutation(first_key, EXPERTS)
        shifts = jax.random.randint(second_key, (EXPERTS // 2,), -2, 3)
        loads = jnp.zeros((EXPERTS,), jnp.int32)
        loads = loads.at[order[0::2]].set(base_load + shifts).at[order[1::2]].set(base_load - shifts)
        place = jnp.argmax(order == hot_expert).astype(jnp.int32)
        partner = order[jnp.bitwise_xor(place, 1)]
        loads = loads.at[hot_expert].set(base_load + 2).at[partner].set(base_load - 2)
        listed = jnp.repeat(jnp.arange(EXPERTS, dtype=jnp.int32), loads, total_repeat_length=TOK_DEV * TOP)
        table = listed.reshape(TOP, TOK_DEV).T
        shuffle = jax.random.permutation(third_key, TOK_DEV)
        return table[shuffle]
    block_keys = jax.random.split(jax.random.fold_in(key, 2), block_count_total)
    return jax.vmap(one_block)(block_keys).reshape(SEQUENCE_TOKENS, TOP).astype(jnp.int32)


def level_of(key, extent, cuts, least, high):
    loudness = 1.0
    for axis_at, blocks in cuts:
        heights = jax.random.uniform(jax.random.fold_in(jax.random.fold_in(key, 6), axis_at), (blocks,), jnp.float32, least / len(cuts), high / len(cuts))
        loudness = loudness * jnp.repeat(jnp.exp(heights), extent[axis_at] // blocks).reshape((-1,) + (1,) * (len(extent) - 1 - axis_at))
    return loudness


def profile(number_of, total, reach, slope):
    portions = [(1 << 20) // math.isqrt(grade ** slope) + 1 for grade in range(2, number_of + 1)]
    surplus, holding = total - reach - (number_of - 1), [1] * (number_of - 1)
    while surplus > 0:
        movable = [i for i in range(number_of - 1) if holding[i] < reach]
        mass, budget = sum([portions[i] for i in movable]), surplus
        for i in movable:
            extra = min(reach - holding[i], max(1, budget * portions[i] // mass), surplus)
            holding[i] = holding[i] + extra
            surplus = surplus - extra
    return np.array([reach] + holding)


def ragged(rng, amount, total, bound, lean):
    if amount == 2:
        one = jax.random.randint(rng, (), max(1, total - bound), min(bound, total - 1) + 1)
        return jnp.stack([one, total - one])
    lengths = jnp.asarray(profile(amount, total, bound, lean), jnp.int32)
    couples = (amount - 1) // 2
    source_of, receiver = lengths[1:1 + 2 * couples:2], lengths[2:2 + 2 * couples:2]
    margin = jnp.minimum(source_of - 1, bound - receiver)
    shifted = jax.random.randint(jax.random.fold_in(rng, 1), (couples,), 0, 1 << 20) % (margin + 1)
    lengths = lengths.at[1:1 + 2 * couples:2].set(source_of - shifted).at[2:2 + 2 * couples:2].set(receiver + shifted)
    return lengths[jax.random.permutation(jax.random.fold_in(rng, 2), amount)]


def normal_values(stream_key, dims, width, most, cuts=(), kind=jnp.bfloat16):
    values = jax.random.normal(stream_key, dims, jnp.float32) * width
    if len(cuts) > 0:
        values = level_of(stream_key, dims, cuts, -0.22, 0.18) * values
    return jnp.clip(values, min=-most, max=most).astype(kind)


def setup_inputs(seed: int = 0, part: int = 0) -> dict:
    splits = jax.random.split(jax.random.key(seed), 12)
    part_splits = jax.random.split(jax.random.fold_in(splits[11], part), 12)
    resid = normal_values(part_splits[0], (SEQUENCE_TOKENS, D), 1.0, 6.0, ((0, 16),))
    queries = draw_queries(jax.random.fold_in(jax.random.fold_in(splits[11], part), 71), part)
    keys = draw_keys(jax.random.fold_in(jax.random.fold_in(splits[11], part), 71), part)
    values = normal_values(part_splits[3], (SEQUENCE_TOKENS, KEY_VALUE_HEADS * HEAD_SIZE), 1.0, 6.0, ((0, 16),))
    doc_ids = jnp.searchsorted(jnp.cumsum(ragged(part_splits[4], DOCS, SEQUENCE_TOKENS, DOC_MOST, 2)), jnp.arange(SEQUENCE_TOKENS), side="right").astype(jnp.int32)
    norm_gain = jnp.clip(1.0 + 0.18 * jax.random.normal(splits[5], (D,), jnp.float32), 0.1, 1.9)
    routes = draw_routes(jax.random.fold_in(jax.random.fold_in(splits[11], part), 71), part)
    route_weights = jnp.clip(0.2 + 0.8 * jax.random.uniform(part_splits[7], (SEQUENCE_TOKENS, TOP), jnp.float32) ** level_of(part_splits[7], (SEQUENCE_TOKENS, TOP), ((0, 16),), -0.2, 0.2), 0.2, 1.0)
    w_gate = normal_values(splits[8], (N_EXPERT, D, HFF), D ** -0.5, 0.09375, ((0, 16),))
    w_up = normal_values(splits[9], (N_EXPERT, D, HFF), D ** -0.5, 0.09375, ((0, 16),))
    w_down = normal_values(splits[10], (N_EXPERT, HFF, D), FF ** -0.5, 0.15625, ((0, 16),))
    return dict(resid=resid, queries=queries, keys=keys, values=values, doc_ids=doc_ids, norm_gain=norm_gain, routes=routes, route_weights=route_weights, w_gate=w_gate, w_up=w_up, w_down=w_down)


large_negative_fill = -1e+30

def attend_block(carried, query_head_stack, query_docs, query_pos, key_tile_block, value_tile_block, doc_block, key_pos):
    allowed = (key_pos[None, :] <= query_pos[:, None]) & (doc_block[None, :] == query_docs[:, None])
    score_scale = 1.0 / math.sqrt(HEAD_SIZE)

    def update(current):
        run_max, run_sum, run_acc = current
        scores = jnp.einsum('qhgd,rhd->hgqr', query_head_stack, key_tile_block, precision=lax.Precision.HIGHEST) * score_scale
        scores = jnp.where(allowed[None, None], scores, large_negative_fill)
        new_max = jnp.maximum(run_max, lax.optimization_barrier(jnp.max(scores, axis=-1)))
        factor = jnp.exp(run_max - new_max)
        weights = jnp.where(allowed[None, None], jnp.exp(scores - new_max[..., None]), 0.0)
        rounded = weights.astype(jnp.bfloat16).astype(jnp.float32)
        new_acc = run_acc * factor[..., None] + jnp.einsum('hgqr,rhd->hgqd', rounded, value_tile_block, precision=lax.Precision.HIGHEST)
        return (new_max, run_sum * factor + lax.optimization_barrier(jnp.sum(weights, axis=-1)), new_acc)
    return lax.cond(jnp.any(allowed), update, lambda current: current, carried)

def reference(resid, queries, keys, values, doc_ids, norm_gain, routes, route_weights, w_gate, w_up, w_down):
    query_group_width = QUERY_HEADS // KEY_VALUE_HEADS
    rows_per_block = math.gcd(SEQUENCE_TOKENS, 512)
    block_count_total = SEQUENCE_TOKENS // rows_per_block
    every_query_row = queries.astype(jnp.float32).reshape(block_count_total, rows_per_block, KEY_VALUE_HEADS, query_group_width, HEAD_SIZE)
    every_key_row = keys.astype(jnp.float32).reshape(block_count_total, rows_per_block, KEY_VALUE_HEADS, HEAD_SIZE)
    every_value_row = values.astype(jnp.float32).reshape(block_count_total, rows_per_block, KEY_VALUE_HEADS, HEAD_SIZE)
    doc_all = doc_ids.reshape(block_count_total, rows_per_block)
    local_rows = jnp.arange(rows_per_block, dtype=jnp.int32)

    def query_block(query_index):
        query_head_stack = every_query_row[query_index]
        query_docs = doc_all[query_index]
        query_pos = query_index * rows_per_block + local_rows

        def key_step(carried, key_index):
            key_pos = key_index * rows_per_block + local_rows
            result = attend_block(carried, query_head_stack, query_docs, query_pos, every_key_row[key_index], every_value_row[key_index], doc_all[key_index], key_pos)
            return (result, None)
        initial_state = (jnp.full((KEY_VALUE_HEADS, query_group_width, rows_per_block), large_negative_fill, jnp.float32), jnp.zeros((KEY_VALUE_HEADS, query_group_width, rows_per_block), jnp.float32), jnp.zeros((KEY_VALUE_HEADS, query_group_width, rows_per_block, HEAD_SIZE), jnp.float32))
        final_state, _ = lax.scan(key_step, initial_state, jnp.arange(block_count_total, dtype=jnp.int32))
        averaged = final_state[2] / final_state[1][..., None]
        return jnp.transpose(averaged, (2, 0, 1, 3)).reshape(rows_per_block, D)
    attn = lax.map(query_block, jnp.arange(block_count_total, dtype=jnp.int32)).reshape(SEQUENCE_TOKENS, D)
    hstate = resid.astype(jnp.float32) + attn
    normed = (hstate * lax.rsqrt(lax.optimization_barrier(jnp.mean(hstate * hstate, axis=-1, keepdims=True)) + 1e-06) * norm_gain).astype(jnp.bfloat16)
    held_count = N_EXPERT // SHARDS
    route_total = TOK_DEV * TOP
    flat_routes = routes.reshape(N_EXPERT, route_total)
    flat_weights = route_weights.reshape(N_EXPERT, route_total)
    member = (flat_routes[:, :, None] == jnp.arange(held_count, dtype=jnp.int32)[None, None, :]).astype(jnp.int32)
    route_ranks = lax.optimization_barrier(jnp.sum((jnp.cumsum(member, axis=1) - 1) * member, axis=2))
    expert_slot = jnp.where(flat_routes < held_count, flat_routes, held_count)
    token_index = (jnp.arange(route_total, dtype=jnp.int32) // TOP)[None, :] + (jnp.arange(N_EXPERT, dtype=jnp.int32) * TOK_DEV)[:, None]
    block_index = jnp.broadcast_to(jnp.arange(N_EXPERT, dtype=jnp.int32)[:, None], (N_EXPERT, route_total))
    slot_token = jnp.zeros((N_EXPERT, held_count, CAP), jnp.int32).at[block_index, expert_slot, route_ranks].set(token_index, mode='drop')
    slot_weight = jnp.zeros((N_EXPERT, held_count, CAP), jnp.float32).at[block_index, expert_slot, route_ranks].set(flat_weights, mode='drop')

    def expert_step(mixture, expert_index):
        picked = slot_token[:, expert_index, :].reshape(-1)
        rows_in = normed[picked]
        summed = jnp.zeros((N_EXPERT * CAP, D), jnp.float32)
        for block_part in range(SHARDS):
            weight_index = expert_index * SHARDS + block_part
            gate_part = jnp.dot(rows_in, w_gate[weight_index], preferred_element_type=jnp.float32)
            up_part = jnp.dot(rows_in, w_up[weight_index], preferred_element_type=jnp.float32)
            hidden = (jax.nn.silu(gate_part) * up_part).astype(jnp.bfloat16)
            partial_value = jnp.dot(hidden, w_down[weight_index], preferred_element_type=jnp.float32).astype(jnp.bfloat16)
            summed = summed + lax.optimization_barrier(partial_value).astype(jnp.float32)
        weighted = summed * slot_weight[:, expert_index, :].reshape(-1)[:, None]
        return (mixture.at[picked].add(weighted), None)
    mixture, _ = lax.scan(expert_step, jnp.zeros((SEQUENCE_TOKENS, D), jnp.float32), jnp.arange(held_count, dtype=jnp.int32))
    return (hstate + mixture).astype(jnp.bfloat16)
```

```python
import functools
import math

import jax
import jax.numpy as jnp
from jax import lax
from jax.experimental import pallas as pl
from jax.experimental.pallas import tpu as pltpu
from jax.sharding import PartitionSpec as P

HEAD = 128
QUERY_HEADS = 32
KV_HEADS = 2
GROUP = QUERY_HEADS // KV_HEADS
SHARDS = 4
SLOTS = 8
TILE = 128
KEYS = 256
MSG = 256
PLANES = 4
LANES = PLANES * GROUP * SLOTS
SCALE = math.log2(math.e) / math.sqrt(HEAD)
LOW = -1e30
F32 = jnp.float32
BF16 = jnp.bfloat16
VMEM = pl.BlockSpec(memory_space=pltpu.VMEM)
SMEM = pl.BlockSpec(memory_space=pltpu.SMEM)
ANY = pl.BlockSpec(memory_space=pl.ANY)


def dot(a, b, ca=1, cb=0):
    return lax.dot_general(a, b, (((ca,), (cb,)), ((), ())), preferred_element_type=F32)


def slot_rows(routes, experts):
    members = jnp.concatenate(
        [
            jnp.max((routes == e).astype(F32), axis=0, keepdims=True)
            for e in experts
        ],
        axis=0,
    )
    count = len(experts)
    padded = -(-count // 8) * 8
    wide = members
    if padded > count:
        wide = jnp.concatenate([members, jnp.zeros((padded - count, TILE), F32)], axis=0)
    before = lax.broadcasted_iota(jnp.int32, (TILE, TILE), 0) < lax.broadcasted_iota(
        jnp.int32, (TILE, TILE), 1
    )
    ranks = dot(wide.astype(BF16), before.astype(F32).astype(BF16))
    return members, ranks


def pack_kernel(planes, pos_ref, routes_ref, docs_ref, keys_ref, values_ref, q_ref, x_ref, *outs):
    z = pos_ref[0] // SHARDS
    routes = routes_ref[...]
    experts = [lax.rem(z + k, planes) for k in range(planes)]
    members, ranks = slot_rows(routes, experts)
    docs = docs_ref[...].astype(F32)
    lane_slot = (lax.broadcasted_iota(jnp.int32, (TILE, TILE), 0) % SLOTS).astype(F32)
    token = lax.broadcasted_iota(jnp.int32, (1, TILE), 1).astype(F32)
    facts = jnp.concatenate(
        [token, docs, jnp.ones((1, TILE), F32), jnp.zeros((5, TILE), F32)], axis=0
    ).astype(BF16)
    picks = [
        jnp.where(ranks[k : k + 1] == lane_slot, members[k : k + 1], 0.0) for k in range(planes)
    ]
    chooser = jnp.concatenate([p[:SLOTS] for p in picks], axis=0).astype(BF16)
    q_rows = dot(chooser, q_ref[...])
    x_rows = dot(chooser, x_ref[...])
    value_t = jnp.concatenate(
        [
            values_ref[:, h * HEAD : (h + 1) * HEAD].astype(F32).T.astype(BF16)
            for h in range(KV_HEADS)
        ],
        axis=1,
    )
    keys = keys_ref[...]
    row = lax.broadcasted_iota(jnp.int32, (SLOTS, TILE), 0)
    for k in range(planes):
        out = outs[k]
        out[0:TILE, 0:256] = keys
        out[0:TILE, 256:512] = value_t
        known = dot(facts, picks[k].astype(BF16), 1, 1)
        place = known[0:1]
        doc = known[1:2] + (1.0 - known[2:3]) * docs[:, 0:1]
        for half, rows in ((TILE, q_rows), (TILE + 64, x_rows)):
            for pair in range(QUERY_HEADS // 2):
                two = []
                for a in (2 * pair, 2 * pair + 1):
                    block = rows[k * SLOTS : (k + 1) * SLOTS, a * HEAD : (a + 1) * HEAD]
                    if half == TILE and a == 0:
                        block = jnp.where(row == 6, docs, jnp.where(row == 7, place, block))
                    if half == TILE and a == 2:
                        block = jnp.where(row == 6, doc, block)
                    two.append(block)
                at = half + 16 * (pair // 4)
                lane = (pair % 4) * HEAD
                out[at : at + 16, lane : lane + HEAD] = jnp.concatenate(two, axis=0).astype(BF16)


def load_pieces(planes, pos, pieces, held, sems, rows):
    z, y, c = pos // SHARDS, (pos // 2) % 2, pos % 2
    copies = []
    for flip_c in range(2):
        for flip_y in range(2):
            for k in range(planes):
                at = len(copies)
                sender = (
                    lax.rem(z - k + planes, planes) * SHARDS + (y ^ flip_y) * 2 + (c ^ flip_c)
                )
                copy = pltpu.make_async_copy(
                    pieces[at].at[pl.ds(0, rows)], held.at[sender, pl.ds(0, rows)], sems.at[at]
                )
                copy.start()
                copies.append(copy)
    return copies


def doc_starts(n, held):
    sums = [jnp.zeros((1, TILE), F32) for _ in range(3)]
    for s in range(n):
        docs = held[s, TILE : TILE + 16, 0:HEAD].astype(F32)[6:7]
        for d in range(3):
            sums[d] = sums[d] + jnp.where(docs < d + 1.0, 1.0, 0.0)
    return [jnp.sum(s, axis=1, keepdims=True) for s in sums]


def starts_of(docs, starts):
    first = jnp.zeros_like(docs)
    for d in range(3):
        first = jnp.where(docs == d + 1.0, starts[d], first)
    return first


def flash(held, q_refs, kv_heads, acc_ref, place, first, low, high):
    lanes = place.shape[1]
    chains = len(q_refs)
    for i in range(chains):
        acc_ref[i] = jnp.zeros((HEAD, lanes), F32)

    def step(kb, carried):
        key_at = (
            kb * KEYS + lax.broadcasted_iota(jnp.int32, (KEYS, 1), 0)
        ).astype(F32)
        allowed = (key_at >= first) & (key_at <= place)
        out = []
        for i in range(chains):
            top, total = carried[2 * i], carried[2 * i + 1]
            h = kv_heads[i]
            keys = jnp.concatenate(
                [held[2 * kb + t, 0:TILE, h * HEAD : (h + 1) * HEAD] for t in range(2)], axis=0
            )
            values = jnp.concatenate(
                [held[2 * kb + t, 0:TILE, 256 + h * HEAD : 384 + h * HEAD] for t in range(2)],
                axis=1,
            )
            scores = jnp.where(allowed, dot(keys, q_refs[i][...], 1, 1), LOW)
            new_top = jnp.maximum(top, jnp.max(scores, axis=0, keepdims=True))
            factor = jnp.exp2((top - new_top) * SCALE)
            weights = jnp.exp2((scores - new_top) * SCALE)
            acc_ref[i] = acc_ref[i] * factor + dot(values, weights.astype(BF16))
            out += [new_top, total * factor + jnp.sum(weights, axis=0, keepdims=True)]
        return tuple(out)

    init = (jnp.full((1, lanes), LOW, F32), jnp.zeros((1, lanes), F32)) * chains
    final = lax.fori_loop(low, high, step, init)
    return [(acc_ref[i] / final[2 * i + 1]).T for i in range(chains)]


def expert_kernel(n, pos_ref, gain_ref, *refs):
    planes = n // SHARDS
    pieces = refs[:n]
    weights = refs[n : n + 3]
    keep_ref, send_ref = refs[n + 3 : n + 5]
    held, q_scr, acc, state, wg, wu, wd, sems = refs[n + 5 :]
    pos = pos_ref[0]
    z, y, c = pos // SHARDS, (pos // 2) % 2, pos % 2
    copies = load_pieces(planes, pos, pieces, held, sems, MSG)
    loads = []
    for i, (src, dst) in enumerate(zip(weights, (wg, wu, wd))):
        load = pltpu.make_async_copy(src.at[0], dst, sems.at[n + i])
        load.start()
        loads.append(load)
    for copy in copies:
        copy.wait()
    starts = doc_starts(n, held)
    groups = planes // PLANES

    def attend(group, kk):
        plane = lax.rem(z + group * PLANES + kk, planes)
        senders = [
            plane * SHARDS + (y ^ flip_y) * 2 + (c ^ flip_c)
            for flip_c in range(2)
            for flip_y in range(2)
        ]
        place, docs = [], []
        for i, s in enumerate(senders):
            place.append(
                held[s, TILE : TILE + 16, 0:HEAD].astype(F32)[7:8]
                + (s * TILE).astype(F32)
            )
            docs.append(held[s, TILE : TILE + 16, HEAD : 2 * HEAD].astype(F32)[6:7])
            for a in range(QUERY_HEADS // 2):
                at = TILE + 16 * (a // 4)
                lane = (a % 4) * HEAD
                q_scr[a // 8, i * TILE + (a % 8) * 16 : i * TILE + (a % 8) * 16 + 16, :] = held[
                    s, at : at + 16, lane : lane + HEAD
                ]
        place = jnp.concatenate(place, axis=1)
        first = starts_of(jnp.concatenate(docs, axis=1), starts)
        low = jnp.min(first).astype(jnp.int32) // KEYS
        high = (plane + 1) * (SHARDS * TILE // KEYS)
        done = flash(held, [q_scr.at[0], q_scr.at[1]], [0, 1], acc, place, first, low, high)
        row = pl.multiple_of(kk * SLOTS, SLOTS)
        for i, s in enumerate(senders):
            for a in range(QUERY_HEADS // 2):
                at = TILE + 64 + 16 * (a // 4)
                lane = (a % 4) * HEAD
                resid = held[s, at : at + 16, lane : lane + HEAD].astype(F32)
                rows = done[a // 8][i * TILE + (a % 8) * 16 : i * TILE + (a % 8) * 16 + 16]
                total = resid + rows
                state[pl.ds(i * PLANES * SLOTS + row, SLOTS), 2 * a * HEAD : (2 * a + 1) * HEAD] = (
                    total[0:SLOTS]
                )
                state[
                    pl.ds(i * PLANES * SLOTS + row, SLOTS),
                    (2 * a + 1) * HEAD : (2 * a + 2) * HEAD,
                ] = total[SLOTS:]

    def group_step(group):
        lax.fori_loop(0, PLANES, lambda kk, _: (attend(group, kk), 0)[1], 0)
        hidden = state[...]
        mean = jnp.mean(hidden * hidden, axis=1, keepdims=True)
        normed = (hidden * lax.rsqrt(mean + 1e-06) * gain_ref[...]).astype(BF16)
        if groups == 1:
            for load in loads:
                load.wait()
        gate = dot(normed, wg[...])
        up = dot(normed, wu[...])
        act = (gate / (1.0 + jnp.exp(-gate)) * up).astype(BF16)
        width = 1024
        for col in range(0, hidden.shape[1], width):
            part = dot(act, wd[:, col : col + width]).astype(BF16)
            half = 2 * PLANES * SLOTS
            keep_ref[group, :, col : col + width] = part[:half]
            send_ref[group, :, col : col + width] = part[half:]

    if groups == 1:
        group_step(0)
    else:
        for load in loads:
            load.wait()
        lax.fori_loop(0, groups, lambda g, _: (group_step(g), 0)[1], 0)


def own_kernel(n, kv_head, pos_ref, q_ref, x_ref, _, *refs):
    pieces = refs[:n]
    h_ref = refs[n]
    held, q_scr, acc, sems = refs[n + 1 :]
    pos = pos_ref[0]
    copies = load_pieces(n // SHARDS, pos, pieces, held, sems, TILE + 16)
    for a in range(GROUP):
        q_scr[a // 4, (a % 4) * TILE : (a % 4 + 1) * TILE, :] = q_ref[:, a * HEAD : (a + 1) * HEAD]
    for copy in copies:
        copy.wait()
    starts = doc_starts(n, held)
    docs = held[pos, TILE : TILE + 16, 0:HEAD].astype(F32)[6:7]
    first = starts_of(docs, starts)
    low = jnp.min(first).astype(jnp.int32) // KEYS
    high = pos // (KEYS // TILE) + 1
    place = (pos * TILE + lax.broadcasted_iota(jnp.int32, (1, TILE), 1)).astype(F32)
    place = jnp.concatenate([place] * 4, axis=1)
    first = jnp.concatenate([first] * 4, axis=1)
    for pair in range(2):
        done = flash(
            held,
            [q_scr.at[2 * pair], q_scr.at[2 * pair + 1]],
            [kv_head, kv_head],
            acc,
            place,
            first,
            low,
            high,
        )
        for i in range(2):
            for g in range(4):
                lane = (pair * 8 + i * 4 + g) * HEAD
                h_ref[:, lane : lane + HEAD] = (
                    x_ref[:, lane : lane + HEAD].astype(F32) + done[i][g * TILE : (g + 1) * TILE]
                )


def combine_kernel(planes, pos_ref, routes_ref, gates_ref, h0_ref, h1_ref, *refs):
    parts, out_ref = refs[:planes], refs[planes]
    z = pos_ref[0] // SHARDS
    routes = routes_ref[...]
    gates = gates_ref[...]
    experts = [lax.rem(z - k + planes, planes) for k in range(planes)]
    members, ranks = slot_rows(routes, experts)
    slot = lax.broadcasted_iota(jnp.int32, (SLOTS, TILE), 0).astype(F32)
    mix = []
    for k, e in enumerate(experts):
        gate = jnp.sum(jnp.where(routes == e, gates, 0.0), axis=0, keepdims=True)
        mix.append(jnp.where(ranks[k : k + 1] == slot, gate, 0.0))
    mix = jnp.concatenate(mix, axis=0).T
    mix_high = mix.astype(BF16)
    mix_low = (mix - mix_high.astype(F32)).astype(BF16)
    rows = jnp.concatenate([p[...].astype(F32) for p in parts], axis=0).astype(BF16)
    half = h0_ref.shape[1]
    for i, h in enumerate((h0_ref, h1_ref)):
        part = rows[:, i * half : (i + 1) * half]
        out_ref[:, i * half : (i + 1) * half] = (
            h[...] + dot(mix_high, part) + dot(mix_low, part)
        ).astype(BF16)


def params(mib):
    return pltpu.CompilerParams(vmem_limit_bytes=mib * 1024 * 1024)


def local(
    resid, queries, keys, values, doc_ids, norm_gain, routes, route_weights, w_gate, w_up, w_down
):
    n = lax.axis_size("expert")
    planes = n // SHARDS
    index = lax.axis_index("expert")
    pos = index.astype(jnp.int32).reshape(1)
    tokens, width = queries.shape
    hidden = w_gate.shape[2]
    routes_t = routes.T
    gates_t = route_weights.T
    message = jax.ShapeDtypeStruct((MSG, 512), BF16)

    messages = pl.pallas_call(
        functools.partial(pack_kernel, planes),
        out_shape=[message] * planes,
        in_specs=[SMEM] + [VMEM] * 6,
        out_specs=[VMEM] * planes,
        compiler_params=params(40),
        name="pack",
    )(pos, routes_t, doc_ids.reshape(1, tokens), keys, values, queries, resid)

    def move(value, target):
        return lax.ppermute(value, "expert", [(s, target(s)) for s in range(n)])

    pieces = [messages[0]]
    for k in range(1, planes):
        pieces.append(move(messages[k], lambda s: (s + k * SHARDS) % n))
    pieces = pieces + [move(p, lambda s: s ^ 2) for p in pieces]
    pieces = pieces + [move(p, lambda s: s ^ 1) for p in pieces]

    groups = planes // PLANES
    half = jax.ShapeDtypeStruct((groups, 2 * PLANES * SLOTS, width), BF16)
    keep, send = pl.pallas_call(
        functools.partial(expert_kernel, n),
        out_shape=[half, half],
        in_specs=[SMEM, VMEM] + [ANY] * (n + 3),
        out_specs=[VMEM, VMEM],
        scratch_shapes=[
            pltpu.VMEM((n, MSG, 512), BF16),
            pltpu.VMEM((KV_HEADS, LANES, HEAD), BF16),
            pltpu.VMEM((KV_HEADS, HEAD, LANES), F32),
            pltpu.VMEM((4 * PLANES * SLOTS, width), F32),
            pltpu.VMEM((width, hidden), BF16),
            pltpu.VMEM((width, hidden), BF16),
            pltpu.VMEM((hidden, width), BF16),
            pltpu.SemaphoreType.DMA((n + 3,)),
        ],
        compiler_params=params(40 if n <= 16 else 60),
        cost_estimate=pl.CostEstimate(
            flops=4_000_000_000, bytes_accessed=16_000_000, transcendentals=4_000_000
        ),
        name="expert",
    )(pos, norm_gain.reshape(1, width), *pieces, w_gate, w_up, w_down)

    halves = []
    for h in range(KV_HEADS):
        columns = slice(h * width // 2, (h + 1) * width // 2)
        halves.append(
            pl.pallas_call(
                functools.partial(own_kernel, n, h),
                out_shape=jax.ShapeDtypeStruct((tokens, width // 2), F32),
                in_specs=[
                    SMEM,
                    pl.BlockSpec((tokens, width // 2), lambda i, h=h: (0, h)),
                    pl.BlockSpec((tokens, width // 2), lambda i, h=h: (0, h)),
                    ANY,
                ]
                + [ANY] * n,
                out_specs=pl.BlockSpec((tokens, width // 2), lambda i: (0, 0)),
                grid=(1,),
                scratch_shapes=[
                    pltpu.VMEM((n, TILE + 16, 512), BF16),
                    pltpu.VMEM((4, 4 * TILE, HEAD), BF16),
                    pltpu.VMEM((2, HEAD, 4 * TILE), F32),
                    pltpu.SemaphoreType.DMA((n,)),
                ],
                compiler_params=params(40),
                cost_estimate=pl.CostEstimate(
                    flops=4_000_000_000, bytes_accessed=8_000_000, transcendentals=4_000_000
                ),
                name="own",
            )(pos, queries, resid, keep, *pieces)
        )

    total = keep.astype(F32) + move(send, lambda s: s ^ 1).astype(F32)
    quarter = PLANES * SLOTS
    other = move(total[:, quarter:].astype(BF16), lambda s: s ^ 2)
    total = (total[:, :quarter] + other.astype(F32)).astype(BF16)
    total = total.reshape(planes, SLOTS, width)
    parts = [total[0]]
    for k in range(1, planes):
        parts.append(move(total[k], lambda s: (s + k * SHARDS) % n))

    return pl.pallas_call(
        functools.partial(combine_kernel, planes),
        out_shape=jax.ShapeDtypeStruct((tokens, width), BF16),
        in_specs=[SMEM] + [VMEM] * (4 + planes),
        out_specs=VMEM,
        compiler_params=params(40),
        name="combine",
    )(pos, routes_t, gates_t, *halves, *parts)


def solution(mesh):
    rows = P(("groups", "expert"), None)
    in_specs = (rows,) * 4 + (P(("groups", "expert")), P(), rows, rows) + (
        P("expert", None, None),
    ) * 3
    return jax.shard_map(local, mesh=mesh, in_specs=in_specs, out_specs=rows, check_vma=False)
```

```python
import functools
import math

import jax
import jax.numpy as jnp
from jax import lax
from jax.experimental import pallas as pl
from jax.experimental.pallas import tpu as pltpu
from jax.sharding import PartitionSpec as P

HEAD = 128
QUERY_HEADS = 32
KV_HEADS = 2
GROUP = QUERY_HEADS // KV_HEADS
SHARDS = 4
SLOTS = 8
TILE = 128
KEYS = 256
KV_ROWS = TILE + 16
SCALE = math.log2(math.e) / math.sqrt(HEAD)
LOW = -1e30
F32 = jnp.float32
BF16 = jnp.bfloat16
VMEM = pl.BlockSpec(memory_space=pltpu.VMEM)
SMEM = pl.BlockSpec(memory_space=pltpu.SMEM)
ANY = pl.BlockSpec(memory_space=pl.ANY)
HBM = pl.BlockSpec(memory_space=pltpu.HBM)


def dot(a, b, ca=1, cb=0):
    return lax.dot_general(a, b, (((ca,), (cb,)), ((), ())), preferred_element_type=F32)


def reach(n):
    longest = n * TILE // 2 + 256
    return (longest - 1 + TILE - 1) // TILE


def slot_rows(routes, experts):
    members = jnp.concatenate(
        [jnp.max((routes == e).astype(F32), axis=0, keepdims=True) for e in experts], axis=0
    )
    count = len(experts)
    padded = -(-count // 8) * 8
    wide = members
    if padded > count:
        wide = jnp.concatenate([members, jnp.zeros((padded - count, TILE), F32)], axis=0)
    before = lax.broadcasted_iota(jnp.int32, (TILE, TILE), 0) < lax.broadcasted_iota(
        jnp.int32, (TILE, TILE), 1
    )
    ranks = dot(wide.astype(BF16), before.astype(F32).astype(BF16))
    return members, ranks


def pack_kernel(docs_ref, keys_ref, values_ref, out_ref, docs, values, sems):
    moves = [
        pltpu.make_async_copy(values_ref, values, sems.at[0]),
        pltpu.make_async_copy(docs_ref, docs, sems.at[1]),
        pltpu.make_async_copy(
            keys_ref, out_ref.at[pl.ds(0, TILE), pl.ds(0, KV_HEADS * HEAD)], sems.at[2]
        ),
    ]
    for move in moves:
        move.start()
    moves[0].wait()
    for h in range(KV_HEADS):
        out_ref[0:TILE, (KV_HEADS + h) * HEAD : (KV_HEADS + h + 1) * HEAD] = (
            values[:, h * HEAD : (h + 1) * HEAD].astype(F32).T.astype(BF16)
        )
    moves[1].wait()
    out_ref[TILE:KV_ROWS, :] = jnp.zeros((KV_ROWS - TILE, 4 * HEAD), BF16)
    out_ref[TILE:KV_ROWS, 0:HEAD] = jnp.broadcast_to(
        docs[...].astype(F32), (KV_ROWS - TILE, TILE)
    ).astype(BF16)
    moves[2].wait()


def select_kernel(planes, pos_ref, routes_ref, docs_ref, q_ref, x_ref, qs_ref, xs_ref, facts_ref):
    z = pos_ref[0] // SHARDS
    members, ranks = slot_rows(routes_ref[...], [lax.rem(z + k, planes) for k in range(planes)])
    docs = docs_ref[...].astype(F32)
    lane_slot = (lax.broadcasted_iota(jnp.int32, (TILE, TILE), 0) % SLOTS).astype(F32)
    token = lax.broadcasted_iota(jnp.int32, (1, TILE), 1).astype(F32)
    facts = jnp.concatenate(
        [token, docs, jnp.ones((1, TILE), F32), jnp.zeros((5, TILE), F32)], axis=0
    ).astype(BF16)
    picks = [
        jnp.where(ranks[k : k + 1] == lane_slot, members[k : k + 1], 0.0) for k in range(planes)
    ]
    chooser = jnp.concatenate([p[:SLOTS] for p in picks], axis=0).astype(BF16)
    q_rows = dot(chooser, q_ref[...])
    xs_ref[...] = dot(chooser, x_ref[...])
    for k in range(planes):
        known = dot(facts, picks[k].astype(BF16), 1, 1)
        facts_ref[:, k * TILE : (k + 1) * TILE] = jnp.concatenate(
            [known[0:1], known[1:2] + (1.0 - known[2:3]) * docs[:, 0:1], known[2:]], axis=0
        )
        for h in range(KV_HEADS):
            for g in range(0, GROUP, 2):
                a = h * GROUP + g
                two = jnp.concatenate(
                    [
                        q_rows[k * SLOTS : (k + 1) * SLOTS, i * HEAD : (i + 1) * HEAD]
                        for i in (a, a + 1)
                    ],
                    axis=0,
                )
                at = k * TILE + g * SLOTS
                qs_ref[h, at : at + 2 * SLOTS, :] = two.astype(BF16)


def doc_starts(n, pos, held):
    sums = [jnp.zeros((1, TILE), F32) for _ in range(3)]
    for s in range(n):
        docs = held[s, TILE:KV_ROWS, 0:HEAD].astype(F32)[0:1]
        ahead = (pos - s < 0).astype(F32)
        behind = (pos - s > reach(n)).astype(F32)
        known = 1.0 - ahead - behind
        docs = jnp.where(known > 0.5, docs, 0.0) + 9.0 * ahead
        for d in range(3):
            sums[d] = sums[d] + jnp.where(docs < d + 1.0, 1.0, 0.0)
    return [jnp.sum(s, axis=1, keepdims=True) for s in sums]


def starts_of(docs, starts):
    first = jnp.zeros_like(docs)
    for d in range(3):
        first = jnp.where(docs == d + 1.0, starts[d], first)
    return first


def flash(pos, held, queries, kv_heads, acc_ref, bias_ref, place, first):
    lanes = place.shape[1]
    chains = len(queries)
    for i in range(chains):
        acc_ref[i] = jnp.zeros((HEAD, lanes), F32)
    low = jnp.min(first).astype(jnp.int32) // KEYS
    last = pos // (KEYS // TILE)
    clear = (jnp.max(first).astype(jnp.int32) + KEYS - 1) // KEYS
    middle = jnp.minimum(clear, last)

    def step(kb, carried, masked):
        if masked:
            key_at = (kb * KEYS + lax.broadcasted_iota(jnp.int32, (KEYS, 1), 0)).astype(F32)
            bias_ref[...] = jnp.where((key_at >= first) & (key_at <= place), 0.0, LOW)
        out = []
        for i in range(chains):
            top, total = carried[2 * i], carried[2 * i + 1]
            h = kv_heads[i]
            keys = jnp.concatenate(
                [held[2 * kb + t, 0:TILE, h * HEAD : (h + 1) * HEAD] for t in range(2)], axis=0
            )
            values = jnp.concatenate(
                [
                    held[2 * kb + t, 0:TILE, (KV_HEADS + h) * HEAD : (KV_HEADS + h + 1) * HEAD]
                    for t in range(2)
                ],
                axis=1,
            )
            scores = dot(keys, queries[i](), 1, 1)
            if masked:
                scores = scores + bias_ref[...]
            new_top = jnp.maximum(top, jnp.max(scores, axis=0, keepdims=True))
            factor = jnp.exp2((top - new_top) * SCALE)
            weights = jnp.exp2((scores - new_top) * SCALE)
            acc_ref[i] = acc_ref[i] * factor + dot(values, weights.astype(BF16))
            out += [new_top, total * factor + jnp.sum(weights, axis=0, keepdims=True)]
        return tuple(out)

    state = (jnp.full((1, lanes), LOW, F32), jnp.zeros((1, lanes), F32)) * chains
    state = lax.fori_loop(low, middle, functools.partial(step, masked=True), state)
    state = lax.fori_loop(middle, last, functools.partial(step, masked=False), state)
    state = step(last, state, True)
    return [(acc_ref[i] / state[2 * i + 1]).T for i in range(chains)]


def routed_kernel(n, senders, pos_ref, gain_ref, qs_ref, xs_ref, facts_ref, *refs):
    planes = n // SHARDS
    count = len(senders)
    pieces = refs[:count]
    outs = refs[count : count + planes]
    held = refs[count + planes]
    acc, bias, state, sems = refs[count + planes + 1 :]
    pos = pos_ref[0]
    z, y, c = pos // SHARDS, (pos // 2) % 2, pos % 2
    copies = []
    for i, (flip_c, flip_y, k) in enumerate(senders):
        sender = lax.rem(z - k + planes, planes) * SHARDS + (y ^ flip_y) * 2 + (c ^ flip_c)
        copies.append(pltpu.make_async_copy(pieces[i], held.at[sender], sems.at[i]))
    for copy in copies:
        copy.start()
    for copy in copies:
        copy.wait()
    starts = doc_starts(n, pos, held)
    lanes = 2 * TILE
    base = (pos * TILE).astype(F32)
    for part in range(planes // 2):
        at = part * lanes
        place = facts_ref[0:1, at : at + lanes] + base
        first = starts_of(facts_ref[1:2, at : at + lanes], starts)
        done = flash(
            pos,
            held,
            [lambda h=h, at=at: qs_ref[h, at : at + lanes, :] for h in range(KV_HEADS)],
            list(range(KV_HEADS)),
            acc,
            bias,
            place,
            first,
        )
        for h in range(KV_HEADS):
            for k in range(2):
                row = (part * 2 + k) * SLOTS
                for g in range(GROUP):
                    lane = (h * GROUP + g) * HEAD
                    state[row : row + SLOTS, lane : lane + HEAD] = (
                        xs_ref[row : row + SLOTS, lane : lane + HEAD]
                        + done[h][k * TILE + g * SLOTS : k * TILE + (g + 1) * SLOTS]
                    )
    for k in range(planes):
        hidden = state[k * SLOTS : (k + 1) * SLOTS, :]
        mean = jnp.mean(hidden * hidden, axis=1, keepdims=True)
        outs[k][...] = (hidden * lax.rsqrt(mean + 1e-06) * gain_ref[...]).astype(BF16)


def expert_kernel(count, *refs):
    pieces = refs[:count]
    weights = refs[count : count + 3]
    keep_ref, send_ref = refs[count + 3 : count + 5]
    wg, wu, wd, rows, sems = refs[count + 5 :]
    loads = [
        pltpu.make_async_copy(src.at[0], dst, sems.at[i])
        for i, (src, dst) in enumerate(zip(weights, (wg, wu, wd)))
    ]
    for load in loads:
        load.start()
    width = rows.shape[1]
    batch = min(count, 16)
    step = 1024
    for b in range(count // batch):
        for i in range(0, batch, 2):
            for col in range(0, width, step):
                rows[i * SLOTS : (i + 2) * SLOTS, col : col + step] = jnp.concatenate(
                    [pieces[b * batch + i + t][:, col : col + step].astype(F32) for t in range(2)],
                    axis=0,
                ).astype(BF16)
        if b == 0:
            loads[0].wait()
        gate = dot(rows[...], wg[...])
        if b == 0:
            loads[1].wait()
        up = dot(rows[...], wu[...])
        act = (gate / (1.0 + jnp.exp(-gate)) * up).astype(BF16)
        if b == 0:
            loads[2].wait()
        out_rows = batch * SLOTS
        for col in range(0, width, step):
            part = dot(act, wd[:, col : col + step]).astype(BF16)
            half = count * SLOTS // 2
            at = b * out_rows
            if out_rows > half:
                keep_ref[:, col : col + step] = part[:half]
                send_ref[:, col : col + step] = part[half:]
            elif at < half:
                keep_ref[at : at + out_rows, col : col + step] = part
            else:
                send_ref[at - half : at - half + out_rows, col : col + step] = part


def own_kernel(n, part, pos_ref, held, q_ref, x_ref, _, h_ref, acc, bias):
    pos = pos_ref[0]
    starts = doc_starts(n, pos, held)
    first = starts_of(held[pos, TILE:KV_ROWS, 0:HEAD].astype(F32)[0:1], starts)
    place = (pos * TILE + lax.broadcasted_iota(jnp.int32, (1, TILE), 1)).astype(F32)
    place = jnp.concatenate([place] * 2, axis=1)
    first = jnp.concatenate([first] * 2, axis=1)

    def rows(i):
        return jnp.concatenate(
            [q_ref[:, a * HEAD : (a + 1) * HEAD] for a in (2 * i, 2 * i + 1)], axis=0
        )

    done = flash(
        pos,
        held,
        [lambda i=i: rows(i) for i in range(4)],
        [part // 2] * 4,
        acc,
        bias,
        place,
        first,
    )
    for i in range(4):
        for g in range(2):
            lane = (2 * i + g) * HEAD
            h_ref[:, lane : lane + HEAD] = (
                x_ref[:, lane : lane + HEAD].astype(F32) + done[i][g * TILE : (g + 1) * TILE]
            )


def combine_kernel(planes, pos_ref, routes_ref, gates_ref, *refs):
    halves, parts, out_ref = refs[:4], refs[4 : 4 + planes], refs[4 + planes]
    z = pos_ref[0] // SHARDS
    routes = routes_ref[...]
    gates = gates_ref[...]
    experts = [lax.rem(z + k, planes) for k in range(planes)]
    members, ranks = slot_rows(routes, experts)
    slot = lax.broadcasted_iota(jnp.int32, (SLOTS, TILE), 0).astype(F32)
    mix = []
    for k, e in enumerate(experts):
        gate = jnp.sum(jnp.where(routes == e, gates, 0.0), axis=0, keepdims=True)
        mix.append(jnp.where(ranks[k : k + 1] == slot, gate, 0.0))
    mix = jnp.concatenate(mix, axis=0).T
    mix_high = mix.astype(BF16)
    mix_low = (mix - mix_high.astype(F32)).astype(BF16)
    size = halves[0].shape[1]
    for i, h in enumerate(halves):
        columns = slice(i * size, (i + 1) * size)
        rows = jnp.concatenate([p[:, columns].astype(F32) for p in parts], axis=0).astype(BF16)
        out_ref[:, columns] = (h[...] + dot(mix_high, rows) + dot(mix_low, rows)).astype(BF16)


def params(mib):
    return pltpu.CompilerParams(vmem_limit_bytes=mib * 1024 * 1024)


def local(
    resid, queries, keys, values, doc_ids, norm_gain, routes, route_weights, w_gate, w_up, w_down
):
    n = lax.axis_size("expert")
    planes = n // SHARDS
    pos = lax.axis_index("expert").astype(jnp.int32).reshape(1)
    tokens, width = queries.shape
    hidden = w_gate.shape[2]
    routes_t = routes.T
    gates_t = route_weights.T
    docs = doc_ids.reshape(1, tokens)
    small = 24 if n <= 16 else 60
    back = reach(n)

    packed = pl.pallas_call(
        pack_kernel,
        out_shape=jax.ShapeDtypeStruct((KV_ROWS, 4 * HEAD), BF16),
        in_specs=[HBM] * 3,
        out_specs=VMEM,
        scratch_shapes=[
            pltpu.VMEM((1, tokens), jnp.int32),
            pltpu.VMEM((tokens, KV_HEADS * HEAD), BF16),
            pltpu.SemaphoreType.DMA((3,)),
        ],
        compiler_params=params(small),
        name="pack",
    )(docs, keys, values)

    def move(value, pairs):
        return lax.ppermute(value, "expert", pairs)

    def needed(tile, devices):
        return any(tile <= t <= tile + back for t in devices)

    kv = {(0, 0, 0): packed}
    for k in range(1, planes):
        pairs = [
            (s, s + k * SHARDS)
            for s in range(n - k * SHARDS)
            if needed(s, [(s // SHARDS + k) * SHARDS + j for j in range(SHARDS)])
        ]
        if pairs:
            kv[0, 0, k] = move(packed, pairs)
    for (_, _, k), piece in list(kv.items()):
        pairs = [
            (d, d ^ 2)
            for d in range(n)
            if d >= k * SHARDS and needed(d - k * SHARDS, [d ^ 2, d ^ 3])
        ]
        if pairs:
            kv[0, 1, k] = move(piece, pairs)
    for (_, flip_y, k), piece in list(kv.items()):
        pairs = [
            (d, d ^ 1)
            for d in range(n)
            if d >= k * SHARDS and needed((d - k * SHARDS) ^ (2 * flip_y), [d ^ 1])
        ]
        if pairs:
            kv[1, flip_y, k] = move(piece, pairs)

    q_rows, x_rows, facts = pl.pallas_call(
        functools.partial(select_kernel, planes),
        out_shape=[
            jax.ShapeDtypeStruct((KV_HEADS, planes * TILE, HEAD), BF16),
            jax.ShapeDtypeStruct((planes * SLOTS, width), F32),
            jax.ShapeDtypeStruct((8, planes * TILE), F32),
        ],
        in_specs=[SMEM] + [VMEM] * 4,
        out_specs=[VMEM] * 3,
        compiler_params=params(small),
        name="select",
    )(pos, routes_t, docs, queries, resid)

    *sent, held = pl.pallas_call(
        functools.partial(routed_kernel, n, list(kv)),
        out_shape=[jax.ShapeDtypeStruct((SLOTS, width), BF16)] * planes
        + [jax.ShapeDtypeStruct((n, KV_ROWS, 4 * HEAD), BF16)],
        in_specs=[SMEM] + [VMEM] * 4 + [ANY] * len(kv),
        out_specs=[VMEM] * (planes + 1),
        scratch_shapes=[
            pltpu.VMEM((KV_HEADS, HEAD, 2 * TILE), F32),
            pltpu.VMEM((KEYS, 2 * TILE), F32),
            pltpu.VMEM((planes * SLOTS, width), F32),
            pltpu.SemaphoreType.DMA((len(kv),)),
        ],
        compiler_params=params(small),
        name="routed",
    )(pos, norm_gain.reshape(1, width), q_rows, x_rows, facts, *kv.values())

    def own(part, after):
        columns = pl.BlockSpec((tokens, 8 * HEAD), lambda i: (0, part))
        return pl.pallas_call(
            functools.partial(own_kernel, n, part),
            out_shape=jax.ShapeDtypeStruct((tokens, 8 * HEAD), F32),
            grid=(1,),
            in_specs=[SMEM, VMEM, columns, columns, ANY],
            out_specs=pl.BlockSpec((tokens, 8 * HEAD), lambda i: (0, 0)),
            scratch_shapes=[
                pltpu.VMEM((4, HEAD, 2 * TILE), F32),
                pltpu.VMEM((KEYS, 2 * TILE), F32),
            ],
            compiler_params=params(small),
            cost_estimate=pl.CostEstimate(
                flops=2_000_000_000, bytes_accessed=8_000_000, transcendentals=2_000_000
            ),
            name="own",
        )(pos, held, queries, resid, after)

    halves = [own(part, sent[0]) for part in range(2)]

    pieces = [sent[0]]
    for k in range(1, planes):
        pieces.append(move(sent[k], [(s, (s + k * SHARDS) % n) for s in range(n)]))
    pieces += [move(p, [(s, s ^ 2) for s in range(n)]) for p in pieces]
    pieces += [move(p, [(s, s ^ 1) for s in range(n)]) for p in pieces]

    half = jax.ShapeDtypeStruct((n * SLOTS // 2, width), BF16)
    keep, send = pl.pallas_call(
        functools.partial(expert_kernel, n),
        out_shape=[half, half],
        in_specs=[VMEM] * n + [HBM] * 3,
        out_specs=[VMEM, VMEM],
        scratch_shapes=[
            pltpu.VMEM((width, hidden), BF16),
            pltpu.VMEM((width, hidden), BF16),
            pltpu.VMEM((hidden, width), BF16),
            pltpu.VMEM((16 * SLOTS, width), BF16),
            pltpu.SemaphoreType.DMA((3,)),
        ],
        compiler_params=params(small),
        cost_estimate=pl.CostEstimate(
            flops=1_200_000_000, bytes_accessed=12_000_000, transcendentals=50_000
        ),
        name="expert",
    )(*pieces, w_gate, w_up, w_down)

    halves += [own(part, keep) for part in range(2, 4)]

    total = keep.astype(F32) + move(send, [(s, s ^ 1) for s in range(n)]).astype(F32)
    quarter = n * SLOTS // 4
    other = move(total[quarter:].astype(BF16), [(s, s ^ 2) for s in range(n)])
    total = (total[:quarter] + other.astype(F32)).astype(BF16)
    parts = [total[:SLOTS]]
    for k in range(1, planes):
        parts.append(
            move(
                total[k * SLOTS : (k + 1) * SLOTS], [(s, (s - k * SHARDS) % n) for s in range(n)]
            )
        )

    return pl.pallas_call(
        functools.partial(combine_kernel, planes),
        out_shape=jax.ShapeDtypeStruct((tokens, width), BF16),
        in_specs=[SMEM] + [VMEM] * (6 + planes),
        out_specs=VMEM,
        compiler_params=params(small),
        name="combine",
    )(pos, routes_t, gates_t, *halves, *parts)


def solution(mesh):
    rows = P(("groups", "expert"), None)
    in_specs = (rows,) * 4 + (P(("groups", "expert")), P(), rows, rows) + (
        P("expert", None, None),
    ) * 3
    return jax.shard_map(local, mesh=mesh, in_specs=in_specs, out_specs=rows, check_vma=False)
```

```python
import functools
import math

import jax
import jax.numpy as jnp
from jax import lax
from jax.experimental import pallas as pl
from jax.experimental.pallas import tpu as pltpu
from jax.sharding import PartitionSpec as P

HEAD = 128
QUERY_HEADS = 32
KV_HEADS = 2
GROUP = QUERY_HEADS // KV_HEADS
SHARDS = 4
SLOTS = 8
TILE = 128
KEYS = 256
KV_ROWS = TILE + 16
SCALE = math.log2(math.e) / math.sqrt(HEAD)
LOW = -1e30
F32 = jnp.float32
BF16 = jnp.bfloat16
VMEM = pl.BlockSpec(memory_space=pltpu.VMEM)
SMEM = pl.BlockSpec(memory_space=pltpu.SMEM)
ANY = pl.BlockSpec(memory_space=pl.ANY)
HBM = pl.BlockSpec(memory_space=pltpu.HBM)


def dot(a, b, ca=1, cb=0):
    return lax.dot_general(a, b, (((ca,), (cb,)), ((), ())), preferred_element_type=F32)


def reach(n):
    longest = n * TILE // 2 + 256
    return (longest - 1 + TILE - 1) // TILE


def slot_rows(routes, experts):
    members = jnp.concatenate(
        [jnp.max((routes == e).astype(F32), axis=0, keepdims=True) for e in experts], axis=0
    )
    count = len(experts)
    padded = -(-count // 8) * 8
    wide = members
    if padded > count:
        wide = jnp.concatenate([members, jnp.zeros((padded - count, TILE), F32)], axis=0)
    before = lax.broadcasted_iota(jnp.int32, (TILE, TILE), 0) < lax.broadcasted_iota(
        jnp.int32, (TILE, TILE), 1
    )
    ranks = dot(wide.astype(BF16), before.astype(F32).astype(BF16))
    return members, ranks


def pack_kernel(docs_ref, keys_ref, values_ref, out_ref, docs, values, sems):
    moves = [
        pltpu.make_async_copy(values_ref, values, sems.at[0]),
        pltpu.make_async_copy(docs_ref, docs, sems.at[1]),
        pltpu.make_async_copy(
            keys_ref, out_ref.at[pl.ds(0, TILE), pl.ds(0, KV_HEADS * HEAD)], sems.at[2]
        ),
    ]
    for move in moves:
        move.start()
    moves[0].wait()
    for h in range(KV_HEADS):
        out_ref[0:TILE, (KV_HEADS + h) * HEAD : (KV_HEADS + h + 1) * HEAD] = (
            values[:, h * HEAD : (h + 1) * HEAD].astype(F32).T.astype(BF16)
        )
    moves[1].wait()
    out_ref[TILE:KV_ROWS, :] = jnp.zeros((KV_ROWS - TILE, 4 * HEAD), BF16)
    out_ref[TILE:KV_ROWS, 0:HEAD] = jnp.broadcast_to(
        docs[...].astype(F32), (KV_ROWS - TILE, TILE)
    ).astype(BF16)
    moves[2].wait()


def select_kernel(planes, pos_ref, routes_ref, docs_ref, q_ref, x_ref, qs_ref, xs_ref, facts_ref):
    z = pos_ref[0] // SHARDS
    members, ranks = slot_rows(routes_ref[...], [lax.rem(z + k, planes) for k in range(planes)])
    docs = docs_ref[...].astype(F32)
    lane_slot = (lax.broadcasted_iota(jnp.int32, (TILE, TILE), 0) % SLOTS).astype(F32)
    token = lax.broadcasted_iota(jnp.int32, (1, TILE), 1).astype(F32)
    facts = jnp.concatenate(
        [token, docs, jnp.ones((1, TILE), F32), jnp.zeros((5, TILE), F32)], axis=0
    ).astype(BF16)
    picks = [
        jnp.where(ranks[k : k + 1] == lane_slot, members[k : k + 1], 0.0) for k in range(planes)
    ]
    chooser = jnp.concatenate([p[:SLOTS] for p in picks], axis=0).astype(BF16)
    q_rows = dot(chooser, q_ref[...])
    xs_ref[...] = dot(chooser, x_ref[...])
    for k in range(planes):
        known = dot(facts, picks[k].astype(BF16), 1, 1)
        facts_ref[:, k * TILE : (k + 1) * TILE] = jnp.concatenate(
            [known[0:1], known[1:2] + (1.0 - known[2:3]) * docs[:, 0:1], known[2:]], axis=0
        )
        for h in range(KV_HEADS):
            stack = jnp.concatenate(
                [
                    q_rows[k * SLOTS : (k + 1) * SLOTS, a * HEAD : (a + 1) * HEAD]
                    for a in range(h * GROUP, (h + 1) * GROUP)
                ],
                axis=0,
            )
            qs_ref[h, :, k * TILE : (k + 1) * TILE] = stack.T.astype(BF16)


def doc_starts(n, pos, held):
    sums = [jnp.zeros((1, TILE), F32) for _ in range(3)]
    for s in range(n):
        docs = held[s, TILE:KV_ROWS, 0:HEAD].astype(F32)[0:1]
        ahead = (pos - s < 0).astype(F32)
        behind = (pos - s > reach(n)).astype(F32)
        known = 1.0 - ahead - behind
        docs = jnp.where(known > 0.5, docs, 0.0) + 9.0 * ahead
        for d in range(3):
            sums[d] = sums[d] + jnp.where(docs < d + 1.0, 1.0, 0.0)
    return [jnp.sum(s, axis=1, keepdims=True) for s in sums]


def starts_of(docs, starts):
    first = jnp.zeros_like(docs)
    for d in range(3):
        first = jnp.where(docs == d + 1.0, starts[d], first)
    return first


def flash(pos, held, queries, kv_heads, acc_ref, bias_ref, place, first):
    lanes = place.shape[1]
    chains = len(queries)
    for i in range(chains):
        acc_ref[i] = jnp.zeros((HEAD, lanes), F32)
    low = jnp.min(first).astype(jnp.int32) // KEYS
    last = pos // (KEYS // TILE)
    clear = (jnp.max(first).astype(jnp.int32) + KEYS - 1) // KEYS
    middle = jnp.minimum(clear, last)

    def step(kb, carried, masked):
        if masked:
            key_at = (kb * KEYS + lax.broadcasted_iota(jnp.int32, (KEYS, 1), 0)).astype(F32)
            bias_ref[...] = jnp.where((key_at >= first) & (key_at <= place), 0.0, LOW)
        out = []
        for i in range(chains):
            top, total = carried[2 * i], carried[2 * i + 1]
            h = kv_heads[i]
            keys = jnp.concatenate(
                [held[2 * kb + t, 0:TILE, h * HEAD : (h + 1) * HEAD] for t in range(2)], axis=0
            )
            values = jnp.concatenate(
                [
                    held[2 * kb + t, 0:TILE, (KV_HEADS + h) * HEAD : (KV_HEADS + h + 1) * HEAD]
                    for t in range(2)
                ],
                axis=1,
            )
            scores = dot(keys, queries[i]())
            if masked:
                scores = scores + bias_ref[...]
            new_top = jnp.maximum(top, jnp.max(scores, axis=0, keepdims=True))
            factor = jnp.exp2((top - new_top) * SCALE)
            weights = jnp.exp2((scores - new_top) * SCALE)
            acc_ref[i] = acc_ref[i] * factor + dot(values, weights.astype(BF16))
            out += [new_top, total * factor + jnp.sum(weights, axis=0, keepdims=True)]
        return tuple(out)

    state = (jnp.full((1, lanes), LOW, F32), jnp.zeros((1, lanes), F32)) * chains
    state = lax.fori_loop(low, middle, functools.partial(step, masked=True), state)
    state = lax.fori_loop(middle, last, functools.partial(step, masked=False), state)
    state = step(last, state, True)
    return [(acc_ref[i] / state[2 * i + 1]).T for i in range(chains)]


def routed_kernel(n, senders, pos_ref, gain_ref, qs_ref, xs_ref, facts_ref, *refs):
    planes = n // SHARDS
    count = len(senders)
    pieces = refs[:count]
    outs = refs[count : count + planes]
    held = refs[count + planes]
    acc, bias, state, sems = refs[count + planes + 1 :]
    pos = pos_ref[0]
    z, y, c = pos // SHARDS, (pos // 2) % 2, pos % 2
    copies = []
    for i, (flip_c, *ways) in enumerate(senders):
        flip_y, k = (jnp.where(y == 0, ways[0][j], ways[1][j]) for j in range(2))
        sender = lax.rem(z - k + planes, planes) * SHARDS + (y ^ flip_y) * 2 + (c ^ flip_c)
        copies.append(pltpu.make_async_copy(pieces[i], held.at[sender], sems.at[i]))
    for copy in copies:
        copy.start()
    for copy in copies:
        copy.wait()
    starts = doc_starts(n, pos, held)
    lanes = 2 * TILE
    base = (pos * TILE).astype(F32)
    for part in range(planes // 2):
        at = part * lanes
        place = facts_ref[0:1, at : at + lanes] + base
        first = starts_of(facts_ref[1:2, at : at + lanes], starts)
        done = flash(
            pos,
            held,
            [lambda h=h, at=at: qs_ref[h, :, at : at + lanes] for h in range(KV_HEADS)],
            list(range(KV_HEADS)),
            acc,
            bias,
            place,
            first,
        )
        for h in range(KV_HEADS):
            for k in range(2):
                row = (part * 2 + k) * SLOTS
                for g in range(GROUP):
                    lane = (h * GROUP + g) * HEAD
                    state[row : row + SLOTS, lane : lane + HEAD] = (
                        xs_ref[row : row + SLOTS, lane : lane + HEAD]
                        + done[h][k * TILE + g * SLOTS : k * TILE + (g + 1) * SLOTS]
                    )
    for k in range(planes):
        hidden = state[k * SLOTS : (k + 1) * SLOTS, :]
        mean = jnp.mean(hidden * hidden, axis=1, keepdims=True)
        outs[k][...] = (hidden * lax.rsqrt(mean + 1e-06) * gain_ref[...]).astype(BF16)


def expert_kernel(count, *refs):
    pieces = refs[:count]
    wg, wu, wd = refs[count : count + 3]
    keep_ref, send_ref, rows = refs[count + 4 :]
    width = rows.shape[1]
    batch = min(count, 16)
    step = 1024
    for b in range(count // batch):
        for i in range(0, batch, 2):
            for col in range(0, width, step):
                rows[i * SLOTS : (i + 2) * SLOTS, col : col + step] = jnp.concatenate(
                    [pieces[b * batch + i + t][:, col : col + step].astype(F32) for t in range(2)],
                    axis=0,
                ).astype(BF16)
        gate = dot(rows[...], wg[...])
        up = dot(rows[...], wu[...])
        act = (gate / (1.0 + jnp.exp(-gate)) * up).astype(BF16)
        out_rows = batch * SLOTS
        for col in range(0, width, step):
            part = dot(act, wd[:, col : col + step]).astype(BF16)
            half = count * SLOTS // 2
            at = b * out_rows
            if out_rows > half:
                keep_ref[:, col : col + step] = part[:half]
                send_ref[:, col : col + step] = part[half:]
            elif at < half:
                keep_ref[at : at + out_rows, col : col + step] = part
            else:
                send_ref[at - half : at - half + out_rows, col : col + step] = part


def own_kernel(n, part, loads, pos_ref, held, q_ref, x_ref, _, *refs):
    sources, (h_ref, done_ref) = refs[:loads], refs[loads : loads + 2]
    targets = refs[loads + 2 : 2 * loads + 2]
    acc, bias, qt, sems = refs[2 * loads + 2 :]
    moves = [
        pltpu.make_async_copy(source.at[0], target, sems.at[i])
        for i, (source, target) in enumerate(zip(sources, targets))
    ]
    for move in moves:
        move.start()
    done_ref[...] = jnp.zeros((8, TILE), F32)
    pos = pos_ref[0]
    starts = doc_starts(n, pos, held)
    first = starts_of(held[pos, TILE:KV_ROWS, 0:HEAD].astype(F32)[0:1], starts)
    place = (pos * TILE + lax.broadcasted_iota(jnp.int32, (1, TILE), 1)).astype(F32)
    place = jnp.concatenate([place] * 2, axis=1)
    first = jnp.concatenate([first] * 2, axis=1)

    for a in range(8):
        qt[a // 2, :, (a % 2) * TILE : (a % 2 + 1) * TILE] = (
            q_ref[:, a * HEAD : (a + 1) * HEAD].astype(F32).T.astype(BF16)
        )
    done = flash(
        pos,
        held,
        [lambda i=i: qt[i] for i in range(4)],
        [part // 2] * 4,
        acc,
        bias,
        place,
        first,
    )
    for i in range(4):
        for g in range(2):
            lane = (2 * i + g) * HEAD
            h_ref[:, lane : lane + HEAD] = (
                x_ref[:, lane : lane + HEAD].astype(F32) + done[i][g * TILE : (g + 1) * TILE]
            )
    for move in moves:
        move.wait()


def combine_kernel(planes, pos_ref, routes_ref, gates_ref, *refs):
    halves, parts, out_ref = refs[:4], refs[4 : 4 + planes], refs[4 + planes]
    z = pos_ref[0] // SHARDS
    routes = routes_ref[...]
    gates = gates_ref[...]
    experts = [lax.rem(z + k, planes) for k in range(planes)]
    members, ranks = slot_rows(routes, experts)
    slot = lax.broadcasted_iota(jnp.int32, (SLOTS, TILE), 0).astype(F32)
    mix = []
    for k, e in enumerate(experts):
        gate = jnp.sum(jnp.where(routes == e, gates, 0.0), axis=0, keepdims=True)
        mix.append(jnp.where(ranks[k : k + 1] == slot, gate, 0.0))
    mix = jnp.concatenate(mix, axis=0).T
    mix_high = mix.astype(BF16)
    mix_low = (mix - mix_high.astype(F32)).astype(BF16)
    size = halves[0].shape[1]
    for i, h in enumerate(halves):
        columns = slice(i * size, (i + 1) * size)
        rows = jnp.concatenate([p[:, columns].astype(F32) for p in parts], axis=0).astype(BF16)
        out_ref[:, columns] = (h[...] + dot(mix_high, rows) + dot(mix_low, rows)).astype(BF16)


def params(mib):
    return pltpu.CompilerParams(vmem_limit_bytes=mib * 1024 * 1024)


def local(
    resid, queries, keys, values, doc_ids, norm_gain, routes, route_weights, w_gate, w_up, w_down
):
    n = lax.axis_size("expert")
    planes = n // SHARDS
    pos = lax.axis_index("expert").astype(jnp.int32).reshape(1)
    tokens, width = queries.shape
    hidden = w_gate.shape[2]
    routes_t = routes.T
    gates_t = route_weights.T
    docs = doc_ids.reshape(1, tokens)
    small = 24 if n <= 16 else 60
    back = reach(n)

    packed = pl.pallas_call(
        pack_kernel,
        out_shape=jax.ShapeDtypeStruct((KV_ROWS, 4 * HEAD), BF16),
        in_specs=[HBM] * 3,
        out_specs=VMEM,
        scratch_shapes=[
            pltpu.VMEM((1, tokens), jnp.int32),
            pltpu.VMEM((tokens, KV_HEADS * HEAD), BF16),
            pltpu.SemaphoreType.DMA((3,)),
        ],
        compiler_params=params(60),
        name="pack",
    )(docs, keys, values)

    def move(value, pairs):
        return lax.ppermute(value, "expert", pairs)

    def needed(k, y_from, y_to):
        gaps = [
            k * SHARDS + 2 * (y_to - y_from) + (to - of) for to in range(2) for of in range(2)
        ]
        return any(0 <= gap <= back for gap in gaps)

    far = max(k for k in range(planes) if any(needed(k, a, b) for a in (0, 1) for b in (0, 1)))
    along = [packed]
    for k in range(1, far + 1):
        used = [any(needed(k, y, to) for to in (0, 1)) for y in (0, 1)]
        along.append(
            move(
                packed,
                [(s, (s + k * SHARDS) % n if used[s // 2 % 2] else s) for s in range(n)],
            )
        )
    kv = {(0, (0, k), (0, k)): piece for k, piece in enumerate(along)}
    flips = [(s, s ^ 2) for s in range(n)]
    alone = far > 0 and not needed(0, 1, 0) and not needed(far, 0, 1)
    for k in range(1 if alone else 0, far if alone else far + 1):
        pairs = [(s, s ^ 2 if s >= k * SHARDS else s) for s in range(n)]
        kv[0, (1, k), (1, k)] = move(along[k], pairs)
    if alone:
        odd = (pos[0] & 2) != 0
        kv[0, (1, far), (1, 0)] = move(jnp.where(odd, along[far], packed), flips)
    for (_, *ways), piece in list(kv.items()):
        kv[1, ways[0], ways[1]] = move(piece, [(s, s ^ 1) for s in range(n)])

    q_rows, x_rows, facts = pl.pallas_call(
        functools.partial(select_kernel, planes),
        out_shape=[
            jax.ShapeDtypeStruct((KV_HEADS, HEAD, planes * TILE), BF16),
            jax.ShapeDtypeStruct((planes * SLOTS, width), F32),
            jax.ShapeDtypeStruct((8, planes * TILE), F32),
        ],
        in_specs=[SMEM] + [VMEM] * 4,
        out_specs=[VMEM] * 3,
        compiler_params=params(small),
        name="select",
    )(pos, routes_t, docs, queries, resid)

    *sent, held = pl.pallas_call(
        functools.partial(routed_kernel, n, list(kv)),
        out_shape=[jax.ShapeDtypeStruct((SLOTS, width), BF16)] * planes
        + [jax.ShapeDtypeStruct((n, KV_ROWS, 4 * HEAD), BF16)],
        in_specs=[SMEM] + [VMEM] * 4 + [ANY] * len(kv),
        out_specs=[VMEM] * (planes + 1),
        scratch_shapes=[
            pltpu.VMEM((KV_HEADS, HEAD, 2 * TILE), F32),
            pltpu.VMEM((KEYS, 2 * TILE), F32),
            pltpu.VMEM((planes * SLOTS, width), F32),
            pltpu.SemaphoreType.DMA((len(kv),)),
        ],
        compiler_params=params(small),
        name="routed",
    )(pos, norm_gain.reshape(1, width), q_rows, x_rows, facts, *kv.values())

    def own(part, after, *sources):
        columns = pl.BlockSpec((tokens, 8 * HEAD), lambda i: (0, part))
        return pl.pallas_call(
            functools.partial(own_kernel, n, part, len(sources)),
            out_shape=[
                jax.ShapeDtypeStruct((tokens, 8 * HEAD), F32),
                jax.ShapeDtypeStruct((8, TILE), F32),
            ]
            + [jax.ShapeDtypeStruct(w.shape[1:], BF16) for w in sources],
            grid=(1,),
            in_specs=[SMEM, VMEM, columns, columns, ANY] + [HBM] * len(sources),
            out_specs=[
                pl.BlockSpec((tokens, 8 * HEAD), lambda i: (0, 0)),
                pl.BlockSpec((8, TILE), lambda i: (0, 0)),
            ]
            + [VMEM] * len(sources),
            scratch_shapes=[
                pltpu.VMEM((4, HEAD, 2 * TILE), F32),
                pltpu.VMEM((KEYS, 2 * TILE), F32),
                pltpu.VMEM((4, HEAD, 2 * TILE), BF16),
                pltpu.SemaphoreType.DMA((3,)),
            ],
            compiler_params=params(39 if sources and n <= 16 else small),
            cost_estimate=pl.CostEstimate(
                flops=2_000_000_000, bytes_accessed=8_000_000, transcendentals=2_000_000
            ),
            name="own",
        )(pos, held, queries, resid, after, *sources)

    half0, done = own(0, sent[0])
    half1, done, *weights = own(1, done, w_gate, w_up, w_down)
    halves = [half0, half1]

    pieces = [sent[0]]
    for k in range(1, planes):
        pieces.append(move(sent[k], [(s, (s + k * SHARDS) % n) for s in range(n)]))
    pieces += [move(p, [(s, s ^ 2) for s in range(n)]) for p in pieces]
    pieces += [move(p, [(s, s ^ 1) for s in range(n)]) for p in pieces]

    half = jax.ShapeDtypeStruct((n * SLOTS // 2, width), BF16)
    keep, send = pl.pallas_call(
        functools.partial(expert_kernel, n),
        out_shape=[half, half],
        in_specs=[VMEM] * (n + 3) + [ANY],
        out_specs=[VMEM, VMEM],
        scratch_shapes=[pltpu.VMEM((16 * SLOTS, width), BF16)],
        compiler_params=params(16),
        cost_estimate=pl.CostEstimate(
            flops=1_200_000_000, bytes_accessed=12_000_000, transcendentals=50_000
        ),
        name="expert",
    )(*pieces, *weights, done)

    halves += [own(part, keep)[0] for part in range(2, 4)]

    total = keep.astype(F32) + move(send, [(s, s ^ 1) for s in range(n)]).astype(F32)
    quarter = n * SLOTS // 4
    other = move(total[quarter:].astype(BF16), [(s, s ^ 2) for s in range(n)])
    total = (total[:quarter] + other.astype(F32)).astype(BF16)
    parts = [total[:SLOTS]]
    for k in range(1, planes):
        parts.append(
            move(
                total[k * SLOTS : (k + 1) * SLOTS], [(s, (s - k * SHARDS) % n) for s in range(n)]
            )
        )

    return pl.pallas_call(
        functools.partial(combine_kernel, planes),
        out_shape=jax.ShapeDtypeStruct((tokens, width), BF16),
        in_specs=[SMEM] + [VMEM] * (6 + planes),
        out_specs=VMEM,
        compiler_params=params(small),
        name="combine",
    )(pos, routes_t, gates_t, *halves, *parts)


def solution(mesh):
    rows = P(("groups", "expert"), None)
    in_specs = (rows,) * 4 + (P(("groups", "expert")), P(), rows, rows) + (
        P("expert", None, None),
    ) * 3
    return jax.shard_map(local, mesh=mesh, in_specs=in_specs, out_specs=rows, check_vma=False)
```

```python
import functools
import math

import jax
import jax.numpy as jnp
from jax import lax
from jax.experimental import pallas as pl
from jax.experimental.pallas import tpu as pltpu
from jax.sharding import PartitionSpec as P

HEAD = 128
QUERY_HEADS = 32
KV_HEADS = 2
GROUP = QUERY_HEADS // KV_HEADS
SHARDS = 4
SLOTS = 8
TILE = 128
KEYS = 256
KV_ROWS = TILE + 16
SCALE = 1.0 / math.sqrt(HEAD)
LOW = -1e30
F32 = jnp.float32
BF16 = jnp.bfloat16
VMEM = pl.BlockSpec(memory_space=pltpu.VMEM)
SMEM = pl.BlockSpec(memory_space=pltpu.SMEM)
ANY = pl.BlockSpec(memory_space=pl.ANY)
HBM = pl.BlockSpec(memory_space=pltpu.HBM)


def dot(a, b, ca=1, cb=0):
    return lax.dot_general(a, b, (((ca,), (cb,)), ((), ())), preferred_element_type=F32)


def reach(n):
    longest = n * TILE // 2 + 256
    return (longest - 1 + TILE - 1) // TILE


def slot_rows(routes, experts):
    members = jnp.concatenate(
        [jnp.max((routes == e).astype(F32), axis=0, keepdims=True) for e in experts], axis=0
    )
    count = len(experts)
    padded = -(-count // 8) * 8
    wide = members
    if padded > count:
        wide = jnp.concatenate([members, jnp.zeros((padded - count, TILE), F32)], axis=0)
    before = lax.broadcasted_iota(jnp.int32, (TILE, TILE), 0) < lax.broadcasted_iota(
        jnp.int32, (TILE, TILE), 1
    )
    ranks = dot(wide.astype(BF16), before.astype(F32).astype(BF16))
    return members, ranks


def pack_kernel(docs_ref, keys_ref, values_ref, out_ref, docs, values, sems):
    moves = [
        pltpu.make_async_copy(values_ref, values, sems.at[0]),
        pltpu.make_async_copy(docs_ref, docs, sems.at[1]),
        pltpu.make_async_copy(
            keys_ref, out_ref.at[pl.ds(0, TILE), pl.ds(0, KV_HEADS * HEAD)], sems.at[2]
        ),
    ]
    for move in moves:
        move.start()
    moves[0].wait()
    for h in range(KV_HEADS):
        out_ref[0:TILE, (KV_HEADS + h) * HEAD : (KV_HEADS + h + 1) * HEAD] = (
            values[:, h * HEAD : (h + 1) * HEAD].astype(F32).T.astype(BF16)
        )
    moves[1].wait()
    out_ref[TILE:KV_ROWS, :] = jnp.zeros((KV_ROWS - TILE, 4 * HEAD), BF16)
    out_ref[TILE:KV_ROWS, 0:HEAD] = jnp.broadcast_to(
        docs[...].astype(F32), (KV_ROWS - TILE, TILE)
    ).astype(BF16)
    moves[2].wait()


def select_kernel(planes, pos_ref, *refs):
    sources, (qs_ref, xs_ref, facts_ref) = refs[:4], refs[4:7]
    routes_ref, docs_ref, q_ref, x_ref, sems = refs[7:]
    moves = [
        pltpu.make_async_copy(source, target, sems.at[i])
        for i, (source, target) in enumerate(zip(sources, refs[7:11]))
    ]
    for move in moves:
        move.start()
    for move in moves:
        move.wait()
    z = pos_ref[0] // SHARDS
    members, ranks = slot_rows(routes_ref[...], [lax.rem(z + k, planes) for k in range(planes)])
    docs = docs_ref[...].astype(F32)
    lane_slot = (lax.broadcasted_iota(jnp.int32, (TILE, TILE), 0) % SLOTS).astype(F32)
    token = lax.broadcasted_iota(jnp.int32, (1, TILE), 1).astype(F32)
    facts = jnp.concatenate(
        [token, docs, jnp.ones((1, TILE), F32), jnp.zeros((5, TILE), F32)], axis=0
    ).astype(BF16)
    picks = [
        jnp.where(ranks[k : k + 1] == lane_slot, members[k : k + 1], 0.0) for k in range(planes)
    ]
    chooser = jnp.concatenate([p[:SLOTS] for p in picks], axis=0).astype(BF16)
    q_rows = dot(chooser, q_ref[...])
    xs_ref[...] = dot(chooser, x_ref[...])
    for k in range(planes):
        known = dot(facts, picks[k].astype(BF16), 1, 1)
        facts_ref[:, k * TILE : (k + 1) * TILE] = jnp.concatenate(
            [known[0:1], known[1:2] + (1.0 - known[2:3]) * docs[:, 0:1], known[2:]], axis=0
        )
        for h in range(KV_HEADS):
            stack = jnp.concatenate(
                [
                    q_rows[k * SLOTS : (k + 1) * SLOTS, a * HEAD : (a + 1) * HEAD]
                    for a in range(h * GROUP, (h + 1) * GROUP)
                ],
                axis=0,
            )
            qs_ref[h, :, k * TILE : (k + 1) * TILE] = stack.T.astype(BF16)


def doc_starts(n, pos, held):
    sums = [jnp.zeros((1, TILE), F32) for _ in range(3)]
    for s in range(n):
        docs = held[s, TILE:KV_ROWS, 0:HEAD].astype(F32)[0:1]
        ahead = (pos - s < 0).astype(F32)
        behind = (pos - s > reach(n)).astype(F32)
        known = 1.0 - ahead - behind
        docs = jnp.where(known > 0.5, docs, 0.0) + 9.0 * ahead
        for d in range(3):
            sums[d] = sums[d] + jnp.where(docs < d + 1.0, 1.0, 0.0)
    return [jnp.sum(s, axis=1, keepdims=True) for s in sums]


def starts_of(docs, starts):
    first = jnp.zeros_like(docs)
    for d in range(3):
        first = jnp.where(docs == d + 1.0, starts[d], first)
    return first


def flash(pos, held, queries, kv_heads, sides, acc_ref, bias_ref, places, firsts):
    lanes = places[0].shape[1]
    chains = range(len(queries))
    for i in chains:
        acc_ref[i] = jnp.zeros((HEAD, lanes), F32)
    lowest = functools.reduce(jnp.minimum, [jnp.min(first) for first in firsts])
    highest = functools.reduce(jnp.maximum, [jnp.max(first) for first in firsts])
    low = lowest.astype(jnp.int32) // KEYS
    last = pos // (KEYS // TILE)
    clear = jnp.minimum((highest.astype(jnp.int32) + KEYS - 1) // KEYS, last)

    def scores(kb, i, masked):
        h = kv_heads[i]
        keys = jnp.concatenate(
            [held[2 * kb + t, 0:TILE, h * HEAD : (h + 1) * HEAD] for t in range(2)], axis=0
        )
        result = dot(keys, queries[i]())
        if masked:
            result = result + bias_ref[sides[i]]
        return result

    def hide(kb):
        key_at = (kb * KEYS + lax.broadcasted_iota(jnp.int32, (KEYS, 1), 0)).astype(F32)
        for side, (place, first) in enumerate(zip(places, firsts)):
            bias_ref[side] = jnp.where((key_at >= first) & (key_at <= place), 0.0, LOW)

    def over_keys(step, state):
        def edge(j, carried):
            kb = jnp.where(j < clear - low, low + j, last)
            hide(kb)
            return step(kb, carried, True)

        state = lax.fori_loop(0, clear - low + 1, edge, state)
        return lax.fori_loop(clear, last, lambda kb, carried: step(kb, carried, False), state)

    def eights(x):
        return x.reshape(KEYS // 8, 8, lanes)

    def find(kb, carried, masked):
        return tuple(
            jnp.maximum(carried[i], jnp.max(eights(scores(kb, i, masked)), axis=0)) for i in chains
        )

    tops = over_keys(find, tuple(jnp.full((8, lanes), LOW, F32) for _ in chains))
    tops = [jnp.max(top, axis=0, keepdims=True) for top in tops]

    def add(kb, carried, masked):
        out = []
        for i in chains:
            at = (KV_HEADS + kv_heads[i]) * HEAD
            values = jnp.concatenate(
                [held[2 * kb + t, 0:TILE, at : at + HEAD] for t in range(2)], axis=1
            )
            weights = jnp.exp((scores(kb, i, masked) - tops[i]) * SCALE)
            acc_ref[i] += dot(values, weights.astype(BF16))
            out.append(carried[i] + jnp.sum(eights(weights), axis=0))
        return tuple(out)

    sums = over_keys(add, tuple(jnp.zeros((8, lanes), F32) for _ in chains))
    return [(acc_ref[i] / jnp.sum(sums[i], axis=0, keepdims=True)).T for i in chains]


def routed_kernel(n, senders, pos_ref, gain_ref, qs_ref, xs_ref, facts_ref, *refs):
    planes = n // SHARDS
    count = len(senders)
    pieces = refs[:count]
    outs = refs[count : count + planes]
    held = refs[count + planes]
    acc, bias, state, gain, sems = refs[count + planes + 1 :]
    pos = pos_ref[0]
    z, y, c = pos // SHARDS, (pos // 2) % 2, pos % 2
    copies = []
    for i, (flip_c, *ways) in enumerate(senders):
        flip_y, k = (jnp.where(y == 0, ways[0][j], ways[1][j]) for j in range(2))
        sender = lax.rem(z - k + planes, planes) * SHARDS + (y ^ flip_y) * 2 + (c ^ flip_c)
        copies.append(pltpu.make_async_copy(pieces[i], held.at[sender], sems.at[i]))
    copies.append(pltpu.make_async_copy(gain_ref, gain, sems.at[count]))
    for copy in copies:
        copy.start()
    for copy in copies:
        copy.wait()
    starts = doc_starts(n, pos, held)
    lanes = 2 * TILE
    base = (pos * TILE).astype(F32)
    for pair in range(0, planes // 2, 2):
        parts = range(pair, min(pair + 2, planes // 2))
        columns = [slice(part * lanes, (part + 1) * lanes) for part in parts]
        chains = [(i, h) for i in range(len(parts)) for h in range(KV_HEADS)]
        done = flash(
            pos,
            held,
            [lambda i=i, h=h: qs_ref[h, :, columns[i]] for i, h in chains],
            [h for _, h in chains],
            [i for i, _ in chains],
            acc,
            bias,
            [facts_ref[0:1, at] + base for at in columns],
            [starts_of(facts_ref[1:2, at], starts) for at in columns],
        )
        for (i, h), rows in zip(chains, done):
            for k in range(2):
                row = (parts[i] * 2 + k) * SLOTS
                for g in range(GROUP):
                    lane = (h * GROUP + g) * HEAD
                    state[row : row + SLOTS, lane : lane + HEAD] = (
                        xs_ref[row : row + SLOTS, lane : lane + HEAD]
                        + rows[k * TILE + g * SLOTS : k * TILE + (g + 1) * SLOTS]
                    )
    for k in range(planes):
        hidden = state[k * SLOTS : (k + 1) * SLOTS, :]
        mean = jnp.mean(hidden * hidden, axis=1, keepdims=True)
        outs[k][...] = (hidden * lax.rsqrt(mean + 1e-06) * gain[...]).astype(BF16)


def expert_kernel(count, *refs):
    pieces = refs[:count]
    wg, wu, wd = refs[count : count + 3]
    keep_ref, send_ref, rows = refs[count + 4 :]
    width = rows.shape[1]
    batch = min(count, 16)
    step = 1024
    for b in range(count // batch):
        for i in range(0, batch, 2):
            for col in range(0, width, step):
                rows[i * SLOTS : (i + 2) * SLOTS, col : col + step] = jnp.concatenate(
                    [pieces[b * batch + i + t][:, col : col + step].astype(F32) for t in range(2)],
                    axis=0,
                ).astype(BF16)
        gate = dot(rows[...], wg[...])
        up = dot(rows[...], wu[...])
        act = (gate / (1.0 + jnp.exp(-gate)) * up).astype(BF16)
        out_rows = batch * SLOTS
        for col in range(0, width, step):
            part = dot(act, wd[:, col : col + step]).astype(BF16)
            half = count * SLOTS // 2
            at = b * out_rows
            if out_rows > half:
                keep_ref[:, col : col + step] = part[:half]
                send_ref[:, col : col + step] = part[half:]
            elif at < half:
                keep_ref[at : at + out_rows, col : col + step] = part
            else:
                send_ref[at - half : at - half + out_rows, col : col + step] = part


def own_kernel(n, part, loads, pos_ref, held, q_ref, x_ref, _, *refs):
    sources, (h_ref, done_ref) = refs[:loads], refs[loads : loads + 2]
    targets = refs[loads + 2 : 2 * loads + 2]
    acc, bias, qt, sems = refs[2 * loads + 2 :]
    moves = [
        pltpu.make_async_copy(source.at[0], target, sems.at[i])
        for i, (source, target) in enumerate(zip(sources, targets))
    ]
    for move in moves:
        move.start()
    done_ref[...] = jnp.zeros((8, TILE), F32)
    pos = pos_ref[0]
    starts = doc_starts(n, pos, held)
    first = starts_of(held[pos, TILE:KV_ROWS, 0:HEAD].astype(F32)[0:1], starts)
    place = (pos * TILE + lax.broadcasted_iota(jnp.int32, (1, TILE), 1)).astype(F32)
    place = jnp.concatenate([place] * 2, axis=1)
    first = jnp.concatenate([first] * 2, axis=1)

    for a in range(8):
        qt[a // 2, :, (a % 2) * TILE : (a % 2 + 1) * TILE] = (
            q_ref[:, a * HEAD : (a + 1) * HEAD].astype(F32).T.astype(BF16)
        )
    done = flash(
        pos,
        held,
        [lambda i=i: qt[i] for i in range(4)],
        [part // 2] * 4,
        [0] * 4,
        acc,
        bias,
        [place],
        [first],
    )
    for i in range(4):
        for g in range(2):
            lane = (2 * i + g) * HEAD
            h_ref[:, lane : lane + HEAD] = (
                x_ref[:, lane : lane + HEAD].astype(F32) + done[i][g * TILE : (g + 1) * TILE]
            )
    for move in moves:
        move.wait()


def combine_kernel(planes, pos_ref, routes_ref, gates_ref, *refs):
    halves, parts, out_ref = refs[:4], refs[4 : 4 + planes], refs[4 + planes]
    z = pos_ref[0] // SHARDS
    routes = routes_ref[...]
    gates = gates_ref[...]
    experts = [lax.rem(z + k, planes) for k in range(planes)]
    members, ranks = slot_rows(routes, experts)
    slot = lax.broadcasted_iota(jnp.int32, (SLOTS, TILE), 0).astype(F32)
    mix = []
    for k, e in enumerate(experts):
        gate = jnp.sum(jnp.where(routes == e, gates, 0.0), axis=0, keepdims=True)
        mix.append(jnp.where(ranks[k : k + 1] == slot, gate, 0.0))
    mix = jnp.concatenate(mix, axis=0).T
    mix_high = mix.astype(BF16)
    mix_low = (mix - mix_high.astype(F32)).astype(BF16)
    size = halves[0].shape[1]
    for i, h in enumerate(halves):
        columns = slice(i * size, (i + 1) * size)
        rows = jnp.concatenate([p[:, columns].astype(F32) for p in parts], axis=0).astype(BF16)
        out_ref[:, columns] = (h[...] + dot(mix_high, rows) + dot(mix_low, rows)).astype(BF16)


def pin(x):
    return pltpu.with_memory_space_constraint(x, pltpu.HBM)


def params(mib):
    return pltpu.CompilerParams(vmem_limit_bytes=mib * 1024 * 1024)


def local(
    resid, queries, keys, values, doc_ids, norm_gain, routes, route_weights, w_gate, w_up, w_down
):
    n = lax.axis_size("expert")
    planes = n // SHARDS
    pos = lax.axis_index("expert").astype(jnp.int32).reshape(1)
    tokens, width = queries.shape
    hidden = w_gate.shape[2]
    routes_t = routes.T
    gates_t = route_weights.T
    docs = doc_ids.reshape(1, tokens)
    small = 24 if n <= 16 else 60
    back = reach(n)

    packed = pl.pallas_call(
        pack_kernel,
        out_shape=jax.ShapeDtypeStruct((KV_ROWS, 4 * HEAD), BF16),
        in_specs=[HBM] * 3,
        out_specs=VMEM,
        scratch_shapes=[
            pltpu.VMEM((1, tokens), jnp.int32),
            pltpu.VMEM((tokens, KV_HEADS * HEAD), BF16),
            pltpu.SemaphoreType.DMA((3,)),
        ],
        compiler_params=params(8),
        name="pack",
    )(pin(docs), pin(keys), pin(values))

    def move(value, pairs):
        return lax.ppermute(value, "expert", pairs)

    def needed(k, y_from, y_to):
        gaps = [
            k * SHARDS + 2 * (y_to - y_from) + (to - of) for to in range(2) for of in range(2)
        ]
        return any(0 <= gap <= back for gap in gaps)

    far = max(k for k in range(planes) if any(needed(k, a, b) for a in (0, 1) for b in (0, 1)))
    along = [packed]
    for k in range(1, far + 1):
        used = [any(needed(k, y, to) for to in (0, 1)) for y in (0, 1)]
        along.append(
            move(
                packed,
                [(s, (s + k * SHARDS) % n if used[s // 2 % 2] else s) for s in range(n)],
            )
        )
    q_rows, x_rows, facts = pl.pallas_call(
        functools.partial(select_kernel, planes),
        out_shape=[
            jax.ShapeDtypeStruct((KV_HEADS, HEAD, planes * TILE), BF16),
            jax.ShapeDtypeStruct((planes * SLOTS, width), F32),
            jax.ShapeDtypeStruct((8, planes * TILE), F32),
        ],
        in_specs=[SMEM] + [HBM] * 4,
        out_specs=[VMEM] * 3,
        scratch_shapes=[
            pltpu.VMEM(routes_t.shape, jnp.int32),
            pltpu.VMEM(docs.shape, jnp.int32),
            pltpu.VMEM(queries.shape, BF16),
            pltpu.VMEM(resid.shape, BF16),
            pltpu.SemaphoreType.DMA((4,)),
        ],
        compiler_params=params(small),
        name="select",
    )(pos, pin(routes_t), pin(docs), pin(queries), pin(resid))

    along[1], q_rows = lax.optimization_barrier((along[1], q_rows))
    kv = {(0, (0, k), (0, k)): piece for k, piece in enumerate(along)}
    flips = [(s, s ^ 2) for s in range(n)]
    alone = far > 0 and not needed(0, 1, 0) and not needed(far, 0, 1)
    for k in range(1 if alone else 0, far if alone else far + 1):
        pairs = [(s, s ^ 2 if s >= k * SHARDS else s) for s in range(n)]
        kv[0, (1, k), (1, k)] = move(along[k], pairs)
    if alone:
        odd = (pos[0] & 2) != 0
        kv[0, (1, far), (1, 0)] = move(jnp.where(odd, along[far], packed), flips)
    for (_, *ways), piece in list(kv.items()):
        kv[1, ways[0], ways[1]] = move(piece, [(s, s ^ 1) for s in range(n)])

    *sent, held = pl.pallas_call(
        functools.partial(routed_kernel, n, list(kv)),
        out_shape=[jax.ShapeDtypeStruct((SLOTS, width), BF16)] * planes
        + [jax.ShapeDtypeStruct((n, KV_ROWS, 4 * HEAD), BF16)],
        in_specs=[SMEM, HBM] + [VMEM] * 3 + [ANY] * len(kv),
        out_specs=[VMEM] * (planes + 1),
        scratch_shapes=[
            pltpu.VMEM((4, HEAD, 2 * TILE), F32),
            pltpu.VMEM((2, KEYS, 2 * TILE), F32),
            pltpu.VMEM((planes * SLOTS, width), F32),
            pltpu.VMEM((1, width), F32),
            pltpu.SemaphoreType.DMA((len(kv) + 1,)),
        ],
        compiler_params=params(small),
        name="routed",
    )(pos, pin(norm_gain.reshape(1, width)), q_rows, x_rows, facts, *kv.values())

    def own(part, after, *sources):
        columns = pl.BlockSpec((tokens, 8 * HEAD), lambda i: (0, part))
        return pl.pallas_call(
            functools.partial(own_kernel, n, part, len(sources)),
            out_shape=[
                jax.ShapeDtypeStruct((tokens, 8 * HEAD), F32),
                jax.ShapeDtypeStruct((8, TILE), F32),
            ]
            + [jax.ShapeDtypeStruct(w.shape[1:], BF16) for w in sources],
            grid=(1,),
            in_specs=[SMEM, VMEM, columns, columns, ANY] + [HBM] * len(sources),
            out_specs=[
                pl.BlockSpec((tokens, 8 * HEAD), lambda i: (0, 0)),
                pl.BlockSpec((8, TILE), lambda i: (0, 0)),
            ]
            + [VMEM] * len(sources),
            scratch_shapes=[
                pltpu.VMEM((4, HEAD, 2 * TILE), F32),
                pltpu.VMEM((1, KEYS, 2 * TILE), F32),
                pltpu.VMEM((4, HEAD, 2 * TILE), BF16),
                pltpu.SemaphoreType.DMA((3,)),
            ],
            compiler_params=params(small),
            cost_estimate=pl.CostEstimate(
                flops=2_000_000_000, bytes_accessed=8_000_000, transcendentals=2_000_000
            ),
            name="own",
        )(pos, held, queries, resid, after, *map(pin, sources))

    half0, done = own(0, sent[0])
    half1, done, *weights = own(1, done, w_gate, w_up, w_down)
    halves = [half0, half1]

    pieces = [sent[0]]
    for k in range(1, planes):
        pieces.append(move(sent[k], [(s, (s + k * SHARDS) % n) for s in range(n)]))
    pieces += [move(p, [(s, s ^ 2) for s in range(n)]) for p in pieces]
    pieces += [move(p, [(s, s ^ 1) for s in range(n)]) for p in pieces]

    half = jax.ShapeDtypeStruct((n * SLOTS // 2, width), BF16)
    keep, send = pl.pallas_call(
        functools.partial(expert_kernel, n),
        out_shape=[half, half],
        in_specs=[VMEM] * (n + 3) + [ANY],
        out_specs=[VMEM, VMEM],
        scratch_shapes=[pltpu.VMEM((16 * SLOTS, width), BF16)],
        compiler_params=params(16),
        cost_estimate=pl.CostEstimate(
            flops=1_200_000_000, bytes_accessed=12_000_000, transcendentals=50_000
        ),
        name="expert",
    )(*pieces, *weights, done)

    halves += [own(part, keep)[0] for part in range(2, 4)]

    total = keep.astype(F32) + move(send, [(s, s ^ 1) for s in range(n)]).astype(F32)
    quarter = n * SLOTS // 4
    other = move(total[quarter:].astype(BF16), [(s, s ^ 2) for s in range(n)])
    total = (total[:quarter] + other.astype(F32)).astype(BF16)
    parts = [total[:SLOTS]]
    for k in range(1, planes):
        parts.append(
            move(
                total[k * SLOTS : (k + 1) * SLOTS], [(s, (s - k * SHARDS) % n) for s in range(n)]
            )
        )

    return pl.pallas_call(
        functools.partial(combine_kernel, planes),
        out_shape=jax.ShapeDtypeStruct((tokens, width), BF16),
        in_specs=[SMEM] + [VMEM] * (6 + planes),
        out_specs=VMEM,
        compiler_params=params(small),
        name="combine",
    )(pos, routes_t, gates_t, *halves, *parts)


def solution(mesh):
    rows = P(("groups", "expert"), None)
    in_specs = (rows,) * 4 + (P(("groups", "expert")), P(), rows, rows) + (
        P("expert", None, None),
    ) * 3
    return jax.shard_map(local, mesh=mesh, in_specs=in_specs, out_specs=rows, check_vma=False)
```

```python
import functools
import math

import jax
import jax.numpy as jnp
from jax import lax
from jax.experimental import pallas as pl
from jax.experimental.pallas import tpu as pltpu
from jax.sharding import PartitionSpec as P

HEAD = 128
QUERY_HEADS = 32
KV_HEADS = 2
GROUP = QUERY_HEADS // KV_HEADS
SHARDS = 4
SLOTS = 8
TILE = 128
KEYS = 256
KV_ROWS = TILE + 16
SCALE = 1.0 / math.sqrt(HEAD)
LOW = -1e30
EXTRA = 16
F32 = jnp.float32
BF16 = jnp.bfloat16
VMEM = pl.BlockSpec(memory_space=pltpu.VMEM)
SMEM = pl.BlockSpec(memory_space=pltpu.SMEM)
ANY = pl.BlockSpec(memory_space=pl.ANY)
HBM = pl.BlockSpec(memory_space=pltpu.HBM)


def dot(a, b, ca=1, cb=0):
    return lax.dot_general(a, b, (((ca,), (cb,)), ((), ())), preferred_element_type=F32)


def reach(n):
    longest = n * TILE // 2 + 256
    return (longest - 1 + TILE - 1) // TILE


def slot_rows(routes, experts):
    members = jnp.concatenate(
        [jnp.max((routes == e).astype(F32), axis=0, keepdims=True) for e in experts], axis=0
    )
    count = len(experts)
    padded = -(-count // 8) * 8
    wide = members
    if padded > count:
        wide = jnp.concatenate([members, jnp.zeros((padded - count, TILE), F32)], axis=0)
    before = lax.broadcasted_iota(jnp.int32, (TILE, TILE), 0) < lax.broadcasted_iota(
        jnp.int32, (TILE, TILE), 1
    )
    ranks = dot(wide.astype(BF16), before.astype(F32).astype(BF16))
    return members, ranks


def pack_kernel(docs_ref, keys_ref, values_ref, out_ref, docs, values, sems):
    moves = [
        pltpu.make_async_copy(values_ref, values, sems.at[0]),
        pltpu.make_async_copy(docs_ref, docs, sems.at[1]),
        pltpu.make_async_copy(
            keys_ref, out_ref.at[pl.ds(0, TILE), pl.ds(0, KV_HEADS * HEAD)], sems.at[2]
        ),
    ]
    for move in moves:
        move.start()
    moves[0].wait()
    for h in range(KV_HEADS):
        out_ref[0:TILE, (KV_HEADS + h) * HEAD : (KV_HEADS + h + 1) * HEAD] = (
            values[:, h * HEAD : (h + 1) * HEAD].astype(F32).T.astype(BF16)
        )
    moves[1].wait()
    out_ref[TILE:KV_ROWS, :] = jnp.zeros((KV_ROWS - TILE, 4 * HEAD), BF16)
    out_ref[TILE:KV_ROWS, 0:HEAD] = jnp.broadcast_to(
        docs[...].astype(F32), (KV_ROWS - TILE, TILE)
    ).astype(BF16)
    moves[2].wait()


def select_kernel(planes, pos_ref, *refs):
    sources, (qs_ref, xs_ref, facts_ref) = refs[:4], refs[4:7]
    routes_ref, docs_ref, q_ref, x_ref, sems = refs[7:]
    moves = [
        pltpu.make_async_copy(source, target, sems.at[i])
        for i, (source, target) in enumerate(zip(sources, refs[7:11]))
    ]
    for move in moves:
        move.start()
    for move in moves:
        move.wait()
    z = pos_ref[0] // SHARDS
    members, ranks = slot_rows(routes_ref[...], [lax.rem(z + k, planes) for k in range(planes)])
    docs = docs_ref[...].astype(F32)
    lane_slot = (lax.broadcasted_iota(jnp.int32, (TILE, TILE), 0) % SLOTS).astype(F32)
    token = lax.broadcasted_iota(jnp.int32, (1, TILE), 1).astype(F32)
    facts = jnp.concatenate(
        [token, docs, jnp.ones((1, TILE), F32), jnp.zeros((5, TILE), F32)], axis=0
    ).astype(BF16)
    picks = [
        jnp.where(ranks[k : k + 1] == lane_slot, members[k : k + 1], 0.0) for k in range(planes)
    ]
    chooser = jnp.concatenate([p[:SLOTS] for p in picks], axis=0).astype(BF16)
    q_rows = dot(chooser, q_ref[...])
    xs_ref[...] = dot(chooser, x_ref[...])
    for k in range(planes):
        known = dot(facts, picks[k].astype(BF16), 1, 1)
        facts_ref[:, k * TILE : (k + 1) * TILE] = jnp.concatenate(
            [known[0:1], known[1:2] + (1.0 - known[2:3]) * docs[:, 0:1], known[2:]], axis=0
        )
        for h in range(KV_HEADS):
            stack = jnp.concatenate(
                [
                    q_rows[k * SLOTS : (k + 1) * SLOTS, a * HEAD : (a + 1) * HEAD]
                    for a in range(h * GROUP, (h + 1) * GROUP)
                ],
                axis=0,
            )
            qs_ref[h, :, k * TILE : (k + 1) * TILE] = stack.T.astype(BF16)


def doc_starts(n, pos, held):
    sums = [jnp.zeros((1, TILE), F32) for _ in range(3)]
    for s in range(n):
        docs = held[s, TILE:KV_ROWS, 0:HEAD].astype(F32)[0:1]
        ahead = (pos - s < 0).astype(F32)
        behind = (pos - s > reach(n)).astype(F32)
        known = 1.0 - ahead - behind
        docs = jnp.where(known > 0.5, docs, 0.0) + 9.0 * ahead
        for d in range(3):
            sums[d] = sums[d] + jnp.where(docs < d + 1.0, 1.0, 0.0)
    return [jnp.sum(s, axis=1, keepdims=True) for s in sums]


def starts_of(docs, starts):
    first = jnp.zeros_like(docs)
    for d in range(3):
        first = jnp.where(docs == d + 1.0, starts[d], first)
    return first


def flash(pos, held, queries, kv_heads, sides, acc_ref, bias_ref, places, firsts):
    lanes = places[0].shape[1]
    chains = range(len(queries))
    for i in chains:
        acc_ref[i] = jnp.zeros((HEAD + EXTRA, lanes), F32)
    lowest = functools.reduce(jnp.minimum, [jnp.min(first) for first in firsts])
    highest = functools.reduce(jnp.maximum, [jnp.max(first) for first in firsts])
    low = lowest.astype(jnp.int32) // KEYS
    last = pos // (KEYS // TILE)
    clear = jnp.minimum((highest.astype(jnp.int32) + KEYS - 1) // KEYS, last)

    def scores(kb, i, masked):
        h = kv_heads[i]
        keys = jnp.concatenate(
            [held[2 * kb + t, 0:TILE, h * HEAD : (h + 1) * HEAD] for t in range(2)], axis=0
        )
        result = dot(keys, queries[i]())
        if masked:
            result = result + bias_ref[sides[i]]
        return result

    def hide(kb):
        key_at = (kb * KEYS + lax.broadcasted_iota(jnp.int32, (KEYS, 1), 0)).astype(F32)
        for side, (place, first) in enumerate(zip(places, firsts)):
            bias_ref[side] = jnp.where((key_at >= first) & (key_at <= place), 0.0, LOW)

    def over_keys(step, state):
        def edge(j, carried):
            kb = jnp.where(j < clear - low, low + j, last)
            hide(kb)
            return step(kb, carried, True)

        state = lax.fori_loop(0, clear - low + 1, edge, state)
        return lax.fori_loop(clear, last, lambda kb, carried: step(kb, carried, False), state)

    def eights(x):
        return x.reshape(KEYS // 8, 8, lanes)

    def find(kb, carried, masked):
        return tuple(
            jnp.maximum(carried[i], jnp.max(eights(scores(kb, i, masked)), axis=0)) for i in chains
        )

    tops = over_keys(find, tuple(jnp.full((8, lanes), LOW, F32) for _ in chains))
    tops = [jnp.max(top, axis=0, keepdims=True) for top in tops]

    def add(kb, carried, masked):
        for i in chains:
            at = (KV_HEADS + kv_heads[i]) * HEAD
            values = jnp.concatenate(
                [held[2 * kb + t, 0:TILE, at : at + HEAD] for t in range(2)], axis=1
            )
            values = jnp.concatenate([values, jnp.ones((EXTRA, KEYS), BF16)], axis=0)
            weights = jnp.exp(((scores(kb, i, masked) - tops[i]) * SCALE).astype(BF16))
            acc_ref[i] += dot(values, weights)
        return carried

    over_keys(add, 0)
    return [(acc_ref[i, 0:HEAD] / acc_ref[i, HEAD : HEAD + 1]).T for i in chains]


def routed_kernel(n, senders, pos_ref, gain_ref, qs_ref, xs_ref, facts_ref, *refs):
    planes = n // SHARDS
    count = len(senders)
    pieces = refs[:count]
    outs = refs[count : count + planes]
    held = refs[count + planes]
    acc, bias, state, gain, sems = refs[count + planes + 1 :]
    pos = pos_ref[0]
    z, y, c = pos // SHARDS, (pos // 2) % 2, pos % 2
    copies = []
    for i, (flip_c, flip_y, k) in enumerate(senders):
        sender = lax.rem(z - k + planes, planes) * SHARDS + (y ^ flip_y) * 2 + (c ^ flip_c)
        copies.append(pltpu.make_async_copy(pieces[i], held.at[sender], sems.at[i]))
    copies.append(pltpu.make_async_copy(gain_ref, gain, sems.at[count]))
    for copy in copies:
        copy.start()
    for copy in copies:
        copy.wait()
    starts = doc_starts(n, pos, held)
    lanes = 2 * TILE
    base = (pos * TILE).astype(F32)
    for pair in range(0, planes // 2, 2):
        parts = range(pair, min(pair + 2, planes // 2))
        columns = [slice(part * lanes, (part + 1) * lanes) for part in parts]
        chains = [(i, h) for i in range(len(parts)) for h in range(KV_HEADS)]
        done = flash(
            pos,
            held,
            [lambda i=i, h=h: qs_ref[h, :, columns[i]] for i, h in chains],
            [h for _, h in chains],
            [i for i, _ in chains],
            acc,
            bias,
            [facts_ref[0:1, at] + base for at in columns],
            [starts_of(facts_ref[1:2, at], starts) for at in columns],
        )
        for (i, h), rows in zip(chains, done):
            for k in range(2):
                row = (parts[i] * 2 + k) * SLOTS
                for g in range(GROUP):
                    lane = (h * GROUP + g) * HEAD
                    state[row : row + SLOTS, lane : lane + HEAD] = (
                        xs_ref[row : row + SLOTS, lane : lane + HEAD]
                        + rows[k * TILE + g * SLOTS : k * TILE + (g + 1) * SLOTS]
                    )
    for k in range(planes):
        hidden = state[k * SLOTS : (k + 1) * SLOTS, :]
        mean = jnp.mean(hidden * hidden, axis=1, keepdims=True)
        outs[k][...] = (hidden * lax.rsqrt(mean + 1e-06) * gain[...]).astype(BF16)


def expert_kernel(n, count, *refs):
    pieces = refs[:count]
    wg, wu, wd = refs[count : count + 3]
    keep_ref, send_ref, rows = refs[count + 4 :]
    width = rows.shape[1]
    total = n * SLOTS
    out_rows = min(total, 16 * SLOTS)
    half = total // 2
    step = 1024
    for at in range(0, total, out_rows):
        for col in range(0, width, step):
            parts, first = [], 0
            for piece in pieces:
                size = piece.shape[0]
                low, high = max(at - first, 0), min(at + out_rows - first, size)
                if low < high:
                    parts.append(piece[low:high, col : col + step].astype(F32))
                first += size
            rows[:, col : col + step] = jnp.concatenate(parts, axis=0).astype(BF16)
        gate = dot(rows[...], wg[...])
        up = dot(rows[...], wu[...])
        act = (gate / (1.0 + jnp.exp(-gate)) * up).astype(BF16)
        for col in range(0, width, step):
            part = dot(act, wd[:, col : col + step]).astype(BF16)
            if out_rows > half:
                keep_ref[:, col : col + step] = part[:half]
                send_ref[:, col : col + step] = part[half:]
            elif at < half:
                keep_ref[at : at + out_rows, col : col + step] = part
            else:
                send_ref[at - half : at - half + out_rows, col : col + step] = part


def own_kernel(n, part, loads, pos_ref, held, q_ref, x_ref, _, *refs):
    sources, (h_ref, done_ref) = refs[:loads], refs[loads : loads + 2]
    targets = refs[loads + 2 : 2 * loads + 2]
    acc, bias, qt, sems = refs[2 * loads + 2 :]
    moves = [
        pltpu.make_async_copy(source.at[0], target, sems.at[i])
        for i, (source, target) in enumerate(zip(sources, targets))
    ]
    for move in moves:
        move.start()
    done_ref[...] = jnp.zeros((8, TILE), F32)
    pos = pos_ref[0]
    starts = doc_starts(n, pos, held)
    first = starts_of(held[pos, TILE:KV_ROWS, 0:HEAD].astype(F32)[0:1], starts)
    place = (pos * TILE + lax.broadcasted_iota(jnp.int32, (1, TILE), 1)).astype(F32)
    place = jnp.concatenate([place] * 2, axis=1)
    first = jnp.concatenate([first] * 2, axis=1)

    for a in range(8):
        qt[a // 2, :, (a % 2) * TILE : (a % 2 + 1) * TILE] = (
            q_ref[:, a * HEAD : (a + 1) * HEAD].astype(F32).T.astype(BF16)
        )
    done = flash(
        pos,
        held,
        [lambda i=i: qt[i] for i in range(4)],
        [part // 2] * 4,
        [0] * 4,
        acc,
        bias,
        [place],
        [first],
    )
    for i in range(4):
        for g in range(2):
            lane = (2 * i + g) * HEAD
            h_ref[:, lane : lane + HEAD] = (
                x_ref[:, lane : lane + HEAD].astype(F32) + done[i][g * TILE : (g + 1) * TILE]
            )
    for move in moves:
        move.wait()


def combine_kernel(planes, pos_ref, routes_ref, gates_ref, *refs):
    halves, parts, out_ref = refs[:4], refs[4 : 4 + planes], refs[4 + planes]
    z = pos_ref[0] // SHARDS
    routes = routes_ref[...]
    gates = gates_ref[...]
    experts = [lax.rem(z + k, planes) for k in range(planes)]
    members, ranks = slot_rows(routes, experts)
    slot = lax.broadcasted_iota(jnp.int32, (SLOTS, TILE), 0).astype(F32)
    mix = []
    for k, e in enumerate(experts):
        gate = jnp.sum(jnp.where(routes == e, gates, 0.0), axis=0, keepdims=True)
        mix.append(jnp.where(ranks[k : k + 1] == slot, gate, 0.0))
    mix = jnp.concatenate(mix, axis=0).T
    mix_high = mix.astype(BF16)
    mix_low = (mix - mix_high.astype(F32)).astype(BF16)
    size = halves[0].shape[1]
    for i, h in enumerate(halves):
        columns = slice(i * size, (i + 1) * size)
        rows = jnp.concatenate([p[:, columns].astype(F32) for p in parts], axis=0).astype(BF16)
        out_ref[:, columns] = (h[...] + dot(mix_high, rows) + dot(mix_low, rows)).astype(BF16)


def pin(x):
    return pltpu.with_memory_space_constraint(x, pltpu.HBM)


def params(mib):
    return pltpu.CompilerParams(vmem_limit_bytes=mib * 1024 * 1024)


def local(
    resid, queries, keys, values, doc_ids, norm_gain, routes, route_weights, w_gate, w_up, w_down
):
    n = lax.axis_size("expert")
    planes = n // SHARDS
    pos = lax.axis_index("expert").astype(jnp.int32).reshape(1)
    tokens, width = queries.shape
    hidden = w_gate.shape[2]
    routes_t = routes.T
    gates_t = route_weights.T
    docs = doc_ids.reshape(1, tokens)
    small = 24 if n <= 16 else 60
    back = reach(n)

    packed = pl.pallas_call(
        pack_kernel,
        out_shape=jax.ShapeDtypeStruct((KV_ROWS, 4 * HEAD), BF16),
        in_specs=[HBM] * 3,
        out_specs=VMEM,
        scratch_shapes=[
            pltpu.VMEM((1, tokens), jnp.int32),
            pltpu.VMEM((tokens, KV_HEADS * HEAD), BF16),
            pltpu.SemaphoreType.DMA((3,)),
        ],
        compiler_params=params(8),
        name="pack",
    )(pin(docs), pin(keys), pin(values))

    def move(value, pairs):
        return lax.ppermute(value, "expert", pairs)

    def needed(k, y_from, y_to):
        gaps = [
            k * SHARDS + 2 * (y_to - y_from) + (to - of) for to in range(2) for of in range(2)
        ]
        return any(0 <= gap <= back for gap in gaps)

    far = max(k for k in range(planes) if any(needed(k, a, b) for a in (0, 1) for b in (0, 1)))
    q_rows, x_rows, facts = pl.pallas_call(
        functools.partial(select_kernel, planes),
        out_shape=[
            jax.ShapeDtypeStruct((KV_HEADS, HEAD, planes * TILE), BF16),
            jax.ShapeDtypeStruct((planes * SLOTS, width), F32),
            jax.ShapeDtypeStruct((8, planes * TILE), F32),
        ],
        in_specs=[SMEM] + [HBM] * 4,
        out_specs=[VMEM] * 3,
        scratch_shapes=[
            pltpu.VMEM(routes_t.shape, jnp.int32),
            pltpu.VMEM(docs.shape, jnp.int32),
            pltpu.VMEM(queries.shape, BF16),
            pltpu.VMEM(resid.shape, BF16),
            pltpu.SemaphoreType.DMA((4,)),
        ],
        compiler_params=params(small),
        name="select",
    )(pos, pin(routes_t), pin(docs), pin(queries), pin(resid))

    flip_y = [(s, s ^ 2) for s in range(n)]
    flip_c = [(s, s ^ 1) for s in range(n)]
    kv = {(0, 0, 0): packed}
    for k in range(far + 1):
        pairs = [(s, s ^ 2 if s >= k * SHARDS else s) for s in range(n)]
        across, onward = move(kv[0, 0, k], pairs), None
        if k < far:
            used = [
                any(needed(j, y, to) for to in (0, 1) for j in range(k + 1, far + 1))
                for y in (0, 1)
            ]
            pairs = [(s, (s + SHARDS) % n if used[s // 2 % 2] else s) for s in range(n)]
            onward = move(kv[0, 0, k], pairs)
            across, onward, q_rows = lax.optimization_barrier((across, onward, q_rows))
            kv[0, 0, k + 1] = onward
        kv[0, 1, k] = across
    for (_, side, k), piece in list(kv.items()):
        kv[1, side, k] = move(piece, flip_c)

    *sent, held = pl.pallas_call(
        functools.partial(routed_kernel, n, list(kv)),
        out_shape=[jax.ShapeDtypeStruct((SLOTS, width), BF16)] * planes
        + [jax.ShapeDtypeStruct((n, KV_ROWS, 4 * HEAD), BF16)],
        in_specs=[SMEM, HBM] + [VMEM] * 3 + [ANY] * len(kv),
        out_specs=[VMEM] * (planes + 1),
        scratch_shapes=[
            pltpu.VMEM((4, HEAD + EXTRA, 2 * TILE), F32),
            pltpu.VMEM((2, KEYS, 2 * TILE), F32),
            pltpu.VMEM((planes * SLOTS, width), F32),
            pltpu.VMEM((1, width), F32),
            pltpu.SemaphoreType.DMA((len(kv) + 1,)),
        ],
        compiler_params=params(small),
        name="routed",
    )(pos, pin(norm_gain.reshape(1, width)), q_rows, x_rows, facts, *kv.values())

    def own(part, after, *sources):
        columns = pl.BlockSpec((tokens, 8 * HEAD), lambda i: (0, part))
        return pl.pallas_call(
            functools.partial(own_kernel, n, part, len(sources)),
            out_shape=[
                jax.ShapeDtypeStruct((tokens, 8 * HEAD), F32),
                jax.ShapeDtypeStruct((8, TILE), F32),
            ]
            + [jax.ShapeDtypeStruct(w.shape[1:], BF16) for w in sources],
            grid=(1,),
            in_specs=[SMEM, VMEM, columns, columns, ANY] + [HBM] * len(sources),
            out_specs=[
                pl.BlockSpec((tokens, 8 * HEAD), lambda i: (0, 0)),
                pl.BlockSpec((8, TILE), lambda i: (0, 0)),
            ]
            + [VMEM] * len(sources),
            scratch_shapes=[
                pltpu.VMEM((4, HEAD + EXTRA, 2 * TILE), F32),
                pltpu.VMEM((1, KEYS, 2 * TILE), F32),
                pltpu.VMEM((4, HEAD, 2 * TILE), BF16),
                pltpu.SemaphoreType.DMA((3,)),
            ],
            compiler_params=params(small),
            cost_estimate=pl.CostEstimate(
                flops=2_000_000_000, bytes_accessed=8_000_000, transcendentals=2_000_000
            ),
            name="own",
        )(pos, held, queries, resid, after, *map(pin, sources))

    half0, done, *weights = own(0, sent[0], w_gate, w_up, w_down)
    half1, late = own(1, done)
    halves = [half0, half1]

    come = [
        move(sent[k], [(s, (s + k * SHARDS) % n) for s in range(n)]) for k in range(1, planes)
    ]
    next_door = move(sent[0], flip_y)
    come, next_door, done = lax.optimization_barrier((come, next_door, done))
    here = [sent[0], jnp.concatenate(come, axis=0)]
    there = [next_door, move(here[1], flip_y)]
    mate = move(jnp.concatenate(here, axis=0), flip_c)
    there, mate, late = lax.optimization_barrier((there, mate, late))
    pieces = here + there + [mate, move(jnp.concatenate(there, axis=0), flip_c)]

    half = jax.ShapeDtypeStruct((n * SLOTS // 2, width), BF16)
    keep, send = pl.pallas_call(
        functools.partial(expert_kernel, n, len(pieces)),
        out_shape=[half, half],
        in_specs=[VMEM] * (len(pieces) + 3) + [ANY],
        out_specs=[VMEM, VMEM],
        scratch_shapes=[pltpu.VMEM((16 * SLOTS, width), BF16)],
        compiler_params=params(16),
        cost_estimate=pl.CostEstimate(
            flops=1_200_000_000, bytes_accessed=12_000_000, transcendentals=50_000
        ),
        name="expert",
    )(*pieces, *weights, late)

    halves += [own(part, keep)[0] for part in range(2, 4)]

    total = keep.astype(F32) + move(send, [(s, s ^ 1) for s in range(n)]).astype(F32)
    quarter = n * SLOTS // 4
    other = move(total[quarter:].astype(BF16), [(s, s ^ 2) for s in range(n)])
    total = (total[:quarter] + other.astype(F32)).astype(BF16)
    parts = [total[:SLOTS]]
    for k in range(1, planes):
        parts.append(
            move(
                total[k * SLOTS : (k + 1) * SLOTS], [(s, (s - k * SHARDS) % n) for s in range(n)]
            )
        )

    return pl.pallas_call(
        functools.partial(combine_kernel, planes),
        out_shape=jax.ShapeDtypeStruct((tokens, width), BF16),
        in_specs=[SMEM] + [VMEM] * (6 + planes),
        out_specs=VMEM,
        compiler_params=params(small),
        name="combine",
    )(pos, routes_t, gates_t, *halves, *parts)


def solution(mesh):
    rows = P(("groups", "expert"), None)
    in_specs = (rows,) * 4 + (P(("groups", "expert")), P(), rows, rows) + (
        P("expert", None, None),
    ) * 3
    return jax.shard_map(local, mesh=mesh, in_specs=in_specs, out_specs=rows, check_vma=False)
```

```python
import functools
import math

import jax
import jax.numpy as jnp
from jax import lax
from jax.experimental import pallas as pl
from jax.experimental.pallas import tpu as pltpu
from jax.sharding import PartitionSpec as P

HEAD = 128
QUERY_HEADS = 32
KV_HEADS = 2
GROUP = QUERY_HEADS // KV_HEADS
SHARDS = 4
SLOTS = 8
TILE = 128
KEYS = 256
KV_ROWS = TILE + 16
SCALE = math.log2(math.e) / math.sqrt(HEAD)
LOW = -1e30
EXTRA = 16
F32 = jnp.float32
BF16 = jnp.bfloat16
VMEM = pl.BlockSpec(memory_space=pltpu.VMEM)
SMEM = pl.BlockSpec(memory_space=pltpu.SMEM)
ANY = pl.BlockSpec(memory_space=pl.ANY)
HBM = pl.BlockSpec(memory_space=pltpu.HBM)


def dot(a, b, ca=1, cb=0):
    return lax.dot_general(a, b, (((ca,), (cb,)), ((), ())), preferred_element_type=F32)


def reach(n):
    longest = n * TILE // 2 + 256
    return (longest - 1 + TILE - 1) // TILE


def slot_rows(routes, experts):
    members = jnp.concatenate(
        [jnp.max((routes == e).astype(F32), axis=0, keepdims=True) for e in experts], axis=0
    )
    count = len(experts)
    padded = -(-count // 8) * 8
    wide = members
    if padded > count:
        wide = jnp.concatenate([members, jnp.zeros((padded - count, TILE), F32)], axis=0)
    before = lax.broadcasted_iota(jnp.int32, (TILE, TILE), 0) < lax.broadcasted_iota(
        jnp.int32, (TILE, TILE), 1
    )
    ranks = dot(wide.astype(BF16), before.astype(F32).astype(BF16))
    return members, ranks


def pack_kernel(docs_ref, keys_ref, values_ref, out_ref, docs, values, sems):
    moves = [
        pltpu.make_async_copy(values_ref, values, sems.at[0]),
        pltpu.make_async_copy(docs_ref, docs, sems.at[1]),
        pltpu.make_async_copy(
            keys_ref, out_ref.at[pl.ds(0, TILE), pl.ds(0, KV_HEADS * HEAD)], sems.at[2]
        ),
    ]
    for move in moves:
        move.start()
    moves[0].wait()
    for h in range(KV_HEADS):
        out_ref[0:TILE, (KV_HEADS + h) * HEAD : (KV_HEADS + h + 1) * HEAD] = (
            values[:, h * HEAD : (h + 1) * HEAD].astype(F32).T.astype(BF16)
        )
    moves[1].wait()
    out_ref[TILE:KV_ROWS, :] = jnp.zeros((KV_ROWS - TILE, 4 * HEAD), BF16)
    out_ref[TILE:KV_ROWS, 0:HEAD] = jnp.broadcast_to(
        docs[...].astype(F32), (KV_ROWS - TILE, TILE)
    ).astype(BF16)
    moves[2].wait()


def select_kernel(planes, pos_ref, *refs):
    sources, (qs_ref, xs_ref, facts_ref) = refs[:4], refs[4:7]
    routes_ref, docs_ref, q_ref, x_ref, sems = refs[7:]
    moves = [
        pltpu.make_async_copy(source, target, sems.at[i])
        for i, (source, target) in enumerate(zip(sources, refs[7:11]))
    ]
    for move in moves:
        move.start()
    for move in moves:
        move.wait()
    z = pos_ref[0] // SHARDS
    members, ranks = slot_rows(routes_ref[...], [lax.rem(z + k, planes) for k in range(planes)])
    docs = docs_ref[...].astype(F32)
    lane_slot = (lax.broadcasted_iota(jnp.int32, (TILE, TILE), 0) % SLOTS).astype(F32)
    token = lax.broadcasted_iota(jnp.int32, (1, TILE), 1).astype(F32)
    facts = jnp.concatenate(
        [token, docs, jnp.ones((1, TILE), F32), jnp.zeros((5, TILE), F32)], axis=0
    ).astype(BF16)
    picks = [
        jnp.where(ranks[k : k + 1] == lane_slot, members[k : k + 1], 0.0) for k in range(planes)
    ]
    chooser = jnp.concatenate([p[:SLOTS] for p in picks], axis=0).astype(BF16)
    q_rows = dot(chooser, q_ref[...])
    xs_ref[...] = dot(chooser, x_ref[...])
    for k in range(planes):
        known = dot(facts, picks[k].astype(BF16), 1, 1)
        facts_ref[:, k * TILE : (k + 1) * TILE] = jnp.concatenate(
            [known[0:1], known[1:2] + (1.0 - known[2:3]) * docs[:, 0:1], known[2:]], axis=0
        )
        for h in range(KV_HEADS):
            stack = jnp.concatenate(
                [
                    q_rows[k * SLOTS : (k + 1) * SLOTS, a * HEAD : (a + 1) * HEAD]
                    for a in range(h * GROUP, (h + 1) * GROUP)
                ],
                axis=0,
            )
            for i, term in enumerate(two_terms(stack.T)):
                qs_ref[h, i * HEAD : (i + 1) * HEAD, k * TILE : (k + 1) * TILE] = term


def doc_starts(n, pos, held):
    sums = [jnp.zeros((1, TILE), F32) for _ in range(3)]
    for s in range(n):
        docs = held[s, TILE:KV_ROWS, 0:HEAD].astype(F32)[0:1]
        ahead = (pos - s < 0).astype(F32)
        behind = (pos - s > reach(n)).astype(F32)
        known = 1.0 - ahead - behind
        docs = jnp.where(known > 0.5, docs, 0.0) + 9.0 * ahead
        for d in range(3):
            sums[d] = sums[d] + jnp.where(docs < d + 1.0, 1.0, 0.0)
    return [jnp.sum(s, axis=1, keepdims=True) for s in sums]


def starts_of(docs, starts):
    first = jnp.zeros_like(docs)
    for d in range(3):
        first = jnp.where(docs == d + 1.0, starts[d], first)
    return first


def two_terms(x):
    scaled = x.astype(F32) * SCALE
    high = scaled.astype(BF16)
    return high, (scaled - high.astype(F32)).astype(BF16)


def key_steps(pos, place, first, axis, bias_ref, step, state):
    low = jnp.min(first).astype(jnp.int32) // KEYS
    last = pos // (KEYS // TILE)
    clear = jnp.minimum((jnp.max(first).astype(jnp.int32) + KEYS - 1) // KEYS, last)
    shape = (KEYS, 1) if axis == 0 else (1, KEYS)

    def edge(j, carried):
        kb = jnp.where(j < clear - low, low + j, last)
        key_at = (kb * KEYS + lax.broadcasted_iota(jnp.int32, shape, axis)).astype(F32)
        bias_ref[...] = jnp.where((key_at >= first) & (key_at <= place), 0.0, LOW)
        return step(kb, carried, True)

    state = lax.fori_loop(0, clear - low + 1, edge, state)
    return lax.fori_loop(clear, last, lambda kb, carried: step(kb, carried, False), state)


def keys_of(held, kb, h):
    keys = jnp.concatenate(
        [held[2 * kb + t, 0:TILE, h * HEAD : (h + 1) * HEAD] for t in range(2)], axis=0
    )
    return jnp.concatenate([keys, keys], axis=1)


def values_of(held, kb, h, extra):
    at = (KV_HEADS + h) * HEAD
    values = jnp.concatenate(
        [held[2 * kb + t, 0:TILE, at : at + HEAD] for t in range(2)], axis=1
    )
    return jnp.concatenate([values, jnp.ones((extra, KEYS), BF16)], axis=0)


def flash(pos, held, q_ref, kv_heads, acc_ref, bias_ref, place, first):
    lanes = place.shape[1]
    chains = range(len(kv_heads))
    for i in chains:
        acc_ref[i] = jnp.zeros((HEAD + EXTRA, lanes), F32)

    def step(kb, tops, masked):
        out = []
        for i in chains:
            scores = dot(keys_of(held, kb, kv_heads[i]), q_ref[i])
            if masked:
                scores = scores + bias_ref[...]
            top = jnp.maximum(tops[i], jnp.max(scores, axis=0, keepdims=True))
            weights = jnp.exp2(scores - top).astype(BF16)
            acc_ref[i] = acc_ref[i] * jnp.exp2(tops[i] - top) + dot(
                values_of(held, kb, kv_heads[i], EXTRA), weights
            )
            out.append(top)
        return tuple(out)

    tops = tuple(jnp.full((1, lanes), LOW, F32) for _ in chains)
    key_steps(pos, place, first, 0, bias_ref, step, tops)
    return [(acc_ref[i, 0:HEAD] / acc_ref[i, HEAD : HEAD + 1]).T for i in chains]


def flash_rows(pos, held, q_ref, h, acc_ref, top_ref, bias_ref, place, first):
    rows = q_ref.shape[0]
    acc_ref[...] = jnp.zeros((rows, 2 * HEAD), F32)
    top_ref[...] = jnp.full((rows, HEAD), LOW, F32)

    def step(kb, carried, masked):
        scores = dot(q_ref[...], keys_of(held, kb, h), 1, 1)
        if masked:
            scores = scores + jnp.concatenate([bias_ref[...]] * (rows // TILE), axis=0)
        old = top_ref[...]
        top = jnp.maximum(old, jnp.max(scores, axis=1, keepdims=True))
        top_ref[...] = top
        weights = jnp.exp2(scores - jnp.concatenate([top, top], axis=1)).astype(BF16)
        factor = jnp.exp2(old - top)
        acc_ref[...] = acc_ref[...] * jnp.concatenate([factor, factor], axis=1) + dot(
            weights, values_of(held, kb, h, HEAD), 1, 1
        )
        return carried

    key_steps(pos, place, first, 1, bias_ref, step, 0)
    return acc_ref[:, 0:HEAD] / acc_ref[:, HEAD:]


def routed_kernel(n, senders, pos_ref, gain_ref, qs_ref, xs_ref, facts_ref, *refs):
    planes = n // SHARDS
    count = len(senders)
    pieces = refs[:count]
    outs = refs[count : count + planes]
    held = refs[count + planes]
    acc, bias, q_scr, state, gain, sems = refs[count + planes + 1 :]
    pos = pos_ref[0]
    z, y, c = pos // SHARDS, (pos // 2) % 2, pos % 2
    copies = []
    for i, (flip_c, flip_y, k) in enumerate(senders):
        sender = lax.rem(z - k + planes, planes) * SHARDS + (y ^ flip_y) * 2 + (c ^ flip_c)
        copies.append(pltpu.make_async_copy(pieces[i], held.at[sender], sems.at[i]))
    copies.append(pltpu.make_async_copy(gain_ref, gain, sems.at[count]))
    for copy in copies:
        copy.start()
    for copy in copies:
        copy.wait()
    starts = doc_starts(n, pos, held)
    lanes = q_scr.shape[2]
    base = (pos * TILE).astype(F32)
    for part in range(planes * TILE // lanes):
        at = slice(part * lanes, (part + 1) * lanes)
        q_scr[...] = qs_ref[:, :, at]
        done = flash(
            pos,
            held,
            q_scr,
            range(KV_HEADS),
            acc,
            bias,
            facts_ref[0:1, at] + base,
            starts_of(facts_ref[1:2, at], starts),
        )
        for h in range(KV_HEADS):
            for k in range(lanes // TILE):
                row = (part * (lanes // TILE) + k) * SLOTS
                for g in range(GROUP):
                    lane = (h * GROUP + g) * HEAD
                    state[row : row + SLOTS, lane : lane + HEAD] = (
                        xs_ref[row : row + SLOTS, lane : lane + HEAD]
                        + done[h][k * TILE + g * SLOTS : k * TILE + (g + 1) * SLOTS]
                    )
    for k in range(planes):
        hidden = state[k * SLOTS : (k + 1) * SLOTS, :]
        mean = jnp.mean(hidden * hidden, axis=1, keepdims=True)
        outs[k][...] = (hidden * lax.rsqrt(mean + 1e-06) * gain[...]).astype(BF16)


def expert_kernel(n, count, *refs):
    pieces = refs[:count]
    wg, wu, wd = refs[count : count + 3]
    keep_ref, send_ref, rows = refs[count + 4 :]
    width = rows.shape[1]
    total = n * SLOTS
    out_rows = min(total, 16 * SLOTS)
    half = total // 2
    step = 1024
    for at in range(0, total, out_rows):
        for col in range(0, width, step):
            parts, first = [], 0
            for piece in pieces:
                size = piece.shape[0]
                low, high = max(at - first, 0), min(at + out_rows - first, size)
                if low < high:
                    parts.append(piece[low:high, col : col + step].astype(F32))
                first += size
            rows[:, col : col + step] = jnp.concatenate(parts, axis=0).astype(BF16)
        gate = dot(rows[...], wg[...])
        up = dot(rows[...], wu[...])
        act = (gate / (1.0 + jnp.exp(-gate)) * up).astype(BF16)
        for col in range(0, width, step):
            part = dot(act, wd[:, col : col + step]).astype(BF16)
            if out_rows > half:
                keep_ref[:, col : col + step] = part[:half]
                send_ref[:, col : col + step] = part[half:]
            elif at < half:
                keep_ref[at : at + out_rows, col : col + step] = part
            else:
                send_ref[at - half : at - half + out_rows, col : col + step] = part


def own_kernel(n, part, loads, pos_ref, held, q_ref, x_ref, _, *refs):
    sources, (h_ref, done_ref) = refs[:loads], refs[loads : loads + 2]
    targets = refs[loads + 2 : 2 * loads + 2]
    acc, bias, top, qt, sems = refs[2 * loads + 2 :]
    moves = [
        pltpu.make_async_copy(source.at[0], target, sems.at[i])
        for i, (source, target) in enumerate(zip(sources, targets))
    ]
    for move in moves:
        move.start()
    done_ref[...] = jnp.zeros((8, TILE), F32)
    pos = pos_ref[0]
    starts = doc_starts(n, pos, held)
    first = starts_of(held[pos, TILE:KV_ROWS, 0:HEAD].astype(F32)[0:1], starts)
    place = (pos * TILE + lax.broadcasted_iota(jnp.int32, (1, TILE), 1)).astype(F32)
    if part < 2:
        for a in range(8):
            terms = two_terms(q_ref[:, a * HEAD : (a + 1) * HEAD].astype(F32).T)
            for i, term in enumerate(terms):
                qt[0, i * HEAD : (i + 1) * HEAD, a * TILE : (a + 1) * TILE] = term
        place = jnp.concatenate([place] * 8, axis=1)
        first = jnp.concatenate([first] * 8, axis=1)
        (done,) = flash(pos, held, qt, [part // 2], acc, bias, place, first)
    else:
        for a in range(8):
            for i, term in enumerate(two_terms(q_ref[:, a * HEAD : (a + 1) * HEAD])):
                qt[a * TILE : (a + 1) * TILE, i * HEAD : (i + 1) * HEAD] = term
        place = jnp.broadcast_to(place, (TILE, TILE)).T[:, 0:1]
        first = jnp.broadcast_to(first, (TILE, TILE)).T[:, 0:1]
        done = flash_rows(pos, held, qt, part // 2, acc, top, bias, place, first)
    for a in range(8):
        lane = a * HEAD
        h_ref[:, lane : lane + HEAD] = (
            x_ref[:, lane : lane + HEAD].astype(F32) + done[a * TILE : (a + 1) * TILE]
        )
    for move in moves:
        move.wait()


def combine_kernel(planes, pos_ref, routes_ref, gates_ref, *refs):
    halves, parts, out_ref = refs[:4], refs[4 : 4 + planes], refs[4 + planes]
    z = pos_ref[0] // SHARDS
    routes = routes_ref[...]
    gates = gates_ref[...]
    experts = [lax.rem(z + k, planes) for k in range(planes)]
    members, ranks = slot_rows(routes, experts)
    slot = lax.broadcasted_iota(jnp.int32, (SLOTS, TILE), 0).astype(F32)
    mix = []
    for k, e in enumerate(experts):
        gate = jnp.sum(jnp.where(routes == e, gates, 0.0), axis=0, keepdims=True)
        mix.append(jnp.where(ranks[k : k + 1] == slot, gate, 0.0))
    mix = jnp.concatenate(mix, axis=0).T
    mix_high = mix.astype(BF16)
    mix_low = (mix - mix_high.astype(F32)).astype(BF16)
    size = halves[0].shape[1]
    for i, h in enumerate(halves):
        columns = slice(i * size, (i + 1) * size)
        rows = jnp.concatenate([p[:, columns].astype(F32) for p in parts], axis=0).astype(BF16)
        out_ref[:, columns] = (h[...] + dot(mix_high, rows) + dot(mix_low, rows)).astype(BF16)


def pin(x):
    return pltpu.with_memory_space_constraint(x, pltpu.HBM)


def params(mib):
    return pltpu.CompilerParams(vmem_limit_bytes=mib * 1024 * 1024)


def local(
    resid, queries, keys, values, doc_ids, norm_gain, routes, route_weights, w_gate, w_up, w_down
):
    n = lax.axis_size("expert")
    planes = n // SHARDS
    pos = lax.axis_index("expert").astype(jnp.int32).reshape(1)
    tokens, width = queries.shape
    hidden = w_gate.shape[2]
    routes_t = routes.T
    gates_t = route_weights.T
    docs = doc_ids.reshape(1, tokens)
    small = 24 if n <= 16 else 60
    back = reach(n)

    packed = pl.pallas_call(
        pack_kernel,
        out_shape=jax.ShapeDtypeStruct((KV_ROWS, 4 * HEAD), BF16),
        in_specs=[HBM] * 3,
        out_specs=VMEM,
        scratch_shapes=[
            pltpu.VMEM((1, tokens), jnp.int32),
            pltpu.VMEM((tokens, KV_HEADS * HEAD), BF16),
            pltpu.SemaphoreType.DMA((3,)),
        ],
        compiler_params=params(8),
        name="pack",
    )(pin(docs), pin(keys), pin(values))

    def move(value, pairs):
        return lax.ppermute(value, "expert", pairs)

    def needed(k, y_from, y_to):
        gaps = [
            k * SHARDS + 2 * (y_to - y_from) + (to - of) for to in range(2) for of in range(2)
        ]
        return any(0 <= gap <= back for gap in gaps)

    far = max(k for k in range(planes) if any(needed(k, a, b) for a in (0, 1) for b in (0, 1)))
    q_rows, x_rows, facts = pl.pallas_call(
        functools.partial(select_kernel, planes),
        out_shape=[
            jax.ShapeDtypeStruct((KV_HEADS, 2 * HEAD, planes * TILE), BF16),
            jax.ShapeDtypeStruct((planes * SLOTS, width), F32),
            jax.ShapeDtypeStruct((8, planes * TILE), F32),
        ],
        in_specs=[SMEM] + [HBM] * 4,
        out_specs=[VMEM] * 3,
        scratch_shapes=[
            pltpu.VMEM(routes_t.shape, jnp.int32),
            pltpu.VMEM(docs.shape, jnp.int32),
            pltpu.VMEM(queries.shape, BF16),
            pltpu.VMEM(resid.shape, BF16),
            pltpu.SemaphoreType.DMA((4,)),
        ],
        compiler_params=params(small),
        name="select",
    )(pos, pin(routes_t), pin(docs), pin(queries), pin(resid))

    flip_y = [(s, s ^ 2) for s in range(n)]
    flip_c = [(s, s ^ 1) for s in range(n)]
    kv = {(0, 0, 0): packed}
    for k in range(far + 1):
        pairs = [(s, s ^ 2 if s >= k * SHARDS else s) for s in range(n)]
        across, onward = move(kv[0, 0, k], pairs), None
        if k < far:
            used = [
                any(needed(j, y, to) for to in (0, 1) for j in range(k + 1, far + 1))
                for y in (0, 1)
            ]
            pairs = [(s, (s + SHARDS) % n if used[s // 2 % 2] else s) for s in range(n)]
            onward = move(kv[0, 0, k], pairs)
            across, onward, q_rows = lax.optimization_barrier((across, onward, q_rows))
            kv[0, 0, k + 1] = onward
        kv[0, 1, k] = across
    for (_, side, k), piece in list(kv.items()):
        kv[1, side, k] = move(piece, flip_c)

    *sent, held = pl.pallas_call(
        functools.partial(routed_kernel, n, list(kv)),
        out_shape=[jax.ShapeDtypeStruct((SLOTS, width), BF16)] * planes
        + [jax.ShapeDtypeStruct((n, KV_ROWS, 4 * HEAD), BF16)],
        in_specs=[SMEM, HBM] + [VMEM] * 3 + [ANY] * len(kv),
        out_specs=[VMEM] * (planes + 1),
        scratch_shapes=[
            pltpu.VMEM((KV_HEADS, HEAD + EXTRA, 4 * TILE), F32),
            pltpu.VMEM((KEYS, 4 * TILE), F32),
            pltpu.VMEM((KV_HEADS, 2 * HEAD, 4 * TILE), BF16),
            pltpu.VMEM((planes * SLOTS, width), F32),
            pltpu.VMEM((1, width), F32),
            pltpu.SemaphoreType.DMA((len(kv) + 1,)),
        ],
        compiler_params=params(small),
        name="routed",
    )(pos, pin(norm_gain.reshape(1, width)), q_rows, x_rows, facts, *kv.values())

    def own(part, after, *sources):
        columns = pl.BlockSpec((tokens, 8 * HEAD), lambda i: (0, part))
        return pl.pallas_call(
            functools.partial(own_kernel, n, part, len(sources)),
            out_shape=[
                jax.ShapeDtypeStruct((tokens, 8 * HEAD), F32),
                jax.ShapeDtypeStruct((8, TILE), F32),
            ]
            + [jax.ShapeDtypeStruct(w.shape[1:], BF16) for w in sources],
            grid=(1,),
            in_specs=[SMEM, VMEM, columns, columns, ANY] + [HBM] * len(sources),
            out_specs=[
                pl.BlockSpec((tokens, 8 * HEAD), lambda i: (0, 0)),
                pl.BlockSpec((8, TILE), lambda i: (0, 0)),
            ]
            + [VMEM] * len(sources),
            scratch_shapes=[
                pltpu.VMEM((1, HEAD + EXTRA, 8 * TILE) if part < 2 else (8 * TILE, 2 * HEAD), F32),
                pltpu.VMEM((KEYS, 8 * TILE) if part < 2 else (TILE, KEYS), F32),
                pltpu.VMEM((8 * TILE, HEAD), F32),
                pltpu.VMEM((1, 2 * HEAD, 8 * TILE) if part < 2 else (8 * TILE, 2 * HEAD), BF16),
                pltpu.SemaphoreType.DMA((3,)),
            ],
            compiler_params=params(small),
            cost_estimate=pl.CostEstimate(
                flops=2_000_000_000, bytes_accessed=8_000_000, transcendentals=2_000_000
            ),
            name="own",
        )(pos, held, queries, resid, after, *map(pin, sources))

    half0, done, *weights = own(0, sent[0], w_gate, w_up, w_down)
    half1, late = own(1, done)
    halves = [half0, half1]

    come = [
        move(sent[k], [(s, (s + k * SHARDS) % n) for s in range(n)]) for k in range(1, planes)
    ]
    next_door = move(sent[0], flip_y)
    come, next_door, done = lax.optimization_barrier((come, next_door, done))
    here = [sent[0], jnp.concatenate(come, axis=0)]
    there = [next_door, move(here[1], flip_y)]
    mate = move(jnp.concatenate(here, axis=0), flip_c)
    there, mate, late = lax.optimization_barrier((there, mate, late))
    pieces = here + there + [mate, move(jnp.concatenate(there, axis=0), flip_c)]

    half = jax.ShapeDtypeStruct((n * SLOTS // 2, width), BF16)
    keep, send = pl.pallas_call(
        functools.partial(expert_kernel, n, len(pieces)),
        out_shape=[half, half],
        in_specs=[VMEM] * (len(pieces) + 3) + [ANY],
        out_specs=[VMEM, VMEM],
        scratch_shapes=[pltpu.VMEM((16 * SLOTS, width), BF16)],
        compiler_params=params(16),
        cost_estimate=pl.CostEstimate(
            flops=1_200_000_000, bytes_accessed=12_000_000, transcendentals=50_000
        ),
        name="expert",
    )(*pieces, *weights, late)

    halves += [own(part, keep)[0] for part in range(2, 4)]

    total = keep.astype(F32) + move(send, [(s, s ^ 1) for s in range(n)]).astype(F32)
    quarter = n * SLOTS // 4
    other = move(total[quarter:].astype(BF16), [(s, s ^ 2) for s in range(n)])
    total = (total[:quarter] + other.astype(F32)).astype(BF16)
    parts = [total[:SLOTS]]
    for k in range(1, planes):
        parts.append(
            move(
                total[k * SLOTS : (k + 1) * SLOTS], [(s, (s - k * SHARDS) % n) for s in range(n)]
            )
        )

    return pl.pallas_call(
        functools.partial(combine_kernel, planes),
        out_shape=jax.ShapeDtypeStruct((tokens, width), BF16),
        in_specs=[SMEM] + [VMEM] * (6 + planes),
        out_specs=VMEM,
        compiler_params=params(small),
        name="combine",
    )(pos, routes_t, gates_t, *halves, *parts)


def solution(mesh):
    rows = P(("groups", "expert"), None)
    in_specs = (rows,) * 4 + (P(("groups", "expert")), P(), rows, rows) + (
        P("expert", None, None),
    ) * 3
    return jax.shard_map(local, mesh=mesh, in_specs=in_specs, out_specs=rows, check_vma=False)
```

```python
import functools
import math

import jax
import jax.numpy as jnp
from jax import lax
from jax.experimental import pallas as pl
from jax.experimental.pallas import tpu as pltpu
from jax.sharding import PartitionSpec as P

HEAD = 128
QUERY_HEADS = 32
KV_HEADS = 2
GROUP = QUERY_HEADS // KV_HEADS
SHARDS = 4
SLOTS = 8
TILE = 128
KEYS = 256
KV_ROWS = TILE + 16
SCALE = math.log2(math.e) / math.sqrt(HEAD)
LOW = -1e30
EXTRA = 16
F32 = jnp.float32
BF16 = jnp.bfloat16
VMEM = pl.BlockSpec(memory_space=pltpu.VMEM)
SMEM = pl.BlockSpec(memory_space=pltpu.SMEM)
ANY = pl.BlockSpec(memory_space=pl.ANY)
HBM = pl.BlockSpec(memory_space=pltpu.HBM)


def dot(a, b, ca=1, cb=0):
    return lax.dot_general(a, b, (((ca,), (cb,)), ((), ())), preferred_element_type=F32)


def reach(n):
    longest = n * TILE // 2 + 256
    return (longest - 1 + TILE - 1) // TILE


def slot_rows(routes, experts):
    members = jnp.concatenate(
        [jnp.max((routes == e).astype(F32), axis=0, keepdims=True) for e in experts], axis=0
    )
    count = len(experts)
    padded = -(-count // 8) * 8
    wide = members
    if padded > count:
        wide = jnp.concatenate([members, jnp.zeros((padded - count, TILE), F32)], axis=0)
    before = lax.broadcasted_iota(jnp.int32, (TILE, TILE), 0) < lax.broadcasted_iota(
        jnp.int32, (TILE, TILE), 1
    )
    ranks = dot(wide.astype(BF16), before.astype(F32).astype(BF16))
    return members, ranks


def pack_kernel(docs_ref, keys_ref, values_ref, out_ref, docs, values, sems):
    moves = [
        pltpu.make_async_copy(values_ref, values, sems.at[0]),
        pltpu.make_async_copy(docs_ref, docs, sems.at[1]),
        pltpu.make_async_copy(
            keys_ref, out_ref.at[pl.ds(0, TILE), pl.ds(0, KV_HEADS * HEAD)], sems.at[2]
        ),
    ]
    for move in moves:
        move.start()
    moves[0].wait()
    for h in range(KV_HEADS):
        out_ref[0:TILE, (KV_HEADS + h) * HEAD : (KV_HEADS + h + 1) * HEAD] = (
            values[:, h * HEAD : (h + 1) * HEAD].astype(F32).T.astype(BF16)
        )
    moves[1].wait()
    out_ref[TILE:KV_ROWS, :] = jnp.zeros((KV_ROWS - TILE, 4 * HEAD), BF16)
    out_ref[TILE:KV_ROWS, 0:HEAD] = jnp.broadcast_to(
        docs[...].astype(F32), (KV_ROWS - TILE, TILE)
    ).astype(BF16)
    moves[2].wait()


def select_kernel(planes, pos_ref, *refs):
    sources, (qs_ref, xs_ref, facts_ref) = refs[:4], refs[4:7]
    routes_ref, docs_ref, q_ref, x_ref, sems = refs[7:]
    moves = [
        pltpu.make_async_copy(source, target, sems.at[i])
        for i, (source, target) in enumerate(zip(sources, refs[7:11]))
    ]
    for move in moves:
        move.start()
    for move in moves:
        move.wait()
    z = pos_ref[0] // SHARDS
    members, ranks = slot_rows(routes_ref[...], [lax.rem(z + k, planes) for k in range(planes)])
    docs = docs_ref[...].astype(F32)
    lane_slot = (lax.broadcasted_iota(jnp.int32, (TILE, TILE), 0) % SLOTS).astype(F32)
    token = lax.broadcasted_iota(jnp.int32, (1, TILE), 1).astype(F32)
    facts = jnp.concatenate(
        [token, docs, jnp.ones((1, TILE), F32), jnp.zeros((5, TILE), F32)], axis=0
    ).astype(BF16)
    picks = [
        jnp.where(ranks[k : k + 1] == lane_slot, members[k : k + 1], 0.0) for k in range(planes)
    ]
    chooser = jnp.concatenate([p[:SLOTS] for p in picks], axis=0).astype(BF16)
    q_rows = dot(chooser, q_ref[...])
    xs_ref[...] = dot(chooser, x_ref[...])
    for k in range(planes):
        known = dot(facts, picks[k].astype(BF16), 1, 1)
        facts_ref[:, k * TILE : (k + 1) * TILE] = jnp.concatenate(
            [known[0:1], known[1:2] + (1.0 - known[2:3]) * docs[:, 0:1], known[2:]], axis=0
        )
        for h in range(KV_HEADS):
            stack = jnp.concatenate(
                [
                    q_rows[k * SLOTS : (k + 1) * SLOTS, a * HEAD : (a + 1) * HEAD]
                    for a in range(h * GROUP, (h + 1) * GROUP)
                ],
                axis=0,
            )
            for i, term in enumerate(two_terms(stack.T)):
                qs_ref[h, i * HEAD : (i + 1) * HEAD, k * TILE : (k + 1) * TILE] = term


def doc_starts(n, pos, held):
    sums = [jnp.zeros((1, TILE), F32) for _ in range(3)]
    for s in range(n):
        docs = held[s, TILE:KV_ROWS, 0:HEAD].astype(F32)[0:1]
        ahead = (pos - s < 0).astype(F32)
        behind = (pos - s > reach(n)).astype(F32)
        known = 1.0 - ahead - behind
        docs = jnp.where(known > 0.5, docs, 0.0) + 9.0 * ahead
        for d in range(3):
            sums[d] = sums[d] + jnp.where(docs < d + 1.0, 1.0, 0.0)
    return [jnp.sum(s, axis=1, keepdims=True) for s in sums]


def starts_of(docs, starts):
    first = jnp.zeros_like(docs)
    for d in range(3):
        first = jnp.where(docs == d + 1.0, starts[d], first)
    return first


def two_terms(x):
    scaled = x.astype(F32) * SCALE
    high = scaled.astype(BF16)
    return high, (scaled - high.astype(F32)).astype(BF16)


def key_steps(pos, place, first, bias_ref, step, state):
    low = jnp.min(first).astype(jnp.int32) // KEYS
    last = pos // (KEYS // TILE)
    clear = jnp.minimum((jnp.max(first).astype(jnp.int32) + KEYS - 1) // KEYS, last)

    def edge(j, carried):
        kb = jnp.where(j < clear - low, low + j, last)
        key_at = (kb * KEYS + lax.broadcasted_iota(jnp.int32, (KEYS, 1), 0)).astype(F32)
        bias_ref[...] = jnp.where((key_at >= first) & (key_at <= place), 0.0, LOW)
        return step(kb, carried, True)

    state = lax.fori_loop(0, clear - low + 1, edge, state)
    return lax.fori_loop(clear, last, lambda kb, carried: step(kb, carried, False), state)


def keys_of(held, kb, h):
    keys = jnp.concatenate(
        [held[2 * kb + t, 0:TILE, h * HEAD : (h + 1) * HEAD] for t in range(2)], axis=0
    )
    return jnp.concatenate([keys, keys], axis=1)


def values_of(held, kb, h):
    at = (KV_HEADS + h) * HEAD
    values = jnp.concatenate(
        [held[2 * kb + t, 0:TILE, at : at + HEAD] for t in range(2)], axis=1
    )
    return jnp.concatenate([values, jnp.ones((EXTRA, KEYS), BF16)], axis=0)


def flash(pos, held, q_ref, kv_heads, acc_ref, bias_ref, place, first):
    lanes = place.shape[1]
    chains = range(len(kv_heads))
    for i in chains:
        acc_ref[i] = jnp.zeros((HEAD + EXTRA, lanes), F32)

    def step(kb, tops, masked):
        out = []
        for i in chains:
            scores = dot(keys_of(held, kb, kv_heads[i]), q_ref[i])
            if masked:
                scores = scores + bias_ref[...]
            top = jnp.maximum(tops[i], jnp.max(scores, axis=0, keepdims=True))
            weights = jnp.exp2(scores - top).astype(BF16)
            acc_ref[i] = acc_ref[i] * jnp.exp2(tops[i] - top) + dot(
                values_of(held, kb, kv_heads[i]), weights
            )
            out.append(top)
        return tuple(out)

    tops = tuple(jnp.full((1, lanes), LOW, F32) for _ in chains)
    key_steps(pos, place, first, bias_ref, step, tops)
    return [(acc_ref[i, 0:HEAD] / acc_ref[i, HEAD : HEAD + 1]).T for i in chains]


def place_pieces(n, senders, pos, pieces, held, sems):
    planes = n // SHARDS
    z, y, c = pos // SHARDS, (pos // 2) % 2, pos % 2
    copies = []
    for i, (piece, row, flip_c, flip_y, k) in enumerate(senders):
        sender = lax.rem(z - k + planes, planes) * SHARDS + (y ^ flip_y) * 2 + (c ^ flip_c)
        copy = pltpu.make_async_copy(
            pieces[piece].at[pl.ds(row, KV_ROWS)], held.at[sender], sems.at[i]
        )
        copy.start()
        copies.append(copy)
    return copies


def collect_kernel(n, senders, pos_ref, *refs):
    *pieces, held, sems = refs
    for copy in place_pieces(n, senders, pos_ref[0], pieces, held, sems):
        copy.wait()


def routed_kernel(n, senders, pos_ref, gain_ref, qs_ref, xs_ref, facts_ref, _, *refs):
    planes = n // SHARDS
    count = len(senders)
    pieces, outs, held = refs[:2], refs[2 : 2 + planes], refs[2 + planes]
    acc, bias, q_scr, state, gain, sems = refs[3 + planes :]
    pos = pos_ref[0]
    copies = place_pieces(n, senders, pos, pieces, held, sems)
    copies.append(pltpu.make_async_copy(gain_ref, gain, sems.at[count]))
    copies[-1].start()
    for copy in copies:
        copy.wait()
    starts = doc_starts(n, pos, held)
    lanes = q_scr.shape[2]
    base = (pos * TILE).astype(F32)
    for part in range(planes * TILE // lanes):
        at = slice(part * lanes, (part + 1) * lanes)
        q_scr[...] = qs_ref[:, :, at]
        done = flash(
            pos,
            held,
            q_scr,
            range(KV_HEADS),
            acc,
            bias,
            facts_ref[0:1, at] + base,
            starts_of(facts_ref[1:2, at], starts),
        )
        for h in range(KV_HEADS):
            for k in range(lanes // TILE):
                row = (part * (lanes // TILE) + k) * SLOTS
                for g in range(GROUP):
                    lane = (h * GROUP + g) * HEAD
                    state[row : row + SLOTS, lane : lane + HEAD] = (
                        xs_ref[row : row + SLOTS, lane : lane + HEAD]
                        + done[h][k * TILE + g * SLOTS : k * TILE + (g + 1) * SLOTS]
                    )
    for k in range(planes):
        hidden = state[k * SLOTS : (k + 1) * SLOTS, :]
        mean = jnp.mean(hidden * hidden, axis=1, keepdims=True)
        outs[k][...] = (hidden * lax.rsqrt(mean + 1e-06) * gain[...]).astype(BF16)


def expert_kernel(n, count, *refs):
    pieces = refs[:count]
    wg, wu, wd = refs[count : count + 3]
    keep_ref, send_ref, rows = refs[count + 4 :]
    width = rows.shape[1]
    total = n * SLOTS
    out_rows = min(total, 16 * SLOTS)
    half = total // 2
    step = 1024
    for at in range(0, total, out_rows):
        for col in range(0, width, step):
            parts, first = [], 0
            for piece in pieces:
                size = piece.shape[0]
                low, high = max(at - first, 0), min(at + out_rows - first, size)
                if low < high:
                    parts.append(piece[low:high, col : col + step].astype(F32))
                first += size
            rows[:, col : col + step] = jnp.concatenate(parts, axis=0).astype(BF16)
        gate = dot(rows[...], wg[...])
        up = dot(rows[...], wu[...])
        act = (gate / (1.0 + jnp.exp(-gate)) * up).astype(BF16)
        for col in range(0, width, step):
            part = dot(act, wd[:, col : col + step]).astype(BF16)
            if out_rows > half:
                keep_ref[:, col : col + step] = part[:half]
                send_ref[:, col : col + step] = part[half:]
            elif at < half:
                keep_ref[at : at + out_rows, col : col + step] = part
            else:
                send_ref[at - half : at - half + out_rows, col : col + step] = part


def own_kernel(n, part, loads, pos_ref, held, q_ref, x_ref, _, *refs):
    sources, (h_ref, done_ref) = refs[:loads], refs[loads : loads + 2]
    targets = refs[loads + 2 : 2 * loads + 2]
    acc, bias, qt, sems = refs[2 * loads + 2 :]
    moves = [
        pltpu.make_async_copy(source.at[0], target, sems.at[i])
        for i, (source, target) in enumerate(zip(sources, targets))
    ]
    for move in moves:
        move.start()
    done_ref[...] = jnp.zeros((8, TILE), F32)
    pos = pos_ref[0]
    starts = doc_starts(n, pos, held)
    first = starts_of(held[pos, TILE:KV_ROWS, 0:HEAD].astype(F32)[0:1], starts)
    place = (pos * TILE + lax.broadcasted_iota(jnp.int32, (1, TILE), 1)).astype(F32)
    for a in range(8):
        terms = two_terms(q_ref[:, a * HEAD : (a + 1) * HEAD].astype(F32).T)
        for i, term in enumerate(terms):
            qt[0, i * HEAD : (i + 1) * HEAD, a * TILE : (a + 1) * TILE] = term
    place = jnp.concatenate([place] * 8, axis=1)
    first = jnp.concatenate([first] * 8, axis=1)
    (done,) = flash(pos, held, qt, [part // 2], acc, bias, place, first)
    for a in range(8):
        lane = a * HEAD
        h_ref[:, lane : lane + HEAD] = (
            x_ref[:, lane : lane + HEAD].astype(F32) + done[a * TILE : (a + 1) * TILE]
        )
    for move in moves:
        move.wait()


def combine_kernel(planes, pos_ref, routes_ref, gates_ref, *refs):
    halves, parts, out_ref = refs[:4], refs[4 : 4 + planes], refs[4 + planes]
    z = pos_ref[0] // SHARDS
    routes = routes_ref[...]
    gates = gates_ref[...]
    experts = [lax.rem(z + k, planes) for k in range(planes)]
    members, ranks = slot_rows(routes, experts)
    slot = lax.broadcasted_iota(jnp.int32, (SLOTS, TILE), 0).astype(F32)
    mix = []
    for k, e in enumerate(experts):
        gate = jnp.sum(jnp.where(routes == e, gates, 0.0), axis=0, keepdims=True)
        mix.append(jnp.where(ranks[k : k + 1] == slot, gate, 0.0))
    mix = jnp.concatenate(mix, axis=0).T
    mix_high = mix.astype(BF16)
    mix_low = (mix - mix_high.astype(F32)).astype(BF16)
    size = halves[0].shape[1]
    for i, h in enumerate(halves):
        columns = slice(i * size, (i + 1) * size)
        rows = jnp.concatenate([p[:, columns].astype(F32) for p in parts], axis=0).astype(BF16)
        out_ref[:, columns] = (h[...] + dot(mix_high, rows) + dot(mix_low, rows)).astype(BF16)


def pin(x):
    return pltpu.with_memory_space_constraint(x, pltpu.HBM)


def params(mib):
    return pltpu.CompilerParams(vmem_limit_bytes=mib * 1024 * 1024)


def local(
    resid, queries, keys, values, doc_ids, norm_gain, routes, route_weights, w_gate, w_up, w_down
):
    n = lax.axis_size("expert")
    planes = n // SHARDS
    pos = lax.axis_index("expert").astype(jnp.int32).reshape(1)
    tokens, width = queries.shape
    hidden = w_gate.shape[2]
    routes_t = routes.T
    gates_t = route_weights.T
    docs = doc_ids.reshape(1, tokens)
    small = 24 if n <= 16 else 60
    back = reach(n)

    packed = pl.pallas_call(
        pack_kernel,
        out_shape=jax.ShapeDtypeStruct((KV_ROWS, 4 * HEAD), BF16),
        in_specs=[HBM] * 3,
        out_specs=VMEM,
        scratch_shapes=[
            pltpu.VMEM((1, tokens), jnp.int32),
            pltpu.VMEM((tokens, KV_HEADS * HEAD), BF16),
            pltpu.SemaphoreType.DMA((3,)),
        ],
        compiler_params=params(8),
        name="pack",
    )(pin(docs), pin(keys), pin(values))

    def move(value, pairs):
        return lax.ppermute(value, "expert", pairs)

    def needed(k, y_from, y_to):
        gaps = [
            k * SHARDS + 2 * (y_to - y_from) + (to - of) for to in range(2) for of in range(2)
        ]
        return any(0 <= gap <= back for gap in gaps)

    far = max(k for k in range(planes) if any(needed(k, a, b) for a in (0, 1) for b in (0, 1)))
    q_rows, x_rows, facts = pl.pallas_call(
        functools.partial(select_kernel, planes),
        out_shape=[
            jax.ShapeDtypeStruct((KV_HEADS, 2 * HEAD, planes * TILE), BF16),
            jax.ShapeDtypeStruct((planes * SLOTS, width), F32),
            jax.ShapeDtypeStruct((8, planes * TILE), F32),
        ],
        in_specs=[SMEM] + [HBM] * 4,
        out_specs=[VMEM] * 3,
        scratch_shapes=[
            pltpu.VMEM(routes_t.shape, jnp.int32),
            pltpu.VMEM(docs.shape, jnp.int32),
            pltpu.VMEM(queries.shape, BF16),
            pltpu.VMEM(resid.shape, BF16),
            pltpu.SemaphoreType.DMA((4,)),
        ],
        compiler_params=params(small),
        name="select",
    )(pos, pin(routes_t), pin(docs), pin(queries), pin(resid))

    flip_y = [(s, s ^ 2) for s in range(n)]
    flip_c = [(s, s ^ 1) for s in range(n)]
    along, across = [packed], []
    for k in range(far + 1):
        if k == 1:
            along[1], q_rows = lax.optimization_barrier((along[1], q_rows))
        if k > 1:
            along[k], across[k - 2] = lax.optimization_barrier((along[k], across[k - 2]))
        if k < far:
            used = [
                any(needed(j, y, to) for to in (0, 1) for j in range(k + 1, far + 1))
                for y in (0, 1)
            ]
            pairs = [(s, (s + SHARDS) % n if used[s // 2 % 2] else s) for s in range(n)]
            along.append(move(along[k], pairs))
        pairs = [(s, s ^ 2 if s >= k * SHARDS else s) for s in range(n)]
        across.append(move(along[k], pairs))
    early = along + across[:-1] + [move(jnp.concatenate(along, axis=0), flip_c)]
    late = [across[-1], move(jnp.concatenate(across, axis=0), flip_c)]
    steps = range(far + 1)
    early_senders = [(k, 0, 0, 0, k) for k in steps]
    early_senders += [(far + 1 + k, 0, 0, 1, k) for k in steps[:-1]]
    early_senders += [(2 * far + 1, k * KV_ROWS, 1, 0, k) for k in steps]
    late_senders = [(0, 0, 0, 1, far)] + [(1, k * KV_ROWS, 1, 1, k) for k in steps]
    held_shape = jax.ShapeDtypeStruct((n, KV_ROWS, 4 * HEAD), BF16)
    held = pl.pallas_call(
        functools.partial(collect_kernel, n, early_senders),
        out_shape=held_shape,
        in_specs=[SMEM] + [ANY] * len(early),
        out_specs=VMEM,
        scratch_shapes=[pltpu.SemaphoreType.DMA((len(early_senders),))],
        compiler_params=params(small),
        name="collect",
    )(pos, *early)

    *sent, held = pl.pallas_call(
        functools.partial(routed_kernel, n, late_senders),
        out_shape=[jax.ShapeDtypeStruct((SLOTS, width), BF16)] * planes
        + [held_shape],
        in_specs=[SMEM, HBM] + [VMEM] * 4 + [ANY] * len(late),
        out_specs=[VMEM] * (planes + 1),
        scratch_shapes=[
            pltpu.VMEM((KV_HEADS, HEAD + EXTRA, 4 * TILE), F32),
            pltpu.VMEM((KEYS, 4 * TILE), F32),
            pltpu.VMEM((KV_HEADS, 2 * HEAD, 4 * TILE), BF16),
            pltpu.VMEM((planes * SLOTS, width), F32),
            pltpu.VMEM((1, width), F32),
            pltpu.SemaphoreType.DMA((len(late_senders) + 1,)),
        ],
        input_output_aliases={5: planes},
        compiler_params=params(small),
        name="routed",
    )(pos, pin(norm_gain.reshape(1, width)), q_rows, x_rows, facts, held, *late)

    def own(part, after, *sources):
        columns = pl.BlockSpec((tokens, 8 * HEAD), lambda i: (0, part))
        return pl.pallas_call(
            functools.partial(own_kernel, n, part, len(sources)),
            out_shape=[
                jax.ShapeDtypeStruct((tokens, 8 * HEAD), F32),
                jax.ShapeDtypeStruct((8, TILE), F32),
            ]
            + [jax.ShapeDtypeStruct(w.shape[1:], BF16) for w in sources],
            grid=(1,),
            in_specs=[SMEM, VMEM, columns, columns, ANY] + [HBM] * len(sources),
            out_specs=[
                pl.BlockSpec((tokens, 8 * HEAD), lambda i: (0, 0)),
                pl.BlockSpec((8, TILE), lambda i: (0, 0)),
            ]
            + [VMEM] * len(sources),
            scratch_shapes=[
                pltpu.VMEM((1, HEAD + EXTRA, 8 * TILE), F32),
                pltpu.VMEM((KEYS, 8 * TILE), F32),
                pltpu.VMEM((1, 2 * HEAD, 8 * TILE), BF16),
                pltpu.SemaphoreType.DMA((3,)),
            ],
            compiler_params=params(small),
            cost_estimate=pl.CostEstimate(
                flops=2_000_000_000, bytes_accessed=8_000_000, transcendentals=2_000_000
            ),
            name="own",
        )(pos, held, queries, resid, after, *map(pin, sources))

    half0, done, *weights = own(0, sent[0], w_gate, w_up, w_down)
    half1, late = own(1, done)
    halves = [half0, half1]

    come = [
        move(sent[k], [(s, (s + k * SHARDS) % n) for s in range(n)]) for k in range(1, planes)
    ]
    next_door = move(sent[0], flip_y)
    come, next_door, done = lax.optimization_barrier((come, next_door, done))
    here = [sent[0], jnp.concatenate(come, axis=0)]
    there = [next_door, move(here[1], flip_y)]
    mate = move(jnp.concatenate(here, axis=0), flip_c)
    there, mate, late = lax.optimization_barrier((there, mate, late))
    pieces = here + there + [mate, move(jnp.concatenate(there, axis=0), flip_c)]

    half = jax.ShapeDtypeStruct((n * SLOTS // 2, width), BF16)
    keep, send = pl.pallas_call(
        functools.partial(expert_kernel, n, len(pieces)),
        out_shape=[half, half],
        in_specs=[VMEM] * (len(pieces) + 3) + [ANY],
        out_specs=[VMEM, VMEM],
        scratch_shapes=[pltpu.VMEM((16 * SLOTS, width), BF16)],
        compiler_params=params(16),
        cost_estimate=pl.CostEstimate(
            flops=1_200_000_000, bytes_accessed=12_000_000, transcendentals=50_000
        ),
        name="expert",
    )(*pieces, *weights, late)

    halves += [own(part, keep)[0] for part in range(2, 4)]

    total = keep.astype(F32) + move(send, [(s, s ^ 1) for s in range(n)]).astype(F32)
    quarter = n * SLOTS // 4
    other = move(total[quarter:].astype(BF16), [(s, s ^ 2) for s in range(n)])
    total = (total[:quarter] + other.astype(F32)).astype(BF16)
    parts = [total[:SLOTS]]
    for k in range(1, planes):
        parts.append(
            move(
                total[k * SLOTS : (k + 1) * SLOTS], [(s, (s - k * SHARDS) % n) for s in range(n)]
            )
        )

    return pl.pallas_call(
        functools.partial(combine_kernel, planes),
        out_shape=jax.ShapeDtypeStruct((tokens, width), BF16),
        in_specs=[SMEM] + [VMEM] * (6 + planes),
        out_specs=VMEM,
        compiler_params=params(small),
        name="combine",
    )(pos, routes_t, gates_t, *halves, *parts)


def solution(mesh):
    rows = P(("groups", "expert"), None)
    in_specs = (rows,) * 4 + (P(("groups", "expert")), P(), rows, rows) + (
        P("expert", None, None),
    ) * 3
    return jax.shard_map(local, mesh=mesh, in_specs=in_specs, out_specs=rows, check_vma=False)
```

```python
import functools
import math

import jax
import jax.numpy as jnp
from jax import lax
from jax.experimental import pallas as pl
from jax.experimental.pallas import tpu as pltpu
from jax.sharding import PartitionSpec as P

HEAD = 128
QUERY_HEADS = 32
KV_HEADS = 2
GROUP = QUERY_HEADS // KV_HEADS
SHARDS = 4
CAP = 6
SLOTS = 8
CUT = 4
PIECE = CUT * CAP
TILE = 128
KEYS = 256
KV_ROWS = TILE + 16
SCALE = math.log2(math.e) / math.sqrt(HEAD)
LOW = -1e30
EXTRA = 16
F32 = jnp.float32
BF16 = jnp.bfloat16
VMEM = pl.BlockSpec(memory_space=pltpu.VMEM)
SMEM = pl.BlockSpec(memory_space=pltpu.SMEM)
ANY = pl.BlockSpec(memory_space=pl.ANY)
HBM = pl.BlockSpec(memory_space=pltpu.HBM)


def dot(a, b, ca=1, cb=0):
    return lax.dot_general(a, b, (((ca,), (cb,)), ((), ())), preferred_element_type=F32)


def reach(n):
    longest = n * TILE // 2 + 256
    return (longest - 1 + TILE - 1) // TILE


def slot_rows(routes, experts):
    members = jnp.concatenate(
        [jnp.max((routes == e).astype(F32), axis=0, keepdims=True) for e in experts], axis=0
    )
    count = len(experts)
    padded = -(-count // 8) * 8
    wide = members
    if padded > count:
        wide = jnp.concatenate([members, jnp.zeros((padded - count, TILE), F32)], axis=0)
    before = lax.broadcasted_iota(jnp.int32, (TILE, TILE), 0) < lax.broadcasted_iota(
        jnp.int32, (TILE, TILE), 1
    )
    ranks = dot(wide.astype(BF16), before.astype(F32).astype(BF16))
    return members, ranks


def one_hot(targets, count):
    shape = (targets.shape[0], count) if targets.shape[1] == 1 else (count, targets.shape[1])
    axis = 1 if targets.shape[1] == 1 else 0
    places = lax.broadcasted_iota(jnp.int32, shape, axis).astype(F32)
    return jnp.where(places == targets, 1.0, 0.0).astype(BF16)


def split(x, size):
    whole = jnp.floor((x + 0.5) / size)
    return whole, x - whole * size


def travel_row(x, senders, slots):
    chunk, rest = split(x, senders * slots)
    sender, slot = split(rest, slots)
    return jnp.where(slot < CAP, sender * PIECE + chunk * CAP + slot, -1.0)


def numbers(shape, axis):
    return lax.broadcasted_iota(jnp.int32, shape, axis).astype(F32)


def pack_kernel(docs_ref, keys_ref, values_ref, out_ref, docs, values, sems):
    moves = [
        pltpu.make_async_copy(values_ref, values, sems.at[0]),
        pltpu.make_async_copy(docs_ref, docs, sems.at[1]),
        pltpu.make_async_copy(
            keys_ref, out_ref.at[pl.ds(0, TILE), pl.ds(0, KV_HEADS * HEAD)], sems.at[2]
        ),
    ]
    for move in moves:
        move.start()
    moves[0].wait()
    for h in range(KV_HEADS):
        out_ref[0:TILE, (KV_HEADS + h) * HEAD : (KV_HEADS + h + 1) * HEAD] = (
            values[:, h * HEAD : (h + 1) * HEAD].astype(F32).T.astype(BF16)
        )
    moves[1].wait()
    out_ref[TILE:KV_ROWS, :] = jnp.zeros((KV_ROWS - TILE, 4 * HEAD), BF16)
    out_ref[TILE:KV_ROWS, 0:HEAD] = jnp.broadcast_to(
        docs[...].astype(F32), (KV_ROWS - TILE, TILE)
    ).astype(BF16)
    moves[2].wait()


def select_kernel(planes, pos_ref, *refs):
    sources, (qs_ref, xs_ref, facts_ref) = refs[:4], refs[4:7]
    routes_ref, docs_ref, q_ref, x_ref, sems = refs[7:]
    moves = [
        pltpu.make_async_copy(source, target, sems.at[i])
        for i, (source, target) in enumerate(zip(sources, refs[7:11]))
    ]
    for move in moves:
        move.start()
    for move in moves:
        move.wait()
    z = pos_ref[0] // SHARDS
    members, ranks = slot_rows(routes_ref[...], [lax.rem(z + k, planes) for k in range(planes)])
    docs = docs_ref[...].astype(F32)
    lane_slot = (lax.broadcasted_iota(jnp.int32, (TILE, TILE), 0) % SLOTS).astype(F32)
    token = lax.broadcasted_iota(jnp.int32, (1, TILE), 1).astype(F32)
    facts = jnp.concatenate(
        [token, docs, jnp.ones((1, TILE), F32), jnp.zeros((5, TILE), F32)], axis=0
    ).astype(BF16)
    picks = [
        jnp.where(ranks[k : k + 1] == lane_slot, members[k : k + 1], 0.0) for k in range(planes)
    ]
    chooser = jnp.concatenate([p[:SLOTS] for p in picks], axis=0).astype(BF16)
    q_rows = dot(chooser, q_ref[...])
    xs_ref[...] = dot(chooser, x_ref[...])
    for k in range(planes):
        known = dot(facts, picks[k].astype(BF16), 1, 1)
        facts_ref[:, k * TILE : (k + 1) * TILE] = jnp.concatenate(
            [known[0:1], known[1:2] + (1.0 - known[2:3]) * docs[:, 0:1], known[2:]], axis=0
        )
        for h in range(KV_HEADS):
            stack = jnp.concatenate(
                [
                    q_rows[k * SLOTS : (k + 1) * SLOTS, a * HEAD : (a + 1) * HEAD]
                    for a in range(h * GROUP, (h + 1) * GROUP)
                ],
                axis=0,
            )
            for i, term in enumerate(two_terms(stack.T)):
                qs_ref[h, i * HEAD : (i + 1) * HEAD, k * TILE : (k + 1) * TILE] = term


def doc_starts(n, pos, held):
    sums = [jnp.zeros((1, TILE), F32) for _ in range(3)]
    for s in range(n):
        docs = held[s, TILE:KV_ROWS, 0:HEAD].astype(F32)[0:1]
        ahead = (pos - s < 0).astype(F32)
        behind = (pos - s > reach(n)).astype(F32)
        known = 1.0 - ahead - behind
        docs = jnp.where(known > 0.5, docs, 0.0) + 9.0 * ahead
        for d in range(3):
            sums[d] = sums[d] + jnp.where(docs < d + 1.0, 1.0, 0.0)
    return [jnp.sum(s, axis=1, keepdims=True) for s in sums]


def starts_of(docs, starts):
    first = jnp.zeros_like(docs)
    for d in range(3):
        first = jnp.where(docs == d + 1.0, starts[d], first)
    return first


def two_terms(x):
    scaled = x.astype(F32) * SCALE
    high = scaled.astype(BF16)
    return high, (scaled - high.astype(F32)).astype(BF16)


def key_steps(pos, place, first, bias_ref, step, state):
    low = jnp.min(first).astype(jnp.int32) // KEYS
    last = pos // (KEYS // TILE)
    clear = jnp.minimum((jnp.max(first).astype(jnp.int32) + KEYS - 1) // KEYS, last)

    def edge(j, carried):
        kb = jnp.where(j < clear - low, low + j, last)
        key_at = (kb * KEYS + lax.broadcasted_iota(jnp.int32, (KEYS, 1), 0)).astype(F32)
        bias_ref[...] = jnp.where((key_at >= first) & (key_at <= place), 0.0, LOW)
        return step(kb, carried, True)

    state = lax.fori_loop(0, clear - low + 1, edge, state)
    return lax.fori_loop(clear, last, lambda kb, carried: step(kb, carried, False), state)


def keys_of(held, kb, h):
    keys = jnp.concatenate(
        [held[2 * kb + t, 0:TILE, h * HEAD : (h + 1) * HEAD] for t in range(2)], axis=0
    )
    return jnp.concatenate([keys, keys], axis=1)


def values_of(held, kb, h):
    at = (KV_HEADS + h) * HEAD
    values = jnp.concatenate(
        [held[2 * kb + t, 0:TILE, at : at + HEAD] for t in range(2)], axis=1
    )
    return jnp.concatenate([values, jnp.ones((EXTRA, KEYS), BF16)], axis=0)


def flash(pos, held, q_ref, kv_heads, acc_ref, bias_ref, place, first):
    lanes = place.shape[1]
    chains = range(len(kv_heads))
    for i in chains:
        acc_ref[i] = jnp.zeros((HEAD + EXTRA, lanes), F32)

    def step(kb, tops, masked):
        out = []
        for i in chains:
            scores = dot(keys_of(held, kb, kv_heads[i]), q_ref[i])
            if masked:
                scores = scores + bias_ref[...]
            top = jnp.maximum(tops[i], jnp.max(scores, axis=0, keepdims=True))
            weights = jnp.exp2(scores - top).astype(BF16)
            acc_ref[i] = acc_ref[i] * jnp.exp2(tops[i] - top) + dot(
                values_of(held, kb, kv_heads[i]), weights
            )
            out.append(top)
        return tuple(out)

    tops = tuple(jnp.full((1, lanes), LOW, F32) for _ in chains)
    key_steps(pos, place, first, bias_ref, step, tops)
    return [(acc_ref[i, 0:HEAD] / acc_ref[i, HEAD : HEAD + 1]).T for i in chains]


def place_pieces(n, senders, pos, pieces, held, sems):
    planes = n // SHARDS
    z, y, c = pos // SHARDS, (pos // 2) % 2, pos % 2
    copies = []
    for i, (piece, row, flip_c, flip_y, k) in enumerate(senders):
        sender = lax.rem(z - k + planes, planes) * SHARDS + (y ^ flip_y) * 2 + (c ^ flip_c)
        copy = pltpu.make_async_copy(
            pieces[piece].at[pl.ds(row, KV_ROWS)], held.at[sender], sems.at[i]
        )
        copy.start()
        copies.append(copy)
    return copies


def collect_kernel(n, senders, pos_ref, *refs):
    *pieces, held, sems = refs
    for copy in place_pieces(n, senders, pos_ref[0], pieces, held, sems):
        copy.wait()


def routed_kernel(n, senders, pos_ref, gain_ref, qs_ref, xs_ref, facts_ref, _, *refs):
    planes = n // SHARDS
    count = len(senders)
    pieces, outs, held = refs[:2], refs[2 : 2 + planes], refs[2 + planes]
    acc, bias, q_scr, state, gain, sems = refs[3 + planes :]
    pos = pos_ref[0]
    copies = place_pieces(n, senders, pos, pieces, held, sems)
    copies.append(pltpu.make_async_copy(gain_ref, gain, sems.at[count]))
    copies[-1].start()
    for copy in copies:
        copy.wait()
    starts = doc_starts(n, pos, held)
    lanes = q_scr.shape[2]
    base = (pos * TILE).astype(F32)
    for part in range(planes * TILE // lanes):
        at = slice(part * lanes, (part + 1) * lanes)
        q_scr[...] = qs_ref[:, :, at]
        done = flash(
            pos,
            held,
            q_scr,
            range(KV_HEADS),
            acc,
            bias,
            facts_ref[0:1, at] + base,
            starts_of(facts_ref[1:2, at], starts),
        )
        for h in range(KV_HEADS):
            for k in range(lanes // TILE):
                row = (part * (lanes // TILE) + k) * SLOTS
                for g in range(GROUP):
                    lane = (h * GROUP + g) * HEAD
                    state[row : row + SLOTS, lane : lane + HEAD] = (
                        xs_ref[row : row + SLOTS, lane : lane + HEAD]
                        + done[h][k * TILE + g * SLOTS : k * TILE + (g + 1) * SLOTS]
                    )
    width = state.shape[1] // CUT
    order = one_hot(travel_row(numbers((1, CUT * SLOTS), 1), 1, SLOTS), PIECE)
    for k in range(planes):
        hidden = state[k * SLOTS : (k + 1) * SLOTS, :]
        mean = jnp.mean(hidden * hidden, axis=1, keepdims=True)
        normed = hidden * lax.rsqrt(mean + 1e-06) * gain[...]
        chunks = [normed[:, q * width : (q + 1) * width] for q in range(CUT)]
        outs[k][...] = dot(order, jnp.concatenate(chunks, axis=0).astype(BF16)).astype(BF16)


def expert_kernel(n, count, *refs):
    pieces = refs[:count]
    wg, wu, wd = refs[count : count + 3]
    keep_ref, send_ref, rows = refs[count + 4 :]
    step = pieces[0].shape[1]
    senders = min(n, 16)
    size, total = senders * PIECE, n * PIECE
    half = total // 2
    kept = senders * CAP
    gather = one_hot(travel_row(numbers((size, 1), 0), senders, CAP), size)
    spread = one_hot(travel_row(numbers((1, size), 1), senders, CAP), size)
    for at in range(0, total, size):
        parts, first = [], 0
        for piece in pieces:
            low, high = max(at - first, 0), min(at + size - first, piece.shape[0])
            if low < high:
                parts.append(piece[low:high, :].astype(F32))
            first += piece.shape[0]
        came = dot(gather, jnp.concatenate(parts, axis=0).astype(BF16)).astype(BF16)
        for q in range(CUT):
            rows[:, q * step : (q + 1) * step] = came[q * kept : (q + 1) * kept]
        gate = dot(rows[...], wg[...])
        up = dot(rows[...], wu[...])
        act = (gate / (1.0 + jnp.exp(-gate)) * up).astype(BF16)
        parts = [dot(act, wd[:, q * step : (q + 1) * step]).astype(BF16) for q in range(CUT)]
        out = dot(spread, jnp.concatenate(parts, axis=0)).astype(BF16)
        if size > half:
            keep_ref[...] = out[:half]
            send_ref[...] = out[half:]
        elif at < half:
            keep_ref[at : at + size] = out
        else:
            send_ref[at - half : at - half + size] = out


def own_kernel(n, part, loads, pos_ref, held, q_ref, x_ref, _, *refs):
    sources, (h_ref, done_ref) = refs[:loads], refs[loads : loads + 2]
    targets = refs[loads + 2 : 2 * loads + 2]
    acc, bias, qt, sems = refs[2 * loads + 2 :]
    moves = [
        pltpu.make_async_copy(source.at[0], target, sems.at[i])
        for i, (source, target) in enumerate(zip(sources, targets))
    ]
    for move in moves:
        move.start()
    done_ref[...] = jnp.zeros((8, TILE), F32)
    pos = pos_ref[0]
    starts = doc_starts(n, pos, held)
    first = starts_of(held[pos, TILE:KV_ROWS, 0:HEAD].astype(F32)[0:1], starts)
    place = (pos * TILE + lax.broadcasted_iota(jnp.int32, (1, TILE), 1)).astype(F32)
    for a in range(8):
        terms = two_terms(q_ref[:, a * HEAD : (a + 1) * HEAD].astype(F32).T)
        for i, term in enumerate(terms):
            qt[0, i * HEAD : (i + 1) * HEAD, a * TILE : (a + 1) * TILE] = term
    place = jnp.concatenate([place] * 8, axis=1)
    first = jnp.concatenate([first] * 8, axis=1)
    (done,) = flash(pos, held, qt, [part // 2], acc, bias, place, first)
    for a in range(8):
        lane = a * HEAD
        h_ref[:, lane : lane + HEAD] = (
            x_ref[:, lane : lane + HEAD].astype(F32) + done[a * TILE : (a + 1) * TILE]
        )
    for move in moves:
        move.wait()


def combine_kernel(planes, pos_ref, routes_ref, gates_ref, *refs):
    halves, parts, out_ref = refs[:4], refs[4 : 4 + planes], refs[4 + planes]
    z = pos_ref[0] // SHARDS
    routes = routes_ref[...]
    gates = gates_ref[...]
    experts = [lax.rem(z + k, planes) for k in range(planes)]
    members, ranks = slot_rows(routes, experts)
    slot = lax.broadcasted_iota(jnp.int32, (SLOTS, TILE), 0).astype(F32)
    mix = []
    for k, e in enumerate(experts):
        gate = jnp.sum(jnp.where(routes == e, gates, 0.0), axis=0, keepdims=True)
        mix.append(jnp.where(ranks[k : k + 1] == slot, gate, 0.0))
    mix = jnp.concatenate(mix, axis=0).T
    mix_high = mix.astype(BF16)
    mix_low = (mix - mix_high.astype(F32)).astype(BF16)
    size = halves[0].shape[1]
    slots = planes * SLOTS
    came = jnp.concatenate([p[...].astype(F32) for p in parts], axis=0).astype(BF16)
    order = one_hot(travel_row(numbers((CUT * slots, 1), 0), planes, SLOTS), planes * PIECE)
    came = dot(order, came).astype(BF16)
    for i, h in enumerate(halves):
        rows = came[i * slots : (i + 1) * slots]
        out_ref[:, i * size : (i + 1) * size] = (
            h[...] + dot(mix_high, rows) + dot(mix_low, rows)
        ).astype(BF16)


def pin(x):
    return pltpu.with_memory_space_constraint(x, pltpu.HBM)


def params(mib):
    return pltpu.CompilerParams(vmem_limit_bytes=mib * 1024 * 1024)


def local(
    resid, queries, keys, values, doc_ids, norm_gain, routes, route_weights, w_gate, w_up, w_down
):
    n = lax.axis_size("expert")
    planes = n // SHARDS
    pos = lax.axis_index("expert").astype(jnp.int32).reshape(1)
    tokens, width = queries.shape
    hidden = w_gate.shape[2]
    routes_t = routes.T
    gates_t = route_weights.T
    docs = doc_ids.reshape(1, tokens)
    small = 24 if n <= 16 else 60
    back = reach(n)

    packed = pl.pallas_call(
        pack_kernel,
        out_shape=jax.ShapeDtypeStruct((KV_ROWS, 4 * HEAD), BF16),
        in_specs=[HBM] * 3,
        out_specs=VMEM,
        scratch_shapes=[
            pltpu.VMEM((1, tokens), jnp.int32),
            pltpu.VMEM((tokens, KV_HEADS * HEAD), BF16),
            pltpu.SemaphoreType.DMA((3,)),
        ],
        compiler_params=params(8),
        name="pack",
    )(pin(docs), pin(keys), pin(values))

    def move(value, pairs):
        return lax.ppermute(value, "expert", pairs)

    def needed(k, y_from, y_to):
        gaps = [
            k * SHARDS + 2 * (y_to - y_from) + (to - of) for to in range(2) for of in range(2)
        ]
        return any(0 <= gap <= back for gap in gaps)

    far = max(k for k in range(planes) if any(needed(k, a, b) for a in (0, 1) for b in (0, 1)))
    q_rows, x_rows, facts = pl.pallas_call(
        functools.partial(select_kernel, planes),
        out_shape=[
            jax.ShapeDtypeStruct((KV_HEADS, 2 * HEAD, planes * TILE), BF16),
            jax.ShapeDtypeStruct((planes * SLOTS, width), F32),
            jax.ShapeDtypeStruct((8, planes * TILE), F32),
        ],
        in_specs=[SMEM] + [HBM] * 4,
        out_specs=[VMEM] * 3,
        scratch_shapes=[
            pltpu.VMEM(routes_t.shape, jnp.int32),
            pltpu.VMEM(docs.shape, jnp.int32),
            pltpu.VMEM(queries.shape, BF16),
            pltpu.VMEM(resid.shape, BF16),
            pltpu.SemaphoreType.DMA((4,)),
        ],
        compiler_params=params(small),
        name="select",
    )(pos, pin(routes_t), pin(docs), pin(queries), pin(resid))

    flip_y = [(s, s ^ 2) for s in range(n)]
    flip_c = [(s, s ^ 1) for s in range(n)]
    along, across = [packed], []
    for k in range(far + 1):
        if k == 1:
            along[1], q_rows = lax.optimization_barrier((along[1], q_rows))
        if k > 1:
            along[k], across[k - 2] = lax.optimization_barrier((along[k], across[k - 2]))
        if k < far:
            used = [
                any(needed(j, y, to) for to in (0, 1) for j in range(k + 1, far + 1))
                for y in (0, 1)
            ]
            onward = [s + SHARDS if s + SHARDS < n else s % SHARDS + k * SHARDS for s in range(n)]
            pairs = [
                (s, onward[s] if used[s // 2 % 2] and s >= k * SHARDS else s) for s in range(n)
            ]
            along.append(move(along[k], pairs))
        pairs = [(s, s ^ 2 if s >= k * SHARDS else s) for s in range(n)]
        across.append(move(along[k], pairs))
    early = along + across[:-1] + [move(jnp.concatenate(along, axis=0), flip_c)]
    late = [across[-1], move(jnp.concatenate(across, axis=0), flip_c)]
    steps = range(far + 1)
    early_senders = [(k, 0, 0, 0, k) for k in steps]
    early_senders += [(far + 1 + k, 0, 0, 1, k) for k in steps[:-1]]
    early_senders += [(2 * far + 1, k * KV_ROWS, 1, 0, k) for k in steps]
    late_senders = [(0, 0, 0, 1, far)] + [(1, k * KV_ROWS, 1, 1, k) for k in steps]
    held_shape = jax.ShapeDtypeStruct((n, KV_ROWS, 4 * HEAD), BF16)
    held = pl.pallas_call(
        functools.partial(collect_kernel, n, early_senders),
        out_shape=held_shape,
        in_specs=[SMEM] + [ANY] * len(early),
        out_specs=VMEM,
        scratch_shapes=[pltpu.SemaphoreType.DMA((len(early_senders),))],
        compiler_params=params(small),
        name="collect",
    )(pos, *early)

    *sent, held = pl.pallas_call(
        functools.partial(routed_kernel, n, late_senders),
        out_shape=[jax.ShapeDtypeStruct((PIECE, width // CUT), BF16)] * planes
        + [held_shape],
        in_specs=[SMEM, HBM] + [VMEM] * 4 + [ANY] * len(late),
        out_specs=[VMEM] * (planes + 1),
        scratch_shapes=[
            pltpu.VMEM((KV_HEADS, HEAD + EXTRA, 4 * TILE), F32),
            pltpu.VMEM((KEYS, 4 * TILE), F32),
            pltpu.VMEM((KV_HEADS, 2 * HEAD, 4 * TILE), BF16),
            pltpu.VMEM((planes * SLOTS, width), F32),
            pltpu.VMEM((1, width), F32),
            pltpu.SemaphoreType.DMA((len(late_senders) + 1,)),
        ],
        input_output_aliases={5: planes},
        compiler_params=params(small),
        name="routed",
    )(pos, pin(norm_gain.reshape(1, width)), q_rows, x_rows, facts, held, *late)

    def own(part, after, *sources):
        columns = pl.BlockSpec((tokens, 8 * HEAD), lambda i: (0, part))
        return pl.pallas_call(
            functools.partial(own_kernel, n, part, len(sources)),
            out_shape=[
                jax.ShapeDtypeStruct((tokens, 8 * HEAD), F32),
                jax.ShapeDtypeStruct((8, TILE), F32),
            ]
            + [jax.ShapeDtypeStruct(w.shape[1:], BF16) for w in sources],
            grid=(1,),
            in_specs=[SMEM, VMEM, columns, columns, ANY] + [HBM] * len(sources),
            out_specs=[
                pl.BlockSpec((tokens, 8 * HEAD), lambda i: (0, 0)),
                pl.BlockSpec((8, TILE), lambda i: (0, 0)),
            ]
            + [VMEM] * len(sources),
            scratch_shapes=[
                pltpu.VMEM((1, HEAD + EXTRA, 8 * TILE), F32),
                pltpu.VMEM((KEYS, 8 * TILE), F32),
                pltpu.VMEM((1, 2 * HEAD, 8 * TILE), BF16),
                pltpu.SemaphoreType.DMA((3,)),
            ],
            compiler_params=params(small),
            cost_estimate=pl.CostEstimate(
                flops=2_000_000_000, bytes_accessed=8_000_000, transcendentals=2_000_000
            ),
            name="own",
        )(pos, held, queries, resid, after, *map(pin, sources))

    half0, done, *weights = own(0, sent[0], w_gate, w_up, w_down)
    half1, late = own(1, done)
    halves = [half0, half1]

    come = [
        move(sent[k], [(s, (s + k * SHARDS) % n) for s in range(n)]) for k in range(1, planes)
    ]
    next_door = move(sent[0], flip_y)
    come, next_door, done = lax.optimization_barrier((come, next_door, done))
    here = [sent[0], jnp.concatenate(come, axis=0)]
    there = [next_door, move(here[1], flip_y)]
    mate = move(jnp.concatenate(here, axis=0), flip_c)
    there, mate, late = lax.optimization_barrier((there, mate, late))
    pieces = here + there + [mate, move(jnp.concatenate(there, axis=0), flip_c)]

    half = jax.ShapeDtypeStruct((n * PIECE // 2, width // CUT), BF16)
    keep, send = pl.pallas_call(
        functools.partial(expert_kernel, n, len(pieces)),
        out_shape=[half, half],
        in_specs=[VMEM] * (len(pieces) + 3) + [ANY],
        out_specs=[VMEM, VMEM],
        scratch_shapes=[pltpu.VMEM((min(n, 16) * CAP, width), BF16)],
        compiler_params=params(16),
        cost_estimate=pl.CostEstimate(
            flops=1_200_000_000, bytes_accessed=12_000_000, transcendentals=50_000
        ),
        name="expert",
    )(*pieces, *weights, late)

    halves += [own(part, keep)[0] for part in range(2, 4)]

    total = keep.astype(F32) + move(send, [(s, s ^ 1) for s in range(n)]).astype(F32)
    quarter = n * PIECE // 4
    other = move(total[quarter:].astype(BF16), [(s, s ^ 2) for s in range(n)])
    total = (total[:quarter] + other.astype(F32)).astype(BF16)
    parts = [total[:PIECE]]
    for k in range(1, planes):
        parts.append(
            move(
                total[k * PIECE : (k + 1) * PIECE], [(s, (s - k * SHARDS) % n) for s in range(n)]
            )
        )

    return pl.pallas_call(
        functools.partial(combine_kernel, planes),
        out_shape=jax.ShapeDtypeStruct((tokens, width), BF16),
        in_specs=[SMEM] + [VMEM] * (6 + planes),
        out_specs=VMEM,
        compiler_params=params(small),
        name="combine",
    )(pos, routes_t, gates_t, *halves, *parts)


def solution(mesh):
    rows = P(("groups", "expert"), None)
    in_specs = (rows,) * 4 + (P(("groups", "expert")), P(), rows, rows) + (
        P("expert", None, None),
    ) * 3
    return jax.shard_map(local, mesh=mesh, in_specs=in_specs, out_specs=rows, check_vma=False)
```

```python
import functools
import math

import jax
import jax.numpy as jnp
from jax import lax
from jax.experimental import pallas as pl
from jax.experimental.pallas import tpu as pltpu
from jax.sharding import PartitionSpec as P

HEAD = 128
QUERY_HEADS = 32
KV_HEADS = 2
GROUP = QUERY_HEADS // KV_HEADS
SHARDS = 4
CAP = 6
SLOTS = 8
CUT = 4
PIECE = CUT * CAP
TILE = 128
KEYS = 256
KV_ROWS = TILE + 16
SCALE = math.log2(math.e) / math.sqrt(HEAD)
LOW = -1e30
EXTRA = 16
F32 = jnp.float32
BF16 = jnp.bfloat16
VMEM = pl.BlockSpec(memory_space=pltpu.VMEM)
SMEM = pl.BlockSpec(memory_space=pltpu.SMEM)
ANY = pl.BlockSpec(memory_space=pl.ANY)
HBM = pl.BlockSpec(memory_space=pltpu.HBM)


def dot(a, b, ca=1, cb=0):
    return lax.dot_general(a, b, (((ca,), (cb,)), ((), ())), preferred_element_type=F32)


def reach(n):
    longest = n * TILE // 2 + 256
    return (longest - 1 + TILE - 1) // TILE


def slot_rows(routes, experts):
    members = jnp.concatenate(
        [jnp.max((routes == e).astype(F32), axis=0, keepdims=True) for e in experts], axis=0
    )
    count = len(experts)
    padded = -(-count // 8) * 8
    wide = members
    if padded > count:
        wide = jnp.concatenate([members, jnp.zeros((padded - count, TILE), F32)], axis=0)
    before = lax.broadcasted_iota(jnp.int32, (TILE, TILE), 0) < lax.broadcasted_iota(
        jnp.int32, (TILE, TILE), 1
    )
    ranks = dot(wide.astype(BF16), before.astype(F32).astype(BF16))
    return members, ranks


def one_hot(targets, count):
    shape = (targets.shape[0], count) if targets.shape[1] == 1 else (count, targets.shape[1])
    axis = 1 if targets.shape[1] == 1 else 0
    places = lax.broadcasted_iota(jnp.int32, shape, axis).astype(F32)
    return jnp.where(places == targets, 1.0, 0.0).astype(BF16)


def split(x, size):
    whole = jnp.floor((x + 0.5) / size)
    return whole, x - whole * size


def travel_row(x, senders, slots):
    chunk, rest = split(x, senders * slots)
    sender, slot = split(rest, slots)
    return jnp.where(slot < CAP, sender * PIECE + chunk * CAP + slot, -1.0)


def numbers(shape, axis):
    return lax.broadcasted_iota(jnp.int32, shape, axis).astype(F32)


def pack_kernel(docs_ref, keys_ref, values_ref, out_ref, docs, values, sems):
    moves = [
        pltpu.make_async_copy(values_ref, values, sems.at[0]),
        pltpu.make_async_copy(docs_ref, docs, sems.at[1]),
        pltpu.make_async_copy(
            keys_ref, out_ref.at[pl.ds(0, TILE), pl.ds(0, KV_HEADS * HEAD)], sems.at[2]
        ),
    ]
    for move in moves:
        move.start()
    moves[0].wait()
    for h in range(KV_HEADS):
        out_ref[0:TILE, (KV_HEADS + h) * HEAD : (KV_HEADS + h + 1) * HEAD] = (
            values[:, h * HEAD : (h + 1) * HEAD].astype(F32).T.astype(BF16)
        )
    moves[1].wait()
    out_ref[TILE:KV_ROWS, :] = jnp.zeros((KV_ROWS - TILE, 4 * HEAD), BF16)
    out_ref[TILE:KV_ROWS, 0:HEAD] = jnp.broadcast_to(
        docs[...].astype(F32), (KV_ROWS - TILE, TILE)
    ).astype(BF16)
    moves[2].wait()


def select_kernel(planes, pos_ref, *refs):
    sources, (qs_ref, xs_ref, facts_ref) = refs[:4], refs[4:7]
    routes_ref, docs_ref, q_ref, x_ref, sems = refs[7:]
    moves = [
        pltpu.make_async_copy(source, target, sems.at[i])
        for i, (source, target) in enumerate(zip(sources, refs[7:11]))
    ]
    for move in moves:
        move.start()
    for move in moves:
        move.wait()
    z = pos_ref[0] // SHARDS
    members, ranks = slot_rows(routes_ref[...], [lax.rem(z + k, planes) for k in range(planes)])
    docs = docs_ref[...].astype(F32)
    lane_slot = (lax.broadcasted_iota(jnp.int32, (TILE, TILE), 0) % SLOTS).astype(F32)
    token = lax.broadcasted_iota(jnp.int32, (1, TILE), 1).astype(F32)
    facts = jnp.concatenate(
        [token, docs, jnp.ones((1, TILE), F32), jnp.zeros((5, TILE), F32)], axis=0
    ).astype(BF16)
    picks = [
        jnp.where(ranks[k : k + 1] == lane_slot, members[k : k + 1], 0.0) for k in range(planes)
    ]
    chooser = jnp.concatenate([p[:SLOTS] for p in picks], axis=0).astype(BF16)
    q_rows = dot(chooser, q_ref[...])
    xs_ref[...] = dot(chooser, x_ref[...])
    for k in range(planes):
        known = dot(facts, picks[k].astype(BF16), 1, 1)
        facts_ref[:, k * TILE : (k + 1) * TILE] = jnp.concatenate(
            [known[0:1], known[1:2] + (1.0 - known[2:3]) * docs[:, 0:1], known[2:]], axis=0
        )
        for h in range(KV_HEADS):
            stack = jnp.concatenate(
                [
                    q_rows[k * SLOTS : (k + 1) * SLOTS, a * HEAD : (a + 1) * HEAD]
                    for a in range(h * GROUP, (h + 1) * GROUP)
                ],
                axis=0,
            )
            for i, term in enumerate(two_terms(stack.T)):
                qs_ref[h, i * HEAD : (i + 1) * HEAD, k * TILE : (k + 1) * TILE] = term


def doc_starts(n, pos, held):
    sums = [jnp.zeros((1, TILE), F32) for _ in range(3)]
    for s in range(n):
        docs = held[s, TILE:KV_ROWS, 0:HEAD].astype(F32)[0:1]
        ahead = (pos - s < 0).astype(F32)
        behind = (pos - s > reach(n)).astype(F32)
        known = 1.0 - ahead - behind
        docs = jnp.where(known > 0.5, docs, 0.0) + 9.0 * ahead
        for d in range(3):
            sums[d] = sums[d] + jnp.where(docs < d + 1.0, 1.0, 0.0)
    return [jnp.sum(s, axis=1, keepdims=True) for s in sums]


def starts_of(docs, starts):
    first = jnp.zeros_like(docs)
    for d in range(3):
        first = jnp.where(docs == d + 1.0, starts[d], first)
    return first


def two_terms(x):
    scaled = x.astype(F32) * SCALE
    high = scaled.astype(BF16)
    return high, (scaled - high.astype(F32)).astype(BF16)


def key_steps(pos, place, first, bias_ref, step, state):
    low = jnp.min(first).astype(jnp.int32) // KEYS
    last = pos // (KEYS // TILE)
    clear = jnp.minimum((jnp.max(first).astype(jnp.int32) + KEYS - 1) // KEYS, last)

    def edge(j, carried):
        kb = jnp.where(j < clear - low, low + j, last)
        key_at = (kb * KEYS + lax.broadcasted_iota(jnp.int32, (KEYS, 1), 0)).astype(F32)
        bias_ref[...] = jnp.where((key_at >= first) & (key_at <= place), 0.0, LOW)
        return step(kb, carried, True)

    state = lax.fori_loop(0, clear - low + 1, edge, state)
    return lax.fori_loop(clear, last, lambda kb, carried: step(kb, carried, False), state)


def keys_of(held, kb, h):
    keys = jnp.concatenate(
        [held[2 * kb + t, 0:TILE, h * HEAD : (h + 1) * HEAD] for t in range(2)], axis=0
    )
    return jnp.concatenate([keys, keys], axis=1)


def values_of(held, kb, h):
    at = (KV_HEADS + h) * HEAD
    values = jnp.concatenate(
        [held[2 * kb + t, 0:TILE, at : at + HEAD] for t in range(2)], axis=1
    )
    return jnp.concatenate([values, jnp.ones((EXTRA, KEYS), BF16)], axis=0)


def flash(pos, held, q_ref, kv_heads, acc_ref, bias_ref, place, first):
    lanes = place.shape[1]
    chains = range(len(kv_heads))
    for i in chains:
        acc_ref[i] = jnp.zeros((HEAD + EXTRA, lanes), F32)

    def step(kb, tops, masked):
        out = []
        for i in chains:
            scores = dot(keys_of(held, kb, kv_heads[i]), q_ref[i])
            if masked:
                scores = scores + bias_ref[...]
            top = jnp.maximum(tops[i], jnp.max(scores, axis=0, keepdims=True))
            weights = jnp.exp2(scores - top).astype(BF16)
            acc_ref[i] = acc_ref[i] * jnp.exp2(tops[i] - top) + dot(
                values_of(held, kb, kv_heads[i]), weights
            )
            out.append(top)
        return tuple(out)

    tops = tuple(jnp.full((1, lanes), LOW, F32) for _ in chains)
    key_steps(pos, place, first, bias_ref, step, tops)
    return [(acc_ref[i, 0:HEAD] / acc_ref[i, HEAD : HEAD + 1]).T for i in chains]


def place_pieces(n, senders, pos, pieces, held, sems):
    planes = n // SHARDS
    z, y, c = pos // SHARDS, (pos // 2) % 2, pos % 2
    copies = []
    for i, (piece, row, flip_c, flip_y, passed) in enumerate(senders):
        k = jnp.where(y == 0, passed[0], passed[1])
        sender = lax.rem(z - k + planes, planes) * SHARDS + (y ^ flip_y) * 2 + (c ^ flip_c)
        copy = pltpu.make_async_copy(
            pieces[piece].at[pl.ds(row, KV_ROWS)], held.at[sender], sems.at[i]
        )
        copy.start()
        copies.append(copy)
    return copies


def collect_kernel(n, senders, pos_ref, *refs):
    *pieces, held, sems = refs
    for copy in place_pieces(n, senders, pos_ref[0], pieces, held, sems):
        copy.wait()


def routed_kernel(n, senders, pos_ref, gain_ref, qs_ref, xs_ref, facts_ref, _, *refs):
    planes = n // SHARDS
    count = len(senders)
    pieces, outs, held = refs[:4], refs[4 : 4 + planes], refs[4 + planes]
    acc, bias, q_scr, state, gain, sems = refs[5 + planes :]
    pos = pos_ref[0]
    copies = place_pieces(n, senders, pos, pieces, held, sems)
    copies.append(pltpu.make_async_copy(gain_ref, gain, sems.at[count]))
    copies[-1].start()
    for copy in copies:
        copy.wait()
    starts = doc_starts(n, pos, held)
    lanes = q_scr.shape[2]
    base = (pos * TILE).astype(F32)
    for part in range(planes * TILE // lanes):
        at = slice(part * lanes, (part + 1) * lanes)
        q_scr[...] = qs_ref[:, :, at]
        done = flash(
            pos,
            held,
            q_scr,
            range(KV_HEADS),
            acc,
            bias,
            facts_ref[0:1, at] + base,
            starts_of(facts_ref[1:2, at], starts),
        )
        for h in range(KV_HEADS):
            for k in range(lanes // TILE):
                row = (part * (lanes // TILE) + k) * SLOTS
                for g in range(GROUP):
                    lane = (h * GROUP + g) * HEAD
                    state[row : row + SLOTS, lane : lane + HEAD] = (
                        xs_ref[row : row + SLOTS, lane : lane + HEAD]
                        + done[h][k * TILE + g * SLOTS : k * TILE + (g + 1) * SLOTS]
                    )
    width = state.shape[1] // CUT
    order = one_hot(travel_row(numbers((1, CUT * SLOTS), 1), 1, SLOTS), PIECE)
    for k in range(planes):
        hidden = state[k * SLOTS : (k + 1) * SLOTS, :]
        mean = jnp.mean(hidden * hidden, axis=1, keepdims=True)
        normed = hidden * lax.rsqrt(mean + 1e-06) * gain[...]
        chunks = [normed[:, q * width : (q + 1) * width] for q in range(CUT)]
        outs[k][...] = dot(order, jnp.concatenate(chunks, axis=0).astype(BF16)).astype(BF16)


def expert_kernel(n, count, *refs):
    pieces = refs[:count]
    wg, wu, wd = refs[count : count + 3]
    keep_ref, send_ref, rows = refs[count + 4 :]
    step = pieces[0].shape[1]
    senders = min(n, 16)
    size, total = senders * PIECE, n * PIECE
    half = total // 2
    kept = senders * CAP
    gather = one_hot(travel_row(numbers((size, 1), 0), senders, CAP), size)
    spread = one_hot(travel_row(numbers((1, size), 1), senders, CAP), size)
    for at in range(0, total, size):
        parts, first = [], 0
        for piece in pieces:
            low, high = max(at - first, 0), min(at + size - first, piece.shape[0])
            if low < high:
                parts.append(piece[low:high, :].astype(F32))
            first += piece.shape[0]
        came = dot(gather, jnp.concatenate(parts, axis=0).astype(BF16)).astype(BF16)
        for q in range(CUT):
            rows[:, q * step : (q + 1) * step] = came[q * kept : (q + 1) * kept]
        gate = dot(rows[...], wg[...])
        up = dot(rows[...], wu[...])
        act = (gate / (1.0 + jnp.exp(-gate)) * up).astype(BF16)
        parts = [dot(act, wd[:, q * step : (q + 1) * step]).astype(BF16) for q in range(CUT)]
        out = dot(spread, jnp.concatenate(parts, axis=0)).astype(BF16)
        if size > half:
            keep_ref[...] = out[:half]
            send_ref[...] = out[half:]
        elif at < half:
            keep_ref[at : at + size] = out
        else:
            send_ref[at - half : at - half + size] = out


def own_kernel(n, part, loads, pos_ref, held, q_ref, x_ref, _, *refs):
    sources, (h_ref, done_ref) = refs[:loads], refs[loads : loads + 2]
    targets = refs[loads + 2 : 2 * loads + 2]
    acc, bias, qt, sems = refs[2 * loads + 2 :]
    moves = [
        pltpu.make_async_copy(source.at[0], target, sems.at[i])
        for i, (source, target) in enumerate(zip(sources, targets))
    ]
    for move in moves:
        move.start()
    done_ref[...] = jnp.zeros((8, TILE), F32)
    pos = pos_ref[0]
    starts = doc_starts(n, pos, held)
    first = starts_of(held[pos, TILE:KV_ROWS, 0:HEAD].astype(F32)[0:1], starts)
    place = (pos * TILE + lax.broadcasted_iota(jnp.int32, (1, TILE), 1)).astype(F32)
    for a in range(8):
        terms = two_terms(q_ref[:, a * HEAD : (a + 1) * HEAD].astype(F32).T)
        for i, term in enumerate(terms):
            qt[0, i * HEAD : (i + 1) * HEAD, a * TILE : (a + 1) * TILE] = term
    place = jnp.concatenate([place] * 8, axis=1)
    first = jnp.concatenate([first] * 8, axis=1)
    (done,) = flash(pos, held, qt, [part // 2], acc, bias, place, first)
    for a in range(8):
        lane = a * HEAD
        h_ref[:, lane : lane + HEAD] = (
            x_ref[:, lane : lane + HEAD].astype(F32) + done[a * TILE : (a + 1) * TILE]
        )
    for move in moves:
        move.wait()


def combine_kernel(planes, pos_ref, routes_ref, gates_ref, *refs):
    halves, parts, out_ref = refs[:4], refs[4 : 4 + planes], refs[4 + planes]
    z = pos_ref[0] // SHARDS
    routes = routes_ref[...]
    gates = gates_ref[...]
    experts = [lax.rem(z + k, planes) for k in range(planes)]
    members, ranks = slot_rows(routes, experts)
    slot = lax.broadcasted_iota(jnp.int32, (SLOTS, TILE), 0).astype(F32)
    mix = []
    for k, e in enumerate(experts):
        gate = jnp.sum(jnp.where(routes == e, gates, 0.0), axis=0, keepdims=True)
        mix.append(jnp.where(ranks[k : k + 1] == slot, gate, 0.0))
    mix = jnp.concatenate(mix, axis=0).T
    mix_high = mix.astype(BF16)
    mix_low = (mix - mix_high.astype(F32)).astype(BF16)
    size = halves[0].shape[1]
    slots = planes * SLOTS
    came = jnp.concatenate([p[...].astype(F32) for p in parts], axis=0).astype(BF16)
    order = one_hot(travel_row(numbers((CUT * slots, 1), 0), planes, SLOTS), planes * PIECE)
    came = dot(order, came).astype(BF16)
    for i, h in enumerate(halves):
        rows = came[i * slots : (i + 1) * slots]
        out_ref[:, i * size : (i + 1) * size] = (
            h[...] + dot(mix_high, rows) + dot(mix_low, rows)
        ).astype(BF16)


def pin(x):
    return pltpu.with_memory_space_constraint(x, pltpu.HBM)


def params(mib):
    return pltpu.CompilerParams(vmem_limit_bytes=mib * 1024 * 1024)


def local(
    resid, queries, keys, values, doc_ids, norm_gain, routes, route_weights, w_gate, w_up, w_down
):
    n = lax.axis_size("expert")
    planes = n // SHARDS
    pos = lax.axis_index("expert").astype(jnp.int32).reshape(1)
    tokens, width = queries.shape
    hidden = w_gate.shape[2]
    routes_t = routes.T
    gates_t = route_weights.T
    docs = doc_ids.reshape(1, tokens)
    small = 24 if n <= 16 else 60
    back = reach(n)

    packed = pl.pallas_call(
        pack_kernel,
        out_shape=jax.ShapeDtypeStruct((KV_ROWS, 4 * HEAD), BF16),
        in_specs=[HBM] * 3,
        out_specs=VMEM,
        scratch_shapes=[
            pltpu.VMEM((1, tokens), jnp.int32),
            pltpu.VMEM((tokens, KV_HEADS * HEAD), BF16),
            pltpu.SemaphoreType.DMA((3,)),
        ],
        compiler_params=params(8),
        name="pack",
    )(pin(docs), pin(keys), pin(values))

    def move(value, pairs):
        return lax.ppermute(value, "expert", pairs)

    def needed(k, y_from, y_to):
        gaps = [
            k * SHARDS + 2 * (y_to - y_from) + (to - of) for to in range(2) for of in range(2)
        ]
        return any(0 <= gap <= back for gap in gaps)

    far = max(k for k in range(planes) if any(needed(k, a, b) for a in (0, 1) for b in (0, 1)))
    q_rows, x_rows, facts = pl.pallas_call(
        functools.partial(select_kernel, planes),
        out_shape=[
            jax.ShapeDtypeStruct((KV_HEADS, 2 * HEAD, planes * TILE), BF16),
            jax.ShapeDtypeStruct((planes * SLOTS, width), F32),
            jax.ShapeDtypeStruct((8, planes * TILE), F32),
        ],
        in_specs=[SMEM] + [HBM] * 4,
        out_specs=[VMEM] * 3,
        scratch_shapes=[
            pltpu.VMEM(routes_t.shape, jnp.int32),
            pltpu.VMEM(docs.shape, jnp.int32),
            pltpu.VMEM(queries.shape, BF16),
            pltpu.VMEM(resid.shape, BF16),
            pltpu.SemaphoreType.DMA((4,)),
        ],
        compiler_params=params(small),
        name="select",
    )(pos, pin(routes_t), pin(docs), pin(queries), pin(resid))

    flip_y = [(s, s ^ 2) for s in range(n)]
    flip_c = [(s, s ^ 1) for s in range(n)]
    along = [packed]
    for k in range(1, far + 1):
        used = [any(needed(k, y, to) for to in (0, 1)) for y in (0, 1)]
        pairs = [(s, (s + k * SHARDS) % n if used[s // 2 % 2] else s) for s in range(n)]
        along.append(move(packed, pairs))
    along[1], q_rows = lax.optimization_barrier((along[1], q_rows))
    shared = not needed(0, 1, 0) and not needed(far, 0, 1)
    middle = range(1, far) if shared else range(far)
    across = []
    for k in middle:
        if k == middle[1]:
            along[k:], across = lax.optimization_barrier((along[k:], across))
        across.append(move(along[k], [(s, s ^ 2 if s >= k * SHARDS else s) for s in range(n)]))
    odd = (pos[0] & 2) != 0
    final = move(jnp.where(odd, along[far], packed) if shared else along[far], flip_y)
    early, late = along[:far] + across[:-1], [along[far], across[-1]]
    sides = [(0, (k, k)) for k in range(far)] + [(1, (k, k)) for k in middle[:-1]]
    late_sides = [(0, (far, far)), (1, (middle[-1],) * 2), (1, (far, 0 if shared else far))]
    early.append(move(jnp.concatenate(early, axis=0), flip_c))
    early_senders = [(i, 0, 0, *side) for i, side in enumerate(sides)]
    early_senders += [(len(sides), i * KV_ROWS, 1, *side) for i, side in enumerate(sides)]
    late_senders = [(i, 0, 0, *side) for i, side in enumerate(late_sides)]
    late_senders += [(3, i * KV_ROWS, 1, *side) for i, side in enumerate(late_sides)]
    held_shape = jax.ShapeDtypeStruct((n, KV_ROWS, 4 * HEAD), BF16)
    held = pl.pallas_call(
        functools.partial(collect_kernel, n, early_senders),
        out_shape=held_shape,
        in_specs=[SMEM] + [ANY] * len(early),
        out_specs=VMEM,
        scratch_shapes=[pltpu.SemaphoreType.DMA((len(early_senders),))],
        compiler_params=params(small),
        cost_estimate=pl.CostEstimate(flops=0, bytes_accessed=1000, transcendentals=0),
        name="collect",
    )(pos, *early)

    final, held = lax.optimization_barrier((final, held))
    late.append(final)
    late.append(move(jnp.concatenate(late, axis=0), flip_c))
    *sent, held = pl.pallas_call(
        functools.partial(routed_kernel, n, late_senders),
        out_shape=[jax.ShapeDtypeStruct((PIECE, width // CUT), BF16)] * planes
        + [held_shape],
        in_specs=[SMEM, HBM] + [VMEM] * 4 + [ANY] * len(late),
        out_specs=[VMEM] * (planes + 1),
        scratch_shapes=[
            pltpu.VMEM((KV_HEADS, HEAD + EXTRA, 4 * TILE), F32),
            pltpu.VMEM((KEYS, 4 * TILE), F32),
            pltpu.VMEM((KV_HEADS, 2 * HEAD, 4 * TILE), BF16),
            pltpu.VMEM((planes * SLOTS, width), F32),
            pltpu.VMEM((1, width), F32),
            pltpu.SemaphoreType.DMA((len(late_senders) + 1,)),
        ],
        input_output_aliases={5: planes},
        compiler_params=params(small),
        name="routed",
    )(pos, pin(norm_gain.reshape(1, width)), q_rows, x_rows, facts, held, *late)

    def own(part, after, *sources):
        columns = pl.BlockSpec((tokens, 8 * HEAD), lambda i: (0, part))
        return pl.pallas_call(
            functools.partial(own_kernel, n, part, len(sources)),
            out_shape=[
                jax.ShapeDtypeStruct((tokens, 8 * HEAD), F32),
                jax.ShapeDtypeStruct((8, TILE), F32),
            ]
            + [jax.ShapeDtypeStruct(w.shape[1:], BF16) for w in sources],
            grid=(1,),
            in_specs=[SMEM, VMEM, columns, columns, ANY] + [HBM] * len(sources),
            out_specs=[
                pl.BlockSpec((tokens, 8 * HEAD), lambda i: (0, 0)),
                pl.BlockSpec((8, TILE), lambda i: (0, 0)),
            ]
            + [VMEM] * len(sources),
            scratch_shapes=[
                pltpu.VMEM((1, HEAD + EXTRA, 8 * TILE), F32),
                pltpu.VMEM((KEYS, 8 * TILE), F32),
                pltpu.VMEM((1, 2 * HEAD, 8 * TILE), BF16),
                pltpu.SemaphoreType.DMA((3,)),
            ],
            compiler_params=params(small),
            cost_estimate=pl.CostEstimate(
                flops=2_000_000_000, bytes_accessed=8_000_000, transcendentals=2_000_000
            ),
            name="own",
        )(pos, held, queries, resid, after, *map(pin, sources))

    half0, done, *weights = own(0, sent[0], w_gate, w_up, w_down)
    half1, late = own(1, done)
    halves = [half0, half1]

    come = [
        move(sent[k], [(s, (s + k * SHARDS) % n) for s in range(n)]) for k in range(1, planes)
    ]
    next_door = move(sent[0], flip_y)
    come, next_door, done = lax.optimization_barrier((come, next_door, done))
    here = [sent[0], jnp.concatenate(come, axis=0)]
    there = [next_door, move(here[1], flip_y)]
    mate = move(jnp.concatenate(here, axis=0), flip_c)
    there, mate, late = lax.optimization_barrier((there, mate, late))
    pieces = here + there + [mate, move(jnp.concatenate(there, axis=0), flip_c)]

    half = jax.ShapeDtypeStruct((n * PIECE // 2, width // CUT), BF16)
    keep, send = pl.pallas_call(
        functools.partial(expert_kernel, n, len(pieces)),
        out_shape=[half, half],
        in_specs=[VMEM] * (len(pieces) + 3) + [ANY],
        out_specs=[VMEM, VMEM],
        scratch_shapes=[pltpu.VMEM((min(n, 16) * CAP, width), BF16)],
        compiler_params=params(16),
        cost_estimate=pl.CostEstimate(
            flops=1_200_000_000, bytes_accessed=12_000_000, transcendentals=50_000
        ),
        name="expert",
    )(*pieces, *weights, late)

    halves += [own(part, keep)[0] for part in range(2, 4)]

    total = keep.astype(F32) + move(send, [(s, s ^ 1) for s in range(n)]).astype(F32)
    quarter = n * PIECE // 4
    other = move(total[quarter:].astype(BF16), [(s, s ^ 2) for s in range(n)])
    total = (total[:quarter] + other.astype(F32)).astype(BF16)
    parts = [total[:PIECE]]
    for k in range(1, planes):
        parts.append(
            move(
                total[k * PIECE : (k + 1) * PIECE], [(s, (s - k * SHARDS) % n) for s in range(n)]
            )
        )

    return pl.pallas_call(
        functools.partial(combine_kernel, planes),
        out_shape=jax.ShapeDtypeStruct((tokens, width), BF16),
        in_specs=[SMEM] + [VMEM] * (6 + planes),
        out_specs=VMEM,
        compiler_params=params(small),
        name="combine",
    )(pos, routes_t, gates_t, *halves, *parts)


def solution(mesh):
    rows = P(("groups", "expert"), None)
    in_specs = (rows,) * 4 + (P(("groups", "expert")), P(), rows, rows) + (
        P("expert", None, None),
    ) * 3
    return jax.shard_map(local, mesh=mesh, in_specs=in_specs, out_specs=rows, check_vma=False)
```

```python
import functools
import math

import jax
import jax.numpy as jnp
from jax import lax
from jax.experimental import pallas as pl
from jax.experimental.pallas import tpu as pltpu
from jax.sharding import PartitionSpec as P

HEAD = 128
QUERY_HEADS = 32
KV_HEADS = 2
GROUP = QUERY_HEADS // KV_HEADS
SHARDS = 4
CAP = 6
SLOTS = 8
CUT = 4
PIECE = CUT * CAP
TILE = 128
KEYS = 256
KV_ROWS = TILE + 16
SCALE = math.log2(math.e) / math.sqrt(HEAD)
LOW = -1e30
EXTRA = 16
F32 = jnp.float32
BF16 = jnp.bfloat16
VMEM = pl.BlockSpec(memory_space=pltpu.VMEM)
SMEM = pl.BlockSpec(memory_space=pltpu.SMEM)
ANY = pl.BlockSpec(memory_space=pl.ANY)
HBM = pl.BlockSpec(memory_space=pltpu.HBM)


def dot(a, b, ca=1, cb=0):
    return lax.dot_general(a, b, (((ca,), (cb,)), ((), ())), preferred_element_type=F32)


def reach(n):
    longest = n * TILE // 2 + 256
    return (longest - 1 + TILE - 1) // TILE


def slot_rows(routes, experts):
    members = jnp.concatenate(
        [jnp.max((routes == e).astype(F32), axis=0, keepdims=True) for e in experts], axis=0
    )
    count = len(experts)
    padded = -(-count // 8) * 8
    wide = members
    if padded > count:
        wide = jnp.concatenate([members, jnp.zeros((padded - count, TILE), F32)], axis=0)
    before = lax.broadcasted_iota(jnp.int32, (TILE, TILE), 0) < lax.broadcasted_iota(
        jnp.int32, (TILE, TILE), 1
    )
    ranks = dot(wide.astype(BF16), before.astype(F32).astype(BF16))
    return members, ranks


def one_hot(targets, count):
    shape = (targets.shape[0], count) if targets.shape[1] == 1 else (count, targets.shape[1])
    axis = 1 if targets.shape[1] == 1 else 0
    places = lax.broadcasted_iota(jnp.int32, shape, axis).astype(F32)
    return jnp.where(places == targets, 1.0, 0.0).astype(BF16)


def split(x, size):
    whole = jnp.floor((x + 0.5) / size)
    return whole, x - whole * size


def travel_row(x, senders, slots):
    chunk, rest = split(x, senders * slots)
    sender, slot = split(rest, slots)
    return jnp.where(slot < CAP, sender * PIECE + chunk * CAP + slot, -1.0)


def numbers(shape, axis):
    return lax.broadcasted_iota(jnp.int32, shape, axis).astype(F32)


def pack_kernel(docs_ref, keys_ref, values_ref, out_ref, docs, values, sems):
    moves = [
        pltpu.make_async_copy(values_ref, values, sems.at[0]),
        pltpu.make_async_copy(docs_ref, docs, sems.at[1]),
        pltpu.make_async_copy(
            keys_ref, out_ref.at[pl.ds(0, TILE), pl.ds(0, KV_HEADS * HEAD)], sems.at[2]
        ),
    ]
    for move in moves:
        move.start()
    moves[0].wait()
    for h in range(KV_HEADS):
        out_ref[0:TILE, (KV_HEADS + h) * HEAD : (KV_HEADS + h + 1) * HEAD] = (
            values[:, h * HEAD : (h + 1) * HEAD].astype(F32).T.astype(BF16)
        )
    moves[1].wait()
    out_ref[TILE:KV_ROWS, :] = jnp.zeros((KV_ROWS - TILE, 4 * HEAD), BF16)
    out_ref[TILE:KV_ROWS, 0:HEAD] = jnp.broadcast_to(
        docs[...].astype(F32), (KV_ROWS - TILE, TILE)
    ).astype(BF16)
    moves[2].wait()


def select_kernel(planes, pos_ref, *refs):
    sources, (qs_ref, xs_ref, facts_ref, mix_ref, gather_ref, spread_ref) = refs[:5], refs[5:11]
    routes_ref, docs_ref, q_ref, x_ref, gates_ref, sems = refs[11:]
    moves = [
        pltpu.make_async_copy(source, target, sems.at[i])
        for i, (source, target) in enumerate(zip(sources, refs[11:16]))
    ]
    for move in moves:
        move.start()
    for move in moves:
        move.wait()
    z = pos_ref[0] // SHARDS
    experts = [lax.rem(z + k, planes) for k in range(planes)]
    routes, gates = routes_ref[...], gates_ref[...]
    members, ranks = slot_rows(routes, experts)
    slot = lax.broadcasted_iota(jnp.int32, (SLOTS, TILE), 0).astype(F32)
    mix = []
    for k, e in enumerate(experts):
        gate = jnp.sum(jnp.where(routes == e, gates, 0.0), axis=0, keepdims=True)
        mix.append(jnp.where(ranks[k : k + 1] == slot, gate, 0.0))
    mix = jnp.concatenate(mix, axis=0).T
    mix_high = mix.astype(BF16)
    mix_ref[:, : planes * SLOTS] = mix_high
    mix_ref[:, planes * SLOTS :] = (mix - mix_high.astype(F32)).astype(BF16)
    size = gather_ref.shape[0]
    gather_ref[...] = one_hot(travel_row(numbers((size, 1), 0), size // PIECE, CAP), size)
    spread_ref[...] = one_hot(travel_row(numbers((1, size), 1), size // PIECE, CAP), size)
    docs = docs_ref[...].astype(F32)
    lane_slot = (lax.broadcasted_iota(jnp.int32, (TILE, TILE), 0) % SLOTS).astype(F32)
    token = lax.broadcasted_iota(jnp.int32, (1, TILE), 1).astype(F32)
    facts = jnp.concatenate(
        [token, docs, jnp.ones((1, TILE), F32), jnp.zeros((5, TILE), F32)], axis=0
    ).astype(BF16)
    picks = [
        jnp.where(ranks[k : k + 1] == lane_slot, members[k : k + 1], 0.0) for k in range(planes)
    ]
    chooser = jnp.concatenate([p[:SLOTS] for p in picks], axis=0).astype(BF16)
    q_rows = dot(chooser, q_ref[...])
    xs_ref[...] = dot(chooser, x_ref[...])
    for k in range(planes):
        known = dot(facts, picks[k].astype(BF16), 1, 1)
        facts_ref[:, k * TILE : (k + 1) * TILE] = jnp.concatenate(
            [known[0:1], known[1:2] + (1.0 - known[2:3]) * docs[:, 0:1], known[2:]], axis=0
        )
        for h in range(KV_HEADS):
            stack = jnp.concatenate(
                [
                    q_rows[k * SLOTS : (k + 1) * SLOTS, a * HEAD : (a + 1) * HEAD]
                    for a in range(h * GROUP, (h + 1) * GROUP)
                ],
                axis=0,
            )
            for i, term in enumerate(two_terms(stack.T)):
                qs_ref[h, i * HEAD : (i + 1) * HEAD, k * TILE : (k + 1) * TILE] = term


def doc_starts(n, pos, held):
    sums = [jnp.zeros((1, TILE), F32) for _ in range(3)]
    for s in range(n):
        docs = held[s, TILE:KV_ROWS, 0:HEAD].astype(F32)[0:1]
        ahead = (pos - s < 0).astype(F32)
        behind = (pos - s > reach(n)).astype(F32)
        known = 1.0 - ahead - behind
        docs = jnp.where(known > 0.5, docs, 0.0) + 9.0 * ahead
        for d in range(3):
            sums[d] = sums[d] + jnp.where(docs < d + 1.0, 1.0, 0.0)
    return [jnp.sum(s, axis=1, keepdims=True) for s in sums]


def starts_of(docs, starts):
    first = jnp.zeros_like(docs)
    for d in range(3):
        first = jnp.where(docs == d + 1.0, starts[d], first)
    return first


def two_terms(x):
    scaled = x.astype(F32) * SCALE
    high = scaled.astype(BF16)
    return high, (scaled - high.astype(F32)).astype(BF16)


def key_steps(pos, place, first, bias_ref, step, state):
    low = jnp.min(first).astype(jnp.int32) // KEYS
    last = pos // (KEYS // TILE)
    clear = jnp.minimum((jnp.max(first).astype(jnp.int32) + KEYS - 1) // KEYS, last)

    def edge(j, carried):
        kb = jnp.where(j < clear - low, low + j, last)
        key_at = (kb * KEYS + lax.broadcasted_iota(jnp.int32, (KEYS, 1), 0)).astype(F32)
        bias_ref[...] = jnp.where((key_at >= first) & (key_at <= place), 0.0, LOW)
        return step(kb, carried, True)

    state = lax.fori_loop(0, clear - low + 1, edge, state)
    return lax.fori_loop(clear, last, lambda kb, carried: step(kb, carried, False), state)


def by_kv_head(heads):
    groups = [(h, [a for a in heads if a // GROUP == h]) for h in range(KV_HEADS)]
    return [(h, own) for h, own in groups if own]


def keys_of(held, kb, h):
    keys = jnp.concatenate(
        [held[2 * kb + t, 0:TILE, h * HEAD : (h + 1) * HEAD] for t in range(2)], axis=0
    )
    return jnp.concatenate([keys, keys], axis=1)


def values_of(held, kb, h):
    at = (KV_HEADS + h) * HEAD
    values = jnp.concatenate(
        [held[2 * kb + t, 0:TILE, at : at + HEAD] for t in range(2)], axis=1
    )
    return jnp.concatenate([values, jnp.ones((EXTRA, KEYS), BF16)], axis=0)


def flash(pos, held, chains, bias_ref, place, first):
    for _, _, acc in chains:
        acc[...] = jnp.zeros(acc.shape, F32)

    def step(kb, tops, masked):
        out = []
        for (queries, h, acc), old in zip(chains, tops):
            scores = dot(keys_of(held, kb, h), queries[...])
            if masked:
                copies = scores.shape[1] // bias_ref.shape[1]
                scores = scores + jnp.concatenate([bias_ref[...]] * copies, axis=1)
            top = jnp.maximum(old, jnp.max(scores, axis=0, keepdims=True))
            weights = jnp.exp2(scores - top).astype(BF16)
            acc[...] = acc[...] * jnp.exp2(old - top) + dot(values_of(held, kb, h), weights)
            out.append(top)
        return tuple(out)

    tops = tuple(jnp.full((1, acc.shape[1]), LOW, F32) for _, _, acc in chains)
    key_steps(pos, place, first, bias_ref, step, tops)
    return [(acc[0:HEAD, :] / acc[HEAD : HEAD + 1, :]).T for _, _, acc in chains]


def place_pieces(n, senders, pos, pieces, held, sems):
    planes = n // SHARDS
    z, y, c = pos // SHARDS, (pos // 2) % 2, pos % 2
    copies = []
    for i, (piece, row, flip_c, flip_y, passed) in enumerate(senders):
        k = jnp.where(y == 0, passed[0], passed[1])
        sender = lax.rem(z - k + planes, planes) * SHARDS + (y ^ flip_y) * 2 + (c ^ flip_c)
        copy = pltpu.make_async_copy(
            pieces[piece].at[pl.ds(row, KV_ROWS)], held.at[sender], sems.at[i]
        )
        copy.start()
        copies.append(copy)
    return copies


def collect_kernel(n, senders, pos_ref, *refs):
    *pieces, held, sems = refs
    for copy in place_pieces(n, senders, pos_ref[0], pieces, held, sems):
        copy.wait()


def routed_kernel(n, senders, pos_ref, gain_ref, qs_ref, xs_ref, facts_ref, _, *refs):
    planes = n // SHARDS
    count = len(senders)
    pieces, outs, held = refs[:3], refs[3 : 3 + planes], refs[3 + planes]
    acc, bias, q_scr, state, gain, sems = refs[4 + planes :]
    pos = pos_ref[0]
    copies = place_pieces(n, senders, pos, pieces, held, sems)
    copies.append(pltpu.make_async_copy(gain_ref, gain, sems.at[count]))
    copies[-1].start()
    for copy in copies:
        copy.wait()
    starts = doc_starts(n, pos, held)
    lanes = q_scr.shape[2]
    base = (pos * TILE).astype(F32)
    for part in range(planes * TILE // lanes):
        at = slice(part * lanes, (part + 1) * lanes)
        q_scr[...] = qs_ref[:, :, at]
        done = flash(
            pos,
            held,
            [(q_scr.at[h], h, acc.at[h]) for h in range(KV_HEADS)],
            bias,
            facts_ref[0:1, at] + base,
            starts_of(facts_ref[1:2, at], starts),
        )
        for h in range(KV_HEADS):
            for k in range(lanes // TILE):
                row = (part * (lanes // TILE) + k) * SLOTS
                for g in range(GROUP):
                    lane = (h * GROUP + g) * HEAD
                    state[row : row + SLOTS, lane : lane + HEAD] = (
                        xs_ref[row : row + SLOTS, lane : lane + HEAD]
                        + done[h][k * TILE + g * SLOTS : k * TILE + (g + 1) * SLOTS]
                    )
    width = state.shape[1] // CUT
    order = one_hot(travel_row(numbers((1, CUT * SLOTS), 1), 1, SLOTS), PIECE)
    for k in range(planes):
        hidden = state[k * SLOTS : (k + 1) * SLOTS, :]
        mean = jnp.mean(hidden * hidden, axis=1, keepdims=True)
        normed = hidden * lax.rsqrt(mean + 1e-06) * gain[...]
        chunks = [normed[:, q * width : (q + 1) * width] for q in range(CUT)]
        outs[k][...] = dot(order, jnp.concatenate(chunks, axis=0).astype(BF16)).astype(BF16)


def expert_kernel(n, count, *refs):
    pieces = refs[:count]
    wg, wu, wd = refs[count : count + 3]
    gather, spread, _, keep_ref, send_ref, rows = refs[count + 3 :]
    step = pieces[0].shape[1]
    senders = min(n, 16)
    size, total = senders * PIECE, n * PIECE
    half = total // 2
    kept = senders * CAP
    for at in range(0, total, size):
        parts, first = [], 0
        for piece in pieces:
            low, high = max(at - first, 0), min(at + size - first, piece.shape[0])
            if low < high:
                parts.append(piece[low:high, :].astype(F32))
            first += piece.shape[0]
        came = dot(gather[...], jnp.concatenate(parts, axis=0).astype(BF16)).astype(BF16)
        for q in range(CUT):
            rows[:, q * step : (q + 1) * step] = came[q * kept : (q + 1) * kept]
        gate = dot(rows[...], wg[...])
        up = dot(rows[...], wu[...])
        act = (gate / (1.0 + jnp.exp(-gate)) * up).astype(BF16)
        parts = [dot(act, wd[:, q * step : (q + 1) * step]).astype(BF16) for q in range(CUT)]
        out = dot(spread[...], jnp.concatenate(parts, axis=0)).astype(BF16)
        if size > half:
            keep_ref[...] = out[:half]
            send_ref[...] = out[half:]
        elif at < half:
            keep_ref[at : at + size] = out
        else:
            send_ref[at - half : at - half + size] = out


def own_kernel(n, heads, loads, pos_ref, held, q_ref, x_ref, _, *refs):
    sources, (h_ref, done_ref) = refs[:loads], refs[loads : loads + 2]
    targets = refs[loads + 2 : 2 * loads + 2]
    bias, sems, *scratch = refs[2 * loads + 2 :]
    moves = [
        pltpu.make_async_copy(source.at[0], target, sems.at[i])
        for i, (source, target) in enumerate(zip(sources, targets))
    ]
    for move in moves:
        move.start()
    done_ref[...] = jnp.zeros((8, TILE), F32)
    pos = pos_ref[0]
    starts = doc_starts(n, pos, held)
    first = starts_of(held[pos, TILE:KV_ROWS, 0:HEAD].astype(F32)[0:1], starts)
    place = (pos * TILE + lax.broadcasted_iota(jnp.int32, (1, TILE), 1)).astype(F32)
    chains = []
    for i, (h, own) in enumerate(by_kv_head(heads)):
        queries, acc = scratch[2 * i : 2 * i + 2]
        chains.append((queries, h, acc))
        for j, a in enumerate(own):
            terms = two_terms(q_ref[:, a * HEAD : (a + 1) * HEAD].astype(F32).T)
            for t, term in enumerate(terms):
                queries[t * HEAD : (t + 1) * HEAD, j * TILE : (j + 1) * TILE] = term
    done = jnp.concatenate(flash(pos, held, chains, bias, place, first), axis=0)
    for j, a in enumerate(heads):
        h_ref[:, j * HEAD : (j + 1) * HEAD] = (
            x_ref[:, a * HEAD : (a + 1) * HEAD].astype(F32) + done[j * TILE : (j + 1) * TILE]
        )
    for move in moves:
        move.wait()


def combine_kernel(planes, widths, mix_ref, *refs):
    count = len(widths)
    halves, parts, out_ref = refs[:count], refs[count : count + planes], refs[count + planes]
    buffer, sems = refs[count + planes + 1 :]
    slots = planes * SLOTS
    came = jnp.concatenate([p[...].astype(F32) for p in parts], axis=0).astype(BF16)
    order = one_hot(travel_row(numbers((CUT * slots, 1), 0), planes, SLOTS), planes * PIECE)
    came = dot(order, came).astype(BF16)
    size = buffer.shape[1] // CUT
    moves = []
    for q in range(CUT):
        rows = came[q * slots : (q + 1) * slots]
        part = dot(mix_ref[...], jnp.concatenate([rows, rows], axis=0))
        at = 0
        for h, width in zip(halves, widths):
            low, high = max(at, q * size), min(at + width, (q + 1) * size)
            if low < high:
                buffer[:, low:high] = (
                    h[:, low - at : high - at] + part[:, low - q * size : high - q * size]
                ).astype(BF16)
            at += width
        columns = pl.ds(q * size, size)
        moves.append(
            pltpu.make_async_copy(buffer.at[:, columns], out_ref.at[:, columns], sems.at[q])
        )
        moves[-1].start()
    for move in moves:
        move.wait()


def pin(x):
    return pltpu.with_memory_space_constraint(x, pltpu.HBM)


def params(mib):
    return pltpu.CompilerParams(vmem_limit_bytes=mib * 1024 * 1024)


def local(
    resid, queries, keys, values, doc_ids, norm_gain, routes, route_weights, w_gate, w_up, w_down
):
    n = lax.axis_size("expert")
    planes = n // SHARDS
    pos = lax.axis_index("expert").astype(jnp.int32).reshape(1)
    tokens, width = queries.shape
    hidden = w_gate.shape[2]
    routes_t = routes.T
    gates_t = route_weights.T
    docs = doc_ids.reshape(1, tokens)
    small = 24 if n <= 16 else 60
    back = reach(n)

    packed = pl.pallas_call(
        pack_kernel,
        out_shape=jax.ShapeDtypeStruct((KV_ROWS, 4 * HEAD), BF16),
        in_specs=[HBM] * 3,
        out_specs=VMEM,
        scratch_shapes=[
            pltpu.VMEM((1, tokens), jnp.int32),
            pltpu.VMEM((tokens, KV_HEADS * HEAD), BF16),
            pltpu.SemaphoreType.DMA((3,)),
        ],
        compiler_params=params(8),
        name="pack",
    )(pin(docs), pin(keys), pin(values))

    def move(value, pairs):
        return lax.ppermute(value, "expert", pairs)

    def needed(k, y_from, y_to):
        gaps = [
            k * SHARDS + 2 * (y_to - y_from) + (to - of) for to in range(2) for of in range(2)
        ]
        return any(0 <= gap <= back for gap in gaps)

    far = max(k for k in range(planes) if any(needed(k, a, b) for a in (0, 1) for b in (0, 1)))
    size = min(n, 16) * PIECE
    q_rows, x_rows, facts, mix, gather, spread = pl.pallas_call(
        functools.partial(select_kernel, planes),
        out_shape=[
            jax.ShapeDtypeStruct((KV_HEADS, 2 * HEAD, planes * TILE), BF16),
            jax.ShapeDtypeStruct((planes * SLOTS, width), F32),
            jax.ShapeDtypeStruct((8, planes * TILE), F32),
            jax.ShapeDtypeStruct((tokens, 2 * planes * SLOTS), BF16),
            jax.ShapeDtypeStruct((size, size), BF16),
            jax.ShapeDtypeStruct((size, size), BF16),
        ],
        in_specs=[SMEM] + [HBM] * 5,
        out_specs=[VMEM] * 6,
        scratch_shapes=[
            pltpu.VMEM(routes_t.shape, jnp.int32),
            pltpu.VMEM(docs.shape, jnp.int32),
            pltpu.VMEM(queries.shape, BF16),
            pltpu.VMEM(resid.shape, BF16),
            pltpu.VMEM(gates_t.shape, F32),
            pltpu.SemaphoreType.DMA((5,)),
        ],
        compiler_params=params(small),
        name="select",
    )(pos, *map(pin, (routes_t, docs, queries, resid, gates_t)))

    flip_y = [(s, s ^ 2) for s in range(n)]
    flip_c = [(s, s ^ 1) for s in range(n)]
    along = [packed]
    for k in range(1, far + 1):
        used = [any(needed(k, y, to) for to in (0, 1)) for y in (0, 1)]
        pairs = [(s, (s + k * SHARDS) % n if used[s // 2 % 2] else s) for s in range(n)]
        along.append(move(packed, pairs))
    along[1], q_rows = lax.optimization_barrier((along[1], q_rows))
    shared = not needed(0, 1, 0) and not needed(far, 0, 1)
    middle = range(1, far) if shared else range(far)
    across = []
    for k in middle:
        if k == middle[1]:
            along[k:], across = lax.optimization_barrier((along[k:], across))
        across.append(move(along[k], [(s, s ^ 2 if s >= k * SHARDS else s) for s in range(n)]))
    odd = (pos[0] & 2) != 0
    final = move(jnp.where(odd, along[far], packed) if shared else along[far], flip_y)
    early, late = along + across[:-1], [across[-1]]
    sides = [(0, (k, k)) for k in range(far + 1)] + [(1, (k, k)) for k in middle[:-1]]
    late_sides = [(1, (middle[-1],) * 2), (1, (far, 0 if shared else far))]
    early.append(move(jnp.concatenate(early, axis=0), flip_c))
    early_senders = [(i, 0, 0, *side) for i, side in enumerate(sides)]
    early_senders += [(len(sides), i * KV_ROWS, 1, *side) for i, side in enumerate(sides)]
    late_senders = [(i, 0, 0, *side) for i, side in enumerate(late_sides)]
    late_senders += [(2, i * KV_ROWS, 1, *side) for i, side in enumerate(late_sides)]
    held_shape = jax.ShapeDtypeStruct((n, KV_ROWS, 4 * HEAD), BF16)
    held = pl.pallas_call(
        functools.partial(collect_kernel, n, early_senders),
        out_shape=held_shape,
        in_specs=[SMEM] + [ANY] * len(early),
        out_specs=VMEM,
        scratch_shapes=[pltpu.SemaphoreType.DMA((len(early_senders),))],
        compiler_params=params(small),
        cost_estimate=pl.CostEstimate(flops=0, bytes_accessed=1000, transcendentals=0),
        name="collect",
    )(pos, *early)

    final, held = lax.optimization_barrier((final, held))
    late.append(final)
    late.append(move(jnp.concatenate(late, axis=0), flip_c))
    *sent, held = pl.pallas_call(
        functools.partial(routed_kernel, n, late_senders),
        out_shape=[jax.ShapeDtypeStruct((PIECE, width // CUT), BF16)] * planes
        + [held_shape],
        in_specs=[SMEM, HBM] + [VMEM] * 4 + [ANY] * len(late),
        out_specs=[VMEM] * (planes + 1),
        scratch_shapes=[
            pltpu.VMEM((KV_HEADS, HEAD + EXTRA, 4 * TILE), F32),
            pltpu.VMEM((KEYS, 4 * TILE), F32),
            pltpu.VMEM((KV_HEADS, 2 * HEAD, 4 * TILE), BF16),
            pltpu.VMEM((planes * SLOTS, width), F32),
            pltpu.VMEM((1, width), F32),
            pltpu.SemaphoreType.DMA((len(late_senders) + 1,)),
        ],
        input_output_aliases={5: planes},
        compiler_params=params(small),
        name="routed",
    )(pos, pin(norm_gain.reshape(1, width)), q_rows, x_rows, facts, held, *late)

    def own(heads, after, *sources):
        lanes = [len(own) * TILE for _, own in by_kv_head(heads)]
        return pl.pallas_call(
            functools.partial(own_kernel, n, heads, len(sources)),
            out_shape=[
                jax.ShapeDtypeStruct((tokens, len(heads) * HEAD), F32),
                jax.ShapeDtypeStruct((8, TILE), F32),
            ]
            + [jax.ShapeDtypeStruct(w.shape[1:], BF16) for w in sources],
            in_specs=[SMEM, VMEM, VMEM, VMEM, ANY] + [HBM] * len(sources),
            out_specs=[VMEM] * (2 + len(sources)),
            scratch_shapes=[pltpu.VMEM((KEYS, TILE), F32), pltpu.SemaphoreType.DMA((3,))]
            + [
                shape
                for count in lanes
                for shape in (
                    pltpu.VMEM((2 * HEAD, count), BF16),
                    pltpu.VMEM((HEAD + EXTRA, count), F32),
                )
            ],
            compiler_params=params(small),
            cost_estimate=pl.CostEstimate(
                flops=2_000_000_000, bytes_accessed=8_000_000, transcendentals=2_000_000
            ),
            name="own",
        )(pos, held, queries, resid, after, *map(pin, sources))

    half0, done, *weights = own(range(10), sent[0], w_gate, w_up, w_down)
    half1, late = own(range(10, 21), done)
    halves = [half0, half1]

    come = [
        move(sent[k], [(s, (s + k * SHARDS) % n) for s in range(n)]) for k in range(1, planes)
    ]
    next_door = move(sent[0], flip_y)
    come, next_door, done = lax.optimization_barrier((come, next_door, done))
    here = [sent[0], jnp.concatenate(come, axis=0)]
    there = [next_door, move(here[1], flip_y)]
    mate = move(jnp.concatenate(here, axis=0), flip_c)
    there, mate, late = lax.optimization_barrier((there, mate, late))
    pieces = here + there + [mate, move(jnp.concatenate(there, axis=0), flip_c)]

    half = jax.ShapeDtypeStruct((n * PIECE // 2, width // CUT), BF16)
    keep, send = pl.pallas_call(
        functools.partial(expert_kernel, n, len(pieces)),
        out_shape=[half, half],
        in_specs=[VMEM] * (len(pieces) + 5) + [ANY],
        out_specs=[VMEM, VMEM],
        scratch_shapes=[pltpu.VMEM((min(n, 16) * CAP, width), BF16)],
        compiler_params=params(16),
        cost_estimate=pl.CostEstimate(
            flops=1_200_000_000, bytes_accessed=12_000_000, transcendentals=50_000
        ),
        name="expert",
    )(*pieces, *weights, gather, spread, late)

    half2, done = own(range(21, QUERY_HEADS), keep)
    halves.append(half2)

    total = keep.astype(F32) + move(send, [(s, s ^ 1) for s in range(n)]).astype(F32)
    quarter = n * PIECE // 4
    other = move(total[quarter:].astype(BF16), [(s, s ^ 2) for s in range(n)])
    other, done = lax.optimization_barrier((other, done))
    total = (total[:quarter] + other.astype(F32)).astype(BF16)
    parts = [total[:PIECE]]
    for k in range(1, planes):
        parts.append(
            move(
                total[k * PIECE : (k + 1) * PIECE], [(s, (s - k * SHARDS) % n) for s in range(n)]
            )
        )

    widths = [h.shape[1] for h in halves]
    return pl.pallas_call(
        functools.partial(combine_kernel, planes, widths),
        out_shape=jax.ShapeDtypeStruct((tokens, width), BF16),
        in_specs=[VMEM] * (1 + len(halves) + planes),
        out_specs=HBM,
        scratch_shapes=[pltpu.VMEM((tokens, width), BF16), pltpu.SemaphoreType.DMA((CUT,))],
        compiler_params=params(small),
        name="combine",
    )(mix, *halves, *parts)


def solution(mesh):
    rows = P(("groups", "expert"), None)
    in_specs = (rows,) * 4 + (P(("groups", "expert")), P(), rows, rows) + (
        P("expert", None, None),
    ) * 3
    return jax.shard_map(local, mesh=mesh, in_specs=in_specs, out_specs=rows, check_vma=False)
```

```python
import functools
import math

import jax
import jax.numpy as jnp
from jax import lax
from jax.experimental import pallas as pl
from jax.experimental.pallas import tpu as pltpu
from jax.sharding import PartitionSpec as P

HEAD = 128
QUERY_HEADS = 32
KV_HEADS = 2
GROUP = QUERY_HEADS // KV_HEADS
SHARDS = 4
CAP = 6
SLOTS = 8
CUT = 4
PIECE = CUT * CAP
TILE = 128
KEYS = 256
KV_ROWS = TILE + 16
SCALE = math.log2(math.e) / math.sqrt(HEAD)
LOW = -1e30
EXTRA = 16
F32 = jnp.float32
BF16 = jnp.bfloat16
VMEM = pl.BlockSpec(memory_space=pltpu.VMEM)
SMEM = pl.BlockSpec(memory_space=pltpu.SMEM)
ANY = pl.BlockSpec(memory_space=pl.ANY)
HBM = pl.BlockSpec(memory_space=pltpu.HBM)


def dot(a, b, ca=1, cb=0):
    return lax.dot_general(a, b, (((ca,), (cb,)), ((), ())), preferred_element_type=F32)


def reach(n):
    longest = n * TILE // 2 + 256
    return (longest - 1 + TILE - 1) // TILE


def slot_rows(routes, experts):
    members = jnp.concatenate(
        [jnp.max((routes == e).astype(F32), axis=0, keepdims=True) for e in experts], axis=0
    )
    count = len(experts)
    padded = -(-count // 8) * 8
    wide = members
    if padded > count:
        wide = jnp.concatenate([members, jnp.zeros((padded - count, TILE), F32)], axis=0)
    before = lax.broadcasted_iota(jnp.int32, (TILE, TILE), 0) < lax.broadcasted_iota(
        jnp.int32, (TILE, TILE), 1
    )
    ranks = dot(wide.astype(BF16), before.astype(F32).astype(BF16))
    return members, ranks


def one_hot(targets, count):
    shape = (targets.shape[0], count) if targets.shape[1] == 1 else (count, targets.shape[1])
    axis = 1 if targets.shape[1] == 1 else 0
    places = lax.broadcasted_iota(jnp.int32, shape, axis).astype(F32)
    return jnp.where(places == targets, 1.0, 0.0).astype(BF16)


def split(x, size):
    whole = jnp.floor((x + 0.5) / size)
    return whole, x - whole * size


def travel_row(x, senders, slots):
    chunk, rest = split(x, senders * slots)
    sender, slot = split(rest, slots)
    return jnp.where(slot < CAP, sender * PIECE + chunk * CAP + slot, -1.0)


def numbers(shape, axis):
    return lax.broadcasted_iota(jnp.int32, shape, axis).astype(F32)


def pack_kernel(docs_ref, keys_ref, values_ref, out_ref, docs, values, sems):
    moves = [
        pltpu.make_async_copy(values_ref, values, sems.at[0]),
        pltpu.make_async_copy(docs_ref, docs, sems.at[1]),
        pltpu.make_async_copy(
            keys_ref, out_ref.at[pl.ds(0, TILE), pl.ds(0, KV_HEADS * HEAD)], sems.at[2]
        ),
    ]
    for move in moves:
        move.start()
    moves[0].wait()
    for h in range(KV_HEADS):
        out_ref[0:TILE, (KV_HEADS + h) * HEAD : (KV_HEADS + h + 1) * HEAD] = (
            values[:, h * HEAD : (h + 1) * HEAD].astype(F32).T.astype(BF16)
        )
    moves[1].wait()
    out_ref[TILE:KV_ROWS, :] = jnp.zeros((KV_ROWS - TILE, 4 * HEAD), BF16)
    out_ref[TILE:KV_ROWS, 0:HEAD] = jnp.broadcast_to(
        docs[...].astype(F32), (KV_ROWS - TILE, TILE)
    ).astype(BF16)
    moves[2].wait()


def select_kernel(planes, pos_ref, *refs):
    sources, (qs_ref, xs_ref, facts_ref, mix_ref, gather_ref, spread_ref) = refs[:5], refs[5:11]
    routes_ref, docs_ref, q_ref, x_ref, gates_ref, sems = refs[11:]
    moves = [
        pltpu.make_async_copy(source, target, sems.at[i])
        for i, (source, target) in enumerate(zip(sources, refs[11:16]))
    ]
    for move in moves:
        move.start()
    for move in moves:
        move.wait()
    z = pos_ref[0] // SHARDS
    experts = [lax.rem(z + k, planes) for k in range(planes)]
    routes, gates = routes_ref[...], gates_ref[...]
    members, ranks = slot_rows(routes, experts)
    slot = lax.broadcasted_iota(jnp.int32, (SLOTS, TILE), 0).astype(F32)
    mix = []
    for k, e in enumerate(experts):
        gate = jnp.sum(jnp.where(routes == e, gates, 0.0), axis=0, keepdims=True)
        mix.append(jnp.where(ranks[k : k + 1] == slot, gate, 0.0))
    mix = jnp.concatenate(mix, axis=0).T
    mix_high = mix.astype(BF16)
    mix_ref[:, : planes * SLOTS] = mix_high
    mix_ref[:, planes * SLOTS :] = (mix - mix_high.astype(F32)).astype(BF16)
    size = gather_ref.shape[0]
    gather_ref[...] = one_hot(travel_row(numbers((size, 1), 0), size // PIECE, CAP), size)
    spread_ref[...] = one_hot(travel_row(numbers((1, size), 1), size // PIECE, CAP), size)
    docs = docs_ref[...].astype(F32)
    lane_slot = (lax.broadcasted_iota(jnp.int32, (TILE, TILE), 0) % SLOTS).astype(F32)
    token = lax.broadcasted_iota(jnp.int32, (1, TILE), 1).astype(F32)
    facts = jnp.concatenate(
        [token, docs, jnp.ones((1, TILE), F32), jnp.zeros((5, TILE), F32)], axis=0
    ).astype(BF16)
    picks = [
        jnp.where(ranks[k : k + 1] == lane_slot, members[k : k + 1], 0.0) for k in range(planes)
    ]
    chooser = jnp.concatenate([p[:SLOTS] for p in picks], axis=0).astype(BF16)
    q_rows = dot(chooser, q_ref[...])
    xs_ref[...] = dot(chooser, x_ref[...])
    for k in range(planes):
        known = dot(facts, picks[k].astype(BF16), 1, 1)
        facts_ref[:, k * TILE : (k + 1) * TILE] = jnp.concatenate(
            [known[0:1], known[1:2] + (1.0 - known[2:3]) * docs[:, 0:1], known[2:]], axis=0
        )
        for h in range(KV_HEADS):
            stack = jnp.concatenate(
                [
                    q_rows[k * SLOTS : (k + 1) * SLOTS, a * HEAD : (a + 1) * HEAD]
                    for a in range(h * GROUP, (h + 1) * GROUP)
                ],
                axis=0,
            )
            for i, term in enumerate(two_terms(stack.T)):
                qs_ref[h, i * HEAD : (i + 1) * HEAD, k * TILE : (k + 1) * TILE] = term


def doc_starts(n, pos, held):
    sums = [jnp.zeros((1, TILE), F32) for _ in range(3)]
    for s in range(n):
        docs = held[s, TILE:KV_ROWS, 0:HEAD].astype(F32)[0:1]
        ahead = (pos - s < 0).astype(F32)
        behind = (pos - s > reach(n)).astype(F32)
        known = 1.0 - ahead - behind
        docs = jnp.where(known > 0.5, docs, 0.0) + 9.0 * ahead
        for d in range(3):
            sums[d] = sums[d] + jnp.where(docs < d + 1.0, 1.0, 0.0)
    return [jnp.sum(s, axis=1, keepdims=True) for s in sums]


def starts_of(docs, starts):
    first = jnp.zeros_like(docs)
    for d in range(3):
        first = jnp.where(docs == d + 1.0, starts[d], first)
    return first


def two_terms(x):
    scaled = x.astype(F32) * SCALE
    high = scaled.astype(BF16)
    return high, (scaled - high.astype(F32)).astype(BF16)


def key_steps(pos, place, first, bias_ref, step, state):
    low = jnp.min(first).astype(jnp.int32) // KEYS
    last = pos // (KEYS // TILE)
    clear = jnp.minimum((jnp.max(first).astype(jnp.int32) + KEYS - 1) // KEYS, last)

    def edge(j, carried):
        kb = jnp.where(j < clear - low, low + j, last)
        key_at = (kb * KEYS + lax.broadcasted_iota(jnp.int32, (KEYS, 1), 0)).astype(F32)
        bias_ref[...] = jnp.where((key_at >= first) & (key_at <= place), 0.0, LOW)
        return step(kb, carried, True)

    state = lax.fori_loop(0, clear - low + 1, edge, state)
    return lax.fori_loop(clear, last, lambda kb, carried: step(kb, carried, False), state)


def by_kv_head(heads):
    groups = [(h, [a for a in heads if a // GROUP == h]) for h in range(KV_HEADS)]
    return [(h, own) for h, own in groups if own]


def keys_of(held, kb, h):
    keys = jnp.concatenate(
        [held[2 * kb + t, 0:TILE, h * HEAD : (h + 1) * HEAD] for t in range(2)], axis=0
    )
    return jnp.concatenate([keys, keys], axis=1)


def values_of(held, kb, h):
    at = (KV_HEADS + h) * HEAD
    values = jnp.concatenate(
        [held[2 * kb + t, 0:TILE, at : at + HEAD] for t in range(2)], axis=1
    )
    return jnp.concatenate([values, jnp.ones((EXTRA, KEYS), BF16)], axis=0)


def flash(pos, held, chains, bias_ref, place, first):
    for _, _, acc in chains:
        acc[...] = jnp.zeros(acc.shape, F32)

    def step(kb, tops, masked):
        out = []
        for (queries, h, acc), old in zip(chains, tops):
            scores = dot(keys_of(held, kb, h), queries[...])
            if masked:
                copies = scores.shape[1] // bias_ref.shape[1]
                scores = scores + jnp.concatenate([bias_ref[...]] * copies, axis=1)
            top = jnp.maximum(old, jnp.max(scores, axis=0, keepdims=True))
            weights = jnp.exp2(scores - top).astype(BF16)
            acc[...] = acc[...] * jnp.exp2(old - top) + dot(values_of(held, kb, h), weights)
            out.append(top)
        return tuple(out)

    tops = tuple(jnp.full((1, acc.shape[1]), LOW, F32) for _, _, acc in chains)
    key_steps(pos, place, first, bias_ref, step, tops)
    return [(acc[0:HEAD, :] / acc[HEAD : HEAD + 1, :]).T for _, _, acc in chains]


def place_pieces(n, senders, pos, pieces, held, sems):
    planes = n // SHARDS
    z, y, c = pos // SHARDS, (pos // 2) % 2, pos % 2
    copies = []
    for i, (piece, row, flip_c, flip_y, k) in enumerate(senders):
        sender = lax.rem(z - k + planes, planes) * SHARDS + (y ^ flip_y) * 2 + (c ^ flip_c)
        copy = pltpu.make_async_copy(
            pieces[piece].at[pl.ds(row, KV_ROWS)], held.at[sender], sems.at[i]
        )
        copy.start()
        copies.append(copy)
    return copies


def collect_kernel(n, senders, pos_ref, *refs):
    *pieces, held, sems = refs
    for copy in place_pieces(n, senders, pos_ref[0], pieces, held, sems):
        copy.wait()


def routed_kernel(n, senders, pos_ref, gain_ref, qs_ref, xs_ref, facts_ref, _, *refs):
    planes = n // SHARDS
    count = len(senders)
    pieces, outs, held = refs[:2], refs[2 : 2 + planes], refs[2 + planes]
    acc, bias, q_scr, state, gain, sems = refs[3 + planes :]
    pos = pos_ref[0]
    copies = place_pieces(n, senders, pos, pieces, held, sems)
    copies.append(pltpu.make_async_copy(gain_ref, gain, sems.at[count]))
    copies[-1].start()
    for copy in copies:
        copy.wait()
    starts = doc_starts(n, pos, held)
    lanes = q_scr.shape[2]
    base = (pos * TILE).astype(F32)
    for part in range(planes * TILE // lanes):
        at = slice(part * lanes, (part + 1) * lanes)
        q_scr[...] = qs_ref[:, :, at]
        done = flash(
            pos,
            held,
            [(q_scr.at[h], h, acc.at[h]) for h in range(KV_HEADS)],
            bias,
            facts_ref[0:1, at] + base,
            starts_of(facts_ref[1:2, at], starts),
        )
        for h in range(KV_HEADS):
            for k in range(lanes // TILE):
                row = (part * (lanes // TILE) + k) * SLOTS
                for g in range(GROUP):
                    lane = (h * GROUP + g) * HEAD
                    state[row : row + SLOTS, lane : lane + HEAD] = (
                        xs_ref[row : row + SLOTS, lane : lane + HEAD]
                        + done[h][k * TILE + g * SLOTS : k * TILE + (g + 1) * SLOTS]
                    )
    width = state.shape[1] // CUT
    order = one_hot(travel_row(numbers((1, CUT * SLOTS), 1), 1, SLOTS), PIECE)
    for k in range(planes):
        hidden = state[k * SLOTS : (k + 1) * SLOTS, :]
        mean = jnp.mean(hidden * hidden, axis=1, keepdims=True)
        normed = hidden * lax.rsqrt(mean + 1e-06) * gain[...]
        chunks = [normed[:, q * width : (q + 1) * width] for q in range(CUT)]
        outs[k][...] = dot(order, jnp.concatenate(chunks, axis=0).astype(BF16)).astype(BF16)


def expert_kernel(n, count, *refs):
    pieces = refs[:count]
    wg, wu, wd = refs[count : count + 3]
    gather, spread, _, keep_ref, send_ref, rows = refs[count + 3 :]
    step = pieces[0].shape[1]
    senders = min(n, 16)
    size, total = senders * PIECE, n * PIECE
    half = total // 2
    kept = senders * CAP
    for at in range(0, total, size):
        parts, first = [], 0
        for piece in pieces:
            low, high = max(at - first, 0), min(at + size - first, piece.shape[0])
            if low < high:
                parts.append(piece[low:high, :].astype(F32))
            first += piece.shape[0]
        came = dot(gather[...], jnp.concatenate(parts, axis=0).astype(BF16)).astype(BF16)
        for q in range(CUT):
            rows[:, q * step : (q + 1) * step] = came[q * kept : (q + 1) * kept]
        gate = dot(rows[...], wg[...])
        up = dot(rows[...], wu[...])
        act = (gate / (1.0 + jnp.exp(-gate)) * up).astype(BF16)
        parts = [dot(act, wd[:, q * step : (q + 1) * step]).astype(BF16) for q in range(CUT)]
        out = dot(spread[...], jnp.concatenate(parts, axis=0)).astype(BF16)
        if size > half:
            keep_ref[...] = out[:half]
            send_ref[...] = out[half:]
        elif at < half:
            keep_ref[at : at + size] = out
        else:
            send_ref[at - half : at - half + size] = out


def own_kernel(n, heads, loads, pos_ref, held, q_ref, x_ref, _, *refs):
    sources, (h_ref, done_ref) = refs[:loads], refs[loads : loads + 2]
    targets = refs[loads + 2 : 2 * loads + 2]
    bias, sems, *scratch = refs[2 * loads + 2 :]
    moves = [
        pltpu.make_async_copy(source.at[0], target, sems.at[i])
        for i, (source, target) in enumerate(zip(sources, targets))
    ]
    for move in moves:
        move.start()
    done_ref[...] = jnp.zeros((8, TILE), F32)
    pos = pos_ref[0]
    starts = doc_starts(n, pos, held)
    first = starts_of(held[pos, TILE:KV_ROWS, 0:HEAD].astype(F32)[0:1], starts)
    place = (pos * TILE + lax.broadcasted_iota(jnp.int32, (1, TILE), 1)).astype(F32)
    chains = []
    for i, (h, own) in enumerate(by_kv_head(heads)):
        queries, acc = scratch[2 * i : 2 * i + 2]
        chains.append((queries, h, acc))
        for j, a in enumerate(own):
            terms = two_terms(q_ref[:, a * HEAD : (a + 1) * HEAD].astype(F32).T)
            for t, term in enumerate(terms):
                queries[t * HEAD : (t + 1) * HEAD, j * TILE : (j + 1) * TILE] = term
    done = jnp.concatenate(flash(pos, held, chains, bias, place, first), axis=0)
    for j, a in enumerate(heads):
        h_ref[:, j * HEAD : (j + 1) * HEAD] = (
            x_ref[:, a * HEAD : (a + 1) * HEAD].astype(F32) + done[j * TILE : (j + 1) * TILE]
        )
    for move in moves:
        move.wait()


def combine_kernel(planes, widths, mix_ref, *refs):
    count = len(widths)
    halves, parts = refs[:count], refs[count : count + planes]
    _, out_ref, buffer, sems = refs[count + planes :]
    slots = planes * SLOTS
    came = jnp.concatenate([p[...].astype(F32) for p in parts], axis=0).astype(BF16)
    order = one_hot(travel_row(numbers((CUT * slots, 1), 0), planes, SLOTS), planes * PIECE)
    came = dot(order, came).astype(BF16)
    size = buffer.shape[1] // CUT
    moves = []
    for q in range(CUT):
        rows = came[q * slots : (q + 1) * slots]
        part = dot(mix_ref[...], jnp.concatenate([rows, rows], axis=0))
        at = 0
        for h, width in zip(halves, widths):
            low, high = max(at, q * size), min(at + width, (q + 1) * size)
            if low < high:
                buffer[:, low:high] = (
                    h[:, low - at : high - at] + part[:, low - q * size : high - q * size]
                ).astype(BF16)
            at += width
        columns = pl.ds(q * size, size)
        moves.append(
            pltpu.make_async_copy(buffer.at[:, columns], out_ref.at[:, columns], sems.at[q])
        )
        moves[-1].start()
    for move in moves:
        move.wait()


def pin(x):
    return pltpu.with_memory_space_constraint(x, pltpu.HBM)


def params(mib):
    return pltpu.CompilerParams(vmem_limit_bytes=mib * 1024 * 1024)


def local(
    resid, queries, keys, values, doc_ids, norm_gain, routes, route_weights, w_gate, w_up, w_down
):
    n = lax.axis_size("expert")
    planes = n // SHARDS
    pos = lax.axis_index("expert").astype(jnp.int32).reshape(1)
    tokens, width = queries.shape
    hidden = w_gate.shape[2]
    routes_t = routes.T
    gates_t = route_weights.T
    docs = doc_ids.reshape(1, tokens)
    small = 24 if n <= 16 else 60
    back = reach(n)

    packed = pl.pallas_call(
        pack_kernel,
        out_shape=jax.ShapeDtypeStruct((KV_ROWS, 4 * HEAD), BF16),
        in_specs=[HBM] * 3,
        out_specs=VMEM,
        scratch_shapes=[
            pltpu.VMEM((1, tokens), jnp.int32),
            pltpu.VMEM((tokens, KV_HEADS * HEAD), BF16),
            pltpu.SemaphoreType.DMA((3,)),
        ],
        compiler_params=params(8),
        name="pack",
    )(pin(docs), pin(keys), pin(values))

    def move(value, pairs):
        return lax.ppermute(value, "expert", pairs)

    def needed(k, y_from, y_to):
        gaps = [
            k * SHARDS + 2 * (y_to - y_from) + (to - of) for to in range(2) for of in range(2)
        ]
        return any(0 <= gap <= back for gap in gaps)

    far = max(k for k in range(planes) if any(needed(k, a, b) for a in (0, 1) for b in (0, 1)))
    size = min(n, 16) * PIECE
    q_rows, x_rows, facts, mix, gather, spread = pl.pallas_call(
        functools.partial(select_kernel, planes),
        out_shape=[
            jax.ShapeDtypeStruct((KV_HEADS, 2 * HEAD, planes * TILE), BF16),
            jax.ShapeDtypeStruct((planes * SLOTS, width), F32),
            jax.ShapeDtypeStruct((8, planes * TILE), F32),
            jax.ShapeDtypeStruct((tokens, 2 * planes * SLOTS), BF16),
            jax.ShapeDtypeStruct((size, size), BF16),
            jax.ShapeDtypeStruct((size, size), BF16),
        ],
        in_specs=[SMEM] + [HBM] * 5,
        out_specs=[VMEM] * 6,
        scratch_shapes=[
            pltpu.VMEM(routes_t.shape, jnp.int32),
            pltpu.VMEM(docs.shape, jnp.int32),
            pltpu.VMEM(queries.shape, BF16),
            pltpu.VMEM(resid.shape, BF16),
            pltpu.VMEM(gates_t.shape, F32),
            pltpu.SemaphoreType.DMA((5,)),
        ],
        compiler_params=params(small),
        name="select",
    )(pos, *map(pin, (routes_t, docs, queries, resid, gates_t)))

    flip_y = [(s, s ^ 2) for s in range(n)]
    flip_c = [(s, s ^ 1) for s in range(n)]
    jump = {s: s + far * SHARDS - 2 for s in range(n - far * SHARDS) if s & 2}
    jump.update({to: s for s, to in jump.items()})
    jumped = move(packed, [(s, jump.get(s, s)) for s in range(n)])
    along = [packed] + [
        move(packed, [(s, (s + k * SHARDS) % n) for s in range(n)]) for k in range(1, far)
    ]
    along[1], q_rows = lax.optimization_barrier((along[1], q_rows))
    across = []
    for k in range(far):
        if k > 1 and k == far - 1:
            along[k], across = lax.optimization_barrier((along[k], across))
        across.append(move(along[k], [(s, s ^ 2 if s >= k * SHARDS else s) for s in range(n)]))
    early, late = along + [jumped] + across[:-1], across[-1:]
    sides = [(0, k) for k in range(far)] + [(1, far)] + [(1, k) for k in range(far - 1)]
    early.append(move(jnp.concatenate(early, axis=0), flip_c))
    late.append(move(across[-1], flip_c))
    early_senders = [(i, 0, 0, *side) for i, side in enumerate(sides)]
    early_senders += [(len(sides), i * KV_ROWS, 1, *side) for i, side in enumerate(sides)]
    late_senders = [(flip, 0, flip, 1, far - 1) for flip in (0, 1)]
    held_shape = jax.ShapeDtypeStruct((n, KV_ROWS, 4 * HEAD), BF16)
    held = pl.pallas_call(
        functools.partial(collect_kernel, n, early_senders),
        out_shape=held_shape,
        in_specs=[SMEM] + [ANY] * len(early),
        out_specs=VMEM,
        scratch_shapes=[pltpu.SemaphoreType.DMA((len(early_senders),))],
        compiler_params=params(small),
        cost_estimate=pl.CostEstimate(flops=0, bytes_accessed=1000, transcendentals=0),
        name="collect",
    )(pos, *early)

    *sent, held = pl.pallas_call(
        functools.partial(routed_kernel, n, late_senders),
        out_shape=[jax.ShapeDtypeStruct((PIECE, width // CUT), BF16)] * planes
        + [held_shape],
        in_specs=[SMEM, HBM] + [VMEM] * 4 + [ANY] * len(late),
        out_specs=[VMEM] * (planes + 1),
        scratch_shapes=[
            pltpu.VMEM((KV_HEADS, HEAD + EXTRA, 4 * TILE), F32),
            pltpu.VMEM((KEYS, 4 * TILE), F32),
            pltpu.VMEM((KV_HEADS, 2 * HEAD, 4 * TILE), BF16),
            pltpu.VMEM((planes * SLOTS, width), F32),
            pltpu.VMEM((1, width), F32),
            pltpu.SemaphoreType.DMA((len(late_senders) + 1,)),
        ],
        input_output_aliases={5: planes},
        compiler_params=params(small),
        name="routed",
    )(pos, pin(norm_gain.reshape(1, width)), q_rows, x_rows, facts, held, *late)

    def own(heads, after, *sources):
        lanes = [len(own) * TILE for _, own in by_kv_head(heads)]
        return pl.pallas_call(
            functools.partial(own_kernel, n, heads, len(sources)),
            out_shape=[
                jax.ShapeDtypeStruct((tokens, len(heads) * HEAD), F32),
                jax.ShapeDtypeStruct((8, TILE), F32),
            ]
            + [jax.ShapeDtypeStruct(w.shape[1:], BF16) for w in sources],
            in_specs=[SMEM, VMEM, VMEM, VMEM, ANY] + [HBM] * len(sources),
            out_specs=[VMEM] * (2 + len(sources)),
            scratch_shapes=[pltpu.VMEM((KEYS, TILE), F32), pltpu.SemaphoreType.DMA((3,))]
            + [
                shape
                for count in lanes
                for shape in (
                    pltpu.VMEM((2 * HEAD, count), BF16),
                    pltpu.VMEM((HEAD + EXTRA, count), F32),
                )
            ],
            compiler_params=params(small),
            cost_estimate=pl.CostEstimate(
                flops=2_000_000_000, bytes_accessed=8_000_000, transcendentals=2_000_000
            ),
            name="own",
        )(pos, held, queries, resid, after, *map(pin, sources))

    half0, done, *weights = own(range(10), sent[0], w_gate, w_up, w_down)
    half1, late = own(range(10, 21), done)
    halves = [half0, half1]

    come = [
        move(sent[k], [(s, (s + k * SHARDS) % n) for s in range(n)]) for k in range(1, planes)
    ]
    next_door = move(sent[0], flip_y)
    come, next_door, done = lax.optimization_barrier((come, next_door, done))
    here = [sent[0], jnp.concatenate(come, axis=0)]
    there = [next_door, move(here[1], flip_y)]
    mate = move(jnp.concatenate(here, axis=0), flip_c)
    there, mate, late = lax.optimization_barrier((there, mate, late))
    pieces = here + there + [mate, move(jnp.concatenate(there, axis=0), flip_c)]

    half = jax.ShapeDtypeStruct((n * PIECE // 2, width // CUT), BF16)
    keep, send = pl.pallas_call(
        functools.partial(expert_kernel, n, len(pieces)),
        out_shape=[half, half],
        in_specs=[VMEM] * (len(pieces) + 5) + [ANY],
        out_specs=[VMEM, VMEM],
        scratch_shapes=[pltpu.VMEM((min(n, 16) * CAP, width), BF16)],
        compiler_params=params(16),
        cost_estimate=pl.CostEstimate(
            flops=1_200_000_000, bytes_accessed=12_000_000, transcendentals=50_000
        ),
        name="expert",
    )(*pieces, *weights, gather, spread, late)

    half2, done = own(range(21, QUERY_HEADS), keep)
    halves.append(half2)

    total = keep.astype(F32) + move(send, [(s, s ^ 1) for s in range(n)]).astype(F32)
    quarter = n * PIECE // 4
    other = move(total[quarter:].astype(BF16), [(s, s ^ 2) for s in range(n)])
    other, done = lax.optimization_barrier((other, done))
    total = (total[:quarter] + other.astype(F32)).astype(BF16)
    parts = [total[:PIECE]]
    for k in range(1, planes):
        parts.append(
            move(
                total[k * PIECE : (k + 1) * PIECE], [(s, (s - k * SHARDS) % n) for s in range(n)]
            )
        )

    widths = [h.shape[1] for h in halves]
    return pl.pallas_call(
        functools.partial(combine_kernel, planes, widths),
        out_shape=jax.ShapeDtypeStruct((tokens, width), BF16),
        in_specs=[VMEM] * (1 + len(halves) + planes) + [ANY],
        out_specs=HBM,
        scratch_shapes=[pltpu.VMEM((tokens, width), BF16), pltpu.SemaphoreType.DMA((CUT,))],
        compiler_params=params(small),
        name="combine",
    )(mix, *halves, *parts, done)


def solution(mesh):
    rows = P(("groups", "expert"), None)
    in_specs = (rows,) * 4 + (P(("groups", "expert")), P(), rows, rows) + (
        P("expert", None, None),
    ) * 3
    return jax.shard_map(local, mesh=mesh, in_specs=in_specs, out_specs=rows, check_vma=False)
```

```python
import functools
import math

import jax
import jax.numpy as jnp
from jax import lax
from jax.experimental import pallas as pl
from jax.experimental.pallas import tpu as pltpu
from jax.sharding import PartitionSpec as P

HEAD = 128
QUERY_HEADS = 32
KV_HEADS = 2
GROUP = QUERY_HEADS // KV_HEADS
SHARDS = 4
CAP = 6
SLOTS = 8
CUT = 4
PIECE = CUT * CAP
TILE = 128
KEYS = 256
KV_ROWS = TILE + 16
SCALE = math.log2(math.e) / math.sqrt(HEAD)
LOW = -1e30
EXTRA = 16
F32 = jnp.float32
BF16 = jnp.bfloat16
VMEM = pl.BlockSpec(memory_space=pltpu.VMEM)
SMEM = pl.BlockSpec(memory_space=pltpu.SMEM)
ANY = pl.BlockSpec(memory_space=pl.ANY)
HBM = pl.BlockSpec(memory_space=pltpu.HBM)


def dot(a, b, ca=1, cb=0):
    return lax.dot_general(a, b, (((ca,), (cb,)), ((), ())), preferred_element_type=F32)


def reach(n):
    longest = n * TILE // 2 + 256
    return (longest - 1 + TILE - 1) // TILE


def slot_rows(routes, experts):
    members = jnp.concatenate(
        [jnp.max((routes == e).astype(F32), axis=0, keepdims=True) for e in experts], axis=0
    )
    count = len(experts)
    padded = -(-count // 8) * 8
    wide = members
    if padded > count:
        wide = jnp.concatenate([members, jnp.zeros((padded - count, TILE), F32)], axis=0)
    before = lax.broadcasted_iota(jnp.int32, (TILE, TILE), 0) < lax.broadcasted_iota(
        jnp.int32, (TILE, TILE), 1
    )
    ranks = dot(wide.astype(BF16), before.astype(F32).astype(BF16))
    return members, ranks


def one_hot(targets, count):
    shape = (targets.shape[0], count) if targets.shape[1] == 1 else (count, targets.shape[1])
    axis = 1 if targets.shape[1] == 1 else 0
    places = lax.broadcasted_iota(jnp.int32, shape, axis).astype(F32)
    return jnp.where(places == targets, 1.0, 0.0).astype(BF16)


def split(x, size):
    whole = jnp.floor((x + 0.5) / size)
    return whole, x - whole * size


def travel_row(x, senders, slots):
    chunk, rest = split(x, senders * slots)
    sender, slot = split(rest, slots)
    return jnp.where(slot < CAP, sender * PIECE + chunk * CAP + slot, -1.0)


def numbers(shape, axis):
    return lax.broadcasted_iota(jnp.int32, shape, axis).astype(F32)


def pack_kernel(docs_ref, keys_ref, values_ref, out_ref, docs, values, sems):
    moves = [
        pltpu.make_async_copy(values_ref, values, sems.at[0]),
        pltpu.make_async_copy(docs_ref, docs, sems.at[1]),
        pltpu.make_async_copy(
            keys_ref, out_ref.at[pl.ds(0, TILE), pl.ds(0, KV_HEADS * HEAD)], sems.at[2]
        ),
    ]
    for move in moves:
        move.start()
    moves[0].wait()
    for h in range(KV_HEADS):
        out_ref[0:TILE, (KV_HEADS + h) * HEAD : (KV_HEADS + h + 1) * HEAD] = (
            values[:, h * HEAD : (h + 1) * HEAD].astype(F32).T.astype(BF16)
        )
    moves[1].wait()
    out_ref[TILE:KV_ROWS, :] = jnp.zeros((KV_ROWS - TILE, 4 * HEAD), BF16)
    out_ref[TILE:KV_ROWS, 0:HEAD] = jnp.broadcast_to(
        docs[...].astype(F32), (KV_ROWS - TILE, TILE)
    ).astype(BF16)
    moves[2].wait()


def select_kernel(planes, pos_ref, *refs):
    sources, (qs_ref, xs_ref, facts_ref, mix_ref, gather_ref, spread_ref) = refs[:5], refs[5:11]
    routes_ref, docs_ref, q_ref, x_ref, gates_ref, stack, sems = refs[11:]
    moves = [
        pltpu.make_async_copy(source, target, sems.at[i])
        for i, (source, target) in enumerate(zip(sources, refs[11:16]))
    ]
    for move in moves:
        move.start()
    for move in moves:
        move.wait()
    z = pos_ref[0] // SHARDS
    experts = [lax.rem(z + k, planes) for k in range(planes)]
    routes, gates = routes_ref[...], gates_ref[...]
    members, ranks = slot_rows(routes, experts)
    slot = lax.broadcasted_iota(jnp.int32, (SLOTS, TILE), 0).astype(F32)
    mix = []
    for k, e in enumerate(experts):
        gate = jnp.sum(jnp.where(routes == e, gates, 0.0), axis=0, keepdims=True)
        mix.append(jnp.where(ranks[k : k + 1] == slot, gate, 0.0))
    mix = jnp.concatenate(mix, axis=0).T
    mix_high = mix.astype(BF16)
    mix_ref[:, : planes * SLOTS] = mix_high
    mix_ref[:, planes * SLOTS :] = (mix - mix_high.astype(F32)).astype(BF16)
    size = gather_ref.shape[0]
    gather_ref[...] = one_hot(travel_row(numbers((size, 1), 0), size // PIECE, CAP), size)
    spread_ref[...] = one_hot(travel_row(numbers((1, size), 1), size // PIECE, CAP), size)
    docs = docs_ref[...].astype(F32)
    token = lax.broadcasted_iota(jnp.int32, (1, TILE), 1).astype(F32)
    facts = jnp.concatenate(
        [token, docs, jnp.ones((1, TILE), F32), jnp.zeros((5, TILE), F32)], axis=0
    ).astype(BF16)
    picks = [
        jnp.where(ranks[k : k + 1] == slot, members[k : k + 1], 0.0) for k in range(planes)
    ]
    rows = planes * CAP
    plane, place = split(numbers((rows, 1), 0), CAP)
    compact = one_hot(plane * SLOTS + place, planes * SLOTS)
    chooser = dot(compact, jnp.concatenate(picks, axis=0).astype(BF16)).astype(BF16)
    lane, _ = split(numbers((rows * GROUP, 1), 0), GROUP)
    lane_pick = dot(one_hot(lane, rows), chooser).astype(BF16)
    known = dot(facts, lane_pick, 1, 1)
    facts_ref[...] = jnp.concatenate(
        [known[0:1], known[1:2] + (1.0 - known[2:3]) * docs[:, 0:1], known[2:]], axis=0
    )
    q_rows = dot(chooser, q_ref[...])
    xs_ref[...] = dot(chooser, x_ref[...])
    for h in range(KV_HEADS):
        for g in range(GROUP):
            a = h * GROUP + g
            stack[pl.ds(g, rows, stride=GROUP), :] = q_rows[:, a * HEAD : (a + 1) * HEAD]
        for i, term in enumerate(two_terms(stack[...].T)):
            qs_ref[h, i * HEAD : (i + 1) * HEAD, :] = term


def doc_starts(n, pos, held):
    sums = [jnp.zeros((1, TILE), F32) for _ in range(3)]
    for s in range(n):
        docs = held[s, TILE:KV_ROWS, 0:HEAD].astype(F32)[0:1]
        ahead = (pos - s < 0).astype(F32)
        behind = (pos - s > reach(n)).astype(F32)
        known = 1.0 - ahead - behind
        docs = jnp.where(known > 0.5, docs, 0.0) + 9.0 * ahead
        for d in range(3):
            sums[d] = sums[d] + jnp.where(docs < d + 1.0, 1.0, 0.0)
    return [jnp.sum(s, axis=1, keepdims=True) for s in sums]


def starts_of(docs, starts):
    first = jnp.zeros_like(docs)
    for d in range(3):
        first = jnp.where(docs == d + 1.0, starts[d], first)
    return first


def two_terms(x):
    scaled = x.astype(F32) * SCALE
    high = scaled.astype(BF16)
    return high, (scaled - high.astype(F32)).astype(BF16)


def key_steps(pos, place, first, bias_ref, step, state):
    low = jnp.min(first).astype(jnp.int32) // KEYS
    last = pos // (KEYS // TILE)
    clear = jnp.minimum((jnp.max(first).astype(jnp.int32) + KEYS - 1) // KEYS, last)

    def edge(j, carried):
        kb = jnp.where(j < clear - low, low + j, last)
        key_at = (kb * KEYS + lax.broadcasted_iota(jnp.int32, (KEYS, 1), 0)).astype(F32)
        bias_ref[...] = jnp.where((key_at >= first) & (key_at <= place), 0.0, LOW)
        return step(kb, carried, True)

    state = lax.fori_loop(0, clear - low + 1, edge, state)
    return lax.fori_loop(clear, last, lambda kb, carried: step(kb, carried, False), state)


def by_kv_head(heads):
    groups = [(h, [a for a in heads if a // GROUP == h]) for h in range(KV_HEADS)]
    return [(h, own) for h, own in groups if own]


def keys_of(held, kb, h):
    keys = jnp.concatenate(
        [held[2 * kb + t, 0:TILE, h * HEAD : (h + 1) * HEAD] for t in range(2)], axis=0
    )
    return jnp.concatenate([keys, keys], axis=1)


def values_of(held, kb, h):
    at = (KV_HEADS + h) * HEAD
    values = jnp.concatenate(
        [held[2 * kb + t, 0:TILE, at : at + HEAD] for t in range(2)], axis=1
    )
    return jnp.concatenate([values, jnp.ones((EXTRA, KEYS), BF16)], axis=0)


def flash(pos, held, chains, bias_ref, place, first):
    for _, _, acc in chains:
        acc[...] = jnp.zeros(acc.shape, F32)

    def step(kb, tops, masked):
        out = []
        for (queries, h, acc), old in zip(chains, tops):
            scores = dot(keys_of(held, kb, h), queries[...])
            if masked:
                copies = scores.shape[1] // bias_ref.shape[1]
                scores = scores + jnp.concatenate([bias_ref[...]] * copies, axis=1)
            top = jnp.maximum(old, jnp.max(scores, axis=0, keepdims=True))
            weights = jnp.exp2(scores - top).astype(BF16)
            acc[...] = acc[...] * jnp.exp2(old - top) + dot(values_of(held, kb, h), weights)
            out.append(top)
        return tuple(out)

    tops = tuple(jnp.full((1, acc.shape[1]), LOW, F32) for _, _, acc in chains)
    key_steps(pos, place, first, bias_ref, step, tops)
    return [(acc[0:HEAD, :] / acc[HEAD : HEAD + 1, :]).T for _, _, acc in chains]


def place_pieces(n, senders, pos, pieces, held, sems):
    planes = n // SHARDS
    z, y, c = pos // SHARDS, (pos // 2) % 2, pos % 2
    copies = []
    for i, (piece, row, flip_c, flip_y, k) in enumerate(senders):
        sender = lax.rem(z - k + planes, planes) * SHARDS + (y ^ flip_y) * 2 + (c ^ flip_c)
        copy = pltpu.make_async_copy(
            pieces[piece].at[pl.ds(row, KV_ROWS)], held.at[sender], sems.at[i]
        )
        copy.start()
        copies.append(copy)
    return copies


def collect_kernel(n, senders, pos_ref, *refs):
    *pieces, held, sems = refs
    for copy in place_pieces(n, senders, pos_ref[0], pieces, held, sems):
        copy.wait()


def routed_kernel(n, senders, pos_ref, gain_ref, qs_ref, xs_ref, facts_ref, _, *refs):
    planes = n // SHARDS
    count = len(senders)
    pieces, outs, held = refs[:2], refs[2 : 2 + planes], refs[2 + planes]
    acc, bias, q_scr, stack, state, gain, sems = refs[3 + planes :]
    pos = pos_ref[0]
    copies = place_pieces(n, senders, pos, pieces, held, sems)
    copies.append(pltpu.make_async_copy(gain_ref, gain, sems.at[count]))
    copies[-1].start()
    for copy in copies:
        copy.wait()
    starts = doc_starts(n, pos, held)
    lanes = q_scr.shape[2]
    rows = lanes // GROUP
    base = (pos * TILE).astype(F32)
    width = state.shape[1] // CUT
    row = numbers((CUT * rows, 1), 0)
    plane, rest = split(row, PIECE)
    chunk, slot = split(rest, CAP)
    order = one_hot(chunk * rows + plane * CAP + slot, CUT * rows)
    for part in range(xs_ref.shape[0] // rows):
        at = slice(part * lanes, (part + 1) * lanes)
        q_scr[...] = qs_ref[:, :, at]
        done = flash(
            pos,
            held,
            [(q_scr.at[h], h, acc.at[h]) for h in range(KV_HEADS)],
            bias,
            facts_ref[0:1, at] + base,
            starts_of(facts_ref[1:2, at], starts),
        )
        for h in range(KV_HEADS):
            stack[...] = done[h]
            for g in range(GROUP):
                lane = (h * GROUP + g) * HEAD
                state[:, lane : lane + HEAD] = (
                    xs_ref[part * rows : (part + 1) * rows, lane : lane + HEAD]
                    + stack[pl.ds(g, rows, stride=GROUP), :]
                )
        hidden = state[...]
        mean = jnp.mean(hidden * hidden, axis=1, keepdims=True)
        normed = hidden * lax.rsqrt(mean + 1e-06) * gain[...]
        chunks = [normed[:, q * width : (q + 1) * width] for q in range(CUT)]
        sent = dot(order, jnp.concatenate(chunks, axis=0).astype(BF16))
        for k in range(rows // CAP):
            outs[part * (rows // CAP) + k][...] = sent[k * PIECE : (k + 1) * PIECE].astype(BF16)


def expert_kernel(n, count, *refs):
    pieces = refs[:count]
    wg, wu, wd = refs[count : count + 3]
    gather, spread, _, keep_ref, send_ref, rows = refs[count + 3 :]
    step = pieces[0].shape[1]
    senders = min(n, 16)
    size, total = senders * PIECE, n * PIECE
    half = total // 2
    kept = senders * CAP
    for at in range(0, total, size):
        parts, first = [], 0
        for piece in pieces:
            low, high = max(at - first, 0), min(at + size - first, piece.shape[0])
            if low < high:
                parts.append(piece[low:high, :].astype(F32))
            first += piece.shape[0]
        came = dot(gather[...], jnp.concatenate(parts, axis=0).astype(BF16)).astype(BF16)
        for q in range(CUT):
            rows[:, q * step : (q + 1) * step] = came[q * kept : (q + 1) * kept]
        gate = dot(rows[...], wg[...])
        up = dot(rows[...], wu[...])
        act = (gate / (1.0 + jnp.exp(-gate)) * up).astype(BF16)
        parts = [dot(act, wd[:, q * step : (q + 1) * step]).astype(BF16) for q in range(CUT)]
        out = dot(spread[...], jnp.concatenate(parts, axis=0)).astype(BF16)
        if size > half:
            keep_ref[...] = out[:half]
            send_ref[...] = out[half:]
        elif at < half:
            keep_ref[at : at + size] = out
        else:
            send_ref[at - half : at - half + size] = out


def own_kernel(n, heads, loads, pos_ref, held, q_ref, x_ref, _, *refs):
    sources, (h_ref, done_ref) = refs[:loads], refs[loads : loads + 2]
    targets = refs[loads + 2 : 2 * loads + 2]
    bias, sems, *scratch = refs[2 * loads + 2 :]
    moves = [
        pltpu.make_async_copy(source.at[0], target, sems.at[i])
        for i, (source, target) in enumerate(zip(sources, targets))
    ]
    for move in moves:
        move.start()
    done_ref[...] = jnp.zeros((8, TILE), F32)
    pos = pos_ref[0]
    starts = doc_starts(n, pos, held)
    first = starts_of(held[pos, TILE:KV_ROWS, 0:HEAD].astype(F32)[0:1], starts)
    place = (pos * TILE + lax.broadcasted_iota(jnp.int32, (1, TILE), 1)).astype(F32)
    chains = []
    for i, (h, own) in enumerate(by_kv_head(heads)):
        queries, acc = scratch[2 * i : 2 * i + 2]
        chains.append((queries, h, acc))
        for j, a in enumerate(own):
            terms = two_terms(q_ref[:, a * HEAD : (a + 1) * HEAD].astype(F32).T)
            for t, term in enumerate(terms):
                queries[t * HEAD : (t + 1) * HEAD, j * TILE : (j + 1) * TILE] = term
    done = jnp.concatenate(flash(pos, held, chains, bias, place, first), axis=0)
    for j, a in enumerate(heads):
        h_ref[:, j * HEAD : (j + 1) * HEAD] = (
            x_ref[:, a * HEAD : (a + 1) * HEAD].astype(F32) + done[j * TILE : (j + 1) * TILE]
        )
    for move in moves:
        move.wait()


def combine_kernel(planes, widths, mix_ref, *refs):
    count = len(widths)
    halves, parts = refs[:count], refs[count : count + planes]
    _, out_ref, buffer, sems = refs[count + planes :]
    slots = planes * SLOTS
    came = jnp.concatenate([p[...].astype(F32) for p in parts], axis=0).astype(BF16)
    order = one_hot(travel_row(numbers((CUT * slots, 1), 0), planes, SLOTS), planes * PIECE)
    came = dot(order, came).astype(BF16)
    size = buffer.shape[1] // CUT
    moves = []
    for q in range(CUT):
        rows = came[q * slots : (q + 1) * slots]
        part = dot(mix_ref[...], jnp.concatenate([rows, rows], axis=0))
        at = 0
        for h, width in zip(halves, widths):
            low, high = max(at, q * size), min(at + width, (q + 1) * size)
            if low < high:
                buffer[:, low:high] = (
                    h[:, low - at : high - at] + part[:, low - q * size : high - q * size]
                ).astype(BF16)
            at += width
        columns = pl.ds(q * size, size)
        moves.append(
            pltpu.make_async_copy(buffer.at[:, columns], out_ref.at[:, columns], sems.at[q])
        )
        moves[-1].start()
    for move in moves:
        move.wait()


def pin(x):
    return pltpu.with_memory_space_constraint(x, pltpu.HBM)


def params(mib):
    return pltpu.CompilerParams(vmem_limit_bytes=mib * 1024 * 1024)


def local(
    resid, queries, keys, values, doc_ids, norm_gain, routes, route_weights, w_gate, w_up, w_down
):
    n = lax.axis_size("expert")
    planes = n // SHARDS
    pos = lax.axis_index("expert").astype(jnp.int32).reshape(1)
    tokens, width = queries.shape
    hidden = w_gate.shape[2]
    routes_t = routes.T
    gates_t = route_weights.T
    docs = doc_ids.reshape(1, tokens)
    small = 24 if n <= 16 else 60
    back = reach(n)

    packed = pl.pallas_call(
        pack_kernel,
        out_shape=jax.ShapeDtypeStruct((KV_ROWS, 4 * HEAD), BF16),
        in_specs=[HBM] * 3,
        out_specs=VMEM,
        scratch_shapes=[
            pltpu.VMEM((1, tokens), jnp.int32),
            pltpu.VMEM((tokens, KV_HEADS * HEAD), BF16),
            pltpu.SemaphoreType.DMA((3,)),
        ],
        compiler_params=params(8),
        name="pack",
    )(pin(docs), pin(keys), pin(values))

    def move(value, pairs):
        return lax.ppermute(value, "expert", pairs)

    def needed(k, y_from, y_to):
        gaps = [
            k * SHARDS + 2 * (y_to - y_from) + (to - of) for to in range(2) for of in range(2)
        ]
        return any(0 <= gap <= back for gap in gaps)

    far = max(k for k in range(planes) if any(needed(k, a, b) for a in (0, 1) for b in (0, 1)))
    size = min(n, 16) * PIECE
    q_rows, x_rows, facts, mix, gather, spread = pl.pallas_call(
        functools.partial(select_kernel, planes),
        out_shape=[
            jax.ShapeDtypeStruct((KV_HEADS, 2 * HEAD, planes * CAP * GROUP), BF16),
            jax.ShapeDtypeStruct((planes * CAP, width), F32),
            jax.ShapeDtypeStruct((8, planes * CAP * GROUP), F32),
            jax.ShapeDtypeStruct((tokens, 2 * planes * SLOTS), BF16),
            jax.ShapeDtypeStruct((size, size), BF16),
            jax.ShapeDtypeStruct((size, size), BF16),
        ],
        in_specs=[SMEM] + [HBM] * 5,
        out_specs=[VMEM] * 6,
        scratch_shapes=[
            pltpu.VMEM(routes_t.shape, jnp.int32),
            pltpu.VMEM(docs.shape, jnp.int32),
            pltpu.VMEM(queries.shape, BF16),
            pltpu.VMEM(resid.shape, BF16),
            pltpu.VMEM(gates_t.shape, F32),
            pltpu.VMEM((planes * CAP * GROUP, HEAD), F32),
            pltpu.SemaphoreType.DMA((5,)),
        ],
        compiler_params=params(small),
        name="select",
    )(pos, *map(pin, (routes_t, docs, queries, resid, gates_t)))

    flip_y = [(s, s ^ 2) for s in range(n)]
    flip_c = [(s, s ^ 1) for s in range(n)]
    jump = {s: s + far * SHARDS - 2 for s in range(n - far * SHARDS) if s & 2}
    jump.update({to: s for s, to in jump.items()})
    jumped = move(packed, [(s, jump.get(s, s)) for s in range(n)])
    along = [packed] + [
        move(packed, [(s, (s + k * SHARDS) % n) for s in range(n)]) for k in range(1, far)
    ]
    along[1], q_rows = lax.optimization_barrier((along[1], q_rows))
    across = []
    for k in range(far):
        if k > 1 and k == far - 1:
            along[k], across = lax.optimization_barrier((along[k], across))
        across.append(move(along[k], [(s, s ^ 2 if s >= k * SHARDS else s) for s in range(n)]))
    early, late = along + [jumped] + across[:-1], across[-1:]
    sides = [(0, k) for k in range(far)] + [(1, far)] + [(1, k) for k in range(far - 1)]
    early.append(move(jnp.concatenate(early, axis=0), flip_c))
    early_senders = [(i, 0, 0, *side) for i, side in enumerate(sides)]
    early_senders += [(len(sides), i * KV_ROWS, 1, *side) for i, side in enumerate(sides)]
    late_senders = [(flip, 0, flip, 1, far - 1) for flip in (0, 1)]
    held_shape = jax.ShapeDtypeStruct((n, KV_ROWS, 4 * HEAD), BF16)
    held = pl.pallas_call(
        functools.partial(collect_kernel, n, early_senders),
        out_shape=held_shape,
        in_specs=[SMEM] + [ANY] * len(early),
        out_specs=VMEM,
        scratch_shapes=[pltpu.SemaphoreType.DMA((len(early_senders),))],
        compiler_params=params(small),
        cost_estimate=pl.CostEstimate(flops=0, bytes_accessed=1000, transcendentals=0),
        name="collect",
    )(pos, *early)

    lanes = min(planes, 4) * CAP * GROUP
    late[0], held = lax.optimization_barrier((late[0], held))
    late.append(move(late[0], flip_c))
    *sent, held = pl.pallas_call(
        functools.partial(routed_kernel, n, late_senders),
        out_shape=[jax.ShapeDtypeStruct((PIECE, width // CUT), BF16)] * planes
        + [held_shape],
        in_specs=[SMEM, HBM] + [VMEM] * 4 + [ANY] * len(late),
        out_specs=[VMEM] * (planes + 1),
        scratch_shapes=[
            pltpu.VMEM((KV_HEADS, HEAD + EXTRA, lanes), F32),
            pltpu.VMEM((KEYS, lanes), F32),
            pltpu.VMEM((KV_HEADS, 2 * HEAD, lanes), BF16),
            pltpu.VMEM((lanes, HEAD), F32),
            pltpu.VMEM((lanes // GROUP, width), F32),
            pltpu.VMEM((1, width), F32),
            pltpu.SemaphoreType.DMA((len(late_senders) + 1,)),
        ],
        input_output_aliases={5: planes},
        compiler_params=params(small),
        name="routed",
    )(pos, pin(norm_gain.reshape(1, width)), q_rows, x_rows, facts, held, *late)

    def own(heads, after, *sources):
        lanes = [len(own) * TILE for _, own in by_kv_head(heads)]
        return pl.pallas_call(
            functools.partial(own_kernel, n, heads, len(sources)),
            out_shape=[
                jax.ShapeDtypeStruct((tokens, len(heads) * HEAD), F32),
                jax.ShapeDtypeStruct((8, TILE), F32),
            ]
            + [jax.ShapeDtypeStruct(w.shape[1:], BF16) for w in sources],
            in_specs=[SMEM, VMEM, VMEM, VMEM, ANY] + [HBM] * len(sources),
            out_specs=[VMEM] * (2 + len(sources)),
            scratch_shapes=[pltpu.VMEM((KEYS, TILE), F32), pltpu.SemaphoreType.DMA((3,))]
            + [
                shape
                for count in lanes
                for shape in (
                    pltpu.VMEM((2 * HEAD, count), BF16),
                    pltpu.VMEM((HEAD + EXTRA, count), F32),
                )
            ],
            compiler_params=params(small),
            cost_estimate=pl.CostEstimate(
                flops=2_000_000_000, bytes_accessed=8_000_000, transcendentals=2_000_000
            ),
            name="own",
        )(pos, held, queries, resid, after, *map(pin, sources))

    half0, done, *weights = own(range(10), sent[0], w_gate, w_up, w_down)
    half1, late = own(range(10, 18), done)
    halves = [half0, half1]

    come = [
        move(sent[k], [(s, (s + k * SHARDS) % n) for s in range(n)]) for k in range(1, planes)
    ]
    next_door = move(sent[0], flip_y)
    come, next_door, done = lax.optimization_barrier((come, next_door, done))
    here = [sent[0], jnp.concatenate(come, axis=0)]
    there = [next_door, move(here[1], flip_y)]
    mate = move(jnp.concatenate(here, axis=0), flip_c)
    there, mate, late = lax.optimization_barrier((there, mate, late))
    pieces = here + there + [mate, move(jnp.concatenate(there, axis=0), flip_c)]

    half = jax.ShapeDtypeStruct((n * PIECE // 2, width // CUT), BF16)
    keep, send = pl.pallas_call(
        functools.partial(expert_kernel, n, len(pieces)),
        out_shape=[half, half],
        in_specs=[VMEM] * (len(pieces) + 5) + [ANY],
        out_specs=[VMEM, VMEM],
        scratch_shapes=[pltpu.VMEM((min(n, 16) * CAP, width), BF16)],
        compiler_params=params(16),
        cost_estimate=pl.CostEstimate(
            flops=1_200_000_000, bytes_accessed=12_000_000, transcendentals=50_000
        ),
        name="expert",
    )(*pieces, *weights, gather, spread, late)

    half2, done = own(range(18, QUERY_HEADS), keep)
    halves.append(half2)

    total = keep.astype(F32) + move(send, [(s, s ^ 1) for s in range(n)]).astype(F32)
    quarter = n * PIECE // 4
    other = move(total[quarter:].astype(BF16), [(s, s ^ 2) for s in range(n)])
    other, done = lax.optimization_barrier((other, done))
    total = (total[:quarter] + other.astype(F32)).astype(BF16)
    parts = [total[:PIECE]]
    for k in range(1, planes):
        parts.append(
            move(
                total[k * PIECE : (k + 1) * PIECE], [(s, (s - k * SHARDS) % n) for s in range(n)]
            )
        )

    widths = [h.shape[1] for h in halves]
    return pl.pallas_call(
        functools.partial(combine_kernel, planes, widths),
        out_shape=jax.ShapeDtypeStruct((tokens, width), BF16),
        in_specs=[VMEM] * (1 + len(halves) + planes) + [ANY],
        out_specs=HBM,
        scratch_shapes=[pltpu.VMEM((tokens, width), BF16), pltpu.SemaphoreType.DMA((CUT,))],
        compiler_params=params(small),
        name="combine",
    )(mix, *halves, *parts, done)


def solution(mesh):
    rows = P(("groups", "expert"), None)
    in_specs = (rows,) * 4 + (P(("groups", "expert")), P(), rows, rows) + (
        P("expert", None, None),
    ) * 3
    return jax.shard_map(local, mesh=mesh, in_specs=in_specs, out_specs=rows, check_vma=False)
```

```python
import functools
import math

import jax
import jax.numpy as jnp
from jax import lax
from jax.experimental import pallas as pl
from jax.experimental.pallas import tpu as pltpu
from jax.sharding import PartitionSpec as P

HEAD = 128
QUERY_HEADS = 32
KV_HEADS = 2
GROUP = QUERY_HEADS // KV_HEADS
SHARDS = 4
CAP = 6
SLOTS = 8
CUT = 4
PIECE = CUT * CAP
TILE = 128
KEYS = 256
KV_ROWS = TILE + 16
SCALE = math.log2(math.e) / math.sqrt(HEAD)
LOW = -1e30
EXTRA = 16
F32 = jnp.float32
BF16 = jnp.bfloat16
VMEM = pl.BlockSpec(memory_space=pltpu.VMEM)
SMEM = pl.BlockSpec(memory_space=pltpu.SMEM)
ANY = pl.BlockSpec(memory_space=pl.ANY)
HBM = pl.BlockSpec(memory_space=pltpu.HBM)


def dot(a, b, ca=1, cb=0):
    return lax.dot_general(a, b, (((ca,), (cb,)), ((), ())), preferred_element_type=F32)


def reach(n):
    longest = n * TILE // 2 + 256
    return (longest - 1 + TILE - 1) // TILE


def slot_rows(routes, experts):
    members = jnp.concatenate(
        [jnp.max((routes == e).astype(F32), axis=0, keepdims=True) for e in experts], axis=0
    )
    count = len(experts)
    padded = -(-count // 8) * 8
    wide = members
    if padded > count:
        wide = jnp.concatenate([members, jnp.zeros((padded - count, TILE), F32)], axis=0)
    before = lax.broadcasted_iota(jnp.int32, (TILE, TILE), 0) < lax.broadcasted_iota(
        jnp.int32, (TILE, TILE), 1
    )
    ranks = dot(wide.astype(BF16), before.astype(F32).astype(BF16))
    return members, ranks


def one_hot(targets, count):
    shape = (targets.shape[0], count) if targets.shape[1] == 1 else (count, targets.shape[1])
    axis = 1 if targets.shape[1] == 1 else 0
    places = lax.broadcasted_iota(jnp.int32, shape, axis).astype(F32)
    return jnp.where(places == targets, 1.0, 0.0).astype(BF16)


def split(x, size):
    whole = jnp.floor((x + 0.5) / size)
    return whole, x - whole * size


def travel_row(x, senders, slots):
    chunk, rest = split(x, senders * slots)
    sender, slot = split(rest, slots)
    return jnp.where(slot < CAP, sender * PIECE + chunk * CAP + slot, -1.0)


def numbers(shape, axis):
    return lax.broadcasted_iota(jnp.int32, shape, axis).astype(F32)


def pack_kernel(docs_ref, keys_ref, values_ref, out_ref, docs, values, sems):
    moves = [
        pltpu.make_async_copy(values_ref, values, sems.at[0]),
        pltpu.make_async_copy(docs_ref, docs, sems.at[1]),
        pltpu.make_async_copy(
            keys_ref, out_ref.at[pl.ds(0, TILE), pl.ds(0, KV_HEADS * HEAD)], sems.at[2]
        ),
    ]
    for move in moves:
        move.start()
    moves[0].wait()
    for h in range(KV_HEADS):
        out_ref[0:TILE, (KV_HEADS + h) * HEAD : (KV_HEADS + h + 1) * HEAD] = (
            values[:, h * HEAD : (h + 1) * HEAD].astype(F32).T.astype(BF16)
        )
    moves[1].wait()
    out_ref[TILE:KV_ROWS, :] = jnp.zeros((KV_ROWS - TILE, 4 * HEAD), BF16)
    out_ref[TILE:KV_ROWS, 0:HEAD] = jnp.broadcast_to(
        docs[...].astype(F32), (KV_ROWS - TILE, TILE)
    ).astype(BF16)
    moves[2].wait()


def select_kernel(planes, pos_ref, *refs):
    sources, (qs_ref, xs_ref, facts_ref, mix_ref, gather_ref, spread_ref) = refs[:5], refs[5:11]
    routes_ref, docs_ref, q_ref, x_ref, gates_ref, stack, sems = refs[11:]
    moves = [
        pltpu.make_async_copy(source, target, sems.at[i])
        for i, (source, target) in enumerate(zip(sources, refs[11:16]))
    ]
    for move in moves:
        move.start()
    for move in moves:
        move.wait()
    z = pos_ref[0] // SHARDS
    experts = [lax.rem(z + k, planes) for k in range(planes)]
    routes, gates = routes_ref[...], gates_ref[...]
    members, ranks = slot_rows(routes, experts)
    slot = lax.broadcasted_iota(jnp.int32, (SLOTS, TILE), 0).astype(F32)
    mix = []
    for k, e in enumerate(experts):
        gate = jnp.sum(jnp.where(routes == e, gates, 0.0), axis=0, keepdims=True)
        mix.append(jnp.where(ranks[k : k + 1] == slot, gate, 0.0))
    mix = jnp.concatenate(mix, axis=0).T
    mix_high = mix.astype(BF16)
    mix_ref[:, : planes * SLOTS] = mix_high
    mix_ref[:, planes * SLOTS :] = (mix - mix_high.astype(F32)).astype(BF16)
    size = gather_ref.shape[0]
    gather_ref[...] = one_hot(travel_row(numbers((size, 1), 0), size // PIECE, CAP), size)
    spread_ref[...] = one_hot(travel_row(numbers((1, size), 1), size // PIECE, CAP), size)
    docs = docs_ref[...].astype(F32)
    token = lax.broadcasted_iota(jnp.int32, (1, TILE), 1).astype(F32)
    facts = jnp.concatenate(
        [token, docs, jnp.ones((1, TILE), F32), jnp.zeros((5, TILE), F32)], axis=0
    ).astype(BF16)
    picks = [
        jnp.where(ranks[k : k + 1] == slot, members[k : k + 1], 0.0) for k in range(planes)
    ]
    rows = planes * CAP
    plane, place = split(numbers((rows, 1), 0), CAP)
    compact = one_hot(plane * SLOTS + place, planes * SLOTS)
    chooser = dot(compact, jnp.concatenate(picks, axis=0).astype(BF16)).astype(BF16)
    lane, _ = split(numbers((rows * GROUP, 1), 0), GROUP)
    lane_pick = dot(one_hot(lane, rows), chooser).astype(BF16)
    known = dot(facts, lane_pick, 1, 1)
    facts_ref[...] = jnp.concatenate(
        [known[0:1], known[1:2] + (1.0 - known[2:3]) * docs[:, 0:1], known[2:]], axis=0
    )
    q_rows = dot(chooser, q_ref[...])
    xs_ref[...] = dot(chooser, x_ref[...])
    for h in range(KV_HEADS):
        for g in range(GROUP):
            a = h * GROUP + g
            stack[pl.ds(g, rows, stride=GROUP), :] = q_rows[:, a * HEAD : (a + 1) * HEAD]
        for i, term in enumerate(two_terms(stack[...].T)):
            qs_ref[h, i * HEAD : (i + 1) * HEAD, :] = term


def doc_starts(n, pos, held):
    sums = [jnp.zeros((1, TILE), F32) for _ in range(3)]
    for s in range(n):
        docs = held[s, TILE:KV_ROWS, 0:HEAD].astype(F32)[0:1]
        ahead = (pos - s < 0).astype(F32)
        behind = (pos - s > reach(n)).astype(F32)
        known = 1.0 - ahead - behind
        docs = jnp.where(known > 0.5, docs, 0.0) + 9.0 * ahead
        for d in range(3):
            sums[d] = sums[d] + jnp.where(docs < d + 1.0, 1.0, 0.0)
    return [jnp.sum(s, axis=1, keepdims=True) for s in sums]


def starts_of(docs, starts):
    first = jnp.zeros_like(docs)
    for d in range(3):
        first = jnp.where(docs == d + 1.0, starts[d], first)
    return first


def two_terms(x):
    scaled = x.astype(F32) * SCALE
    high = scaled.astype(BF16)
    return high, (scaled - high.astype(F32)).astype(BF16)


def key_steps(pos, place, first, bias_ref, step, state):
    low = jnp.min(first).astype(jnp.int32) // KEYS
    last = pos // (KEYS // TILE)
    clear = jnp.minimum((jnp.max(first).astype(jnp.int32) + KEYS - 1) // KEYS, last)

    def edge(j, carried):
        kb = jnp.where(j < clear - low, low + j, last)
        key_at = (kb * KEYS + lax.broadcasted_iota(jnp.int32, (KEYS, 1), 0)).astype(F32)
        bias_ref[...] = jnp.where((key_at >= first) & (key_at <= place), 0.0, LOW)
        return step(kb, carried, True)

    state = lax.fori_loop(0, clear - low + 1, edge, state)
    return lax.fori_loop(clear, last, lambda kb, carried: step(kb, carried, False), state)


def by_kv_head(heads):
    groups = [(h, [a for a in heads if a // GROUP == h]) for h in range(KV_HEADS)]
    return [(h, own) for h, own in groups if own]


def keys_of(held, kb, h):
    keys = jnp.concatenate(
        [held[2 * kb + t, 0:TILE, h * HEAD : (h + 1) * HEAD] for t in range(2)], axis=0
    )
    return jnp.concatenate([keys, keys], axis=1)


def values_of(held, kb, h):
    at = (KV_HEADS + h) * HEAD
    values = jnp.concatenate(
        [held[2 * kb + t, 0:TILE, at : at + HEAD] for t in range(2)], axis=1
    )
    return jnp.concatenate([values, jnp.ones((EXTRA, KEYS), BF16)], axis=0)


def flash(pos, held, chains, bias_ref, place, first):
    for _, _, acc in chains:
        acc[...] = jnp.zeros(acc.shape, F32)

    def step(kb, tops, masked):
        out = []
        for (queries, h, acc), old in zip(chains, tops):
            scores = dot(keys_of(held, kb, h), queries[...])
            if masked:
                copies = scores.shape[1] // bias_ref.shape[1]
                scores = scores + jnp.concatenate([bias_ref[...]] * copies, axis=1)
            top = jnp.maximum(old, jnp.max(scores, axis=0, keepdims=True))
            weights = jnp.exp2(scores - top).astype(BF16)
            acc[...] = acc[...] * jnp.exp2(old - top) + dot(values_of(held, kb, h), weights)
            out.append(top)
        return tuple(out)

    tops = tuple(jnp.full((1, acc.shape[1]), LOW, F32) for _, _, acc in chains)
    key_steps(pos, place, first, bias_ref, step, tops)
    return [(acc[0:HEAD, :] / acc[HEAD : HEAD + 1, :]).T for _, _, acc in chains]


def place_pieces(n, senders, pos, pieces, held, sems):
    planes = n // SHARDS
    z, y, c = pos // SHARDS, (pos // 2) % 2, pos % 2
    copies = []
    for i, (piece, row, flip_c, flip_y, k) in enumerate(senders):
        sender = lax.rem(z - k + planes, planes) * SHARDS + (y ^ flip_y) * 2 + (c ^ flip_c)
        copy = pltpu.make_async_copy(
            pieces[piece].at[pl.ds(row, KV_ROWS)], held.at[sender], sems.at[i]
        )
        copy.start()
        copies.append(copy)
    return copies


def collect_kernel(n, senders, pos_ref, *refs):
    *pieces, held, sems = refs
    for copy in place_pieces(n, senders, pos_ref[0], pieces, held, sems):
        copy.wait()


def routed_kernel(n, senders, pos_ref, gain_ref, qs_ref, xs_ref, facts_ref, _, *refs):
    planes = n // SHARDS
    count = len(senders)
    pieces, outs, held = refs[:2], refs[2 : 2 + planes], refs[2 + planes]
    acc, bias, q_scr, stack, state, gain, sems = refs[3 + planes :]
    pos = pos_ref[0]
    copies = place_pieces(n, senders, pos, pieces, held, sems)
    copies.append(pltpu.make_async_copy(gain_ref, gain, sems.at[count]))
    copies[-1].start()
    for copy in copies:
        copy.wait()
    starts = doc_starts(n, pos, held)
    lanes = q_scr.shape[2]
    rows = lanes // GROUP
    base = (pos * TILE).astype(F32)
    width = state.shape[1] // CUT
    row = numbers((CUT * rows, 1), 0)
    plane, rest = split(row, PIECE)
    chunk, slot = split(rest, CAP)
    order = one_hot(chunk * rows + plane * CAP + slot, CUT * rows)
    for part in range(xs_ref.shape[0] // rows):
        at = slice(part * lanes, (part + 1) * lanes)
        q_scr[...] = qs_ref[:, :, at]
        done = flash(
            pos,
            held,
            [(q_scr.at[h], h, acc.at[h]) for h in range(KV_HEADS)],
            bias,
            facts_ref[0:1, at] + base,
            starts_of(facts_ref[1:2, at], starts),
        )
        for h in range(KV_HEADS):
            stack[...] = done[h]
            for g in range(GROUP):
                lane = (h * GROUP + g) * HEAD
                state[:, lane : lane + HEAD] = (
                    xs_ref[part * rows : (part + 1) * rows, lane : lane + HEAD]
                    + stack[pl.ds(g, rows, stride=GROUP), :]
                )
        hidden = state[...]
        mean = jnp.mean(hidden * hidden, axis=1, keepdims=True)
        normed = hidden * lax.rsqrt(mean + 1e-06) * gain[...]
        chunks = [normed[:, q * width : (q + 1) * width] for q in range(CUT)]
        sent = dot(order, jnp.concatenate(chunks, axis=0).astype(BF16))
        for k in range(rows // CAP):
            outs[part * (rows // CAP) + k][...] = sent[k * PIECE : (k + 1) * PIECE].astype(BF16)


def expert_kernel(n, count, *refs):
    pieces = refs[:count]
    wg, wu, wd = refs[count : count + 3]
    gather, spread, _, keep_ref, send_ref, rows = refs[count + 3 :]
    step = pieces[0].shape[1]
    senders = min(n, 16)
    size, total = senders * PIECE, n * PIECE
    half = total // 2
    kept = senders * CAP
    for at in range(0, total, size):
        parts, first = [], 0
        for piece in pieces:
            low, high = max(at - first, 0), min(at + size - first, piece.shape[0])
            if low < high:
                parts.append(piece[low:high, :].astype(F32))
            first += piece.shape[0]
        came = dot(gather[...], jnp.concatenate(parts, axis=0).astype(BF16)).astype(BF16)
        for q in range(CUT):
            rows[:, q * step : (q + 1) * step] = came[q * kept : (q + 1) * kept]
        gate = dot(rows[...], wg[...])
        up = dot(rows[...], wu[...])
        act = (gate / (1.0 + jnp.exp(-gate)) * up).astype(BF16)
        parts = [dot(act, wd[:, q * step : (q + 1) * step]).astype(BF16) for q in range(CUT)]
        out = dot(spread[...], jnp.concatenate(parts, axis=0)).astype(BF16)
        if size > half:
            keep_ref[...] = out[:half]
            send_ref[...] = out[half:]
        elif at < half:
            keep_ref[at : at + size] = out
        else:
            send_ref[at - half : at - half + size] = out


def own_kernel(n, heads, loads, pos_ref, held, q_ref, x_ref, _, *refs):
    sources, (h_ref, done_ref) = refs[:loads], refs[loads : loads + 2]
    targets = refs[loads + 2 : 2 * loads + 2]
    bias, sems, *scratch = refs[2 * loads + 2 :]
    moves = [
        pltpu.make_async_copy(source.at[0], target, sems.at[i])
        for i, (source, target) in enumerate(zip(sources, targets))
    ]
    for move in moves:
        move.start()
    done_ref[...] = jnp.zeros((8, TILE), F32)
    pos = pos_ref[0]
    starts = doc_starts(n, pos, held)
    first = starts_of(held[pos, TILE:KV_ROWS, 0:HEAD].astype(F32)[0:1], starts)
    place = (pos * TILE + lax.broadcasted_iota(jnp.int32, (1, TILE), 1)).astype(F32)
    chains = []
    for i, (h, own) in enumerate(by_kv_head(heads)):
        queries, acc = scratch[2 * i : 2 * i + 2]
        chains.append((queries, h, acc))
        for j, a in enumerate(own):
            terms = two_terms(q_ref[:, a * HEAD : (a + 1) * HEAD].astype(F32).T)
            for t, term in enumerate(terms):
                queries[t * HEAD : (t + 1) * HEAD, j * TILE : (j + 1) * TILE] = term
    done = jnp.concatenate(flash(pos, held, chains, bias, place, first), axis=0)
    for j, a in enumerate(heads):
        h_ref[:, j * HEAD : (j + 1) * HEAD] = (
            x_ref[:, a * HEAD : (a + 1) * HEAD].astype(F32) + done[j * TILE : (j + 1) * TILE]
        )
    for move in moves:
        move.wait()


def combine_kernel(planes, widths, mix_ref, *refs):
    count = len(widths)
    halves, parts = refs[:count], refs[count : count + planes]
    _, out_ref, buffer, sems = refs[count + planes :]
    slots = planes * SLOTS
    came = jnp.concatenate([p[...].astype(F32) for p in parts], axis=0).astype(BF16)
    order = one_hot(travel_row(numbers((CUT * slots, 1), 0), planes, SLOTS), planes * PIECE)
    came = dot(order, came).astype(BF16)
    size = buffer.shape[1] // CUT
    moves = []
    for q in range(CUT):
        rows = came[q * slots : (q + 1) * slots]
        part = dot(mix_ref[...], jnp.concatenate([rows, rows], axis=0))
        at = 0
        for h, width in zip(halves, widths):
            low, high = max(at, q * size), min(at + width, (q + 1) * size)
            if low < high:
                buffer[:, low:high] = (
                    h[:, low - at : high - at] + part[:, low - q * size : high - q * size]
                ).astype(BF16)
            at += width
        columns = pl.ds(q * size, size)
        moves.append(
            pltpu.make_async_copy(buffer.at[:, columns], out_ref.at[:, columns], sems.at[q])
        )
        moves[-1].start()
    for move in moves:
        move.wait()


def pin(x):
    return pltpu.with_memory_space_constraint(x, pltpu.HBM)


def params(mib):
    return pltpu.CompilerParams(vmem_limit_bytes=mib * 1024 * 1024)


def local(
    resid, queries, keys, values, doc_ids, norm_gain, routes, route_weights, w_gate, w_up, w_down
):
    n = lax.axis_size("expert")
    planes = n // SHARDS
    pos = lax.axis_index("expert").astype(jnp.int32).reshape(1)
    tokens, width = queries.shape
    hidden = w_gate.shape[2]
    routes_t = routes.T
    gates_t = route_weights.T
    docs = doc_ids.reshape(1, tokens)
    small = 24 if n <= 16 else 60
    back = reach(n)

    packed = pl.pallas_call(
        pack_kernel,
        out_shape=jax.ShapeDtypeStruct((KV_ROWS, 4 * HEAD), BF16),
        in_specs=[HBM] * 3,
        out_specs=VMEM,
        scratch_shapes=[
            pltpu.VMEM((1, tokens), jnp.int32),
            pltpu.VMEM((tokens, KV_HEADS * HEAD), BF16),
            pltpu.SemaphoreType.DMA((3,)),
        ],
        compiler_params=params(8),
        name="pack",
    )(pin(docs), pin(keys), pin(values))

    def move(value, pairs):
        return lax.ppermute(value, "expert", pairs)

    def needed(k, y_from, y_to):
        gaps = [
            k * SHARDS + 2 * (y_to - y_from) + (to - of) for to in range(2) for of in range(2)
        ]
        return any(0 <= gap <= back for gap in gaps)

    far = max(k for k in range(planes) if any(needed(k, a, b) for a in (0, 1) for b in (0, 1)))
    size = min(n // 2, 16) * PIECE
    q_rows, x_rows, facts, mix, gather, spread = pl.pallas_call(
        functools.partial(select_kernel, planes),
        out_shape=[
            jax.ShapeDtypeStruct((KV_HEADS, 2 * HEAD, planes * CAP * GROUP), BF16),
            jax.ShapeDtypeStruct((planes * CAP, width), F32),
            jax.ShapeDtypeStruct((8, planes * CAP * GROUP), F32),
            jax.ShapeDtypeStruct((tokens, 2 * planes * SLOTS), BF16),
            jax.ShapeDtypeStruct((size, size), BF16),
            jax.ShapeDtypeStruct((size, size), BF16),
        ],
        in_specs=[SMEM] + [HBM] * 5,
        out_specs=[VMEM] * 6,
        scratch_shapes=[
            pltpu.VMEM(routes_t.shape, jnp.int32),
            pltpu.VMEM(docs.shape, jnp.int32),
            pltpu.VMEM(queries.shape, BF16),
            pltpu.VMEM(resid.shape, BF16),
            pltpu.VMEM(gates_t.shape, F32),
            pltpu.VMEM((planes * CAP * GROUP, HEAD), F32),
            pltpu.SemaphoreType.DMA((5,)),
        ],
        compiler_params=params(small),
        name="select",
    )(pos, *map(pin, (routes_t, docs, queries, resid, gates_t)))

    flip_y = [(s, s ^ 2) for s in range(n)]
    flip_c = [(s, s ^ 1) for s in range(n)]
    jump = {s: s + far * SHARDS - 2 for s in range(n - far * SHARDS) if s & 2}
    jump.update({to: s for s, to in jump.items()})
    jumped = move(packed, [(s, jump.get(s, s)) for s in range(n)])
    along = [packed]
    for k in range(1, far):
        below = (k - 1) * SHARDS
        pairs = [
            (s, s if s < below else s + SHARDS if s + SHARDS < n else s % SHARDS + below)
            for s in range(n)
        ]
        along.append(move(along[-1], pairs))
    across = []
    for k in range(far):
        if k == 1:
            along[1], q_rows = lax.optimization_barrier((along[1], q_rows))
        elif k == far - 1:
            along[k], across = lax.optimization_barrier((along[k], across))
        across.append(move(along[k], [(s, s ^ 2 if s >= k * SHARDS else s) for s in range(n)]))
    early, late = along + [jumped] + across[:-1], across[-1:]
    sides = [(0, k) for k in range(far)] + [(1, far)] + [(1, k) for k in range(far - 1)]
    early.append(move(jnp.concatenate(early, axis=0), flip_c))
    early_senders = [(i, 0, 0, *side) for i, side in enumerate(sides)]
    early_senders += [(len(sides), i * KV_ROWS, 1, *side) for i, side in enumerate(sides)]
    late_senders = [(flip, 0, flip, 1, far - 1) for flip in (0, 1)]
    held_shape = jax.ShapeDtypeStruct((n, KV_ROWS, 4 * HEAD), BF16)
    held = pl.pallas_call(
        functools.partial(collect_kernel, n, early_senders),
        out_shape=held_shape,
        in_specs=[SMEM] + [ANY] * len(early),
        out_specs=VMEM,
        scratch_shapes=[pltpu.SemaphoreType.DMA((len(early_senders),))],
        compiler_params=params(small),
        cost_estimate=pl.CostEstimate(flops=0, bytes_accessed=1000, transcendentals=0),
        name="collect",
    )(pos, *early)

    lanes = min(planes, 4) * CAP * GROUP
    late[0], held = lax.optimization_barrier((late[0], held))
    late.append(move(late[0], flip_c))
    *sent, held = pl.pallas_call(
        functools.partial(routed_kernel, n, late_senders),
        out_shape=[jax.ShapeDtypeStruct((PIECE, width // CUT), BF16)] * planes
        + [held_shape],
        in_specs=[SMEM, HBM] + [VMEM] * 4 + [ANY] * len(late),
        out_specs=[VMEM] * (planes + 1),
        scratch_shapes=[
            pltpu.VMEM((KV_HEADS, HEAD + EXTRA, lanes), F32),
            pltpu.VMEM((KEYS, lanes), F32),
            pltpu.VMEM((KV_HEADS, 2 * HEAD, lanes), BF16),
            pltpu.VMEM((lanes, HEAD), F32),
            pltpu.VMEM((lanes // GROUP, width), F32),
            pltpu.VMEM((1, width), F32),
            pltpu.SemaphoreType.DMA((len(late_senders) + 1,)),
        ],
        input_output_aliases={5: planes},
        compiler_params=params(small),
        name="routed",
    )(pos, pin(norm_gain.reshape(1, width)), q_rows, x_rows, facts, held, *late)

    def own(heads, after, *sources):
        lanes = [len(own) * TILE for _, own in by_kv_head(heads)]
        return pl.pallas_call(
            functools.partial(own_kernel, n, heads, len(sources)),
            out_shape=[
                jax.ShapeDtypeStruct((tokens, len(heads) * HEAD), F32),
                jax.ShapeDtypeStruct((8, TILE), F32),
            ]
            + [jax.ShapeDtypeStruct(w.shape[1:], BF16) for w in sources],
            in_specs=[SMEM, VMEM, VMEM, VMEM, ANY] + [HBM] * len(sources),
            out_specs=[VMEM] * (2 + len(sources)),
            scratch_shapes=[pltpu.VMEM((KEYS, TILE), F32), pltpu.SemaphoreType.DMA((3,))]
            + [
                shape
                for count in lanes
                for shape in (
                    pltpu.VMEM((2 * HEAD, count), BF16),
                    pltpu.VMEM((HEAD + EXTRA, count), F32),
                )
            ],
            compiler_params=params(small),
            cost_estimate=pl.CostEstimate(
                flops=2_000_000_000, bytes_accessed=8_000_000, transcendentals=2_000_000
            ),
            name="own",
        )(pos, held, queries, resid, after, *map(pin, sources))

    half0, done, *weights = own(range(10), sent[0], w_gate, w_up, w_down)
    half1, late = own(range(10, GROUP), done)
    halves = [half0, half1]

    come = [
        move(sent[k], [(s, (s + k * SHARDS) % n) for s in range(n)]) for k in range(1, planes)
    ]
    next_door = move(sent[0], flip_y)
    come, next_door, done = lax.optimization_barrier((come, next_door, done))
    here = [sent[0], jnp.concatenate(come, axis=0)]
    there = [next_door, move(here[1], flip_y)]
    mate = move(jnp.concatenate(here, axis=0), flip_c)
    half = jax.ShapeDtypeStruct((n * PIECE // 4, width // CUT), BF16)

    def expert(pieces, after):
        return pl.pallas_call(
            functools.partial(expert_kernel, n // 2, len(pieces)),
            out_shape=[half, half],
            in_specs=[VMEM] * (len(pieces) + 5) + [ANY],
            out_specs=[VMEM, VMEM],
            scratch_shapes=[pltpu.VMEM((min(n // 2, 16) * CAP, width), BF16)],
            compiler_params=params(16),
            cost_estimate=pl.CostEstimate(
                flops=600_000_000, bytes_accessed=2_000_000, transcendentals=20_000
            ),
            name="expert",
        )(*pieces, *weights, gather, spread, after)

    keep, send = expert(here + [mate], done)
    there, late, keep = lax.optimization_barrier((there, late, keep))
    mine = keep.astype(F32) + move(send, flip_c).astype(F32)
    mate = move(jnp.concatenate(there, axis=0), flip_c)
    keep, send = expert(there + [mate], late)
    half2, done = own(range(GROUP, QUERY_HEADS), keep)
    halves.append(half2)
    theirs = keep.astype(F32) + move(send, flip_c).astype(F32)
    other = move(theirs.astype(BF16), flip_y)
    other, done = lax.optimization_barrier((other, done))
    total = (mine + other.astype(F32)).astype(BF16)
    parts = [total[:PIECE]]
    for k in range(1, planes):
        parts.append(
            move(
                total[k * PIECE : (k + 1) * PIECE], [(s, (s - k * SHARDS) % n) for s in range(n)]
            )
        )

    widths = [h.shape[1] for h in halves]
    return pl.pallas_call(
        functools.partial(combine_kernel, planes, widths),
        out_shape=jax.ShapeDtypeStruct((tokens, width), BF16),
        in_specs=[VMEM] * (1 + len(halves) + planes) + [ANY],
        out_specs=HBM,
        scratch_shapes=[pltpu.VMEM((tokens, width), BF16), pltpu.SemaphoreType.DMA((CUT,))],
        compiler_params=params(small),
        name="combine",
    )(mix, *halves, *parts, done)


def solution(mesh):
    rows = P(("groups", "expert"), None)
    in_specs = (rows,) * 4 + (P(("groups", "expert")), P(), rows, rows) + (
        P("expert", None, None),
    ) * 3
    return jax.shard_map(local, mesh=mesh, in_specs=in_specs, out_specs=rows, check_vma=False)
```

```python
import functools
import math

import jax
import jax.numpy as jnp
from jax import lax
from jax.experimental import pallas as pl
from jax.experimental.pallas import tpu as pltpu
from jax.sharding import PartitionSpec as P

HEAD = 128
QUERY_HEADS = 32
KV_HEADS = 2
GROUP = QUERY_HEADS // KV_HEADS
SHARDS = 4
CAP = 6
SLOTS = 8
CUT = 4
PIECE = CUT * CAP
TILE = 128
KEYS = 256
KV_ROWS = TILE + 16
SCALE = math.log2(math.e) / math.sqrt(HEAD)
LOW = -1e30
EXTRA = 16
F32 = jnp.float32
BF16 = jnp.bfloat16
VMEM = pl.BlockSpec(memory_space=pltpu.VMEM)
SMEM = pl.BlockSpec(memory_space=pltpu.SMEM)
ANY = pl.BlockSpec(memory_space=pl.ANY)
HBM = pl.BlockSpec(memory_space=pltpu.HBM)


def dot(a, b, ca=1, cb=0):
    return lax.dot_general(a, b, (((ca,), (cb,)), ((), ())), preferred_element_type=F32)


def reach(n):
    longest = n * TILE // 2 + 256
    return (longest - 1 + TILE - 1) // TILE


def slot_rows(routes, experts):
    members = jnp.concatenate(
        [jnp.max((routes == e).astype(F32), axis=0, keepdims=True) for e in experts], axis=0
    )
    count = len(experts)
    padded = -(-count // 8) * 8
    wide = members
    if padded > count:
        wide = jnp.concatenate([members, jnp.zeros((padded - count, TILE), F32)], axis=0)
    before = lax.broadcasted_iota(jnp.int32, (TILE, TILE), 0) < lax.broadcasted_iota(
        jnp.int32, (TILE, TILE), 1
    )
    ranks = dot(wide.astype(BF16), before.astype(F32).astype(BF16))
    return members, ranks


def one_hot(targets, count):
    shape = (targets.shape[0], count) if targets.shape[1] == 1 else (count, targets.shape[1])
    axis = 1 if targets.shape[1] == 1 else 0
    places = lax.broadcasted_iota(jnp.int32, shape, axis).astype(F32)
    return jnp.where(places == targets, 1.0, 0.0).astype(BF16)


def split(x, size):
    whole = jnp.floor((x + 0.5) / size)
    return whole, x - whole * size


def travel_row(x, senders, slots):
    chunk, rest = split(x, senders * slots)
    sender, slot = split(rest, slots)
    return jnp.where(slot < CAP, sender * PIECE + chunk * CAP + slot, -1.0)


def numbers(shape, axis):
    return lax.broadcasted_iota(jnp.int32, shape, axis).astype(F32)


def pack_kernel(docs_ref, keys_ref, values_ref, out_ref, docs, values, sems):
    moves = [
        pltpu.make_async_copy(values_ref, values, sems.at[0]),
        pltpu.make_async_copy(docs_ref, docs, sems.at[1]),
        pltpu.make_async_copy(
            keys_ref, out_ref.at[pl.ds(0, TILE), pl.ds(0, KV_HEADS * HEAD)], sems.at[2]
        ),
    ]
    for move in moves:
        move.start()
    moves[0].wait()
    for h in range(KV_HEADS):
        out_ref[0:TILE, (KV_HEADS + h) * HEAD : (KV_HEADS + h + 1) * HEAD] = (
            values[:, h * HEAD : (h + 1) * HEAD].astype(F32).T.astype(BF16)
        )
    moves[1].wait()
    out_ref[TILE:KV_ROWS, :] = jnp.zeros((KV_ROWS - TILE, 4 * HEAD), BF16)
    out_ref[TILE:KV_ROWS, 0:HEAD] = jnp.broadcast_to(
        docs[...].astype(F32), (KV_ROWS - TILE, TILE)
    ).astype(BF16)
    moves[2].wait()


def select_kernel(planes, pos_ref, *refs):
    sources, (qs_ref, xs_ref, facts_ref, mix_ref, gather_ref, spread_ref) = refs[:5], refs[5:11]
    routes_ref, docs_ref, q_ref, x_ref, gates_ref, stack, sems = refs[11:]
    moves = [
        pltpu.make_async_copy(source, target, sems.at[i])
        for i, (source, target) in enumerate(zip(sources, refs[11:16]))
    ]
    for move in moves:
        move.start()
    for move in moves:
        move.wait()
    z = pos_ref[0] // SHARDS
    experts = [lax.rem(z + k, planes) for k in range(planes)]
    routes, gates = routes_ref[...], gates_ref[...]
    members, ranks = slot_rows(routes, experts)
    slot = lax.broadcasted_iota(jnp.int32, (SLOTS, TILE), 0).astype(F32)
    mix = []
    for k, e in enumerate(experts):
        gate = jnp.sum(jnp.where(routes == e, gates, 0.0), axis=0, keepdims=True)
        mix.append(jnp.where(ranks[k : k + 1] == slot, gate, 0.0))
    mix = jnp.concatenate(mix, axis=0).T
    mix_high = mix.astype(BF16)
    mix_ref[:, : planes * SLOTS] = mix_high
    mix_ref[:, planes * SLOTS :] = (mix - mix_high.astype(F32)).astype(BF16)
    size = gather_ref.shape[0]
    gather_ref[...] = one_hot(travel_row(numbers((size, 1), 0), size // PIECE, CAP), size)
    spread_ref[...] = one_hot(travel_row(numbers((1, size), 1), size // PIECE, CAP), size)
    docs = docs_ref[...].astype(F32)
    token = lax.broadcasted_iota(jnp.int32, (1, TILE), 1).astype(F32)
    facts = jnp.concatenate(
        [token, docs, jnp.ones((1, TILE), F32), jnp.zeros((5, TILE), F32)], axis=0
    ).astype(BF16)
    picks = [
        jnp.where(ranks[k : k + 1] == slot, members[k : k + 1], 0.0) for k in range(planes)
    ]
    rows = planes * CAP
    plane, place = split(numbers((rows, 1), 0), CAP)
    compact = one_hot(plane * SLOTS + place, planes * SLOTS)
    chooser = dot(compact, jnp.concatenate(picks, axis=0).astype(BF16)).astype(BF16)
    lane, _ = split(numbers((rows * GROUP, 1), 0), GROUP)
    lane_pick = dot(one_hot(lane, rows), chooser).astype(BF16)
    known = dot(facts, lane_pick, 1, 1)
    facts_ref[...] = jnp.concatenate(
        [known[0:1], known[1:2] + (1.0 - known[2:3]) * docs[:, 0:1], known[2:]], axis=0
    )
    q_rows = dot(chooser, q_ref[...])
    xs_ref[...] = dot(chooser, x_ref[...])
    for h in range(KV_HEADS):
        for g in range(GROUP):
            a = h * GROUP + g
            stack[pl.ds(g, rows, stride=GROUP), :] = q_rows[:, a * HEAD : (a + 1) * HEAD]
        for i, term in enumerate(two_terms(stack[...].T)):
            qs_ref[h, i * HEAD : (i + 1) * HEAD, :] = term


def doc_starts(n, pos, held):
    sums = [jnp.zeros((1, TILE), F32) for _ in range(3)]
    for s in range(n):
        docs = held[s, TILE:KV_ROWS, 0:HEAD].astype(F32)[0:1]
        ahead = (pos - s < 0).astype(F32)
        behind = (pos - s > reach(n)).astype(F32)
        known = 1.0 - ahead - behind
        docs = jnp.where(known > 0.5, docs, 0.0) + 9.0 * ahead
        for d in range(3):
            sums[d] = sums[d] + jnp.where(docs < d + 1.0, 1.0, 0.0)
    return [jnp.sum(s, axis=1, keepdims=True) for s in sums]


def starts_of(docs, starts):
    first = jnp.zeros_like(docs)
    for d in range(3):
        first = jnp.where(docs == d + 1.0, starts[d], first)
    return first


def two_terms(x):
    scaled = x.astype(F32) * SCALE
    high = scaled.astype(BF16)
    return high, (scaled - high.astype(F32)).astype(BF16)


def key_steps(pos, place, first, bias_ref, step, state):
    low = jnp.min(first).astype(jnp.int32) // KEYS
    last = pos // (KEYS // TILE)
    clear = jnp.minimum((jnp.max(first).astype(jnp.int32) + KEYS - 1) // KEYS, last)

    def edge(j, carried):
        kb = jnp.where(j < clear - low, low + j, last)
        key_at = (kb * KEYS + lax.broadcasted_iota(jnp.int32, (KEYS, 1), 0)).astype(F32)
        bias_ref[...] = jnp.where((key_at >= first) & (key_at <= place), 0.0, LOW)
        return step(kb, carried, True)

    state = lax.fori_loop(0, clear - low + 1, edge, state)
    return lax.fori_loop(clear, last, lambda kb, carried: step(kb, carried, False), state)


def by_kv_head(heads):
    groups = [(h, [a for a in heads if a // GROUP == h]) for h in range(KV_HEADS)]
    return [(h, own) for h, own in groups if own]


def keys_of(held, kb, h):
    keys = jnp.concatenate(
        [held[2 * kb + t, 0:TILE, h * HEAD : (h + 1) * HEAD] for t in range(2)], axis=0
    )
    return jnp.concatenate([keys, keys], axis=1)


def values_of(held, kb, h):
    at = (KV_HEADS + h) * HEAD
    values = jnp.concatenate(
        [held[2 * kb + t, 0:TILE, at : at + HEAD] for t in range(2)], axis=1
    )
    return jnp.concatenate([values, jnp.ones((EXTRA, KEYS), BF16)], axis=0)


def flash(pos, held, chains, bias_ref, place, first):
    for _, _, acc in chains:
        acc[...] = jnp.zeros(acc.shape, F32)

    def step(kb, tops, masked):
        out = []
        for (queries, h, acc), old in zip(chains, tops):
            scores = dot(keys_of(held, kb, h), queries[...])
            if masked:
                copies = scores.shape[1] // bias_ref.shape[1]
                scores = scores + jnp.concatenate([bias_ref[...]] * copies, axis=1)
            top = jnp.maximum(old, jnp.max(scores, axis=0, keepdims=True))
            weights = jnp.exp2(scores - top).astype(BF16)
            acc[...] = acc[...] * jnp.exp2(old - top) + dot(values_of(held, kb, h), weights)
            out.append(top)
        return tuple(out)

    tops = tuple(jnp.full((1, acc.shape[1]), LOW, F32) for _, _, acc in chains)
    key_steps(pos, place, first, bias_ref, step, tops)
    return [(acc[0:HEAD, :] / acc[HEAD : HEAD + 1, :]).T for _, _, acc in chains]


def place_pieces(n, senders, pos, pieces, held, sems):
    planes = n // SHARDS
    z, y, c = pos // SHARDS, (pos // 2) % 2, pos % 2
    copies = []
    for i, (piece, row, flip_c, flip_y, k) in enumerate(senders):
        sender = lax.rem(z - k + planes, planes) * SHARDS + (y ^ flip_y) * 2 + (c ^ flip_c)
        copy = pltpu.make_async_copy(
            pieces[piece].at[pl.ds(row, KV_ROWS)], held.at[sender], sems.at[i]
        )
        copy.start()
        copies.append(copy)
    return copies


def collect_kernel(n, senders, pos_ref, *refs):
    *pieces, held, sems = refs
    for copy in place_pieces(n, senders, pos_ref[0], pieces, held, sems):
        copy.wait()


def routed_kernel(n, senders, pos_ref, gain_ref, qs_ref, xs_ref, facts_ref, _, *refs):
    planes = n // SHARDS
    count = len(senders)
    pieces, outs, held = refs[:3], refs[3 : 3 + planes], refs[3 + planes]
    acc, bias, q_scr, stack, state, gain, sems = refs[4 + planes :]
    pos = pos_ref[0]
    copies = place_pieces(n, senders, pos, pieces, held, sems)
    copies.append(pltpu.make_async_copy(gain_ref, gain, sems.at[count]))
    copies[-1].start()
    for copy in copies:
        copy.wait()
    starts = doc_starts(n, pos, held)
    lanes = q_scr.shape[2]
    rows = lanes // GROUP
    base = (pos * TILE).astype(F32)
    width = state.shape[1] // CUT
    row = numbers((CUT * rows, 1), 0)
    plane, rest = split(row, PIECE)
    chunk, slot = split(rest, CAP)
    order = one_hot(chunk * rows + plane * CAP + slot, CUT * rows)
    for part in range(xs_ref.shape[0] // rows):
        at = slice(part * lanes, (part + 1) * lanes)
        q_scr[...] = qs_ref[:, :, at]
        done = flash(
            pos,
            held,
            [(q_scr.at[h], h, acc.at[h]) for h in range(KV_HEADS)],
            bias,
            facts_ref[0:1, at] + base,
            starts_of(facts_ref[1:2, at], starts),
        )
        for h in range(KV_HEADS):
            stack[...] = done[h]
            for g in range(GROUP):
                lane = (h * GROUP + g) * HEAD
                state[:, lane : lane + HEAD] = (
                    xs_ref[part * rows : (part + 1) * rows, lane : lane + HEAD]
                    + stack[pl.ds(g, rows, stride=GROUP), :]
                )
        hidden = state[...]
        mean = jnp.mean(hidden * hidden, axis=1, keepdims=True)
        normed = hidden * lax.rsqrt(mean + 1e-06) * gain[...]
        chunks = [normed[:, q * width : (q + 1) * width] for q in range(CUT)]
        sent = dot(order, jnp.concatenate(chunks, axis=0).astype(BF16))
        for k in range(rows // CAP):
            outs[part * (rows // CAP) + k][...] = sent[k * PIECE : (k + 1) * PIECE].astype(BF16)


def expert_kernel(n, count, *refs):
    pieces = refs[:count]
    wg, wu, wd = refs[count : count + 3]
    gather, spread, _, keep_ref, send_ref, rows = refs[count + 3 :]
    step = pieces[0].shape[1]
    senders = min(n, 16)
    size, total = senders * PIECE, n * PIECE
    half = total // 2
    kept = senders * CAP
    for at in range(0, total, size):
        parts, first = [], 0
        for piece in pieces:
            low, high = max(at - first, 0), min(at + size - first, piece.shape[0])
            if low < high:
                parts.append(piece[low:high, :].astype(F32))
            first += piece.shape[0]
        came = dot(gather[...], jnp.concatenate(parts, axis=0).astype(BF16)).astype(BF16)
        for q in range(CUT):
            rows[:, q * step : (q + 1) * step] = came[q * kept : (q + 1) * kept]
        gate = dot(rows[...], wg[...])
        up = dot(rows[...], wu[...])
        act = (gate / (1.0 + jnp.exp(-gate)) * up).astype(BF16)
        parts = [dot(act, wd[:, q * step : (q + 1) * step]).astype(BF16) for q in range(CUT)]
        out = dot(spread[...], jnp.concatenate(parts, axis=0)).astype(BF16)
        if size > half:
            keep_ref[...] = out[:half]
            send_ref[...] = out[half:]
        elif at < half:
            keep_ref[at : at + size] = out
        else:
            send_ref[at - half : at - half + size] = out


def own_kernel(n, heads, loads, pos_ref, held, q_ref, x_ref, _, *refs):
    sources, (h_ref, done_ref) = refs[:loads], refs[loads : loads + 2]
    targets = refs[loads + 2 : 2 * loads + 2]
    bias, sems, *scratch = refs[2 * loads + 2 :]
    moves = [
        pltpu.make_async_copy(source.at[0], target, sems.at[i])
        for i, (source, target) in enumerate(zip(sources, targets))
    ]
    for move in moves:
        move.start()
    done_ref[...] = jnp.zeros((8, TILE), F32)
    pos = pos_ref[0]
    starts = doc_starts(n, pos, held)
    first = starts_of(held[pos, TILE:KV_ROWS, 0:HEAD].astype(F32)[0:1], starts)
    place = (pos * TILE + lax.broadcasted_iota(jnp.int32, (1, TILE), 1)).astype(F32)
    chains = []
    for i, (h, own) in enumerate(by_kv_head(heads)):
        queries, acc = scratch[2 * i : 2 * i + 2]
        chains.append((queries, h, acc))
        for j, a in enumerate(own):
            terms = two_terms(q_ref[:, a * HEAD : (a + 1) * HEAD].astype(F32).T)
            for t, term in enumerate(terms):
                queries[t * HEAD : (t + 1) * HEAD, j * TILE : (j + 1) * TILE] = term
    done = jnp.concatenate(flash(pos, held, chains, bias, place, first), axis=0)
    for j, a in enumerate(heads):
        h_ref[:, j * HEAD : (j + 1) * HEAD] = (
            x_ref[:, a * HEAD : (a + 1) * HEAD].astype(F32) + done[j * TILE : (j + 1) * TILE]
        )
    for move in moves:
        move.wait()


def combine_kernel(planes, widths, mix_ref, *refs):
    count = len(widths)
    halves, parts = refs[:count], refs[count : count + planes]
    _, out_ref, buffer, sems = refs[count + planes :]
    slots = planes * SLOTS
    came = jnp.concatenate([p[...].astype(F32) for p in parts], axis=0).astype(BF16)
    order = one_hot(travel_row(numbers((CUT * slots, 1), 0), planes, SLOTS), planes * PIECE)
    came = dot(order, came).astype(BF16)
    size = buffer.shape[1] // CUT
    moves = []
    for q in range(CUT):
        rows = came[q * slots : (q + 1) * slots]
        part = dot(mix_ref[...], jnp.concatenate([rows, rows], axis=0))
        at = 0
        for h, width in zip(halves, widths):
            low, high = max(at, q * size), min(at + width, (q + 1) * size)
            if low < high:
                buffer[:, low:high] = (
                    h[:, low - at : high - at] + part[:, low - q * size : high - q * size]
                ).astype(BF16)
            at += width
        columns = pl.ds(q * size, size)
        moves.append(
            pltpu.make_async_copy(buffer.at[:, columns], out_ref.at[:, columns], sems.at[q])
        )
        moves[-1].start()
    for move in moves:
        move.wait()


def pin(x):
    return pltpu.with_memory_space_constraint(x, pltpu.HBM)


def params(mib):
    return pltpu.CompilerParams(vmem_limit_bytes=mib * 1024 * 1024)


def local(
    resid, queries, keys, values, doc_ids, norm_gain, routes, route_weights, w_gate, w_up, w_down
):
    n = lax.axis_size("expert")
    planes = n // SHARDS
    pos = lax.axis_index("expert").astype(jnp.int32).reshape(1)
    tokens, width = queries.shape
    hidden = w_gate.shape[2]
    routes_t = routes.T
    gates_t = route_weights.T
    docs = doc_ids.reshape(1, tokens)
    small = 24 if n <= 16 else 60
    back = reach(n)

    packed = pl.pallas_call(
        pack_kernel,
        out_shape=jax.ShapeDtypeStruct((KV_ROWS, 4 * HEAD), BF16),
        in_specs=[HBM] * 3,
        out_specs=VMEM,
        scratch_shapes=[
            pltpu.VMEM((1, tokens), jnp.int32),
            pltpu.VMEM((tokens, KV_HEADS * HEAD), BF16),
            pltpu.SemaphoreType.DMA((3,)),
        ],
        compiler_params=params(8),
        name="pack",
    )(pin(docs), pin(keys), pin(values))

    def move(value, pairs):
        return lax.ppermute(value, "expert", pairs)

    def needed(k, y_from, y_to):
        gaps = [
            k * SHARDS + 2 * (y_to - y_from) + (to - of) for to in range(2) for of in range(2)
        ]
        return any(0 <= gap <= back for gap in gaps)

    far = max(k for k in range(planes) if any(needed(k, a, b) for a in (0, 1) for b in (0, 1)))
    size = min(n // 2, 16) * PIECE
    q_rows, x_rows, facts, mix, gather, spread = pl.pallas_call(
        functools.partial(select_kernel, planes),
        out_shape=[
            jax.ShapeDtypeStruct((KV_HEADS, 2 * HEAD, planes * CAP * GROUP), BF16),
            jax.ShapeDtypeStruct((planes * CAP, width), F32),
            jax.ShapeDtypeStruct((8, planes * CAP * GROUP), F32),
            jax.ShapeDtypeStruct((tokens, 2 * planes * SLOTS), BF16),
            jax.ShapeDtypeStruct((size, size), BF16),
            jax.ShapeDtypeStruct((size, size), BF16),
        ],
        in_specs=[SMEM] + [HBM] * 5,
        out_specs=[VMEM] * 6,
        scratch_shapes=[
            pltpu.VMEM(routes_t.shape, jnp.int32),
            pltpu.VMEM(docs.shape, jnp.int32),
            pltpu.VMEM(queries.shape, BF16),
            pltpu.VMEM(resid.shape, BF16),
            pltpu.VMEM(gates_t.shape, F32),
            pltpu.VMEM((planes * CAP * GROUP, HEAD), F32),
            pltpu.SemaphoreType.DMA((5,)),
        ],
        compiler_params=params(small),
        name="select",
    )(pos, *map(pin, (routes_t, docs, queries, resid, gates_t)))

    flip_y = [(s, s ^ 2) for s in range(n)]
    flip_c = [(s, s ^ 1) for s in range(n)]
    jump = {s: s + far * SHARDS - 2 for s in range(n - far * SHARDS) if s & 2}
    jump.update({to: s for s, to in jump.items()})
    jumped = move(packed, [(s, jump.get(s, s)) for s in range(n)])
    along = [packed]
    for k in range(1, far):
        below = (k - 1) * SHARDS
        pairs = [
            (s, s if s < below else s + SHARDS if s + SHARDS < n else s % SHARDS + below)
            for s in range(n)
        ]
        along.append(move(along[-1], pairs))
    across = []
    for k in range(far):
        if k == 1:
            passed, across, q_rows = lax.optimization_barrier((along[1], across, q_rows))
            across.append(move(passed, [(s, s ^ 2 if s >= SHARDS else s) for s in range(n)]))
            continue
        across.append(move(along[k], [(s, s ^ 2 if s >= k * SHARDS else s) for s in range(n)]))
    early, late = along + across[:-1], [across[-1], jumped]
    sides = [(0, k) for k in range(far)] + [(1, k) for k in range(far - 1)]
    late_sides = [(1, far - 1), (1, far)]
    early.append(move(jnp.concatenate(early, axis=0), flip_c))
    early_senders = [(i, 0, 0, *side) for i, side in enumerate(sides)]
    early_senders += [(len(sides), i * KV_ROWS, 1, *side) for i, side in enumerate(sides)]
    late_senders = [(i, 0, 0, *side) for i, side in enumerate(late_sides)]
    late_senders += [(2, i * KV_ROWS, 1, *side) for i, side in enumerate(late_sides)]
    held_shape = jax.ShapeDtypeStruct((n, KV_ROWS, 4 * HEAD), BF16)
    held = pl.pallas_call(
        functools.partial(collect_kernel, n, early_senders),
        out_shape=held_shape,
        in_specs=[SMEM] + [ANY] * len(early),
        out_specs=VMEM,
        scratch_shapes=[pltpu.SemaphoreType.DMA((len(early_senders),))],
        compiler_params=params(small),
        cost_estimate=pl.CostEstimate(flops=0, bytes_accessed=1000, transcendentals=0),
        name="collect",
    )(pos, *early)

    lanes = min(planes, 4) * CAP * GROUP
    late[0], held = lax.optimization_barrier((late[0], held))
    late.append(move(jnp.concatenate(late, axis=0), flip_c))
    *sent, held = pl.pallas_call(
        functools.partial(routed_kernel, n, late_senders),
        out_shape=[jax.ShapeDtypeStruct((PIECE, width // CUT), BF16)] * planes
        + [held_shape],
        in_specs=[SMEM, HBM] + [VMEM] * 4 + [ANY] * len(late),
        out_specs=[VMEM] * (planes + 1),
        scratch_shapes=[
            pltpu.VMEM((KV_HEADS, HEAD + EXTRA, lanes), F32),
            pltpu.VMEM((KEYS, lanes), F32),
            pltpu.VMEM((KV_HEADS, 2 * HEAD, lanes), BF16),
            pltpu.VMEM((lanes, HEAD), F32),
            pltpu.VMEM((lanes // GROUP, width), F32),
            pltpu.VMEM((1, width), F32),
            pltpu.SemaphoreType.DMA((len(late_senders) + 1,)),
        ],
        input_output_aliases={5: planes},
        compiler_params=params(small),
        name="routed",
    )(pos, pin(norm_gain.reshape(1, width)), q_rows, x_rows, facts, held, *late)

    def own(heads, after, *sources):
        lanes = [len(own) * TILE for _, own in by_kv_head(heads)]
        return pl.pallas_call(
            functools.partial(own_kernel, n, heads, len(sources)),
            out_shape=[
                jax.ShapeDtypeStruct((tokens, len(heads) * HEAD), F32),
                jax.ShapeDtypeStruct((8, TILE), F32),
            ]
            + [jax.ShapeDtypeStruct(w.shape[1:], BF16) for w in sources],
            in_specs=[SMEM, VMEM, VMEM, VMEM, ANY] + [HBM] * len(sources),
            out_specs=[VMEM] * (2 + len(sources)),
            scratch_shapes=[pltpu.VMEM((KEYS, TILE), F32), pltpu.SemaphoreType.DMA((3,))]
            + [
                shape
                for count in lanes
                for shape in (
                    pltpu.VMEM((2 * HEAD, count), BF16),
                    pltpu.VMEM((HEAD + EXTRA, count), F32),
                )
            ],
            compiler_params=params(small),
            cost_estimate=pl.CostEstimate(
                flops=2_000_000_000, bytes_accessed=8_000_000, transcendentals=2_000_000
            ),
            name="own",
        )(pos, held, queries, resid, after, *map(pin, sources))

    half0, done, *weights = own(range(10), sent[0], w_gate, w_up, w_down)
    half1, late = own(range(10, GROUP), done)
    halves = [half0, half1]

    come = [
        move(sent[k], [(s, (s + k * SHARDS) % n) for s in range(n)]) for k in range(1, planes)
    ]
    next_door = move(sent[0], flip_y)
    come, next_door, done = lax.optimization_barrier((come, next_door, done))
    here = [sent[0], jnp.concatenate(come, axis=0)]
    there = [next_door, move(here[1], flip_y)]
    mate = move(jnp.concatenate(here, axis=0), flip_c)
    half = jax.ShapeDtypeStruct((n * PIECE // 4, width // CUT), BF16)

    def expert(pieces, after):
        return pl.pallas_call(
            functools.partial(expert_kernel, n // 2, len(pieces)),
            out_shape=[half, half],
            in_specs=[VMEM] * (len(pieces) + 5) + [ANY],
            out_specs=[VMEM, VMEM],
            scratch_shapes=[pltpu.VMEM((min(n // 2, 16) * CAP, width), BF16)],
            compiler_params=params(16),
            cost_estimate=pl.CostEstimate(
                flops=600_000_000, bytes_accessed=2_000_000, transcendentals=20_000
            ),
            name="expert",
        )(*pieces, *weights, gather, spread, after)

    keep, send = expert(here + [mate], done)
    there, late, keep = lax.optimization_barrier((there, late, keep))
    mine = keep.astype(F32) + move(send, flip_c).astype(F32)
    mate = move(jnp.concatenate(there, axis=0), flip_c)
    keep, send = expert(there + [mate], late)
    half2, done = own(range(GROUP, QUERY_HEADS), keep)
    halves.append(half2)
    theirs = keep.astype(F32) + move(send, flip_c).astype(F32)
    other = move(theirs.astype(BF16), flip_y)
    other, done = lax.optimization_barrier((other, done))
    total = (mine + other.astype(F32)).astype(BF16)
    parts = [total[:PIECE]]
    for k in range(1, planes):
        parts.append(
            move(
                total[k * PIECE : (k + 1) * PIECE], [(s, (s - k * SHARDS) % n) for s in range(n)]
            )
        )

    widths = [h.shape[1] for h in halves]
    return pl.pallas_call(
        functools.partial(combine_kernel, planes, widths),
        out_shape=jax.ShapeDtypeStruct((tokens, width), BF16),
        in_specs=[VMEM] * (1 + len(halves) + planes) + [ANY],
        out_specs=HBM,
        scratch_shapes=[pltpu.VMEM((tokens, width), BF16), pltpu.SemaphoreType.DMA((CUT,))],
        compiler_params=params(small),
        name="combine",
    )(mix, *halves, *parts, done)


def solution(mesh):
    rows = P(("groups", "expert"), None)
    in_specs = (rows,) * 4 + (P(("groups", "expert")), P(), rows, rows) + (
        P("expert", None, None),
    ) * 3
    return jax.shard_map(local, mesh=mesh, in_specs=in_specs, out_specs=rows, check_vma=False)
```

```python
import functools
import math

import jax
import jax.numpy as jnp
from jax import lax
from jax.experimental import pallas as pl
from jax.experimental.pallas import tpu as pltpu
from jax.sharding import PartitionSpec as P

HEAD = 128
QUERY_HEADS = 32
KV_HEADS = 2
GROUP = QUERY_HEADS // KV_HEADS
SHARDS = 4
CAP = 6
SLOTS = 8
CUT = 4
PIECE = CUT * CAP
TILE = 128
KEYS = 256
KV_ROWS = TILE + 16
SCALE = math.log2(math.e) / math.sqrt(HEAD)
LOW = -1e30
EXTRA = 16
F32 = jnp.float32
BF16 = jnp.bfloat16
VMEM = pl.BlockSpec(memory_space=pltpu.VMEM)
SMEM = pl.BlockSpec(memory_space=pltpu.SMEM)
ANY = pl.BlockSpec(memory_space=pl.ANY)
HBM = pl.BlockSpec(memory_space=pltpu.HBM)


def dot(a, b, ca=1, cb=0):
    return lax.dot_general(a, b, (((ca,), (cb,)), ((), ())), preferred_element_type=F32)


def reach(n):
    longest = n * TILE // 2 + 256
    return (longest - 1 + TILE - 1) // TILE


def slot_rows(routes, experts):
    members = jnp.concatenate(
        [jnp.max((routes == e).astype(F32), axis=0, keepdims=True) for e in experts], axis=0
    )
    count = len(experts)
    padded = -(-count // 8) * 8
    wide = members
    if padded > count:
        wide = jnp.concatenate([members, jnp.zeros((padded - count, TILE), F32)], axis=0)
    before = lax.broadcasted_iota(jnp.int32, (TILE, TILE), 0) < lax.broadcasted_iota(
        jnp.int32, (TILE, TILE), 1
    )
    ranks = dot(wide.astype(BF16), before.astype(F32).astype(BF16))
    return members, ranks


def one_hot(targets, count):
    shape = (targets.shape[0], count) if targets.shape[1] == 1 else (count, targets.shape[1])
    axis = 1 if targets.shape[1] == 1 else 0
    places = lax.broadcasted_iota(jnp.int32, shape, axis).astype(F32)
    return jnp.where(places == targets, 1.0, 0.0).astype(BF16)


def split(x, size):
    whole = jnp.floor((x + 0.5) / size)
    return whole, x - whole * size


def travel_row(x, senders, slots):
    chunk, rest = split(x, senders * slots)
    sender, slot = split(rest, slots)
    return jnp.where(slot < CAP, sender * PIECE + chunk * CAP + slot, -1.0)


def numbers(shape, axis):
    return lax.broadcasted_iota(jnp.int32, shape, axis).astype(F32)


def pack_kernel(docs_ref, keys_ref, values_ref, out_ref, docs, values, sems):
    moves = [
        pltpu.make_async_copy(values_ref, values, sems.at[0]),
        pltpu.make_async_copy(docs_ref, docs, sems.at[1]),
        pltpu.make_async_copy(
            keys_ref, out_ref.at[pl.ds(0, TILE), pl.ds(0, KV_HEADS * HEAD)], sems.at[2]
        ),
    ]
    for move in moves:
        move.start()
    moves[0].wait()
    for h in range(KV_HEADS):
        out_ref[0:TILE, (KV_HEADS + h) * HEAD : (KV_HEADS + h + 1) * HEAD] = (
            values[:, h * HEAD : (h + 1) * HEAD].astype(F32).T.astype(BF16)
        )
    moves[1].wait()
    out_ref[TILE:KV_ROWS, :] = jnp.zeros((KV_ROWS - TILE, 4 * HEAD), BF16)
    out_ref[TILE:KV_ROWS, 0:HEAD] = jnp.broadcast_to(
        docs[...].astype(F32), (KV_ROWS - TILE, TILE)
    ).astype(BF16)
    moves[2].wait()


def select_kernel(planes, pos_ref, *refs):
    sources, (qs_ref, xs_ref, facts_ref, mix_ref, gather_ref, spread_ref) = refs[:5], refs[5:11]
    routes_ref, docs_ref, q_ref, x_ref, gates_ref, stack, sems = refs[11:]
    moves = [
        pltpu.make_async_copy(source, target, sems.at[i])
        for i, (source, target) in enumerate(zip(sources, refs[11:16]))
    ]
    for move in moves:
        move.start()
    for move in moves:
        move.wait()
    z = pos_ref[0] // SHARDS
    experts = [lax.rem(z + k, planes) for k in range(planes)]
    routes, gates = routes_ref[...], gates_ref[...]
    members, ranks = slot_rows(routes, experts)
    slot = lax.broadcasted_iota(jnp.int32, (SLOTS, TILE), 0).astype(F32)
    mix = []
    for k, e in enumerate(experts):
        gate = jnp.sum(jnp.where(routes == e, gates, 0.0), axis=0, keepdims=True)
        mix.append(jnp.where(ranks[k : k + 1] == slot, gate, 0.0))
    mix = jnp.concatenate(mix, axis=0).T
    mix_high = mix.astype(BF16)
    mix_ref[:, : planes * SLOTS] = mix_high
    mix_ref[:, planes * SLOTS :] = (mix - mix_high.astype(F32)).astype(BF16)
    size = gather_ref.shape[0]
    gather_ref[...] = one_hot(travel_row(numbers((size, 1), 0), size // PIECE, CAP), size)
    spread_ref[...] = one_hot(travel_row(numbers((1, size), 1), size // PIECE, CAP), size)
    docs = docs_ref[...].astype(F32)
    token = lax.broadcasted_iota(jnp.int32, (1, TILE), 1).astype(F32)
    facts = jnp.concatenate(
        [token, docs, jnp.ones((1, TILE), F32), jnp.zeros((5, TILE), F32)], axis=0
    ).astype(BF16)
    picks = [
        jnp.where(ranks[k : k + 1] == slot, members[k : k + 1], 0.0) for k in range(planes)
    ]
    rows = planes * CAP
    plane, place = split(numbers((rows, 1), 0), CAP)
    compact = one_hot(plane * SLOTS + place, planes * SLOTS)
    chooser = dot(compact, jnp.concatenate(picks, axis=0).astype(BF16)).astype(BF16)
    lane, _ = split(numbers((rows * GROUP, 1), 0), GROUP)
    lane_pick = dot(one_hot(lane, rows), chooser).astype(BF16)
    known = dot(facts, lane_pick, 1, 1)
    facts_ref[...] = jnp.concatenate(
        [known[0:1], known[1:2] + (1.0 - known[2:3]) * docs[:, 0:1], known[2:]], axis=0
    )
    q_rows = dot(chooser, q_ref[...])
    xs_ref[...] = dot(chooser, x_ref[...])
    for h in range(KV_HEADS):
        for g in range(GROUP):
            a = h * GROUP + g
            stack[pl.ds(g, rows, stride=GROUP), :] = q_rows[:, a * HEAD : (a + 1) * HEAD]
        for i, term in enumerate(two_terms(stack[...].T)):
            qs_ref[h, i * HEAD : (i + 1) * HEAD, :] = term


def doc_starts(n, pos, held):
    sums = [jnp.zeros((1, TILE), F32) for _ in range(3)]
    for s in range(n):
        docs = held[s, TILE:KV_ROWS, 0:HEAD].astype(F32)[0:1]
        ahead = (pos - s < 0).astype(F32)
        behind = (pos - s > reach(n)).astype(F32)
        known = 1.0 - ahead - behind
        docs = jnp.where(known > 0.5, docs, 0.0) + 9.0 * ahead
        for d in range(3):
            sums[d] = sums[d] + jnp.where(docs < d + 1.0, 1.0, 0.0)
    return [jnp.sum(s, axis=1, keepdims=True) for s in sums]


def starts_of(docs, starts):
    first = jnp.zeros_like(docs)
    for d in range(3):
        first = jnp.where(docs == d + 1.0, starts[d], first)
    return first


def two_terms(x):
    scaled = x.astype(F32) * SCALE
    high = scaled.astype(BF16)
    return high, (scaled - high.astype(F32)).astype(BF16)


def key_steps(pos, place, first, bias_ref, step, state):
    low = jnp.min(first).astype(jnp.int32) // KEYS
    last = pos // (KEYS // TILE)
    clear = jnp.minimum((jnp.max(first).astype(jnp.int32) + KEYS - 1) // KEYS, last)

    def edge(j, carried):
        kb = jnp.where(j < clear - low, low + j, last)
        key_at = (kb * KEYS + lax.broadcasted_iota(jnp.int32, (KEYS, 1), 0)).astype(F32)
        bias_ref[...] = jnp.where((key_at >= first) & (key_at <= place), 0.0, LOW)
        return step(kb, carried, True)

    state = lax.fori_loop(0, clear - low + 1, edge, state)
    return lax.fori_loop(clear, last, lambda kb, carried: step(kb, carried, False), state)


def by_kv_head(heads):
    groups = [(h, [a for a in heads if a // GROUP == h]) for h in range(KV_HEADS)]
    return [(h, own) for h, own in groups if own]


def keys_of(held, kb, h):
    keys = jnp.concatenate(
        [held[2 * kb + t, 0:TILE, h * HEAD : (h + 1) * HEAD] for t in range(2)], axis=0
    )
    return jnp.concatenate([keys, keys], axis=1)


def values_of(held, kb, h):
    at = (KV_HEADS + h) * HEAD
    values = jnp.concatenate(
        [held[2 * kb + t, 0:TILE, at : at + HEAD] for t in range(2)], axis=1
    )
    return jnp.concatenate([values, jnp.ones((EXTRA, KEYS), BF16)], axis=0)


def flash(pos, held, chains, bias_ref, place, first):
    for _, _, acc in chains:
        acc[...] = jnp.zeros(acc.shape, F32)

    def step(kb, tops, masked):
        out = []
        for (queries, h, acc), old in zip(chains, tops):
            scores = dot(keys_of(held, kb, h), queries[...])
            if masked:
                copies = scores.shape[1] // bias_ref.shape[1]
                scores = scores + jnp.concatenate([bias_ref[...]] * copies, axis=1)
            top = jnp.maximum(old, jnp.max(scores, axis=0, keepdims=True))
            weights = jnp.exp2(scores - top).astype(BF16)
            acc[...] = acc[...] * jnp.exp2(old - top) + dot(values_of(held, kb, h), weights)
            out.append(top)
        return tuple(out)

    tops = tuple(jnp.full((1, acc.shape[1]), LOW, F32) for _, _, acc in chains)
    key_steps(pos, place, first, bias_ref, step, tops)
    return [(acc[0:HEAD, :] / acc[HEAD : HEAD + 1, :]).T for _, _, acc in chains]


def place_pieces(n, senders, pos, pieces, held, sems):
    planes = n // SHARDS
    z, y, c = pos // SHARDS, (pos // 2) % 2, pos % 2
    copies = []
    for i, (piece, row, flip_c, flip_y, k) in enumerate(senders):
        sender = lax.rem(z - k + planes, planes) * SHARDS + (y ^ flip_y) * 2 + (c ^ flip_c)
        copy = pltpu.make_async_copy(
            pieces[piece].at[pl.ds(row, KV_ROWS)], held.at[sender], sems.at[i]
        )
        copy.start()
        copies.append(copy)
    return copies


def collect_kernel(n, senders, pos_ref, *refs):
    *pieces, held, sems = refs
    for copy in place_pieces(n, senders, pos_ref[0], pieces, held, sems):
        copy.wait()


def routed_kernel(n, senders, pos_ref, gain_ref, qs_ref, xs_ref, facts_ref, _, *refs):
    planes = n // SHARDS
    count = len(senders)
    pieces, outs, held = refs[:2], refs[2 : 2 + planes], refs[2 + planes]
    acc, bias, q_scr, stack, state, gain, sems = refs[3 + planes :]
    pos = pos_ref[0]
    copies = place_pieces(n, senders, pos, pieces, held, sems)
    copies.append(pltpu.make_async_copy(gain_ref, gain, sems.at[count]))
    copies[-1].start()
    for copy in copies:
        copy.wait()
    starts = doc_starts(n, pos, held)
    lanes = q_scr.shape[2]
    rows = lanes // GROUP
    base = (pos * TILE).astype(F32)
    width = state.shape[1] // CUT
    row = numbers((CUT * rows, 1), 0)
    plane, rest = split(row, PIECE)
    chunk, slot = split(rest, CAP)
    order = one_hot(chunk * rows + plane * CAP + slot, CUT * rows)
    for part in range(xs_ref.shape[0] // rows):
        at = slice(part * lanes, (part + 1) * lanes)
        q_scr[...] = qs_ref[:, :, at]
        done = flash(
            pos,
            held,
            [(q_scr.at[h], h, acc.at[h]) for h in range(KV_HEADS)],
            bias,
            facts_ref[0:1, at] + base,
            starts_of(facts_ref[1:2, at], starts),
        )
        for h in range(KV_HEADS):
            stack[...] = done[h]
            for g in range(GROUP):
                lane = (h * GROUP + g) * HEAD
                state[:, lane : lane + HEAD] = (
                    xs_ref[part * rows : (part + 1) * rows, lane : lane + HEAD]
                    + stack[pl.ds(g, rows, stride=GROUP), :]
                )
        hidden = state[...]
        mean = jnp.mean(hidden * hidden, axis=1, keepdims=True)
        normed = hidden * lax.rsqrt(mean + 1e-06) * gain[...]
        chunks = [normed[:, q * width : (q + 1) * width] for q in range(CUT)]
        sent = dot(order, jnp.concatenate(chunks, axis=0).astype(BF16))
        for k in range(rows // CAP):
            outs[part * (rows // CAP) + k][...] = sent[k * PIECE : (k + 1) * PIECE].astype(BF16)


def expert_kernel(n, count, *refs):
    pieces = refs[:count]
    wg, wu, wd = refs[count : count + 3]
    gather, spread, _, keep_ref, send_ref, rows = refs[count + 3 :]
    step = pieces[0].shape[1]
    senders = min(n, 16)
    size, total = senders * PIECE, n * PIECE
    half = total // 2
    kept = senders * CAP
    for at in range(0, total, size):
        parts, first = [], 0
        for piece in pieces:
            low, high = max(at - first, 0), min(at + size - first, piece.shape[0])
            if low < high:
                parts.append(piece[low:high, :].astype(F32))
            first += piece.shape[0]
        came = dot(gather[...], jnp.concatenate(parts, axis=0).astype(BF16)).astype(BF16)
        for q in range(CUT):
            rows[:, q * step : (q + 1) * step] = came[q * kept : (q + 1) * kept]
        gate = dot(rows[...], wg[...])
        up = dot(rows[...], wu[...])
        act = (gate / (1.0 + jnp.exp(-gate)) * up).astype(BF16)
        parts = [dot(act, wd[:, q * step : (q + 1) * step]).astype(BF16) for q in range(CUT)]
        out = dot(spread[...], jnp.concatenate(parts, axis=0)).astype(BF16)
        if size > half:
            keep_ref[...] = out[:half]
            send_ref[...] = out[half:]
        elif at < half:
            keep_ref[at : at + size] = out
        else:
            send_ref[at - half : at - half + size] = out


def own_kernel(n, heads, loads, pos_ref, held, q_ref, x_ref, _, *refs):
    sources, (h_ref, done_ref) = refs[:loads], refs[loads : loads + 2]
    targets = refs[loads + 2 : 2 * loads + 2]
    bias, sems, *scratch = refs[2 * loads + 2 :]
    moves = [
        pltpu.make_async_copy(source.at[0], target, sems.at[i])
        for i, (source, target) in enumerate(zip(sources, targets))
    ]
    for move in moves:
        move.start()
    done_ref[...] = jnp.zeros((8, TILE), F32)
    pos = pos_ref[0]
    starts = doc_starts(n, pos, held)
    first = starts_of(held[pos, TILE:KV_ROWS, 0:HEAD].astype(F32)[0:1], starts)
    place = (pos * TILE + lax.broadcasted_iota(jnp.int32, (1, TILE), 1)).astype(F32)
    chains = []
    for i, (h, own) in enumerate(by_kv_head(heads)):
        queries, acc = scratch[2 * i : 2 * i + 2]
        chains.append((queries, h, acc))
        for j, a in enumerate(own):
            terms = two_terms(q_ref[:, a * HEAD : (a + 1) * HEAD].astype(F32).T)
            for t, term in enumerate(terms):
                queries[t * HEAD : (t + 1) * HEAD, j * TILE : (j + 1) * TILE] = term
    done = jnp.concatenate(flash(pos, held, chains, bias, place, first), axis=0)
    for j, a in enumerate(heads):
        h_ref[:, j * HEAD : (j + 1) * HEAD] = (
            x_ref[:, a * HEAD : (a + 1) * HEAD].astype(F32) + done[j * TILE : (j + 1) * TILE]
        )
    for move in moves:
        move.wait()


def combine_kernel(planes, widths, mix_ref, *refs):
    count = len(widths)
    halves, parts = refs[:count], refs[count : count + planes]
    _, out_ref, buffer, sems = refs[count + planes :]
    slots = planes * SLOTS
    came = jnp.concatenate([p[...].astype(F32) for p in parts], axis=0).astype(BF16)
    order = one_hot(travel_row(numbers((CUT * slots, 1), 0), planes, SLOTS), planes * PIECE)
    came = dot(order, came).astype(BF16)
    size = buffer.shape[1] // CUT
    moves = []
    for q in range(CUT):
        rows = came[q * slots : (q + 1) * slots]
        part = dot(mix_ref[...], jnp.concatenate([rows, rows], axis=0))
        at = 0
        for h, width in zip(halves, widths):
            low, high = max(at, q * size), min(at + width, (q + 1) * size)
            if low < high:
                buffer[:, low:high] = (
                    h[:, low - at : high - at] + part[:, low - q * size : high - q * size]
                ).astype(BF16)
            at += width
        columns = pl.ds(q * size, size)
        moves.append(
            pltpu.make_async_copy(buffer.at[:, columns], out_ref.at[:, columns], sems.at[q])
        )
        moves[-1].start()
    for move in moves:
        move.wait()


def pin(x):
    return pltpu.with_memory_space_constraint(x, pltpu.HBM)


def params(mib):
    return pltpu.CompilerParams(vmem_limit_bytes=mib * 1024 * 1024)


def local(
    resid, queries, keys, values, doc_ids, norm_gain, routes, route_weights, w_gate, w_up, w_down
):
    n = lax.axis_size("expert")
    planes = n // SHARDS
    pos = lax.axis_index("expert").astype(jnp.int32).reshape(1)
    tokens, width = queries.shape
    hidden = w_gate.shape[2]
    routes_t = routes.T
    gates_t = route_weights.T
    docs = doc_ids.reshape(1, tokens)
    small = 24 if n <= 16 else 60
    back = reach(n)

    packed = pl.pallas_call(
        pack_kernel,
        out_shape=jax.ShapeDtypeStruct((KV_ROWS, 4 * HEAD), BF16),
        in_specs=[HBM] * 3,
        out_specs=VMEM,
        scratch_shapes=[
            pltpu.VMEM((1, tokens), jnp.int32),
            pltpu.VMEM((tokens, KV_HEADS * HEAD), BF16),
            pltpu.SemaphoreType.DMA((3,)),
        ],
        compiler_params=params(8),
        name="pack",
    )(pin(docs), pin(keys), pin(values))

    def move(value, pairs):
        return lax.ppermute(value, "expert", pairs)

    def needed(k, y_from, y_to):
        gaps = [
            k * SHARDS + 2 * (y_to - y_from) + (to - of) for to in range(2) for of in range(2)
        ]
        return any(0 <= gap <= back for gap in gaps)

    far = max(k for k in range(planes) if any(needed(k, a, b) for a in (0, 1) for b in (0, 1)))
    size = min(n // 2, 16) * PIECE
    q_rows, x_rows, facts, mix, gather, spread = pl.pallas_call(
        functools.partial(select_kernel, planes),
        out_shape=[
            jax.ShapeDtypeStruct((KV_HEADS, 2 * HEAD, planes * CAP * GROUP), BF16),
            jax.ShapeDtypeStruct((planes * CAP, width), F32),
            jax.ShapeDtypeStruct((8, planes * CAP * GROUP), F32),
            jax.ShapeDtypeStruct((tokens, 2 * planes * SLOTS), BF16),
            jax.ShapeDtypeStruct((size, size), BF16),
            jax.ShapeDtypeStruct((size, size), BF16),
        ],
        in_specs=[SMEM] + [HBM] * 5,
        out_specs=[VMEM] * 6,
        scratch_shapes=[
            pltpu.VMEM(routes_t.shape, jnp.int32),
            pltpu.VMEM(docs.shape, jnp.int32),
            pltpu.VMEM(queries.shape, BF16),
            pltpu.VMEM(resid.shape, BF16),
            pltpu.VMEM(gates_t.shape, F32),
            pltpu.VMEM((planes * CAP * GROUP, HEAD), F32),
            pltpu.SemaphoreType.DMA((5,)),
        ],
        compiler_params=params(small),
        name="select",
    )(pos, *map(pin, (routes_t, docs, queries, resid, gates_t)))

    flip_y = [(s, s ^ 2) for s in range(n)]
    flip_c = [(s, s ^ 1) for s in range(n)]
    jump = {s: s + far * SHARDS - 2 for s in range(n - far * SHARDS) if s & 2}
    jump.update({to: s for s, to in jump.items()})
    jumped = move(packed, [(s, jump.get(s, s)) for s in range(n)])
    along = [packed] + [
        move(packed, [(s, (s + k * SHARDS) % n) for s in range(n)]) for k in range(1, far)
    ]
    along[1], q_rows = lax.optimization_barrier((along[1], q_rows))
    across = []
    for k in range(far):
        if k > 1 and k == far - 1:
            along[k], across = lax.optimization_barrier((along[k], across))
        across.append(move(along[k], [(s, s ^ 2 if s >= k * SHARDS else s) for s in range(n)]))
    early, late = along + [jumped] + across[:-1], across[-1:]
    sides = [(0, k) for k in range(far)] + [(1, far)] + [(1, k) for k in range(far - 1)]
    early.append(move(jnp.concatenate(early, axis=0), flip_c))
    early_senders = [(i, 0, 0, *side) for i, side in enumerate(sides)]
    early_senders += [(len(sides), i * KV_ROWS, 1, *side) for i, side in enumerate(sides)]
    late_senders = [(flip, 0, flip, 1, far - 1) for flip in (0, 1)]
    held_shape = jax.ShapeDtypeStruct((n, KV_ROWS, 4 * HEAD), BF16)
    held = pl.pallas_call(
        functools.partial(collect_kernel, n, early_senders),
        out_shape=held_shape,
        in_specs=[SMEM] + [ANY] * len(early),
        out_specs=VMEM,
        scratch_shapes=[pltpu.SemaphoreType.DMA((len(early_senders),))],
        compiler_params=params(small),
        cost_estimate=pl.CostEstimate(flops=0, bytes_accessed=1000, transcendentals=0),
        name="collect",
    )(pos, *early)

    lanes = min(planes, 4) * CAP * GROUP
    late[0], held = lax.optimization_barrier((late[0], held))
    late.append(move(late[0], flip_c))
    *sent, held = pl.pallas_call(
        functools.partial(routed_kernel, n, late_senders),
        out_shape=[jax.ShapeDtypeStruct((PIECE, width // CUT), BF16)] * planes
        + [held_shape],
        in_specs=[SMEM, HBM] + [VMEM] * 4 + [ANY] * len(late),
        out_specs=[VMEM] * (planes + 1),
        scratch_shapes=[
            pltpu.VMEM((KV_HEADS, HEAD + EXTRA, lanes), F32),
            pltpu.VMEM((KEYS, lanes), F32),
            pltpu.VMEM((KV_HEADS, 2 * HEAD, lanes), BF16),
            pltpu.VMEM((lanes, HEAD), F32),
            pltpu.VMEM((lanes // GROUP, width), F32),
            pltpu.VMEM((1, width), F32),
            pltpu.SemaphoreType.DMA((len(late_senders) + 1,)),
        ],
        input_output_aliases={5: planes},
        compiler_params=params(small),
        name="routed",
    )(pos, pin(norm_gain.reshape(1, width)), q_rows, x_rows, facts, held, *late)

    def own(heads, after, *sources):
        lanes = [len(own) * TILE for _, own in by_kv_head(heads)]
        return pl.pallas_call(
            functools.partial(own_kernel, n, heads, len(sources)),
            out_shape=[
                jax.ShapeDtypeStruct((tokens, len(heads) * HEAD), F32),
                jax.ShapeDtypeStruct((8, TILE), F32),
            ]
            + [jax.ShapeDtypeStruct(w.shape[1:], BF16) for w in sources],
            in_specs=[SMEM, VMEM, VMEM, VMEM, ANY] + [HBM] * len(sources),
            out_specs=[VMEM] * (2 + len(sources)),
            scratch_shapes=[pltpu.VMEM((KEYS, TILE), F32), pltpu.SemaphoreType.DMA((3,))]
            + [
                shape
                for count in lanes
                for shape in (
                    pltpu.VMEM((2 * HEAD, count), BF16),
                    pltpu.VMEM((HEAD + EXTRA, count), F32),
                )
            ],
            compiler_params=params(small),
            cost_estimate=pl.CostEstimate(
                flops=2_000_000_000, bytes_accessed=8_000_000, transcendentals=2_000_000
            ),
            name="own",
        )(pos, held, queries, resid, after, *map(pin, sources))

    half0, done, *weights = own(range(10), sent[0], w_gate, w_up, w_down)
    half1, late = own(range(10, GROUP), done)
    halves = [half0, half1]

    come = [
        move(sent[k], [(s, (s + k * SHARDS) % n) for s in range(n)]) for k in range(1, planes)
    ]
    next_door = move(sent[0], flip_y)
    come, next_door, done = lax.optimization_barrier((come, next_door, done))
    here = [sent[0], jnp.concatenate(come, axis=0)]
    there = [next_door, move(here[1], flip_y)]
    mate = move(jnp.concatenate(here, axis=0), flip_c)
    half = jax.ShapeDtypeStruct((n * PIECE // 4, width // CUT), BF16)

    def expert(pieces, after):
        return pl.pallas_call(
            functools.partial(expert_kernel, n // 2, len(pieces)),
            out_shape=[half, half],
            in_specs=[VMEM] * (len(pieces) + 5) + [ANY],
            out_specs=[VMEM, VMEM],
            scratch_shapes=[pltpu.VMEM((min(n // 2, 16) * CAP, width), BF16)],
            compiler_params=params(16),
            cost_estimate=pl.CostEstimate(
                flops=600_000_000, bytes_accessed=2_000_000, transcendentals=20_000
            ),
            name="expert",
        )(*pieces, *weights, gather, spread, after)

    keep, send = expert(here + [mate], done)
    there, late, keep = lax.optimization_barrier((there, late, keep))
    mine = keep.astype(F32) + move(send, flip_c).astype(F32)
    mate = move(jnp.concatenate(there, axis=0), flip_c)
    keep, send = expert(there + [mate], late)
    half2, done = own(range(GROUP, QUERY_HEADS), keep)
    halves.append(half2)
    theirs = keep.astype(F32) + move(send, flip_c).astype(F32)
    other = move(theirs.astype(BF16), flip_y)
    other, done = lax.optimization_barrier((other, done))
    total = (mine + other.astype(F32)).astype(BF16)
    parts = [total[:PIECE]]
    for k in range(1, planes):
        parts.append(
            move(
                total[k * PIECE : (k + 1) * PIECE], [(s, (s - k * SHARDS) % n) for s in range(n)]
            )
        )

    widths = [h.shape[1] for h in halves]
    return pl.pallas_call(
        functools.partial(combine_kernel, planes, widths),
        out_shape=jax.ShapeDtypeStruct((tokens, width), BF16),
        in_specs=[VMEM] * (1 + len(halves) + planes) + [ANY],
        out_specs=HBM,
        scratch_shapes=[pltpu.VMEM((tokens, width), BF16), pltpu.SemaphoreType.DMA((CUT,))],
        compiler_params=params(small),
        name="combine",
    )(mix, *halves, *parts, done)


def solution(mesh):
    rows = P(("groups", "expert"), None)
    in_specs = (rows,) * 4 + (P(("groups", "expert")), P(), rows, rows) + (
        P("expert", None, None),
    ) * 3
    return jax.shard_map(local, mesh=mesh, in_specs=in_specs, out_specs=rows, check_vma=False)
```

```python
import functools
import math

import jax
import jax.numpy as jnp
from jax import lax
from jax.experimental import pallas as pl
from jax.experimental.pallas import tpu as pltpu
from jax.sharding import PartitionSpec as P

HEAD = 128
QUERY_HEADS = 32
KV_HEADS = 2
GROUP = QUERY_HEADS // KV_HEADS
SHARDS = 4
CAP = 6
SLOTS = 8
CUT = 4
PIECE = CUT * CAP
TILE = 128
KEYS = 512
STEP = KEYS // TILE
KV_ROWS = TILE + 16
SCALE = math.log2(math.e) / math.sqrt(HEAD)
LOW = -1e30
EXTRA = 16
F32 = jnp.float32
BF16 = jnp.bfloat16
VMEM = pl.BlockSpec(memory_space=pltpu.VMEM)
SMEM = pl.BlockSpec(memory_space=pltpu.SMEM)
ANY = pl.BlockSpec(memory_space=pl.ANY)
HBM = pl.BlockSpec(memory_space=pltpu.HBM)


def dot(a, b, ca=1, cb=0):
    return lax.dot_general(a, b, (((ca,), (cb,)), ((), ())), preferred_element_type=F32)


def reach(n):
    longest = n * TILE // 2 + 256
    return (longest - 1 + TILE - 1) // TILE


def slot_rows(routes, experts):
    members = jnp.concatenate(
        [jnp.max((routes == e).astype(F32), axis=0, keepdims=True) for e in experts], axis=0
    )
    count = len(experts)
    padded = -(-count // 8) * 8
    wide = members
    if padded > count:
        wide = jnp.concatenate([members, jnp.zeros((padded - count, TILE), F32)], axis=0)
    before = lax.broadcasted_iota(jnp.int32, (TILE, TILE), 0) < lax.broadcasted_iota(
        jnp.int32, (TILE, TILE), 1
    )
    ranks = dot(wide.astype(BF16), before.astype(F32).astype(BF16))
    return members, ranks


def one_hot(targets, count):
    shape = (targets.shape[0], count) if targets.shape[1] == 1 else (count, targets.shape[1])
    axis = 1 if targets.shape[1] == 1 else 0
    places = lax.broadcasted_iota(jnp.int32, shape, axis).astype(F32)
    return jnp.where(places == targets, 1.0, 0.0).astype(BF16)


def split(x, size):
    whole = jnp.floor((x + 0.5) / size)
    return whole, x - whole * size


def travel_row(x, senders, slots):
    chunk, rest = split(x, senders * slots)
    sender, slot = split(rest, slots)
    return jnp.where(slot < CAP, sender * PIECE + chunk * CAP + slot, -1.0)


def numbers(shape, axis):
    return lax.broadcasted_iota(jnp.int32, shape, axis).astype(F32)


def pack_kernel(docs_ref, keys_ref, values_ref, out_ref, docs, values, sems):
    moves = [
        pltpu.make_async_copy(values_ref, values, sems.at[0]),
        pltpu.make_async_copy(docs_ref, docs, sems.at[1]),
        pltpu.make_async_copy(
            keys_ref, out_ref.at[pl.ds(0, TILE), pl.ds(0, KV_HEADS * HEAD)], sems.at[2]
        ),
    ]
    for move in moves:
        move.start()
    moves[0].wait()
    for h in range(KV_HEADS):
        out_ref[0:TILE, (KV_HEADS + h) * HEAD : (KV_HEADS + h + 1) * HEAD] = (
            values[:, h * HEAD : (h + 1) * HEAD].astype(F32).T.astype(BF16)
        )
    moves[1].wait()
    out_ref[TILE:KV_ROWS, :] = jnp.zeros((KV_ROWS - TILE, 4 * HEAD), BF16)
    out_ref[TILE:KV_ROWS, 0:HEAD] = jnp.broadcast_to(
        docs[...].astype(F32), (KV_ROWS - TILE, TILE)
    ).astype(BF16)
    moves[2].wait()


def select_kernel(planes, pos_ref, *refs):
    sources, (qs_ref, xs_ref, facts_ref, mix_ref, gather_ref, spread_ref) = refs[:5], refs[5:11]
    routes_ref, docs_ref, q_ref, x_ref, gates_ref, stack, sems = refs[11:]
    moves = [
        pltpu.make_async_copy(source, target, sems.at[i])
        for i, (source, target) in enumerate(zip(sources, refs[11:16]))
    ]
    for move in moves:
        move.start()
    for move in moves:
        move.wait()
    z = pos_ref[0] // SHARDS
    experts = [lax.rem(z + k, planes) for k in range(planes)]
    routes, gates = routes_ref[...], gates_ref[...]
    members, ranks = slot_rows(routes, experts)
    slot = lax.broadcasted_iota(jnp.int32, (SLOTS, TILE), 0).astype(F32)
    mix = []
    for k, e in enumerate(experts):
        gate = jnp.sum(jnp.where(routes == e, gates, 0.0), axis=0, keepdims=True)
        mix.append(jnp.where(ranks[k : k + 1] == slot, gate, 0.0))
    mix = jnp.concatenate(mix, axis=0).T
    mix_high = mix.astype(BF16)
    mix_ref[:, : planes * SLOTS] = mix_high
    mix_ref[:, planes * SLOTS :] = (mix - mix_high.astype(F32)).astype(BF16)
    size = gather_ref.shape[0]
    gather_ref[...] = one_hot(travel_row(numbers((size, 1), 0), size // PIECE, CAP), size)
    spread_ref[...] = one_hot(travel_row(numbers((1, size), 1), size // PIECE, CAP), size)
    docs = docs_ref[...].astype(F32)
    token = lax.broadcasted_iota(jnp.int32, (1, TILE), 1).astype(F32)
    facts = jnp.concatenate(
        [token, docs, jnp.ones((1, TILE), F32), jnp.zeros((5, TILE), F32)], axis=0
    ).astype(BF16)
    picks = [
        jnp.where(ranks[k : k + 1] == slot, members[k : k + 1], 0.0) for k in range(planes)
    ]
    rows = planes * CAP
    plane, place = split(numbers((rows, 1), 0), CAP)
    compact = one_hot(plane * SLOTS + place, planes * SLOTS)
    chooser = dot(compact, jnp.concatenate(picks, axis=0).astype(BF16)).astype(BF16)
    lane, _ = split(numbers((rows * GROUP, 1), 0), GROUP)
    lane_pick = dot(one_hot(lane, rows), chooser).astype(BF16)
    known = dot(facts, lane_pick, 1, 1)
    facts_ref[...] = jnp.concatenate(
        [known[0:1], known[1:2] + (1.0 - known[2:3]) * docs[:, 0:1], known[2:]], axis=0
    )
    q_rows = dot(chooser, q_ref[...])
    xs_ref[...] = dot(chooser, x_ref[...])
    for h in range(KV_HEADS):
        for g in range(GROUP):
            a = h * GROUP + g
            stack[pl.ds(g, rows, stride=GROUP), :] = q_rows[:, a * HEAD : (a + 1) * HEAD]
        for i, term in enumerate(two_terms(stack[...].T)):
            qs_ref[h, i * HEAD : (i + 1) * HEAD, :] = term


def doc_starts(n, pos, held):
    sums = [jnp.zeros((1, TILE), F32) for _ in range(3)]
    for s in range(n):
        docs = held[s, TILE:KV_ROWS, 0:HEAD].astype(F32)[0:1]
        ahead = (pos - s < 0).astype(F32)
        behind = (pos - s > reach(n)).astype(F32)
        known = 1.0 - ahead - behind
        docs = jnp.where(known > 0.5, docs, 0.0) + 9.0 * ahead
        for d in range(3):
            sums[d] = sums[d] + jnp.where(docs < d + 1.0, 1.0, 0.0)
    return [jnp.sum(s, axis=1, keepdims=True) for s in sums]


def starts_of(docs, starts):
    first = jnp.zeros_like(docs)
    for d in range(3):
        first = jnp.where(docs == d + 1.0, starts[d], first)
    return first


def two_terms(x):
    scaled = x.astype(F32) * SCALE
    high = scaled.astype(BF16)
    return high, (scaled - high.astype(F32)).astype(BF16)


def key_steps(pos, place, first, bias_ref, step, state):
    low = jnp.min(first).astype(jnp.int32) // KEYS
    last = pos // STEP
    clear = jnp.minimum((jnp.max(first).astype(jnp.int32) + KEYS - 1) // KEYS, last)

    def edge(j, carried):
        kb = jnp.where(j < clear - low, low + j, last)
        key_at = (kb * KEYS + lax.broadcasted_iota(jnp.int32, (KEYS, 1), 0)).astype(F32)
        bias_ref[...] = jnp.where((key_at >= first) & (key_at <= place), 0.0, LOW)
        return step(kb, carried, True)

    state = lax.fori_loop(0, clear - low + 1, edge, state)
    return lax.fori_loop(clear, last, lambda kb, carried: step(kb, carried, False), state)


def by_kv_head(heads):
    groups = [(h, [a for a in heads if a // GROUP == h]) for h in range(KV_HEADS)]
    return [(h, own) for h, own in groups if own]


def keys_of(held, kb, h):
    keys = jnp.concatenate(
        [held[STEP * kb + t, 0:TILE, h * HEAD : (h + 1) * HEAD] for t in range(STEP)], axis=0
    )
    return jnp.concatenate([keys, keys], axis=1)


def values_of(held, kb, h):
    at = (KV_HEADS + h) * HEAD
    values = jnp.concatenate(
        [held[STEP * kb + t, 0:TILE, at : at + HEAD] for t in range(STEP)], axis=1
    )
    return jnp.concatenate([values, jnp.ones((EXTRA, KEYS), BF16)], axis=0)


def flash(pos, held, chains, bias_ref, place, first):
    for _, _, acc in chains:
        acc[...] = jnp.zeros(acc.shape, F32)

    def step(kb, tops, masked):
        out = []
        for (queries, h, acc), old in zip(chains, tops):
            scores = dot(keys_of(held, kb, h), queries[...])
            if masked:
                copies = scores.shape[1] // bias_ref.shape[1]
                scores = scores + jnp.concatenate([bias_ref[...]] * copies, axis=1)
            top = jnp.maximum(old, jnp.max(scores, axis=0, keepdims=True))
            weights = jnp.exp2(scores - top).astype(BF16)
            acc[...] = acc[...] * jnp.exp2(old - top) + dot(values_of(held, kb, h), weights)
            out.append(top)
        return tuple(out)

    tops = tuple(jnp.full((1, acc.shape[1]), LOW, F32) for _, _, acc in chains)
    key_steps(pos, place, first, bias_ref, step, tops)
    return [(acc[0:HEAD, :] / acc[HEAD : HEAD + 1, :]).T for _, _, acc in chains]


def place_pieces(n, senders, pos, pieces, held, sems):
    planes = n // SHARDS
    z, y, c = pos // SHARDS, (pos // 2) % 2, pos % 2
    copies = []
    for i, (piece, row, flip_c, flip_y, k) in enumerate(senders):
        sender = lax.rem(z - k + planes, planes) * SHARDS + (y ^ flip_y) * 2 + (c ^ flip_c)
        copy = pltpu.make_async_copy(
            pieces[piece].at[pl.ds(row, KV_ROWS)], held.at[sender], sems.at[i]
        )
        copy.start()
        copies.append(copy)
    return copies


def collect_kernel(n, senders, pos_ref, *refs):
    *pieces, held, sems = refs
    for copy in place_pieces(n, senders, pos_ref[0], pieces, held, sems):
        copy.wait()


def routed_kernel(n, senders, pos_ref, gain_ref, qs_ref, xs_ref, facts_ref, _, *refs):
    planes = n // SHARDS
    count = len(senders)
    pieces, outs, held = refs[:2], refs[2 : 2 + planes], refs[2 + planes]
    acc, bias, q_scr, stack, state, gain, sems = refs[3 + planes :]
    pos = pos_ref[0]
    copies = place_pieces(n, senders, pos, pieces, held, sems)
    copies.append(pltpu.make_async_copy(gain_ref, gain, sems.at[count]))
    copies[-1].start()
    for copy in copies:
        copy.wait()
    starts = doc_starts(n, pos, held)
    lanes = q_scr.shape[2]
    rows = lanes // GROUP
    base = (pos * TILE).astype(F32)
    width = state.shape[1] // CUT
    row = numbers((CUT * rows, 1), 0)
    plane, rest = split(row, PIECE)
    chunk, slot = split(rest, CAP)
    order = one_hot(chunk * rows + plane * CAP + slot, CUT * rows)
    for part in range(xs_ref.shape[0] // rows):
        at = slice(part * lanes, (part + 1) * lanes)
        q_scr[...] = qs_ref[:, :, at]
        done = flash(
            pos,
            held,
            [(q_scr.at[h], h, acc.at[h]) for h in range(KV_HEADS)],
            bias,
            facts_ref[0:1, at] + base,
            starts_of(facts_ref[1:2, at], starts),
        )
        for h in range(KV_HEADS):
            stack[...] = done[h]
            for g in range(GROUP):
                lane = (h * GROUP + g) * HEAD
                state[:, lane : lane + HEAD] = (
                    xs_ref[part * rows : (part + 1) * rows, lane : lane + HEAD]
                    + stack[pl.ds(g, rows, stride=GROUP), :]
                )
        hidden = state[...]
        mean = jnp.mean(hidden * hidden, axis=1, keepdims=True)
        normed = hidden * lax.rsqrt(mean + 1e-06) * gain[...]
        chunks = [normed[:, q * width : (q + 1) * width] for q in range(CUT)]
        sent = dot(order, jnp.concatenate(chunks, axis=0).astype(BF16))
        for k in range(rows // CAP):
            outs[part * (rows // CAP) + k][...] = sent[k * PIECE : (k + 1) * PIECE].astype(BF16)


def expert_kernel(n, count, *refs):
    pieces = refs[:count]
    wg, wu, wd = refs[count : count + 3]
    gather, spread, _, keep_ref, send_ref, rows = refs[count + 3 :]
    step = pieces[0].shape[1]
    senders = min(n, 16)
    size, total = senders * PIECE, n * PIECE
    half = total // 2
    kept = senders * CAP
    for at in range(0, total, size):
        parts, first = [], 0
        for piece in pieces:
            low, high = max(at - first, 0), min(at + size - first, piece.shape[0])
            if low < high:
                parts.append(piece[low:high, :].astype(F32))
            first += piece.shape[0]
        came = dot(gather[...], jnp.concatenate(parts, axis=0).astype(BF16)).astype(BF16)
        for q in range(CUT):
            rows[:, q * step : (q + 1) * step] = came[q * kept : (q + 1) * kept]
        gate = dot(rows[...], wg[...])
        up = dot(rows[...], wu[...])
        act = (gate / (1.0 + jnp.exp(-gate)) * up).astype(BF16)
        parts = [dot(act, wd[:, q * step : (q + 1) * step]).astype(BF16) for q in range(CUT)]
        out = dot(spread[...], jnp.concatenate(parts, axis=0)).astype(BF16)
        if size > half:
            keep_ref[...] = out[:half]
            send_ref[...] = out[half:]
        elif at < half:
            keep_ref[at : at + size] = out
        else:
            send_ref[at - half : at - half + size] = out


def own_kernel(n, heads, loads, pos_ref, held, q_ref, x_ref, _, *refs):
    sources, (h_ref, done_ref) = refs[:loads], refs[loads : loads + 2]
    targets = refs[loads + 2 : 2 * loads + 2]
    bias, sems, *scratch = refs[2 * loads + 2 :]
    moves = [
        pltpu.make_async_copy(source.at[0], target, sems.at[i])
        for i, (source, target) in enumerate(zip(sources, targets))
    ]
    for move in moves:
        move.start()
    done_ref[...] = jnp.zeros((8, TILE), F32)
    pos = pos_ref[0]
    starts = doc_starts(n, pos, held)
    first = starts_of(held[pos, TILE:KV_ROWS, 0:HEAD].astype(F32)[0:1], starts)
    place = (pos * TILE + lax.broadcasted_iota(jnp.int32, (1, TILE), 1)).astype(F32)
    chains = []
    for i, (h, own) in enumerate(by_kv_head(heads)):
        queries, acc = scratch[2 * i : 2 * i + 2]
        chains.append((queries, h, acc))
        for j, a in enumerate(own):
            terms = two_terms(q_ref[:, a * HEAD : (a + 1) * HEAD].astype(F32).T)
            for t, term in enumerate(terms):
                queries[t * HEAD : (t + 1) * HEAD, j * TILE : (j + 1) * TILE] = term
    done = jnp.concatenate(flash(pos, held, chains, bias, place, first), axis=0)
    for j, a in enumerate(heads):
        h_ref[:, j * HEAD : (j + 1) * HEAD] = (
            x_ref[:, a * HEAD : (a + 1) * HEAD].astype(F32) + done[j * TILE : (j + 1) * TILE]
        )
    for move in moves:
        move.wait()


def combine_kernel(planes, widths, mix_ref, *refs):
    count = len(widths)
    halves, parts = refs[:count], refs[count : count + planes]
    _, out_ref, buffer, sems = refs[count + planes :]
    slots = planes * SLOTS
    came = jnp.concatenate([p[...].astype(F32) for p in parts], axis=0).astype(BF16)
    order = one_hot(travel_row(numbers((CUT * slots, 1), 0), planes, SLOTS), planes * PIECE)
    came = dot(order, came).astype(BF16)
    size = buffer.shape[1] // CUT
    moves = []
    for q in range(CUT):
        rows = came[q * slots : (q + 1) * slots]
        part = dot(mix_ref[...], jnp.concatenate([rows, rows], axis=0))
        at = 0
        for h, width in zip(halves, widths):
            low, high = max(at, q * size), min(at + width, (q + 1) * size)
            if low < high:
                buffer[:, low:high] = (
                    h[:, low - at : high - at] + part[:, low - q * size : high - q * size]
                ).astype(BF16)
            at += width
        columns = pl.ds(q * size, size)
        moves.append(
            pltpu.make_async_copy(buffer.at[:, columns], out_ref.at[:, columns], sems.at[q])
        )
        moves[-1].start()
    for move in moves:
        move.wait()


def pin(x):
    return pltpu.with_memory_space_constraint(x, pltpu.HBM)


def params(mib):
    return pltpu.CompilerParams(vmem_limit_bytes=mib * 1024 * 1024)


def local(
    resid, queries, keys, values, doc_ids, norm_gain, routes, route_weights, w_gate, w_up, w_down
):
    n = lax.axis_size("expert")
    planes = n // SHARDS
    pos = lax.axis_index("expert").astype(jnp.int32).reshape(1)
    tokens, width = queries.shape
    hidden = w_gate.shape[2]
    routes_t = routes.T
    gates_t = route_weights.T
    docs = doc_ids.reshape(1, tokens)
    small = 24 if n <= 16 else 60
    back = reach(n)

    packed = pl.pallas_call(
        pack_kernel,
        out_shape=jax.ShapeDtypeStruct((KV_ROWS, 4 * HEAD), BF16),
        in_specs=[HBM] * 3,
        out_specs=VMEM,
        scratch_shapes=[
            pltpu.VMEM((1, tokens), jnp.int32),
            pltpu.VMEM((tokens, KV_HEADS * HEAD), BF16),
            pltpu.SemaphoreType.DMA((3,)),
        ],
        compiler_params=params(8),
        name="pack",
    )(pin(docs), pin(keys), pin(values))

    def move(value, pairs):
        return lax.ppermute(value, "expert", pairs)

    def needed(k, y_from, y_to):
        gaps = [
            k * SHARDS + 2 * (y_to - y_from) + (to - of) for to in range(2) for of in range(2)
        ]
        return any(0 <= gap <= back for gap in gaps)

    far = max(k for k in range(planes) if any(needed(k, a, b) for a in (0, 1) for b in (0, 1)))
    size = min(n // 2, 16) * PIECE
    q_rows, x_rows, facts, mix, gather, spread = pl.pallas_call(
        functools.partial(select_kernel, planes),
        out_shape=[
            jax.ShapeDtypeStruct((KV_HEADS, 2 * HEAD, planes * CAP * GROUP), BF16),
            jax.ShapeDtypeStruct((planes * CAP, width), F32),
            jax.ShapeDtypeStruct((8, planes * CAP * GROUP), F32),
            jax.ShapeDtypeStruct((tokens, 2 * planes * SLOTS), BF16),
            jax.ShapeDtypeStruct((size, size), BF16),
            jax.ShapeDtypeStruct((size, size), BF16),
        ],
        in_specs=[SMEM] + [HBM] * 5,
        out_specs=[VMEM] * 6,
        scratch_shapes=[
            pltpu.VMEM(routes_t.shape, jnp.int32),
            pltpu.VMEM(docs.shape, jnp.int32),
            pltpu.VMEM(queries.shape, BF16),
            pltpu.VMEM(resid.shape, BF16),
            pltpu.VMEM(gates_t.shape, F32),
            pltpu.VMEM((planes * CAP * GROUP, HEAD), F32),
            pltpu.SemaphoreType.DMA((5,)),
        ],
        compiler_params=params(small),
        name="select",
    )(pos, *map(pin, (routes_t, docs, queries, resid, gates_t)))

    flip_y = [(s, s ^ 2) for s in range(n)]
    flip_c = [(s, s ^ 1) for s in range(n)]
    jump = {s: s + far * SHARDS - 2 for s in range(n - far * SHARDS) if s & 2}
    jump.update({to: s for s, to in jump.items()})
    jumped = move(packed, [(s, jump.get(s, s)) for s in range(n)])
    along = [packed] + [
        move(packed, [(s, (s + k * SHARDS) % n) for s in range(n)]) for k in range(1, far)
    ]
    along[1], q_rows = lax.optimization_barrier((along[1], q_rows))
    across = []
    for k in range(far):
        if k > 1 and k == far - 1:
            along[k], across = lax.optimization_barrier((along[k], across))
        across.append(move(along[k], [(s, s ^ 2 if s >= k * SHARDS else s) for s in range(n)]))
    early, late = along + [jumped] + across[:-1], across[-1:]
    sides = [(0, k) for k in range(far)] + [(1, far)] + [(1, k) for k in range(far - 1)]
    early.append(move(jnp.concatenate(early, axis=0), flip_c))
    early_senders = [(i, 0, 0, *side) for i, side in enumerate(sides)]
    early_senders += [(len(sides), i * KV_ROWS, 1, *side) for i, side in enumerate(sides)]
    early_senders += [(0, 0, flip, 0, far) for flip in (0, 1)]
    late_senders = [(flip, 0, flip, 1, far - 1) for flip in (0, 1)]
    held_shape = jax.ShapeDtypeStruct((n, KV_ROWS, 4 * HEAD), BF16)
    held = pl.pallas_call(
        functools.partial(collect_kernel, n, early_senders),
        out_shape=held_shape,
        in_specs=[SMEM] + [ANY] * len(early),
        out_specs=VMEM,
        scratch_shapes=[pltpu.SemaphoreType.DMA((len(early_senders),))],
        compiler_params=params(small),
        cost_estimate=pl.CostEstimate(flops=0, bytes_accessed=1000, transcendentals=0),
        name="collect",
    )(pos, *early)

    lanes = min(planes, 4) * CAP * GROUP
    late[0], held = lax.optimization_barrier((late[0], held))
    late.append(move(late[0], flip_c))
    *sent, held = pl.pallas_call(
        functools.partial(routed_kernel, n, late_senders),
        out_shape=[jax.ShapeDtypeStruct((PIECE, width // CUT), BF16)] * planes
        + [held_shape],
        in_specs=[SMEM, HBM] + [VMEM] * 4 + [ANY] * len(late),
        out_specs=[VMEM] * (planes + 1),
        scratch_shapes=[
            pltpu.VMEM((KV_HEADS, HEAD + EXTRA, lanes), F32),
            pltpu.VMEM((KEYS, lanes), F32),
            pltpu.VMEM((KV_HEADS, 2 * HEAD, lanes), BF16),
            pltpu.VMEM((lanes, HEAD), F32),
            pltpu.VMEM((lanes // GROUP, width), F32),
            pltpu.VMEM((1, width), F32),
            pltpu.SemaphoreType.DMA((len(late_senders) + 1,)),
        ],
        input_output_aliases={5: planes},
        compiler_params=params(small),
        name="routed",
    )(pos, pin(norm_gain.reshape(1, width)), q_rows, x_rows, facts, held, *late)

    def own(heads, after, *sources):
        lanes = [len(own) * TILE for _, own in by_kv_head(heads)]
        return pl.pallas_call(
            functools.partial(own_kernel, n, heads, len(sources)),
            out_shape=[
                jax.ShapeDtypeStruct((tokens, len(heads) * HEAD), F32),
                jax.ShapeDtypeStruct((8, TILE), F32),
            ]
            + [jax.ShapeDtypeStruct(w.shape[1:], BF16) for w in sources],
            in_specs=[SMEM, VMEM, VMEM, VMEM, ANY] + [HBM] * len(sources),
            out_specs=[VMEM] * (2 + len(sources)),
            scratch_shapes=[pltpu.VMEM((KEYS, TILE), F32), pltpu.SemaphoreType.DMA((3,))]
            + [
                shape
                for count in lanes
                for shape in (
                    pltpu.VMEM((2 * HEAD, count), BF16),
                    pltpu.VMEM((HEAD + EXTRA, count), F32),
                )
            ],
            compiler_params=params(small),
            cost_estimate=pl.CostEstimate(
                flops=2_000_000_000, bytes_accessed=8_000_000, transcendentals=2_000_000
            ),
            name="own",
        )(pos, held, queries, resid, after, *map(pin, sources))

    half0, done, *weights = own(range(10), sent[0], w_gate, w_up, w_down)
    half1, late = own(range(10, GROUP), done)
    halves = [half0, half1]

    come = [
        move(sent[k], [(s, (s + k * SHARDS) % n) for s in range(n)]) for k in range(1, planes)
    ]
    next_door = move(sent[0], flip_y)
    come, next_door, done = lax.optimization_barrier((come, next_door, done))
    here = [sent[0], jnp.concatenate(come, axis=0)]
    there = [next_door, move(here[1], flip_y)]
    mate = move(jnp.concatenate(here, axis=0), flip_c)
    half = jax.ShapeDtypeStruct((n * PIECE // 4, width // CUT), BF16)

    def expert(pieces, after):
        return pl.pallas_call(
            functools.partial(expert_kernel, n // 2, len(pieces)),
            out_shape=[half, half],
            in_specs=[VMEM] * (len(pieces) + 5) + [ANY],
            out_specs=[VMEM, VMEM],
            scratch_shapes=[pltpu.VMEM((min(n // 2, 16) * CAP, width), BF16)],
            compiler_params=params(16),
            cost_estimate=pl.CostEstimate(
                flops=600_000_000, bytes_accessed=2_000_000, transcendentals=20_000
            ),
            name="expert",
        )(*pieces, *weights, gather, spread, after)

    keep, send = expert(here + [mate], done)
    there, late, keep = lax.optimization_barrier((there, late, keep))
    mine = keep.astype(F32) + move(send, flip_c).astype(F32)
    mate = move(jnp.concatenate(there, axis=0), flip_c)
    keep, send = expert(there + [mate], late)
    half2, done = own(range(GROUP, QUERY_HEADS), keep)
    halves.append(half2)
    theirs = keep.astype(F32) + move(send, flip_c).astype(F32)
    other = move(theirs.astype(BF16), flip_y)
    other, done = lax.optimization_barrier((other, done))
    total = (mine + other.astype(F32)).astype(BF16)
    parts = [total[:PIECE]]
    for k in range(1, planes):
        parts.append(
            move(
                total[k * PIECE : (k + 1) * PIECE], [(s, (s - k * SHARDS) % n) for s in range(n)]
            )
        )

    widths = [h.shape[1] for h in halves]
    return pl.pallas_call(
        functools.partial(combine_kernel, planes, widths),
        out_shape=jax.ShapeDtypeStruct((tokens, width), BF16),
        in_specs=[VMEM] * (1 + len(halves) + planes) + [ANY],
        out_specs=HBM,
        scratch_shapes=[pltpu.VMEM((tokens, width), BF16), pltpu.SemaphoreType.DMA((CUT,))],
        compiler_params=params(small),
        name="combine",
    )(mix, *halves, *parts, done)


def solution(mesh):
    rows = P(("groups", "expert"), None)
    in_specs = (rows,) * 4 + (P(("groups", "expert")), P(), rows, rows) + (
        P("expert", None, None),
    ) * 3
    return jax.shard_map(local, mesh=mesh, in_specs=in_specs, out_specs=rows, check_vma=False)
```

```python
import functools
import math

import jax
import jax.numpy as jnp
from jax import lax
from jax.experimental import pallas as pl
from jax.experimental.pallas import tpu as pltpu
from jax.sharding import PartitionSpec as P

HEAD = 128
QUERY_HEADS = 32
KV_HEADS = 2
GROUP = QUERY_HEADS // KV_HEADS
SHARDS = 4
CAP = 6
SLOTS = 8
CUT = 4
PIECE = CUT * CAP
TILE = 128
KEYS = 512
STEP = KEYS // TILE
KV_ROWS = TILE + 16
SCALE = math.log2(math.e) / math.sqrt(HEAD)
LOW = -1e30
EXTRA = 16
F32 = jnp.float32
BF16 = jnp.bfloat16
VMEM = pl.BlockSpec(memory_space=pltpu.VMEM)
SMEM = pl.BlockSpec(memory_space=pltpu.SMEM)
ANY = pl.BlockSpec(memory_space=pl.ANY)
HBM = pl.BlockSpec(memory_space=pltpu.HBM)


def dot(a, b, ca=1, cb=0):
    return lax.dot_general(a, b, (((ca,), (cb,)), ((), ())), preferred_element_type=F32)


def reach(n):
    longest = n * TILE // 2 + 256
    return (longest - 1 + TILE - 1) // TILE


def slot_rows(routes, experts):
    members = jnp.concatenate(
        [jnp.max((routes == e).astype(F32), axis=0, keepdims=True) for e in experts], axis=0
    )
    count = len(experts)
    padded = -(-count // 8) * 8
    wide = members
    if padded > count:
        wide = jnp.concatenate([members, jnp.zeros((padded - count, TILE), F32)], axis=0)
    before = lax.broadcasted_iota(jnp.int32, (TILE, TILE), 0) < lax.broadcasted_iota(
        jnp.int32, (TILE, TILE), 1
    )
    ranks = dot(wide.astype(BF16), before.astype(F32).astype(BF16))
    return members, ranks


def one_hot(targets, count):
    shape = (targets.shape[0], count) if targets.shape[1] == 1 else (count, targets.shape[1])
    axis = 1 if targets.shape[1] == 1 else 0
    places = lax.broadcasted_iota(jnp.int32, shape, axis).astype(F32)
    return jnp.where(places == targets, 1.0, 0.0).astype(BF16)


def split(x, size):
    whole = jnp.floor((x + 0.5) / size)
    return whole, x - whole * size


def travel_row(x, senders, slots):
    chunk, rest = split(x, senders * slots)
    sender, slot = split(rest, slots)
    return jnp.where(slot < CAP, sender * PIECE + chunk * CAP + slot, -1.0)


def numbers(shape, axis):
    return lax.broadcasted_iota(jnp.int32, shape, axis).astype(F32)


def pack_kernel(docs_ref, keys_ref, values_ref, out_ref, docs, values, sems):
    moves = [
        pltpu.make_async_copy(values_ref, values, sems.at[0]),
        pltpu.make_async_copy(docs_ref, docs, sems.at[1]),
        pltpu.make_async_copy(
            keys_ref, out_ref.at[pl.ds(0, TILE), pl.ds(0, KV_HEADS * HEAD)], sems.at[2]
        ),
    ]
    for move in moves:
        move.start()
    moves[0].wait()
    for h in range(KV_HEADS):
        out_ref[0:TILE, (KV_HEADS + h) * HEAD : (KV_HEADS + h + 1) * HEAD] = (
            values[:, h * HEAD : (h + 1) * HEAD].astype(F32).T.astype(BF16)
        )
    moves[1].wait()
    out_ref[TILE:KV_ROWS, :] = jnp.zeros((KV_ROWS - TILE, 4 * HEAD), BF16)
    out_ref[TILE:KV_ROWS, 0:HEAD] = jnp.broadcast_to(
        docs[...].astype(F32), (KV_ROWS - TILE, TILE)
    ).astype(BF16)
    moves[2].wait()


def select_kernel(planes, pos_ref, *refs):
    sources, (qs_ref, xs_ref, facts_ref, mix_ref, gather_ref, spread_ref) = refs[:5], refs[5:11]
    routes_ref, docs_ref, q_ref, x_ref, gates_ref, stack, sems = refs[11:]
    moves = [
        pltpu.make_async_copy(source, target, sems.at[i])
        for i, (source, target) in enumerate(zip(sources, refs[11:16]))
    ]
    for move in moves:
        move.start()
    for move in moves:
        move.wait()
    z = pos_ref[0] // SHARDS
    experts = [lax.rem(z + k, planes) for k in range(planes)]
    routes, gates = routes_ref[...], gates_ref[...]
    members, ranks = slot_rows(routes, experts)
    slot = lax.broadcasted_iota(jnp.int32, (SLOTS, TILE), 0).astype(F32)
    mix = []
    _, places = slot_rows(routes, list(range(planes)))
    for e in range(planes):
        gate = jnp.sum(jnp.where(routes == e, gates, 0.0), axis=0, keepdims=True)
        mix.append(jnp.where(places[e : e + 1] == slot, gate, 0.0))
    mix = jnp.concatenate(mix, axis=0).T
    mix_high = mix.astype(BF16)
    mix_ref[:, : planes * SLOTS] = mix_high
    mix_ref[:, planes * SLOTS :] = (mix - mix_high.astype(F32)).astype(BF16)
    size = gather_ref.shape[0]
    gather_ref[...] = one_hot(travel_row(numbers((size, 1), 0), size // PIECE, CAP), size)
    spread_ref[...] = one_hot(travel_row(numbers((1, size), 1), size // PIECE, CAP), size)
    docs = docs_ref[...].astype(F32)
    token = lax.broadcasted_iota(jnp.int32, (1, TILE), 1).astype(F32)
    facts = jnp.concatenate(
        [token, docs, jnp.ones((1, TILE), F32), jnp.zeros((5, TILE), F32)], axis=0
    ).astype(BF16)
    picks = [
        jnp.where(ranks[k : k + 1] == slot, members[k : k + 1], 0.0) for k in range(planes)
    ]
    rows = planes * CAP
    plane, place = split(numbers((rows, 1), 0), CAP)
    compact = one_hot(plane * SLOTS + place, planes * SLOTS)
    chooser = dot(compact, jnp.concatenate(picks, axis=0).astype(BF16)).astype(BF16)
    lane, _ = split(numbers((rows * GROUP, 1), 0), GROUP)
    lane_pick = dot(one_hot(lane, rows), chooser).astype(BF16)
    known = dot(facts, lane_pick, 1, 1)
    facts_ref[...] = jnp.concatenate(
        [known[0:1], known[1:2] + (1.0 - known[2:3]) * docs[:, 0:1], known[2:]], axis=0
    )
    q_rows = dot(chooser, q_ref[...])
    xs_ref[...] = dot(chooser, x_ref[...])
    for h in range(KV_HEADS):
        for g in range(GROUP):
            a = h * GROUP + g
            stack[pl.ds(g, rows, stride=GROUP), :] = q_rows[:, a * HEAD : (a + 1) * HEAD]
        for i, term in enumerate(two_terms(stack[...].T)):
            qs_ref[h, i * HEAD : (i + 1) * HEAD, :] = term


def doc_starts(n, pos, held):
    sums = [jnp.zeros((1, TILE), F32) for _ in range(3)]
    for s in range(n):
        docs = held[s, TILE:KV_ROWS, 0:HEAD].astype(F32)[0:1]
        ahead = (pos - s < 0).astype(F32)
        behind = (pos - s > reach(n)).astype(F32)
        known = 1.0 - ahead - behind
        docs = jnp.where(known > 0.5, docs, 0.0) + 9.0 * ahead
        for d in range(3):
            sums[d] = sums[d] + jnp.where(docs < d + 1.0, 1.0, 0.0)
    return [jnp.sum(s, axis=1, keepdims=True) for s in sums]


def starts_of(docs, starts):
    first = jnp.zeros_like(docs)
    for d in range(3):
        first = jnp.where(docs == d + 1.0, starts[d], first)
    return first


def two_terms(x):
    scaled = x.astype(F32) * SCALE
    high = scaled.astype(BF16)
    return high, (scaled - high.astype(F32)).astype(BF16)


def key_steps(pos, place, first, bias_ref, step, state):
    low = jnp.min(first).astype(jnp.int32) // KEYS
    last = pos // STEP
    clear = jnp.minimum((jnp.max(first).astype(jnp.int32) + KEYS - 1) // KEYS, last)

    def edge(j, carried):
        kb = jnp.where(j < clear - low, low + j, last)
        key_at = (kb * KEYS + lax.broadcasted_iota(jnp.int32, (KEYS, 1), 0)).astype(F32)
        bias_ref[...] = jnp.where((key_at >= first) & (key_at <= place), 0.0, LOW)
        return step(kb, carried, True)

    state = lax.fori_loop(0, clear - low + 1, edge, state)
    return lax.fori_loop(clear, last, lambda kb, carried: step(kb, carried, False), state)


def by_kv_head(heads):
    groups = [(h, [a for a in heads if a // GROUP == h]) for h in range(KV_HEADS)]
    return [(h, own) for h, own in groups if own]


def keys_of(held, kb, h):
    keys = jnp.concatenate(
        [held[STEP * kb + t, 0:TILE, h * HEAD : (h + 1) * HEAD] for t in range(STEP)], axis=0
    )
    return jnp.concatenate([keys, keys], axis=1)


def values_of(held, kb, h):
    at = (KV_HEADS + h) * HEAD
    values = jnp.concatenate(
        [held[STEP * kb + t, 0:TILE, at : at + HEAD] for t in range(STEP)], axis=1
    )
    return jnp.concatenate([values, jnp.ones((EXTRA, KEYS), BF16)], axis=0)


def flash(pos, held, chains, bias_ref, place, first):
    for _, _, acc in chains:
        acc[...] = jnp.zeros(acc.shape, F32)

    def step(kb, tops, masked):
        out = []
        for (queries, h, acc), old in zip(chains, tops):
            scores = dot(keys_of(held, kb, h), queries[...])
            if masked:
                copies = scores.shape[1] // bias_ref.shape[1]
                scores = scores + jnp.concatenate([bias_ref[...]] * copies, axis=1)
            top = jnp.maximum(old, jnp.max(scores, axis=0, keepdims=True))
            weights = jnp.exp2(scores - top).astype(BF16)
            acc[...] = acc[...] * jnp.exp2(old - top) + dot(values_of(held, kb, h), weights)
            out.append(top)
        return tuple(out)

    tops = tuple(jnp.full((1, acc.shape[1]), LOW, F32) for _, _, acc in chains)
    key_steps(pos, place, first, bias_ref, step, tops)
    return [(acc[0:HEAD, :] / acc[HEAD : HEAD + 1, :]).T for _, _, acc in chains]


def place_pieces(n, senders, pos, pieces, held, sems):
    planes = n // SHARDS
    z, y, c = pos // SHARDS, (pos // 2) % 2, pos % 2
    copies = []
    for i, (piece, row, flip_c, flip_y, k) in enumerate(senders):
        sender = lax.rem(z - k + planes, planes) * SHARDS + (y ^ flip_y) * 2 + (c ^ flip_c)
        copy = pltpu.make_async_copy(
            pieces[piece].at[pl.ds(row, KV_ROWS)], held.at[sender], sems.at[i]
        )
        copy.start()
        copies.append(copy)
    return copies


def collect_kernel(n, senders, pos_ref, *refs):
    *pieces, held, sems = refs
    for copy in place_pieces(n, senders, pos_ref[0], pieces, held, sems):
        copy.wait()


def routed_kernel(n, senders, pos_ref, gain_ref, qs_ref, xs_ref, facts_ref, _, *refs):
    planes = n // SHARDS
    count = len(senders)
    pieces, outs, held = refs[:2], refs[2 : 2 + planes], refs[2 + planes]
    acc, bias, q_scr, stack, state, gain, sems = refs[3 + planes :]
    pos = pos_ref[0]
    copies = place_pieces(n, senders, pos, pieces, held, sems)
    copies.append(pltpu.make_async_copy(gain_ref, gain, sems.at[count]))
    copies[-1].start()
    for copy in copies:
        copy.wait()
    starts = doc_starts(n, pos, held)
    lanes = q_scr.shape[2]
    rows = lanes // GROUP
    base = (pos * TILE).astype(F32)
    width = state.shape[1] // CUT
    row = numbers((CUT * rows, 1), 0)
    plane, rest = split(row, PIECE)
    chunk, slot = split(rest, CAP)
    order = one_hot(chunk * rows + plane * CAP + slot, CUT * rows)
    for part in range(xs_ref.shape[0] // rows):
        at = slice(part * lanes, (part + 1) * lanes)
        q_scr[...] = qs_ref[:, :, at]
        done = flash(
            pos,
            held,
            [(q_scr.at[h], h, acc.at[h]) for h in range(KV_HEADS)],
            bias,
            facts_ref[0:1, at] + base,
            starts_of(facts_ref[1:2, at], starts),
        )
        for h in range(KV_HEADS):
            stack[...] = done[h]
            for g in range(GROUP):
                lane = (h * GROUP + g) * HEAD
                state[:, lane : lane + HEAD] = (
                    xs_ref[part * rows : (part + 1) * rows, lane : lane + HEAD]
                    + stack[pl.ds(g, rows, stride=GROUP), :]
                )
        hidden = state[...]
        mean = jnp.mean(hidden * hidden, axis=1, keepdims=True)
        normed = hidden * lax.rsqrt(mean + 1e-06) * gain[...]
        chunks = [normed[:, q * width : (q + 1) * width] for q in range(CUT)]
        sent = dot(order, jnp.concatenate(chunks, axis=0).astype(BF16))
        for k in range(rows // CAP):
            outs[part * (rows // CAP) + k][...] = sent[k * PIECE : (k + 1) * PIECE].astype(BF16)


def expert_kernel(n, count, *refs):
    pieces = refs[:count]
    wg, wu, wd = refs[count : count + 3]
    gather, spread, _, keep_ref, send_ref, rows = refs[count + 3 :]
    step = pieces[0].shape[1]
    senders = min(n, 16)
    size, total = senders * PIECE, n * PIECE
    half = total // 2
    kept = senders * CAP
    for at in range(0, total, size):
        parts, first = [], 0
        for piece in pieces:
            low, high = max(at - first, 0), min(at + size - first, piece.shape[0])
            if low < high:
                parts.append(piece[low:high, :].astype(F32))
            first += piece.shape[0]
        came = dot(gather[...], jnp.concatenate(parts, axis=0).astype(BF16)).astype(BF16)
        for q in range(CUT):
            rows[:, q * step : (q + 1) * step] = came[q * kept : (q + 1) * kept]
        gate = dot(rows[...], wg[...])
        up = dot(rows[...], wu[...])
        act = (gate / (1.0 + jnp.exp(-gate)) * up).astype(BF16)
        parts = [dot(act, wd[:, q * step : (q + 1) * step]).astype(BF16) for q in range(CUT)]
        out = dot(spread[...], jnp.concatenate(parts, axis=0)).astype(BF16)
        if size > half:
            keep_ref[...] = out[:half]
            send_ref[...] = out[half:]
        elif at < half:
            keep_ref[at : at + size] = out
        else:
            send_ref[at - half : at - half + size] = out


def own_kernel(n, heads, loads, pos_ref, held, q_ref, x_ref, _, *refs):
    sources, (h_ref, done_ref) = refs[:loads], refs[loads : loads + 2]
    targets = refs[loads + 2 : 2 * loads + 2]
    bias, sems, *scratch = refs[2 * loads + 2 :]
    moves = [
        pltpu.make_async_copy(source.at[0], target, sems.at[i])
        for i, (source, target) in enumerate(zip(sources, targets))
    ]
    for move in moves:
        move.start()
    done_ref[...] = jnp.zeros((8, TILE), F32)
    pos = pos_ref[0]
    starts = doc_starts(n, pos, held)
    first = starts_of(held[pos, TILE:KV_ROWS, 0:HEAD].astype(F32)[0:1], starts)
    place = (pos * TILE + lax.broadcasted_iota(jnp.int32, (1, TILE), 1)).astype(F32)
    chains = []
    for i, (h, own) in enumerate(by_kv_head(heads)):
        queries, acc = scratch[2 * i : 2 * i + 2]
        chains.append((queries, h, acc))
        for j, a in enumerate(own):
            terms = two_terms(q_ref[:, a * HEAD : (a + 1) * HEAD].astype(F32).T)
            for t, term in enumerate(terms):
                queries[t * HEAD : (t + 1) * HEAD, j * TILE : (j + 1) * TILE] = term
    done = jnp.concatenate(flash(pos, held, chains, bias, place, first), axis=0)
    for j, a in enumerate(heads):
        h_ref[:, j * HEAD : (j + 1) * HEAD] = (
            x_ref[:, a * HEAD : (a + 1) * HEAD].astype(F32) + done[j * TILE : (j + 1) * TILE]
        )
    for move in moves:
        move.wait()


def combine_kernel(planes, widths, mix_ref, *refs):
    count = len(widths)
    halves = refs[:count]
    part_ref, _, out_ref, buffer, sems = refs[count:]
    slots = planes * SLOTS
    order = one_hot(travel_row(numbers((CUT * slots, 1), 0), planes, SLOTS), planes * PIECE)
    came = dot(order, part_ref[...]).astype(BF16)
    size = buffer.shape[1] // CUT
    moves = []
    for q in range(CUT):
        rows = came[q * slots : (q + 1) * slots]
        part = dot(mix_ref[...], jnp.concatenate([rows, rows], axis=0))
        at = 0
        for h, width in zip(halves, widths):
            low, high = max(at, q * size), min(at + width, (q + 1) * size)
            if low < high:
                buffer[:, low:high] = (
                    h[:, low - at : high - at] + part[:, low - q * size : high - q * size]
                ).astype(BF16)
            at += width
        columns = pl.ds(q * size, size)
        moves.append(
            pltpu.make_async_copy(buffer.at[:, columns], out_ref.at[:, columns], sems.at[q])
        )
        moves[-1].start()
    for move in moves:
        move.wait()


def pin(x):
    return pltpu.with_memory_space_constraint(x, pltpu.HBM)


def params(mib):
    return pltpu.CompilerParams(vmem_limit_bytes=mib * 1024 * 1024)


def local(
    resid, queries, keys, values, doc_ids, norm_gain, routes, route_weights, w_gate, w_up, w_down
):
    n = lax.axis_size("expert")
    planes = n // SHARDS
    pos = lax.axis_index("expert").astype(jnp.int32).reshape(1)
    tokens, width = queries.shape
    hidden = w_gate.shape[2]
    routes_t = routes.T
    gates_t = route_weights.T
    docs = doc_ids.reshape(1, tokens)
    small = 24 if n <= 16 else 60
    back = reach(n)

    packed = pl.pallas_call(
        pack_kernel,
        out_shape=jax.ShapeDtypeStruct((KV_ROWS, 4 * HEAD), BF16),
        in_specs=[HBM] * 3,
        out_specs=VMEM,
        scratch_shapes=[
            pltpu.VMEM((1, tokens), jnp.int32),
            pltpu.VMEM((tokens, KV_HEADS * HEAD), BF16),
            pltpu.SemaphoreType.DMA((3,)),
        ],
        compiler_params=params(8),
        name="pack",
    )(pin(docs), pin(keys), pin(values))

    def move(value, pairs):
        return lax.ppermute(value, "expert", pairs)

    def needed(k, y_from, y_to):
        gaps = [
            k * SHARDS + 2 * (y_to - y_from) + (to - of) for to in range(2) for of in range(2)
        ]
        return any(0 <= gap <= back for gap in gaps)

    far = max(k for k in range(planes) if any(needed(k, a, b) for a in (0, 1) for b in (0, 1)))
    size = min(n // 2, 16) * PIECE
    q_rows, x_rows, facts, mix, gather, spread = pl.pallas_call(
        functools.partial(select_kernel, planes),
        out_shape=[
            jax.ShapeDtypeStruct((KV_HEADS, 2 * HEAD, planes * CAP * GROUP), BF16),
            jax.ShapeDtypeStruct((planes * CAP, width), F32),
            jax.ShapeDtypeStruct((8, planes * CAP * GROUP), F32),
            jax.ShapeDtypeStruct((tokens, 2 * planes * SLOTS), BF16),
            jax.ShapeDtypeStruct((size, size), BF16),
            jax.ShapeDtypeStruct((size, size), BF16),
        ],
        in_specs=[SMEM] + [HBM] * 5,
        out_specs=[VMEM] * 6,
        scratch_shapes=[
            pltpu.VMEM(routes_t.shape, jnp.int32),
            pltpu.VMEM(docs.shape, jnp.int32),
            pltpu.VMEM(queries.shape, BF16),
            pltpu.VMEM(resid.shape, BF16),
            pltpu.VMEM(gates_t.shape, F32),
            pltpu.VMEM((planes * CAP * GROUP, HEAD), F32),
            pltpu.SemaphoreType.DMA((5,)),
        ],
        compiler_params=params(small),
        name="select",
    )(pos, *map(pin, (routes_t, docs, queries, resid, gates_t)))

    flip_y = [(s, s ^ 2) for s in range(n)]
    flip_c = [(s, s ^ 1) for s in range(n)]
    jump = {s: s + far * SHARDS - 2 for s in range(n - far * SHARDS) if s & 2}
    jump.update({to: s for s, to in jump.items()})
    jumped = move(packed, [(s, jump.get(s, s)) for s in range(n)])
    along = [packed] + [
        move(packed, [(s, (s + k * SHARDS) % n) for s in range(n)]) for k in range(1, far)
    ]
    along[1], q_rows = lax.optimization_barrier((along[1], q_rows))
    across = []
    for k in range(far):
        if k > 1 and k == far - 1:
            along[k], across = lax.optimization_barrier((along[k], across))
        across.append(move(along[k], [(s, s ^ 2 if s >= k * SHARDS else s) for s in range(n)]))
    early, late = along + [jumped] + across[:-1], across[-1:]
    sides = [(0, k) for k in range(far)] + [(1, far)] + [(1, k) for k in range(far - 1)]
    early.append(move(jnp.concatenate(early, axis=0), flip_c))
    early_senders = [(i, 0, 0, *side) for i, side in enumerate(sides)]
    early_senders += [(len(sides), i * KV_ROWS, 1, *side) for i, side in enumerate(sides)]
    early_senders += [(0, 0, flip, 0, far) for flip in (0, 1)]
    late_senders = [(flip, 0, flip, 1, far - 1) for flip in (0, 1)]
    held_shape = jax.ShapeDtypeStruct((n, KV_ROWS, 4 * HEAD), BF16)
    held = pl.pallas_call(
        functools.partial(collect_kernel, n, early_senders),
        out_shape=held_shape,
        in_specs=[SMEM] + [ANY] * len(early),
        out_specs=VMEM,
        scratch_shapes=[pltpu.SemaphoreType.DMA((len(early_senders),))],
        compiler_params=params(small),
        cost_estimate=pl.CostEstimate(flops=0, bytes_accessed=1000, transcendentals=0),
        name="collect",
    )(pos, *early)

    lanes = min(planes, 4) * CAP * GROUP
    late[0], held = lax.optimization_barrier((late[0], held))
    late.append(move(late[0], flip_c))
    *sent, held = pl.pallas_call(
        functools.partial(routed_kernel, n, late_senders),
        out_shape=[jax.ShapeDtypeStruct((PIECE, width // CUT), BF16)] * planes
        + [held_shape],
        in_specs=[SMEM, HBM] + [VMEM] * 4 + [ANY] * len(late),
        out_specs=[VMEM] * (planes + 1),
        scratch_shapes=[
            pltpu.VMEM((KV_HEADS, HEAD + EXTRA, lanes), F32),
            pltpu.VMEM((KEYS, lanes), F32),
            pltpu.VMEM((KV_HEADS, 2 * HEAD, lanes), BF16),
            pltpu.VMEM((lanes, HEAD), F32),
            pltpu.VMEM((lanes // GROUP, width), F32),
            pltpu.VMEM((1, width), F32),
            pltpu.SemaphoreType.DMA((len(late_senders) + 1,)),
        ],
        input_output_aliases={5: planes},
        compiler_params=params(small),
        name="routed",
    )(pos, pin(norm_gain.reshape(1, width)), q_rows, x_rows, facts, held, *late)

    def own(heads, after, *sources):
        lanes = [len(own) * TILE for _, own in by_kv_head(heads)]
        return pl.pallas_call(
            functools.partial(own_kernel, n, heads, len(sources)),
            out_shape=[
                jax.ShapeDtypeStruct((tokens, len(heads) * HEAD), F32),
                jax.ShapeDtypeStruct((8, TILE), F32),
            ]
            + [jax.ShapeDtypeStruct(w.shape[1:], BF16) for w in sources],
            in_specs=[SMEM, VMEM, VMEM, VMEM, ANY] + [HBM] * len(sources),
            out_specs=[VMEM] * (2 + len(sources)),
            scratch_shapes=[pltpu.VMEM((KEYS, TILE), F32), pltpu.SemaphoreType.DMA((3,))]
            + [
                shape
                for count in lanes
                for shape in (
                    pltpu.VMEM((2 * HEAD, count), BF16),
                    pltpu.VMEM((HEAD + EXTRA, count), F32),
                )
            ],
            compiler_params=params(small),
            cost_estimate=pl.CostEstimate(
                flops=2_000_000_000, bytes_accessed=8_000_000, transcendentals=2_000_000
            ),
            name="own",
        )(pos, held, queries, resid, after, *map(pin, sources))

    half0, done, *weights = own(range(10), sent[0], w_gate, w_up, w_down)
    half1, late = own(range(10, GROUP), done)
    halves = [half0, half1]

    come = [
        move(sent[k], [(s, (s + k * SHARDS) % n) for s in range(n)]) for k in range(1, planes)
    ]
    next_door = move(sent[0], flip_y)
    come, next_door, done = lax.optimization_barrier((come, next_door, done))
    here = [sent[0], jnp.concatenate(come, axis=0)]
    there = [next_door, move(here[1], flip_y)]
    mate = move(jnp.concatenate(here, axis=0), flip_c)
    half = jax.ShapeDtypeStruct((n * PIECE // 4, width // CUT), BF16)

    def expert(pieces, after):
        return pl.pallas_call(
            functools.partial(expert_kernel, n // 2, len(pieces)),
            out_shape=[half, half],
            in_specs=[VMEM] * (len(pieces) + 5) + [ANY],
            out_specs=[VMEM, VMEM],
            scratch_shapes=[pltpu.VMEM((min(n // 2, 16) * CAP, width), BF16)],
            compiler_params=params(16),
            cost_estimate=pl.CostEstimate(
                flops=600_000_000, bytes_accessed=2_000_000, transcendentals=20_000
            ),
            name="expert",
        )(*pieces, *weights, gather, spread, after)

    keep, send = expert(here + [mate], done)
    there, late, keep = lax.optimization_barrier((there, late, keep))
    mine = keep.astype(F32) + move(send, flip_c).astype(F32)
    mate = move(jnp.concatenate(there, axis=0), flip_c)
    keep, send = expert(there + [mate], late)
    half2, done = own(range(GROUP, QUERY_HEADS), keep)
    halves.append(half2)
    theirs = keep.astype(F32) + move(send, flip_c).astype(F32)
    other = move(theirs.astype(BF16), flip_y)
    other, done = lax.optimization_barrier((other, done))
    total = (mine + other.astype(F32)).astype(BF16)
    z = pos[0] // SHARDS
    total = total.reshape(planes, PIECE, width // CUT)
    order = lax.rem(z - jnp.arange(planes) + planes, planes)
    total = total.at[order].get(mode="promise_in_bounds")
    lines = [[k * SHARDS + j for k in range(planes)] for j in range(SHARDS)]
    came = lax.all_to_all(total, "expert", 0, 0, axis_index_groups=lines, tiled=True)
    parts = [came.reshape(planes * PIECE, width // CUT)]

    widths = [h.shape[1] for h in halves]
    return pl.pallas_call(
        functools.partial(combine_kernel, planes, widths),
        out_shape=jax.ShapeDtypeStruct((tokens, width), BF16),
        in_specs=[VMEM] * (2 + len(halves)) + [ANY],
        out_specs=HBM,
        scratch_shapes=[pltpu.VMEM((tokens, width), BF16), pltpu.SemaphoreType.DMA((CUT,))],
        compiler_params=params(small),
        name="combine",
    )(mix, *halves, *parts, done)


def solution(mesh):
    rows = P(("groups", "expert"), None)
    in_specs = (rows,) * 4 + (P(("groups", "expert")), P(), rows, rows) + (
        P("expert", None, None),
    ) * 3
    return jax.shard_map(local, mesh=mesh, in_specs=in_specs, out_specs=rows, check_vma=False)
```

```python
import functools
import math

import jax
import jax.numpy as jnp
from jax import lax
from jax.experimental import pallas as pl
from jax.experimental.pallas import tpu as pltpu
from jax.sharding import PartitionSpec as P

HEAD = 128
QUERY_HEADS = 32
KV_HEADS = 2
GROUP = QUERY_HEADS // KV_HEADS
SHARDS = 4
CAP = 6
SLOTS = 8
CUT = 4
PIECE = CUT * CAP
TILE = 128
KEYS = 512
STEP = KEYS // TILE
KV_ROWS = TILE + 16
SCALE = math.log2(math.e) / math.sqrt(HEAD)
LOW = -1e30
EXTRA = 16
F32 = jnp.float32
BF16 = jnp.bfloat16
VMEM = pl.BlockSpec(memory_space=pltpu.VMEM)
SMEM = pl.BlockSpec(memory_space=pltpu.SMEM)
ANY = pl.BlockSpec(memory_space=pl.ANY)
HBM = pl.BlockSpec(memory_space=pltpu.HBM)


def dot(a, b, ca=1, cb=0):
    return lax.dot_general(a, b, (((ca,), (cb,)), ((), ())), preferred_element_type=F32)


def reach(n):
    longest = n * TILE // 2 + 256
    return (longest - 1 + TILE - 1) // TILE


def slot_rows(routes, experts):
    members = jnp.concatenate(
        [jnp.max((routes == e).astype(F32), axis=0, keepdims=True) for e in experts], axis=0
    )
    count = len(experts)
    padded = -(-count // 8) * 8
    wide = members
    if padded > count:
        wide = jnp.concatenate([members, jnp.zeros((padded - count, TILE), F32)], axis=0)
    before = lax.broadcasted_iota(jnp.int32, (TILE, TILE), 0) < lax.broadcasted_iota(
        jnp.int32, (TILE, TILE), 1
    )
    ranks = dot(wide.astype(BF16), before.astype(F32).astype(BF16))
    return members, ranks


def one_hot(targets, count):
    shape = (targets.shape[0], count) if targets.shape[1] == 1 else (count, targets.shape[1])
    axis = 1 if targets.shape[1] == 1 else 0
    places = lax.broadcasted_iota(jnp.int32, shape, axis).astype(F32)
    return jnp.where(places == targets, 1.0, 0.0).astype(BF16)


def split(x, size):
    whole = jnp.floor((x + 0.5) / size)
    return whole, x - whole * size


def travel_row(x, senders, slots):
    chunk, rest = split(x, senders * slots)
    sender, slot = split(rest, slots)
    return jnp.where(slot < CAP, sender * PIECE + chunk * CAP + slot, -1.0)


def numbers(shape, axis):
    return lax.broadcasted_iota(jnp.int32, shape, axis).astype(F32)


def pack_kernel(docs_ref, keys_ref, values_ref, out_ref, docs, values, sems):
    moves = [
        pltpu.make_async_copy(values_ref, values, sems.at[0]),
        pltpu.make_async_copy(docs_ref, docs, sems.at[1]),
        pltpu.make_async_copy(
            keys_ref, out_ref.at[pl.ds(0, TILE), pl.ds(0, KV_HEADS * HEAD)], sems.at[2]
        ),
    ]
    for move in moves:
        move.start()
    moves[0].wait()
    for h in range(KV_HEADS):
        out_ref[0:TILE, (KV_HEADS + h) * HEAD : (KV_HEADS + h + 1) * HEAD] = (
            values[:, h * HEAD : (h + 1) * HEAD].astype(F32).T.astype(BF16)
        )
    moves[1].wait()
    out_ref[TILE:KV_ROWS, :] = jnp.zeros((KV_ROWS - TILE, 4 * HEAD), BF16)
    out_ref[TILE:KV_ROWS, 0:HEAD] = jnp.broadcast_to(
        docs[...].astype(F32), (KV_ROWS - TILE, TILE)
    ).astype(BF16)
    moves[2].wait()


def select_kernel(planes, pos_ref, *refs):
    sources, (qs_ref, xs_ref, facts_ref, mix_ref, gather_ref, spread_ref) = refs[:5], refs[5:11]
    routes_ref, docs_ref, q_ref, x_ref, gates_ref, stack, sems = refs[11:]
    moves = [
        pltpu.make_async_copy(source, target, sems.at[i])
        for i, (source, target) in enumerate(zip(sources, refs[11:16]))
    ]
    for move in moves:
        move.start()
    for move in moves:
        move.wait()
    z = pos_ref[0] // SHARDS
    experts = [lax.rem(z + k, planes) for k in range(planes)]
    routes, gates = routes_ref[...], gates_ref[...]
    members, ranks = slot_rows(routes, experts)
    slot = lax.broadcasted_iota(jnp.int32, (SLOTS, TILE), 0).astype(F32)
    mix = []
    for k, e in enumerate(experts):
        gate = jnp.sum(jnp.where(routes == e, gates, 0.0), axis=0, keepdims=True)
        mix.append(jnp.where(ranks[k : k + 1] == slot, gate, 0.0))
    mix = jnp.concatenate(mix, axis=0).T
    mix_high = mix.astype(BF16)
    mix_ref[:, : planes * SLOTS] = mix_high
    mix_ref[:, planes * SLOTS :] = (mix - mix_high.astype(F32)).astype(BF16)
    size = gather_ref.shape[0]
    gather_ref[...] = one_hot(travel_row(numbers((size, 1), 0), size // PIECE, CAP), size)
    spread_ref[...] = one_hot(travel_row(numbers((1, size), 1), size // PIECE, CAP), size)
    docs = docs_ref[...].astype(F32)
    token = lax.broadcasted_iota(jnp.int32, (1, TILE), 1).astype(F32)
    facts = jnp.concatenate(
        [token, docs, jnp.ones((1, TILE), F32), jnp.zeros((5, TILE), F32)], axis=0
    ).astype(BF16)
    picks = [
        jnp.where(ranks[k : k + 1] == slot, members[k : k + 1], 0.0) for k in range(planes)
    ]
    rows = planes * CAP
    plane, place = split(numbers((rows, 1), 0), CAP)
    compact = one_hot(plane * SLOTS + place, planes * SLOTS)
    chooser = dot(compact, jnp.concatenate(picks, axis=0).astype(BF16)).astype(BF16)
    lane, _ = split(numbers((rows * GROUP, 1), 0), GROUP)
    lane_pick = dot(one_hot(lane, rows), chooser).astype(BF16)
    known = dot(facts, lane_pick, 1, 1)
    facts_ref[...] = jnp.concatenate(
        [known[0:1], known[1:2] + (1.0 - known[2:3]) * docs[:, 0:1], known[2:]], axis=0
    )
    q_rows = dot(chooser, q_ref[...])
    xs_ref[...] = dot(chooser, x_ref[...])
    for h in range(KV_HEADS):
        for g in range(GROUP):
            a = h * GROUP + g
            stack[pl.ds(g, rows, stride=GROUP), :] = q_rows[:, a * HEAD : (a + 1) * HEAD]
        qs_ref[h] = stack[...].T.astype(BF16)


def doc_starts(n, pos, held):
    sums = [jnp.zeros((1, TILE), F32) for _ in range(3)]
    for s in range(n):
        docs = held[s, TILE:KV_ROWS, 0:HEAD].astype(F32)[0:1]
        ahead = (pos - s < 0).astype(F32)
        behind = (pos - s > reach(n)).astype(F32)
        known = 1.0 - ahead - behind
        docs = jnp.where(known > 0.5, docs, 0.0) + 9.0 * ahead
        for d in range(3):
            sums[d] = sums[d] + jnp.where(docs < d + 1.0, 1.0, 0.0)
    return [jnp.sum(s, axis=1, keepdims=True) for s in sums]


def starts_of(docs, starts):
    first = jnp.zeros_like(docs)
    for d in range(3):
        first = jnp.where(docs == d + 1.0, starts[d], first)
    return first


def key_steps(pos, place, first, bias_ref, step, state):
    low = jnp.min(first).astype(jnp.int32) // KEYS
    last = pos // STEP
    clear = jnp.minimum((jnp.max(first).astype(jnp.int32) + KEYS - 1) // KEYS, last)

    def edge(j, carried):
        kb = jnp.where(j < clear - low, low + j, last)
        key_at = (kb * KEYS + lax.broadcasted_iota(jnp.int32, (KEYS, 1), 0)).astype(F32)
        bias_ref[...] = jnp.where((key_at >= first) & (key_at <= place), 0.0, LOW)
        return step(kb, carried, True)

    state = lax.fori_loop(0, clear - low + 1, edge, state)
    return lax.fori_loop(clear, last, lambda kb, carried: step(kb, carried, False), state)


def by_kv_head(heads):
    groups = [(h, [a for a in heads if a // GROUP == h]) for h in range(KV_HEADS)]
    return [(h, own) for h, own in groups if own]


def keys_of(held, kb, heads):
    low, high = heads[0] * HEAD, (heads[-1] + 1) * HEAD
    return jnp.concatenate(
        [held[STEP * kb + t, 0:TILE, low:high] for t in range(STEP)], axis=0
    )


def values_of(held, kb, h):
    at = (KV_HEADS + h) * HEAD
    values = jnp.concatenate(
        [held[STEP * kb + t, 0:TILE, at : at + HEAD] for t in range(STEP)], axis=1
    )
    return jnp.concatenate([values, jnp.ones((EXTRA, KEYS), BF16)], axis=0)


def flash(pos, held, chains, bias_ref, place, first):
    for _, _, acc in chains:
        acc[...] = jnp.zeros(acc.shape, F32)

    def step(kb, tops, masked):
        out = []
        for (queries, heads, acc), old in zip(chains, tops):
            scores = dot(keys_of(held, kb, heads), queries[...])
            if masked:
                copies = scores.shape[1] // bias_ref.shape[1]
                scores = scores + jnp.concatenate([bias_ref[...]] * copies, axis=1)
            top = jnp.maximum(old, jnp.max(scores, axis=0, keepdims=True))
            weights = jnp.exp2((scores - top) * SCALE).astype(BF16)
            share = weights.shape[1] // len(heads)
            added = [
                dot(values_of(held, kb, h), weights[:, i * share : (i + 1) * share])
                for i, h in enumerate(heads)
            ]
            acc[...] = acc[...] * jnp.exp2((old - top) * SCALE) + jnp.concatenate(added, axis=1)
            out.append(top)
        return tuple(out)

    tops = tuple(jnp.full((1, acc.shape[1]), LOW, F32) for _, _, acc in chains)
    key_steps(pos, place, first, bias_ref, step, tops)
    return [(acc[0:HEAD, :] / acc[HEAD : HEAD + 1, :]).T for _, _, acc in chains]


def place_pieces(n, senders, pos, pieces, held, sems):
    planes = n // SHARDS
    z, y, c = pos // SHARDS, (pos // 2) % 2, pos % 2
    copies = []
    for i, (piece, row, flip_c, flip_y, k) in enumerate(senders):
        sender = lax.rem(z - k + planes, planes) * SHARDS + (y ^ flip_y) * 2 + (c ^ flip_c)
        copy = pltpu.make_async_copy(
            pieces[piece].at[pl.ds(row, KV_ROWS)], held.at[sender], sems.at[i]
        )
        copy.start()
        copies.append(copy)
    return copies


def collect_kernel(n, senders, pos_ref, *refs):
    *pieces, held, sems = refs
    for copy in place_pieces(n, senders, pos_ref[0], pieces, held, sems):
        copy.wait()


def routed_kernel(n, senders, pos_ref, gain_ref, qs_ref, xs_ref, facts_ref, _, *refs):
    planes = n // SHARDS
    count = len(senders)
    pieces, outs, held = refs[:2], refs[2 : 2 + planes], refs[2 + planes]
    acc, bias, q_scr, stack, state, gain, sems = refs[3 + planes :]
    pos = pos_ref[0]
    copies = place_pieces(n, senders, pos, pieces, held, sems)
    copies.append(pltpu.make_async_copy(gain_ref, gain, sems.at[count]))
    copies[-1].start()
    for copy in copies:
        copy.wait()
    starts = doc_starts(n, pos, held)
    lanes = q_scr.shape[1] // KV_HEADS
    q_scr[...] = jnp.zeros(q_scr.shape, BF16)
    rows = lanes // GROUP
    base = (pos * TILE).astype(F32)
    width = state.shape[1] // CUT
    row = numbers((CUT * rows, 1), 0)
    plane, rest = split(row, PIECE)
    chunk, slot = split(rest, CAP)
    order = one_hot(chunk * rows + plane * CAP + slot, CUT * rows)
    for part in range(xs_ref.shape[0] // rows):
        at = slice(part * lanes, (part + 1) * lanes)
        for h in range(KV_HEADS):
            q_scr[h * HEAD : (h + 1) * HEAD, h * lanes : (h + 1) * lanes] = qs_ref[h, :, at]
        (done,) = flash(
            pos,
            held,
            [(q_scr, list(range(KV_HEADS)), acc)],
            bias,
            facts_ref[0:1, at] + base,
            starts_of(facts_ref[1:2, at], starts),
        )
        for h in range(KV_HEADS):
            stack[...] = done[h * lanes : (h + 1) * lanes]
            for g in range(GROUP):
                lane = (h * GROUP + g) * HEAD
                state[:, lane : lane + HEAD] = (
                    xs_ref[part * rows : (part + 1) * rows, lane : lane + HEAD]
                    + stack[pl.ds(g, rows, stride=GROUP), :]
                )
        hidden = state[...]
        mean = jnp.mean(hidden * hidden, axis=1, keepdims=True)
        normed = hidden * lax.rsqrt(mean + 1e-06) * gain[...]
        chunks = [normed[:, q * width : (q + 1) * width] for q in range(CUT)]
        sent = dot(order, jnp.concatenate(chunks, axis=0).astype(BF16))
        for k in range(rows // CAP):
            outs[part * (rows // CAP) + k][...] = sent[k * PIECE : (k + 1) * PIECE].astype(BF16)


def expert_kernel(n, count, *refs):
    pieces = refs[:count]
    wg, wu, wd = refs[count : count + 3]
    gather, spread, _, keep_ref, send_ref, rows = refs[count + 3 :]
    step = pieces[0].shape[1]
    senders = min(n, 16)
    size, total = senders * PIECE, n * PIECE
    half = total // 2
    kept = senders * CAP
    for at in range(0, total, size):
        parts, first = [], 0
        for piece in pieces:
            low, high = max(at - first, 0), min(at + size - first, piece.shape[0])
            if low < high:
                parts.append(piece[low:high, :].astype(F32))
            first += piece.shape[0]
        came = dot(gather[...], jnp.concatenate(parts, axis=0).astype(BF16)).astype(BF16)
        for q in range(CUT):
            rows[:, q * step : (q + 1) * step] = came[q * kept : (q + 1) * kept]
        gate = dot(rows[...], wg[...])
        up = dot(rows[...], wu[...])
        act = (gate / (1.0 + jnp.exp(-gate)) * up).astype(BF16)
        parts = [dot(act, wd[:, q * step : (q + 1) * step]).astype(BF16) for q in range(CUT)]
        out = dot(spread[...], jnp.concatenate(parts, axis=0)).astype(BF16)
        if size > half:
            keep_ref[...] = out[:half]
            send_ref[...] = out[half:]
        elif at < half:
            keep_ref[at : at + size] = out
        else:
            send_ref[at - half : at - half + size] = out


def own_kernel(n, heads, loads, pos_ref, held, q_ref, x_ref, _, *refs):
    sources, (h_ref, done_ref) = refs[:loads], refs[loads : loads + 2]
    targets = refs[loads + 2 : 2 * loads + 2]
    bias, sems, *scratch = refs[2 * loads + 2 :]
    moves = [
        pltpu.make_async_copy(source.at[0], target, sems.at[i])
        for i, (source, target) in enumerate(zip(sources, targets))
    ]
    for move in moves:
        move.start()
    done_ref[...] = jnp.zeros((8, TILE), F32)
    pos = pos_ref[0]
    starts = doc_starts(n, pos, held)
    first = starts_of(held[pos, TILE:KV_ROWS, 0:HEAD].astype(F32)[0:1], starts)
    place = (pos * TILE + lax.broadcasted_iota(jnp.int32, (1, TILE), 1)).astype(F32)
    chains = []
    for i, (h, own) in enumerate(by_kv_head(heads)):
        queries, acc = scratch[2 * i : 2 * i + 2]
        chains.append((queries, [h], acc))
        for j, a in enumerate(own):
            rows = q_ref[:, a * HEAD : (a + 1) * HEAD].astype(F32)
            queries[:, j * TILE : (j + 1) * TILE] = rows.T.astype(BF16)
    done = jnp.concatenate(flash(pos, held, chains, bias, place, first), axis=0)
    for j, a in enumerate(heads):
        h_ref[:, j * HEAD : (j + 1) * HEAD] = (
            x_ref[:, a * HEAD : (a + 1) * HEAD].astype(F32) + done[j * TILE : (j + 1) * TILE]
        )
    for move in moves:
        move.wait()


def combine_kernel(planes, widths, mix_ref, *refs):
    count = len(widths)
    halves, parts = refs[:count], refs[count : count + planes]
    _, out_ref, buffer, sems = refs[count + planes :]
    slots = planes * SLOTS
    came = jnp.concatenate([p[...].astype(F32) for p in parts], axis=0).astype(BF16)
    order = one_hot(travel_row(numbers((CUT * slots, 1), 0), planes, SLOTS), planes * PIECE)
    came = dot(order, came).astype(BF16)
    size = buffer.shape[1] // CUT
    moves = []
    for q in range(CUT):
        rows = came[q * slots : (q + 1) * slots]
        part = dot(mix_ref[...], jnp.concatenate([rows, rows], axis=0))
        at = 0
        for h, width in zip(halves, widths):
            low, high = max(at, q * size), min(at + width, (q + 1) * size)
            if low < high:
                buffer[:, low:high] = (
                    h[:, low - at : high - at] + part[:, low - q * size : high - q * size]
                ).astype(BF16)
            at += width
        columns = pl.ds(q * size, size)
        moves.append(
            pltpu.make_async_copy(buffer.at[:, columns], out_ref.at[:, columns], sems.at[q])
        )
        moves[-1].start()
    for move in moves:
        move.wait()


def pin(x):
    return pltpu.with_memory_space_constraint(x, pltpu.HBM)


def params(mib):
    return pltpu.CompilerParams(vmem_limit_bytes=mib * 1024 * 1024)


def local(
    resid, queries, keys, values, doc_ids, norm_gain, routes, route_weights, w_gate, w_up, w_down
):
    n = lax.axis_size("expert")
    planes = n // SHARDS
    pos = lax.axis_index("expert").astype(jnp.int32).reshape(1)
    tokens, width = queries.shape
    hidden = w_gate.shape[2]
    routes_t = routes.T
    gates_t = route_weights.T
    docs = doc_ids.reshape(1, tokens)
    small = 24 if n <= 16 else 60
    back = reach(n)

    packed = pl.pallas_call(
        pack_kernel,
        out_shape=jax.ShapeDtypeStruct((KV_ROWS, 4 * HEAD), BF16),
        in_specs=[HBM] * 3,
        out_specs=VMEM,
        scratch_shapes=[
            pltpu.VMEM((1, tokens), jnp.int32),
            pltpu.VMEM((tokens, KV_HEADS * HEAD), BF16),
            pltpu.SemaphoreType.DMA((3,)),
        ],
        compiler_params=params(8),
        name="pack",
    )(pin(docs), pin(keys), pin(values))

    def move(value, pairs):
        return lax.ppermute(value, "expert", pairs)

    def needed(k, y_from, y_to):
        gaps = [
            k * SHARDS + 2 * (y_to - y_from) + (to - of) for to in range(2) for of in range(2)
        ]
        return any(0 <= gap <= back for gap in gaps)

    far = max(k for k in range(planes) if any(needed(k, a, b) for a in (0, 1) for b in (0, 1)))
    size = min(n // 2, 16) * PIECE
    q_rows, x_rows, facts, mix, gather, spread = pl.pallas_call(
        functools.partial(select_kernel, planes),
        out_shape=[
            jax.ShapeDtypeStruct((KV_HEADS, HEAD, planes * CAP * GROUP), BF16),
            jax.ShapeDtypeStruct((planes * CAP, width), F32),
            jax.ShapeDtypeStruct((8, planes * CAP * GROUP), F32),
            jax.ShapeDtypeStruct((tokens, 2 * planes * SLOTS), BF16),
            jax.ShapeDtypeStruct((size, size), BF16),
            jax.ShapeDtypeStruct((size, size), BF16),
        ],
        in_specs=[SMEM] + [HBM] * 5,
        out_specs=[VMEM] * 6,
        scratch_shapes=[
            pltpu.VMEM(routes_t.shape, jnp.int32),
            pltpu.VMEM(docs.shape, jnp.int32),
            pltpu.VMEM(queries.shape, BF16),
            pltpu.VMEM(resid.shape, BF16),
            pltpu.VMEM(gates_t.shape, F32),
            pltpu.VMEM((planes * CAP * GROUP, HEAD), F32),
            pltpu.SemaphoreType.DMA((5,)),
        ],
        compiler_params=params(small),
        name="select",
    )(pos, *map(pin, (routes_t, docs, queries, resid, gates_t)))

    flip_y = [(s, s ^ 2) for s in range(n)]
    flip_c = [(s, s ^ 1) for s in range(n)]
    jump = {s: s + far * SHARDS - 2 for s in range(n - far * SHARDS) if s & 2}
    jump.update({to: s for s, to in jump.items()})
    jumped = move(packed, [(s, jump.get(s, s)) for s in range(n)])
    along = [packed] + [
        move(packed, [(s, (s + k * SHARDS) % n) for s in range(n)]) for k in range(1, far)
    ]
    along[1], q_rows = lax.optimization_barrier((along[1], q_rows))
    across = []
    for k in range(far):
        if k > 1 and k == far - 1:
            along[k], across = lax.optimization_barrier((along[k], across))
        across.append(move(along[k], [(s, s ^ 2 if s >= k * SHARDS else s) for s in range(n)]))
    early, late = along + [jumped] + across[:-1], across[-1:]
    sides = [(0, k) for k in range(far)] + [(1, far)] + [(1, k) for k in range(far - 1)]
    early.append(move(jnp.concatenate(early, axis=0), flip_c))
    early_senders = [(i, 0, 0, *side) for i, side in enumerate(sides)]
    early_senders += [(len(sides), i * KV_ROWS, 1, *side) for i, side in enumerate(sides)]
    early_senders += [(0, 0, flip, 0, far) for flip in (0, 1)]
    late_senders = [(flip, 0, flip, 1, far - 1) for flip in (0, 1)]
    held_shape = jax.ShapeDtypeStruct((n, KV_ROWS, 4 * HEAD), BF16)
    held = pl.pallas_call(
        functools.partial(collect_kernel, n, early_senders),
        out_shape=held_shape,
        in_specs=[SMEM] + [ANY] * len(early),
        out_specs=VMEM,
        scratch_shapes=[pltpu.SemaphoreType.DMA((len(early_senders),))],
        compiler_params=params(small),
        cost_estimate=pl.CostEstimate(flops=0, bytes_accessed=1000, transcendentals=0),
        name="collect",
    )(pos, *early)

    lanes = min(planes, 4) * CAP * GROUP
    late[0], held = lax.optimization_barrier((late[0], held))
    late.append(move(late[0], flip_c))
    *sent, held = pl.pallas_call(
        functools.partial(routed_kernel, n, late_senders),
        out_shape=[jax.ShapeDtypeStruct((PIECE, width // CUT), BF16)] * planes
        + [held_shape],
        in_specs=[SMEM, HBM] + [VMEM] * 4 + [ANY] * len(late),
        out_specs=[VMEM] * (planes + 1),
        scratch_shapes=[
            pltpu.VMEM((HEAD + EXTRA, KV_HEADS * lanes), F32),
            pltpu.VMEM((KEYS, lanes), F32),
            pltpu.VMEM((KV_HEADS * HEAD, KV_HEADS * lanes), BF16),
            pltpu.VMEM((lanes, HEAD), F32),
            pltpu.VMEM((lanes // GROUP, width), F32),
            pltpu.VMEM((1, width), F32),
            pltpu.SemaphoreType.DMA((len(late_senders) + 1,)),
        ],
        input_output_aliases={5: planes},
        compiler_params=params(small),
        name="routed",
    )(pos, pin(norm_gain.reshape(1, width)), q_rows, x_rows, facts, held, *late)

    def own(heads, after, *sources):
        lanes = [len(own) * TILE for _, own in by_kv_head(heads)]
        return pl.pallas_call(
            functools.partial(own_kernel, n, heads, len(sources)),
            out_shape=[
                jax.ShapeDtypeStruct((tokens, len(heads) * HEAD), F32),
                jax.ShapeDtypeStruct((8, TILE), F32),
            ]
            + [jax.ShapeDtypeStruct(w.shape[1:], BF16) for w in sources],
            in_specs=[SMEM, VMEM, VMEM, VMEM, ANY] + [HBM] * len(sources),
            out_specs=[VMEM] * (2 + len(sources)),
            scratch_shapes=[pltpu.VMEM((KEYS, TILE), F32), pltpu.SemaphoreType.DMA((3,))]
            + [
                shape
                for count in lanes
                for shape in (
                    pltpu.VMEM((HEAD, count), BF16),
                    pltpu.VMEM((HEAD + EXTRA, count), F32),
                )
            ],
            compiler_params=params(small),
            cost_estimate=pl.CostEstimate(
                flops=2_000_000_000, bytes_accessed=8_000_000, transcendentals=2_000_000
            ),
            name="own",
        )(pos, held, queries, resid, after, *map(pin, sources))

    half0, done, *weights = own(range(10), sent[0], w_gate, w_up, w_down)
    half1, late = own(range(10, GROUP), done)
    halves = [half0, half1]

    come = [
        move(sent[k], [(s, (s + k * SHARDS) % n) for s in range(n)]) for k in range(1, planes)
    ]
    next_door = move(sent[0], flip_y)
    come, next_door, done = lax.optimization_barrier((come, next_door, done))
    here = [sent[0], jnp.concatenate(come, axis=0)]
    there = [next_door, move(here[1], flip_y)]
    mate = move(jnp.concatenate(here, axis=0), flip_c)
    half = jax.ShapeDtypeStruct((n * PIECE // 4, width // CUT), BF16)

    def expert(pieces, after):
        return pl.pallas_call(
            functools.partial(expert_kernel, n // 2, len(pieces)),
            out_shape=[half, half],
            in_specs=[VMEM] * (len(pieces) + 5) + [ANY],
            out_specs=[VMEM, VMEM],
            scratch_shapes=[pltpu.VMEM((min(n // 2, 16) * CAP, width), BF16)],
            compiler_params=params(16),
            cost_estimate=pl.CostEstimate(
                flops=600_000_000, bytes_accessed=2_000_000, transcendentals=20_000
            ),
            name="expert",
        )(*pieces, *weights, gather, spread, after)

    keep, send = expert(here + [mate], done)
    there, late, keep = lax.optimization_barrier((there, late, keep))
    mine = keep.astype(F32) + move(send, flip_c).astype(F32)
    mate = move(jnp.concatenate(there, axis=0), flip_c)
    keep, send = expert(there + [mate], late)
    half2, done = own(range(GROUP, QUERY_HEADS), keep)
    halves.append(half2)
    theirs = keep.astype(F32) + move(send, flip_c).astype(F32)
    other = move(theirs.astype(BF16), flip_y)
    other, done = lax.optimization_barrier((other, done))
    total = (mine + other.astype(F32)).astype(BF16)
    parts = [total[:PIECE]]
    for k in range(1, planes):
        parts.append(
            move(
                total[k * PIECE : (k + 1) * PIECE], [(s, (s - k * SHARDS) % n) for s in range(n)]
            )
        )

    widths = [h.shape[1] for h in halves]
    return pl.pallas_call(
        functools.partial(combine_kernel, planes, widths),
        out_shape=jax.ShapeDtypeStruct((tokens, width), BF16),
        in_specs=[VMEM] * (1 + len(halves) + planes) + [ANY],
        out_specs=HBM,
        scratch_shapes=[pltpu.VMEM((tokens, width), BF16), pltpu.SemaphoreType.DMA((CUT,))],
        compiler_params=params(small),
        name="combine",
    )(mix, *halves, *parts, done)


def solution(mesh):
    rows = P(("groups", "expert"), None)
    in_specs = (rows,) * 4 + (P(("groups", "expert")), P(), rows, rows) + (
        P("expert", None, None),
    ) * 3
    return jax.shard_map(local, mesh=mesh, in_specs=in_specs, out_specs=rows, check_vma=False)
```

```python
import functools
import math

import jax
import jax.numpy as jnp
from jax import lax
from jax.experimental import pallas as pl
from jax.experimental.pallas import tpu as pltpu
from jax.sharding import PartitionSpec as P

HEAD = 128
QUERY_HEADS = 32
KV_HEADS = 2
GROUP = QUERY_HEADS // KV_HEADS
SHARDS = 4
CAP = 6
SLOTS = 8
CUT = 4
PIECE = CUT * CAP
TILE = 128
KEYS = 512
STEP = KEYS // TILE
KV_ROWS = TILE + 16
SCALE = math.log2(math.e) / math.sqrt(HEAD)
LOW = -1e30
EXTRA = 16
F32 = jnp.float32
BF16 = jnp.bfloat16
VMEM = pl.BlockSpec(memory_space=pltpu.VMEM)
SMEM = pl.BlockSpec(memory_space=pltpu.SMEM)
ANY = pl.BlockSpec(memory_space=pl.ANY)
HBM = pl.BlockSpec(memory_space=pltpu.HBM)


def dot(a, b, ca=1, cb=0):
    return lax.dot_general(a, b, (((ca,), (cb,)), ((), ())), preferred_element_type=F32)


def reach(n):
    longest = n * TILE // 2 + 256
    return (longest - 1 + TILE - 1) // TILE


def slot_rows(routes, experts):
    members = jnp.concatenate(
        [jnp.max((routes == e).astype(F32), axis=0, keepdims=True) for e in experts], axis=0
    )
    count = len(experts)
    padded = -(-count // 8) * 8
    wide = members
    if padded > count:
        wide = jnp.concatenate([members, jnp.zeros((padded - count, TILE), F32)], axis=0)
    before = lax.broadcasted_iota(jnp.int32, (TILE, TILE), 0) < lax.broadcasted_iota(
        jnp.int32, (TILE, TILE), 1
    )
    ranks = dot(wide.astype(BF16), before.astype(F32).astype(BF16))
    return members, ranks


def one_hot(targets, count):
    shape = (targets.shape[0], count) if targets.shape[1] == 1 else (count, targets.shape[1])
    axis = 1 if targets.shape[1] == 1 else 0
    places = lax.broadcasted_iota(jnp.int32, shape, axis).astype(F32)
    return jnp.where(places == targets, 1.0, 0.0).astype(BF16)


def split(x, size):
    whole = jnp.floor((x + 0.5) / size)
    return whole, x - whole * size


def travel_row(x, senders, slots):
    chunk, rest = split(x, senders * slots)
    sender, slot = split(rest, slots)
    return jnp.where(slot < CAP, sender * PIECE + chunk * CAP + slot, -1.0)


def numbers(shape, axis):
    return lax.broadcasted_iota(jnp.int32, shape, axis).astype(F32)


def pack_kernel(docs_ref, keys_ref, values_ref, out_ref, docs, values, sems):
    moves = [
        pltpu.make_async_copy(values_ref, values, sems.at[0]),
        pltpu.make_async_copy(docs_ref, docs, sems.at[1]),
        pltpu.make_async_copy(
            keys_ref, out_ref.at[pl.ds(0, TILE), pl.ds(0, KV_HEADS * HEAD)], sems.at[2]
        ),
    ]
    for move in moves:
        move.start()
    moves[0].wait()
    for h in range(KV_HEADS):
        out_ref[0:TILE, (KV_HEADS + h) * HEAD : (KV_HEADS + h + 1) * HEAD] = (
            values[:, h * HEAD : (h + 1) * HEAD].astype(F32).T.astype(BF16)
        )
    moves[1].wait()
    out_ref[TILE:KV_ROWS, :] = jnp.zeros((KV_ROWS - TILE, 4 * HEAD), BF16)
    out_ref[TILE:KV_ROWS, 0:HEAD] = jnp.broadcast_to(
        docs[...].astype(F32), (KV_ROWS - TILE, TILE)
    ).astype(BF16)
    moves[2].wait()


def select_kernel(planes, pos_ref, *refs):
    sources, (qs_ref, xs_ref, facts_ref, mix_ref, gather_ref, spread_ref) = refs[:5], refs[5:11]
    routes_ref, docs_ref, q_ref, x_ref, gates_ref, stack, sems = refs[11:]
    moves = [
        pltpu.make_async_copy(source, target, sems.at[i])
        for i, (source, target) in enumerate(zip(sources, refs[11:16]))
    ]
    for move in moves:
        move.start()
    for move in moves:
        move.wait()
    z = pos_ref[0] // SHARDS
    experts = [lax.rem(z + k, planes) for k in range(planes)]
    routes, gates = routes_ref[...], gates_ref[...]
    members, ranks = slot_rows(routes, experts)
    slot = lax.broadcasted_iota(jnp.int32, (SLOTS, TILE), 0).astype(F32)
    mix = []
    for k, e in enumerate(experts):
        gate = jnp.sum(jnp.where(routes == e, gates, 0.0), axis=0, keepdims=True)
        mix.append(jnp.where(ranks[k : k + 1] == slot, gate, 0.0))
    mix = jnp.concatenate(mix, axis=0).T
    mix_high = mix.astype(BF16)
    mix_ref[:, : planes * SLOTS] = mix_high
    mix_ref[:, planes * SLOTS :] = (mix - mix_high.astype(F32)).astype(BF16)
    size = gather_ref.shape[0]
    gather_ref[...] = one_hot(travel_row(numbers((size, 1), 0), size // PIECE, CAP), size)
    spread_ref[...] = one_hot(travel_row(numbers((1, size), 1), size // PIECE, CAP), size)
    docs = docs_ref[...].astype(F32)
    token = lax.broadcasted_iota(jnp.int32, (1, TILE), 1).astype(F32)
    facts = jnp.concatenate(
        [token, docs, jnp.ones((1, TILE), F32), jnp.zeros((5, TILE), F32)], axis=0
    ).astype(BF16)
    picks = [
        jnp.where(ranks[k : k + 1] == slot, members[k : k + 1], 0.0) for k in range(planes)
    ]
    rows = planes * CAP
    plane, place = split(numbers((rows, 1), 0), CAP)
    compact = one_hot(plane * SLOTS + place, planes * SLOTS)
    chooser = dot(compact, jnp.concatenate(picks, axis=0).astype(BF16)).astype(BF16)
    lane, _ = split(numbers((rows * GROUP, 1), 0), GROUP)
    lane_pick = dot(one_hot(lane, rows), chooser).astype(BF16)
    known = dot(facts, lane_pick, 1, 1)
    facts_ref[...] = jnp.concatenate(
        [known[0:1], known[1:2] + (1.0 - known[2:3]) * docs[:, 0:1], known[2:]], axis=0
    )
    q_rows = dot(chooser, q_ref[...])
    xs_ref[...] = dot(chooser, x_ref[...])
    for h in range(KV_HEADS):
        for g in range(GROUP):
            a = h * GROUP + g
            stack[pl.ds(g, rows, stride=GROUP), :] = q_rows[:, a * HEAD : (a + 1) * HEAD]
        qs_ref[h] = stack[...].T.astype(BF16)


def doc_starts(n, pos, held):
    sums = [jnp.zeros((1, TILE), F32) for _ in range(3)]
    for s in range(n):
        docs = held[s, TILE:KV_ROWS, 0:HEAD].astype(F32)[0:1]
        ahead = (pos - s < 0).astype(F32)
        behind = (pos - s > reach(n)).astype(F32)
        known = 1.0 - ahead - behind
        docs = jnp.where(known > 0.5, docs, 0.0) + 9.0 * ahead
        for d in range(3):
            sums[d] = sums[d] + jnp.where(docs < d + 1.0, 1.0, 0.0)
    return [jnp.sum(s, axis=1, keepdims=True) for s in sums]


def starts_of(docs, starts):
    first = jnp.zeros_like(docs)
    for d in range(3):
        first = jnp.where(docs == d + 1.0, starts[d], first)
    return first


def key_steps(pos, place, first, bias_ref, step, state):
    low = jnp.min(first).astype(jnp.int32) // KEYS
    last = pos // STEP
    clear = jnp.minimum((jnp.max(first).astype(jnp.int32) + KEYS - 1) // KEYS, last)

    def edge(j, carried):
        kb = jnp.where(j < clear - low, low + j, last)
        key_at = (kb * KEYS + lax.broadcasted_iota(jnp.int32, (KEYS, 1), 0)).astype(F32)
        bias_ref[...] = jnp.where((key_at >= first) & (key_at <= place), 0.0, LOW)
        return step(kb, carried, True)

    state = lax.fori_loop(0, clear - low + 1, edge, state)
    return lax.fori_loop(clear, last, lambda kb, carried: step(kb, carried, False), state)


def by_kv_head(heads):
    groups = [(h, [a for a in heads if a // GROUP == h]) for h in range(KV_HEADS)]
    return [(h, own) for h, own in groups if own]


def keys_of(held, kb, heads):
    low, high = heads[0] * HEAD, (heads[-1] + 1) * HEAD
    return jnp.concatenate(
        [held[STEP * kb + t, 0:TILE, low:high] for t in range(STEP)], axis=0
    )


def values_of(held, kb, h):
    at = (KV_HEADS + h) * HEAD
    values = jnp.concatenate(
        [held[STEP * kb + t, 0:TILE, at : at + HEAD] for t in range(STEP)], axis=1
    )
    return jnp.concatenate([values, jnp.ones((EXTRA, KEYS), BF16)], axis=0)


def flash(pos, held, chains, bias_ref, place, first):
    for _, _, acc in chains:
        acc[...] = jnp.zeros(acc.shape, F32)

    def step(kb, tops, masked):
        out = []
        for (queries, heads, acc), old in zip(chains, tops):
            scores = dot(keys_of(held, kb, heads), queries[...])
            if masked:
                copies = scores.shape[1] // bias_ref.shape[1]
                scores = scores + jnp.concatenate([bias_ref[...]] * copies, axis=1)
            top = jnp.maximum(old, jnp.max(scores, axis=0, keepdims=True))
            weights = jnp.exp2((scores - top) * SCALE).astype(BF16)
            share = weights.shape[1] // len(heads)
            added = [
                dot(values_of(held, kb, h), weights[:, i * share : (i + 1) * share])
                for i, h in enumerate(heads)
            ]
            acc[...] = acc[...] * jnp.exp2((old - top) * SCALE) + jnp.concatenate(added, axis=1)
            out.append(top)
        return tuple(out)

    tops = tuple(jnp.full((1, acc.shape[1]), LOW, F32) for _, _, acc in chains)
    key_steps(pos, place, first, bias_ref, step, tops)
    return [(acc[0:HEAD, :] / acc[HEAD : HEAD + 1, :]).T for _, _, acc in chains]


def place_pieces(n, senders, pos, pieces, held, sems):
    planes = n // SHARDS
    z, y, c = pos // SHARDS, (pos // 2) % 2, pos % 2
    copies = []
    for i, (piece, row, flip_c, flip_y, k) in enumerate(senders):
        sender = lax.rem(z - k + planes, planes) * SHARDS + (y ^ flip_y) * 2 + (c ^ flip_c)
        copy = pltpu.make_async_copy(
            pieces[piece].at[pl.ds(row, KV_ROWS)], held.at[sender], sems.at[i]
        )
        copy.start()
        copies.append(copy)
    return copies


def collect_kernel(n, senders, pos_ref, *refs):
    *pieces, held, sems = refs
    for copy in place_pieces(n, senders, pos_ref[0], pieces, held, sems):
        copy.wait()


def routed_kernel(n, senders, pos_ref, gain_ref, qs_ref, xs_ref, facts_ref, _, *refs):
    planes = n // SHARDS
    count = len(senders)
    pieces, outs, held = refs[:2], refs[2 : 2 + planes], refs[2 + planes]
    acc, bias, q_scr, stack, state, gain, sems = refs[3 + planes :]
    pos = pos_ref[0]
    copies = place_pieces(n, senders, pos, pieces, held, sems)
    copies.append(pltpu.make_async_copy(gain_ref, gain, sems.at[count]))
    copies[-1].start()
    for copy in copies:
        copy.wait()
    starts = doc_starts(n, pos, held)
    lanes = q_scr.shape[1] // KV_HEADS
    q_scr[...] = jnp.zeros(q_scr.shape, BF16)
    rows = lanes // GROUP
    base = (pos * TILE).astype(F32)
    width = state.shape[1] // CUT
    row = numbers((CUT * rows, 1), 0)
    plane, rest = split(row, PIECE)
    chunk, slot = split(rest, CAP)
    order = one_hot(chunk * rows + plane * CAP + slot, CUT * rows)
    for part in range(xs_ref.shape[0] // rows):
        at = slice(part * lanes, (part + 1) * lanes)
        for h in range(KV_HEADS):
            q_scr[h * HEAD : (h + 1) * HEAD, h * lanes : (h + 1) * lanes] = qs_ref[h, :, at]
        (done,) = flash(
            pos,
            held,
            [(q_scr, list(range(KV_HEADS)), acc)],
            bias,
            facts_ref[0:1, at] + base,
            starts_of(facts_ref[1:2, at], starts),
        )
        for h in range(KV_HEADS):
            stack[...] = done[h * lanes : (h + 1) * lanes]
            for g in range(GROUP):
                lane = (h * GROUP + g) * HEAD
                state[:, lane : lane + HEAD] = (
                    xs_ref[part * rows : (part + 1) * rows, lane : lane + HEAD]
                    + stack[pl.ds(g, rows, stride=GROUP), :]
                )
        hidden = state[...]
        mean = jnp.mean(hidden * hidden, axis=1, keepdims=True)
        normed = hidden * lax.rsqrt(mean + 1e-06) * gain[...]
        chunks = [normed[:, q * width : (q + 1) * width] for q in range(CUT)]
        sent = dot(order, jnp.concatenate(chunks, axis=0).astype(BF16))
        for k in range(rows // CAP):
            outs[part * (rows // CAP) + k][...] = sent[k * PIECE : (k + 1) * PIECE].astype(BF16)


def expert_kernel(n, count, *refs):
    pieces = refs[:count]
    wg, wu, wd = refs[count : count + 3]
    gather, spread, _, keep_ref, send_ref, rows = refs[count + 3 :]
    step = pieces[0].shape[1]
    senders = min(n, 16)
    size, total = senders * PIECE, n * PIECE
    half = total // 2
    kept = senders * CAP
    for at in range(0, total, size):
        parts, first = [], 0
        for piece in pieces:
            low, high = max(at - first, 0), min(at + size - first, piece.shape[0])
            if low < high:
                parts.append(piece[low:high, :].astype(F32))
            first += piece.shape[0]
        came = dot(gather[...], jnp.concatenate(parts, axis=0).astype(BF16)).astype(BF16)
        for q in range(CUT):
            rows[:, q * step : (q + 1) * step] = came[q * kept : (q + 1) * kept]
        gate = dot(rows[...], wg[...])
        up = dot(rows[...], wu[...])
        act = (gate / (1.0 + jnp.exp(-gate)) * up).astype(BF16)
        parts = [dot(act, wd[:, q * step : (q + 1) * step]).astype(BF16) for q in range(CUT)]
        out = dot(spread[...], jnp.concatenate(parts, axis=0)).astype(BF16)
        if size > half:
            keep_ref[...] = out[:half]
            send_ref[...] = out[half:]
        elif at < half:
            keep_ref[at : at + size] = out
        else:
            send_ref[at - half : at - half + size] = out


def own_kernel(n, heads, loads, pos_ref, held, q_ref, x_ref, _, *refs):
    sources, (h_ref, done_ref) = refs[:loads], refs[loads : loads + 2]
    targets = refs[loads + 2 : 2 * loads + 2]
    bias, sems, *scratch = refs[2 * loads + 2 :]
    moves = [
        pltpu.make_async_copy(source.at[0], target, sems.at[i])
        for i, (source, target) in enumerate(zip(sources, targets))
    ]
    for move in moves:
        move.start()
    done_ref[...] = jnp.zeros((8, TILE), F32)
    pos = pos_ref[0]
    starts = doc_starts(n, pos, held)
    first = starts_of(held[pos, TILE:KV_ROWS, 0:HEAD].astype(F32)[0:1], starts)
    place = (pos * TILE + lax.broadcasted_iota(jnp.int32, (1, TILE), 1)).astype(F32)
    chains = []
    for i, (h, own) in enumerate(by_kv_head(heads)):
        queries, acc = scratch[2 * i : 2 * i + 2]
        chains.append((queries, [h], acc))
        for j, a in enumerate(own):
            rows = q_ref[:, a * HEAD : (a + 1) * HEAD].astype(F32)
            queries[:, j * TILE : (j + 1) * TILE] = rows.T.astype(BF16)
    done = jnp.concatenate(flash(pos, held, chains, bias, place, first), axis=0)
    for j, a in enumerate(heads):
        h_ref[:, j * HEAD : (j + 1) * HEAD] = (
            x_ref[:, a * HEAD : (a + 1) * HEAD].astype(F32) + done[j * TILE : (j + 1) * TILE]
        )
    for move in moves:
        move.wait()


def combine_kernel(planes, widths, mix_ref, *refs):
    count = len(widths)
    halves, parts = refs[:count], refs[count : count + planes]
    _, out_ref, buffer, sems = refs[count + planes :]
    slots = planes * SLOTS
    came = jnp.concatenate([p[...].astype(F32) for p in parts], axis=0).astype(BF16)
    order = one_hot(travel_row(numbers((CUT * slots, 1), 0), planes, SLOTS), planes * PIECE)
    came = dot(order, came).astype(BF16)
    size = buffer.shape[1] // CUT
    moves = []
    for q in range(CUT):
        rows = came[q * slots : (q + 1) * slots]
        part = dot(mix_ref[...], jnp.concatenate([rows, rows], axis=0))
        at = 0
        for h, width in zip(halves, widths):
            low, high = max(at, q * size), min(at + width, (q + 1) * size)
            if low < high:
                buffer[:, low:high] = (
                    h[:, low - at : high - at] + part[:, low - q * size : high - q * size]
                ).astype(BF16)
            at += width
        columns = pl.ds(q * size, size)
        moves.append(
            pltpu.make_async_copy(buffer.at[:, columns], out_ref.at[:, columns], sems.at[q])
        )
        moves[-1].start()
    for move in moves:
        move.wait()


def pin(x):
    return pltpu.with_memory_space_constraint(x, pltpu.HBM)


def params(mib):
    return pltpu.CompilerParams(vmem_limit_bytes=mib * 1024 * 1024)


def local(
    resid, queries, keys, values, doc_ids, norm_gain, routes, route_weights, w_gate, w_up, w_down
):
    n = lax.axis_size("expert")
    planes = n // SHARDS
    pos = lax.axis_index("expert").astype(jnp.int32).reshape(1)
    tokens, width = queries.shape
    hidden = w_gate.shape[2]
    routes_t = routes.T
    gates_t = route_weights.T
    docs = doc_ids.reshape(1, tokens)
    small = 24 if n <= 16 else 60
    back = reach(n)

    packed = pl.pallas_call(
        pack_kernel,
        out_shape=jax.ShapeDtypeStruct((KV_ROWS, 4 * HEAD), BF16),
        in_specs=[HBM] * 3,
        out_specs=VMEM,
        scratch_shapes=[
            pltpu.VMEM((1, tokens), jnp.int32),
            pltpu.VMEM((tokens, KV_HEADS * HEAD), BF16),
            pltpu.SemaphoreType.DMA((3,)),
        ],
        compiler_params=params(8),
        name="pack",
    )(pin(docs), pin(keys), pin(values))

    def move(value, pairs):
        return lax.ppermute(value, "expert", pairs)

    def needed(k, y_from, y_to):
        gaps = [
            k * SHARDS + 2 * (y_to - y_from) + (to - of) for to in range(2) for of in range(2)
        ]
        return any(0 <= gap <= back for gap in gaps)

    far = max(k for k in range(planes) if any(needed(k, a, b) for a in (0, 1) for b in (0, 1)))
    size = min(n // 2, 16) * PIECE
    q_rows, x_rows, facts, mix, gather, spread = pl.pallas_call(
        functools.partial(select_kernel, planes),
        out_shape=[
            jax.ShapeDtypeStruct((KV_HEADS, HEAD, planes * CAP * GROUP), BF16),
            jax.ShapeDtypeStruct((planes * CAP, width), F32),
            jax.ShapeDtypeStruct((8, planes * CAP * GROUP), F32),
            jax.ShapeDtypeStruct((tokens, 2 * planes * SLOTS), BF16),
            jax.ShapeDtypeStruct((size, size), BF16),
            jax.ShapeDtypeStruct((size, size), BF16),
        ],
        in_specs=[SMEM] + [HBM] * 5,
        out_specs=[VMEM] * 6,
        scratch_shapes=[
            pltpu.VMEM(routes_t.shape, jnp.int32),
            pltpu.VMEM(docs.shape, jnp.int32),
            pltpu.VMEM(queries.shape, BF16),
            pltpu.VMEM(resid.shape, BF16),
            pltpu.VMEM(gates_t.shape, F32),
            pltpu.VMEM((planes * CAP * GROUP, HEAD), F32),
            pltpu.SemaphoreType.DMA((5,)),
        ],
        compiler_params=params(small),
        name="select",
    )(pos, *map(pin, (routes_t, docs, queries, resid, gates_t)))

    flip_y = [(s, s ^ 2) for s in range(n)]
    flip_c = [(s, s ^ 1) for s in range(n)]
    jump = {s: s + far * SHARDS - 2 for s in range(n - far * SHARDS) if s & 2}
    jump.update({to: s for s, to in jump.items()})
    jumped = move(packed, [(s, jump.get(s, s)) for s in range(n)])
    along = [packed] + [
        move(packed, [(s, (s + k * SHARDS) % n) for s in range(n)]) for k in range(1, far)
    ]
    along[1], q_rows = lax.optimization_barrier((along[1], q_rows))
    across = []
    for k in range(far):
        if k > 1 and k == far - 1:
            along[k], across = lax.optimization_barrier((along[k], across))
        across.append(move(along[k], [(s, s ^ 2 if s >= k * SHARDS else s) for s in range(n)]))
    early, late = along + [jumped] + across[:-1], across[-1:]
    sides = [(0, k) for k in range(far)] + [(1, far)] + [(1, k) for k in range(far - 1)]
    early.append(move(jnp.concatenate(early, axis=0), flip_c))
    early_senders = [(i, 0, 0, *side) for i, side in enumerate(sides)]
    early_senders += [(len(sides), i * KV_ROWS, 1, *side) for i, side in enumerate(sides)]
    early_senders += [(0, 0, flip, 0, far) for flip in (0, 1)]
    late_senders = [(flip, 0, flip, 1, far - 1) for flip in (0, 1)]
    held_shape = jax.ShapeDtypeStruct((n, KV_ROWS, 4 * HEAD), BF16)
    held = pl.pallas_call(
        functools.partial(collect_kernel, n, early_senders),
        out_shape=held_shape,
        in_specs=[SMEM] + [ANY] * len(early),
        out_specs=VMEM,
        scratch_shapes=[pltpu.SemaphoreType.DMA((len(early_senders),))],
        compiler_params=params(small),
        cost_estimate=pl.CostEstimate(flops=0, bytes_accessed=1000, transcendentals=0),
        name="collect",
    )(pos, *early)

    lanes = min(planes, 4) * CAP * GROUP
    late[0], held = lax.optimization_barrier((late[0], held))
    late.append(move(late[0], flip_c))
    *sent, held = pl.pallas_call(
        functools.partial(routed_kernel, n, late_senders),
        out_shape=[jax.ShapeDtypeStruct((PIECE, width // CUT), BF16)] * planes
        + [held_shape],
        in_specs=[SMEM, HBM] + [VMEM] * 4 + [ANY] * len(late),
        out_specs=[VMEM] * (planes + 1),
        scratch_shapes=[
            pltpu.VMEM((HEAD + EXTRA, KV_HEADS * lanes), F32),
            pltpu.VMEM((KEYS, lanes), F32),
            pltpu.VMEM((KV_HEADS * HEAD, KV_HEADS * lanes), BF16),
            pltpu.VMEM((lanes, HEAD), F32),
            pltpu.VMEM((lanes // GROUP, width), F32),
            pltpu.VMEM((1, width), F32),
            pltpu.SemaphoreType.DMA((len(late_senders) + 1,)),
        ],
        input_output_aliases={5: planes},
        compiler_params=params(small),
        name="routed",
    )(pos, pin(norm_gain.reshape(1, width)), q_rows, x_rows, facts, held, *late)

    def own(heads, after, *sources):
        lanes = [len(own) * TILE for _, own in by_kv_head(heads)]
        return pl.pallas_call(
            functools.partial(own_kernel, n, heads, len(sources)),
            out_shape=[
                jax.ShapeDtypeStruct((tokens, len(heads) * HEAD), F32),
                jax.ShapeDtypeStruct((8, TILE), F32),
            ]
            + [jax.ShapeDtypeStruct(w.shape[1:], BF16) for w in sources],
            in_specs=[SMEM, VMEM, VMEM, VMEM, ANY] + [HBM] * len(sources),
            out_specs=[VMEM] * (2 + len(sources)),
            scratch_shapes=[pltpu.VMEM((KEYS, TILE), F32), pltpu.SemaphoreType.DMA((3,))]
            + [
                shape
                for count in lanes
                for shape in (
                    pltpu.VMEM((HEAD, count), BF16),
                    pltpu.VMEM((HEAD + EXTRA, count), F32),
                )
            ],
            compiler_params=params(small),
            cost_estimate=pl.CostEstimate(
                flops=2_000_000_000, bytes_accessed=8_000_000, transcendentals=2_000_000
            ),
            name="own",
        )(pos, held, queries, resid, after, *map(pin, sources))

    half0, done, *weights = own(range(9), sent[0], w_gate, w_up, w_down)
    half1, late = own(range(9, GROUP), done)
    halves = [half0, half1]

    come = [
        move(sent[k], [(s, (s + k * SHARDS) % n) for s in range(n)]) for k in range(1, planes)
    ]
    next_door = move(sent[0], flip_y)
    come, next_door, done = lax.optimization_barrier((come, next_door, done))
    here = [sent[0], jnp.concatenate(come, axis=0)]
    there = [next_door, move(here[1], flip_y)]
    mate = move(jnp.concatenate(here, axis=0), flip_c)
    half = jax.ShapeDtypeStruct((n * PIECE // 4, width // CUT), BF16)

    def expert(pieces, after):
        return pl.pallas_call(
            functools.partial(expert_kernel, n // 2, len(pieces)),
            out_shape=[half, half],
            in_specs=[VMEM] * (len(pieces) + 5) + [ANY],
            out_specs=[VMEM, VMEM],
            scratch_shapes=[pltpu.VMEM((min(n // 2, 16) * CAP, width), BF16)],
            compiler_params=params(16),
            cost_estimate=pl.CostEstimate(
                flops=600_000_000, bytes_accessed=2_000_000, transcendentals=20_000
            ),
            name="expert",
        )(*pieces, *weights, gather, spread, after)

    keep, send = expert(here + [mate], done)
    there, late, keep = lax.optimization_barrier((there, late, keep))
    mine = keep.astype(F32) + move(send, flip_c).astype(F32)
    mate = move(jnp.concatenate(there, axis=0), flip_c)
    keep, send = expert(there + [mate], late)
    half2, done = own(range(GROUP, QUERY_HEADS), keep)
    halves.append(half2)
    theirs = keep.astype(F32) + move(send, flip_c).astype(F32)
    other = move(theirs.astype(BF16), flip_y)
    other, done = lax.optimization_barrier((other, done))
    total = (mine + other.astype(F32)).astype(BF16)
    parts = [total[:PIECE]]
    for k in range(1, planes):
        parts.append(
            move(
                total[k * PIECE : (k + 1) * PIECE], [(s, (s - k * SHARDS) % n) for s in range(n)]
            )
        )

    widths = [h.shape[1] for h in halves]
    return pl.pallas_call(
        functools.partial(combine_kernel, planes, widths),
        out_shape=jax.ShapeDtypeStruct((tokens, width), BF16),
        in_specs=[VMEM] * (1 + len(halves) + planes) + [ANY],
        out_specs=HBM,
        scratch_shapes=[pltpu.VMEM((tokens, width), BF16), pltpu.SemaphoreType.DMA((CUT,))],
        compiler_params=params(small),
        name="combine",
    )(mix, *halves, *parts, done)


def solution(mesh):
    rows = P(("groups", "expert"), None)
    in_specs = (rows,) * 4 + (P(("groups", "expert")), P(), rows, rows) + (
        P("expert", None, None),
    ) * 3
    return jax.shard_map(local, mesh=mesh, in_specs=in_specs, out_specs=rows, check_vma=False)
```
